32 devices in a mesh: grp: 2 (over y), gx: 4 (over z), gy: 2 (over x), gz: 2 (over core).
Axes of the slice: x: 2, y: 2, z: 4, core: 2. Of those that a mesh axis runs over, the one named last changes fastest.
Arguments:
- parent_old: float32 [8, 384, 512], P(None, ('grp', 'gx', 'gz'), 'gy'), parts along dimension 1, may hold values from -6 to 6
- parent_source: float32 [8, 384, 512], P(None, ('grp', 'gx', 'gz'), 'gy'), parts along dimension 1, may hold values from -4 to 4
- parent_coefs: float32 [2, 8], replicated, may hold values from 0.02 to 0.1
- nest_old: float32 [8, 1152, 768], P(None, ('grp', 'gx', 'gz'), 'gy'), parts along dimension 1, may hold values from -6 to 6
- nest_source: float32 [8, 1152, 768], P(None, ('grp', 'gx', 'gz'), 'gy'), parts along dimension 1, may hold values from -2 to 2
- nest_coefs: float32 [2, 8], replicated, may hold values from 0.02 to 0.1
- offset_x: int32 [2], P('grp'), parts along dimension 0, may hold values from 1 to 23
- offset_y: int32 [2], P('grp'), parts along dimension 0, may hold values from 1 to 255
Outputs:
- parent_new: float32 [8, 384, 512], P(None, ('grp', 'gx', 'gz'), 'gy'), parts along dimension 1
- nest_new: float32 [8, 1152, 768], P(None, ('grp', 'gx', 'gz'), 'gy'), parts along dimension 1
The draws below stay inside these ranges and needn't reach their ends.
There are 2 independent parts, one for each index of `grp`. The reference program is written for one: setup_inputs(seed, part) draws one part's arguments, and reference() takes and returns one part's arrays. A program takes and returns all parts, laid end to end along the dimension named above; an argument that names none is the same for every part. Nothing has to cross between parts.
All inputs are finite; a program needn't handle non-finite values.
Results may differ from the reference program's by a relative error of at most 0.00002.
Values sent between devices are 32-bit elements; how exact they have to be, the bound alone decides.
No kernel may reach another device: no remote copies, remote signals or barrier semaphores. Data moves between devices by JAX's collectives and lax.ppermute only.
A program may use at most 128 MiB of HBM per device.

```python
import math
import jax
import jax.numpy as jnp
from jax import lax

LEVELS = 8
PX_DEV = 24
RATIO = 3
SUBSTEPS = 3
RIM = 6
PX = 192
PY = 512
BAND = 256
NX = 576
NY = 768


def shard_levels(own_key, dims, pieces, least, high):
    loudness = 1.0
    for axis_at, blocks in pieces:
        steps = jax.random.uniform(jax.random.fold_in(jax.random.fold_in(own_key, 6), axis_at), (blocks,), jnp.float32, least / len(pieces), high / len(pieces))
        loudness = loudness * jnp.repeat(jnp.exp(steps), dims[axis_at] // blocks).reshape((-1,) + (1,) * (len(dims) - 1 - axis_at))
    return loudness


def noise(rng, extent, scale, most, split=(), dtype=jnp.bfloat16):
    values = jax.random.normal(rng, extent, jnp.float32) * scale
    if len(split) > 0:
        values = shard_levels(rng, extent, split, -0.22, 0.18) * values
    return jnp.clip(values, min=-most, max=most).astype(dtype)


def setup_inputs(seed: int = 0, part: int = 0) -> dict:
    key_of = jax.random.split(jax.random.key(seed), 9)
    own_keys = jax.random.split(jax.random.fold_in(key_of[8], part), 9)
    parent_old = noise(own_keys[0], (LEVELS, PX, PY), 1.0, 6.0, ((1, 8), (2, 2)), jnp.float32)
    parent_source = noise(own_keys[1], (LEVELS, PX, PY), 0.3, 4.0, ((1, 8), (2, 2)), jnp.float32)
    parent_coefs = jnp.clip(jnp.exp(jax.random.uniform(key_of[2], (2, LEVELS), jnp.float32, math.log(0.02), math.log(0.1))), 0.02, 0.1)
    nest_old = noise(own_keys[3], (LEVELS, NX, NY), 1.0, 6.0, ((1, 8), (2, 2)), jnp.float32)
    nest_source = noise(own_keys[4], (LEVELS, NX, NY), 0.15, 2.0, ((1, 8), (2, 2)), jnp.float32)
    nest_coefs = jnp.clip(jnp.exp(jax.random.uniform(key_of[5], (2, LEVELS), jnp.float32, math.log(0.02), math.log(0.1))), 0.02, 0.1)
    offset_x = jax.random.randint(own_keys[6], (1,), 1, PX_DEV).astype(jnp.int32)
    offset_y = jax.random.randint(own_keys[7], (1,), 1, PY - BAND).astype(jnp.int32)
    return {"parent_old": parent_old, "parent_source": parent_source, "parent_coefs": parent_coefs, "nest_old": nest_old, "nest_source": nest_source, "nest_coefs": nest_coefs, "offset_x": offset_x, "offset_y": offset_y}


def diffuse(padded, coefs_h, coefs_v, source):
    center = padded[1:-1, 1:-1, 1:-1]
    lateral = padded[1:-1, 2:, 1:-1] + padded[1:-1, :-2, 1:-1] + padded[1:-1, 1:-1, 2:] + padded[1:-1, 1:-1, :-2] - 4.0 * center
    vertical = padded[2:, 1:-1, 1:-1] + padded[:-2, 1:-1, 1:-1] - 2.0 * center
    return center + coefs_h[:, None, None] * lateral + coefs_v[:, None, None] * vertical + source


def pad_channel(grid_field):
    padded = jnp.pad(grid_field, ((1, 1), (0, 0), (1, 1)))
    return jnp.concatenate([padded[:, -1:], padded, padded[:, :1]], axis=1)


def reference(parent_old, parent_source, parent_coefs, nest_old, nest_source, nest_coefs, offset_x, offset_y):
    shift_x = offset_x[0].astype(jnp.int32)
    shift_y = offset_y[0].astype(jnp.int32)
    parent_step = diffuse(pad_channel(parent_old), parent_coefs[0], parent_coefs[1], parent_source)

    def edge_cols(grid_field):
        rolled = jnp.roll(grid_field, -shift_x, axis=1)
        south = lax.dynamic_slice_in_dim(rolled, shift_y, 2, axis=2)
        north = lax.dynamic_slice_in_dim(rolled, shift_y + BAND - 2, 2, axis=2)
        return jnp.concatenate([south, north], axis=2)

    old_edges = edge_cols(parent_old)
    new_edges = edge_cols(parent_step)
    nest_now = nest_old
    for substep in range(1, SUBSTEPS + 1):
        weight = substep / SUBSTEPS
        edge_now = old_edges + weight * (new_edges - old_edges)
        fine_edges = jnp.repeat(edge_now, RATIO, axis=1)
        nest_now = diffuse(pad_channel(nest_now), nest_coefs[0], nest_coefs[1], nest_source)
        nest_now = nest_now.at[:, :, :RIM].set(jnp.repeat(fine_edges[:, :, 0:2], RATIO, axis=2))
        nest_now = nest_now.at[:, :, NY - RIM:].set(jnp.repeat(fine_edges[:, :, 2:4], RATIO, axis=2))
    coarse = nest_now.reshape(LEVELS, PX, RATIO, BAND, RATIO).mean(axis=(2, 4))
    rolled = jnp.roll(parent_step, -shift_x, axis=1)
    rolled = lax.dynamic_update_slice_in_dim(rolled, coarse[:, :, 2:BAND - 2], shift_y + 2, axis=2)
    parent_new = jnp.roll(rolled, shift_x, axis=1)
    return parent_new, nest_now
```

```python
import functools

import jax
import jax.numpy as jnp
from jax import lax
from jax.experimental import pallas as pl
from jax.experimental.pallas import tpu as pltpu
from jax.sharding import PartitionSpec as P

RATIO = 3
SUBSTEPS = 3
RIM = 6
LANES = 128
PARENT_LANE = 48
STRIP_LANE = 64
STRIP_SOURCE = 96
SOURCE_ROW = 24
TAIL_ROW = 40
VMEM = pltpu.VMEM
LIMIT = 24 * 1024 * 1024
HIGHEST = lax.Precision.HIGHEST


def iota(shape, dim):
    return lax.broadcasted_iota(jnp.int32, shape, dim)


def whole():
    return pl.BlockSpec(memory_space=VMEM)


def scalars():
    return pl.BlockSpec(memory_space=pltpu.SMEM)


def params():
    return pltpu.CompilerParams(vmem_limit_bytes=LIMIT)


def cost(flops, moved):
    return pl.CostEstimate(flops=flops, bytes_accessed=moved, transcendentals=0)


def tile(ref, level, index):
    return ref[level, :, index * LANES : (index + 1) * LANES]


def pack_columns(parts, band, oy_ref, nest, source, parent, parent_source, *rest):
    outs, (old_buf, src_buf, sems) = rest[:parts], rest[parts:]
    levels, rows, cols = nest.shape
    parent_cols = parent.shape[2]
    me = lax.axis_index("gy")
    oy = oy_ref[0]
    sides = [1] if parts == 2 else [1, parts - 1]
    copies = []
    for at, step in enumerate(sides):
        right = (me == 0) if parts == 2 else jnp.bool_(step == 1)
        start = pl.multiple_of(jnp.where(right, cols - LANES, 0), LANES)
        pair = [
            pltpu.make_async_copy(
                ref.at[:, :, pl.ds(start, LANES)], buf.at[at], sems.at[at, which]
            )
            for which, (ref, buf) in enumerate(((nest, old_buf), (source, src_buf)))
        ]
        for copy in pair:
            copy.start()
        copies.append((right, pair))
    lane = iota((parent.shape[1], LANES), 1)

    def strip(dest):
        base = jnp.where(dest == 0, oy - 1, oy + band - 3) - me * parent_cols
        total = jnp.zeros(lane.shape, jnp.float32)
        for ref, first in ((parent, STRIP_LANE), (parent_source, STRIP_SOURCE)):
            for level in range(levels):
                found = jnp.zeros(lane.shape, jnp.float32)
                for at in range(parent_cols // LANES):
                    place = lane + (at * LANES - base)
                    found = jnp.where(
                        (place >= 0) & (place < 4), tile(ref, level, at), found
                    )
                turn = (16384 + first + 4 * level - base) & (LANES - 1)
                total = total + pltpu.roll(found, turn, 1)
        return total

    outs[0][...] = strip(me)
    for step in range(1, parts):
        out = outs[step]
        part = strip(lax.rem(me + step, parts))
        if step not in sides:
            out[...] = part
            continue
        at = sides.index(step)
        right, pair = copies[at]
        first = jnp.where(right, LANES - 3, 0)
        for level in range(levels):
            edge = jnp.where(
                right, tile(parent, level, parent_cols // LANES - 1), tile(parent, level, 0)
            )
            edge = jnp.where(lane == jnp.where(right, LANES - 1, 0), edge, 0.0)
            turn = (LANES + PARENT_LANE + level - jnp.where(right, LANES - 1, 0)) & (LANES - 1)
            part = part + pltpu.roll(edge, turn, 1)
        for copy in pair:
            copy.wait()
        fine = iota((rows, LANES), 1) - first
        wanted = (fine >= 0) & (fine < 3)
        total = jnp.zeros((rows, LANES), jnp.float32)
        for level in range(levels):
            for buf, shift in ((old_buf, 0), (src_buf, 3)):
                value = jnp.where(wanted, buf[at, level], 0.0)
                turn = (LANES + 6 * level + shift - first) & (LANES - 1)
                total = total + pltpu.roll(value, turn, 1)
        out[...] = total
        out[: part.shape[0], :] += part


def with_columns(tiles, left, right, me, parts, place):
    lane = iota(left.shape, 1)
    from_right = pltpu.roll(right, (LANES - place) % LANES, 1)
    from_left = pltpu.roll(left, (2 * LANES - 3 - place) % LANES, 1)
    if parts == 2:
        tiles[0] = jnp.where((lane < 3) & (me == 0), from_right, tiles[0])
        tiles[-1] = jnp.where((lane >= LANES - 3) & (me == 1), from_left, tiles[-1])
        return tiles
    extra = jnp.where(lane < 3, from_right, jnp.where(lane >= LANES - 3, from_left, 0.0))
    return tiles + [extra]


def pack_rows(
    parts, old_top, old_end, src_top, src_end, par_top, par_end, own_strip, *rest
):
    columns = rest[: parts - 1]
    up, down, far, strip_out = rest[parts - 1 :]
    levels, _, cols = old_top.shape
    me = lax.axis_index("gy")
    left, right = columns[0], columns[-1]
    rows = left.shape[0]
    strip_rows = own_strip.shape[0]
    lane = iota((strip_rows, LANES), 1)
    strips = own_strip[...]
    for message in columns:
        strips = strips + message[:strip_rows, :]
    strips = jnp.where(lane >= STRIP_LANE, strips, 0.0)
    strip_out[...] = strips
    far[...] = strips[:8]
    pieces = cols // LANES
    for out, old, src, first, at, src_at in (
        (up, old_end, src_end, rows - 8, 5, 6),
        (down, old_top, src_top, 0, 0, 0),
    ):
        y_left = left[first : first + 8, :]
        y_right = right[first : first + 8, :]
        for level in range(levels):
            for ref, shift, row, count, base in (
                (old, 0, at, 3, 0),
                (src, 3, src_at, 2, SOURCE_ROW),
            ):
                tiles = [tile(ref, level, piece) for piece in range(pieces)]
                tiles = with_columns(tiles, y_left, y_right, me, parts, 6 * level + shift)
                for piece, value in enumerate(tiles):
                    out[
                        base + count * level : base + count * (level + 1),
                        piece * LANES : (piece + 1) * LANES,
                    ] = value[row : row + count]
    parent_cols = par_top.shape[2]
    for level in range(levels):
        up[TAIL_ROW + level : TAIL_ROW + level + 1, :parent_cols] = par_end[level, 7:8, :]
        down[TAIL_ROW + level : TAIL_ROW + level + 1, :parent_cols] = par_top[level, 0:1, :]
    up[TAIL_ROW : TAIL_ROW + 8, parent_cols : parent_cols + LANES] = strips[strip_rows - 8 :]
    down[TAIL_ROW : TAIL_ROW + 8, parent_cols : parent_cols + LANES] = strips[:8]
    down[TAIL_ROW + 8 : TAIL_ROW + 16, :LANES] = strips[8:16]
    down[TAIL_ROW + 8 : TAIL_ROW + 16, LANES : 2 * LANES] = strips[16:24]


def nest_steps(
    parts,
    parent_cols,
    ox_ref,
    parent_coefs,
    coefs,
    nest,
    source,
    strips,
    before,
    after,
    beyond,
    y_left,
    y_right,
    nest_out,
    coarse_out,
    ping,
    pong,
    src,
    rim_old,
    rim_diff,
    result,
    thin,
    sems,
):
    levels, rows, cols = nest.shape
    ring = ping.shape[1]
    width = ping.shape[2]
    pieces = cols // LANES
    strip_rows = strips.shape[0]
    me = lax.axis_index("gy")
    ox = ox_ref[0]
    loads = [
        pltpu.make_async_copy(nest, ping.at[1 : levels + 1, :rows, :cols], sems.at[0]),
        pltpu.make_async_copy(source, src.at[:, :rows, :cols], sems.at[1]),
    ]
    for copy in loads:
        copy.start()

    old = jnp.concatenate(
        [
            strips[...],
            after[TAIL_ROW : TAIL_ROW + 8, parent_cols : parent_cols + LANES],
            after[TAIL_ROW + 8 : TAIL_ROW + 16, :LANES],
            after[TAIL_ROW + 8 : TAIL_ROW + 16, LANES : 2 * LANES],
            jnp.where(
                iota((8, LANES), 0) == 0,
                beyond[...],
                jnp.where(
                    iota((8, LANES), 0) == 7,
                    before[TAIL_ROW : TAIL_ROW + 8, parent_cols : parent_cols + LANES],
                    0.0,
                ),
            ),
        ],
        axis=0,
    )
    count = old.shape[0]
    lane = iota(old.shape, 1)
    coef_h = jnp.zeros(old.shape, jnp.float32)
    coef_v = jnp.zeros(old.shape, jnp.float32)
    for level in range(levels):
        here = lane >= STRIP_LANE + 4 * level
        coef_h = jnp.where(here, parent_coefs[0, level], coef_h)
        coef_v = jnp.where(here, parent_coefs[1, level], coef_v)
    lateral = (
        pltpu.roll(old, 1, 0)
        + pltpu.roll(old, count - 1, 0)
        + pltpu.roll(old, 1, 1)
        + pltpu.roll(old, LANES - 1, 1)
        - 4.0 * old
    )
    higher = jnp.where(lane < STRIP_SOURCE - 4, pltpu.roll(old, LANES - 4, 1), 0.0)
    vertical = pltpu.roll(old, 4, 1) + higher - 2.0 * old
    forcing = pltpu.roll(old, LANES - (STRIP_SOURCE - STRIP_LANE), 1)
    diff = coef_h * lateral + coef_v * vertical + forcing
    index = iota((ring, count), 0)
    parent_row = jnp.where(index < rows + 3, (index * 171) >> 9, -1) + ox
    pick = (iota((ring, count), 1) == parent_row).astype(jnp.float32)
    picked = jnp.dot(
        pick,
        jnp.concatenate([old, diff], axis=1),
        precision=HIGHEST,
        preferred_element_type=jnp.float32,
    )
    lane = iota((ring, LANES), 1)
    first = jnp.where(me == 0, 0, LANES - RIM)
    column = jnp.where((lane >= first + 3) & (lane < first + RIM), 2, 1)
    for level in range(levels):
        at = column + (STRIP_LANE + 4 * level)
        rim_old[level] = jnp.take_along_axis(picked[:, :LANES], at, axis=1)
        rim_diff[level] = jnp.take_along_axis(picked[:, LANES:], at, axis=1)

    zero = jnp.zeros((ring, width), jnp.float32)
    for buf in (ping, pong):
        buf[0] = zero
        buf[levels + 1] = zero
    for level in range(levels):
        for buf, lead, base, n in ((ping, 1, 0, 3), (src, 0, SOURCE_ROW, 2)):
            rest = slice(base + n * level, base + n * (level + 1))
            buf[level + lead, rows : rows + n, :] = after[rest, :]
            buf[level + lead, ring - n : ring, :] = before[rest, :]
    for copy in loads:
        copy.wait()
    left = y_left[...]
    right = y_right[...]
    for level in range(levels):
        for buf, lead, shift in ((ping, 1, 0), (src, 0, 3)):
            edges = [
                buf[level + lead, :rows, :LANES],
                buf[level + lead, :rows, cols - LANES : cols],
            ]
            edges = with_columns(edges, left, right, me, parts, 6 * level + shift)
            if parts == 2:
                buf[level + lead, :rows, :LANES] = edges[0]
                buf[level + lead, :rows, cols - LANES : cols] = edges[1]
            else:
                buf[level + lead, :rows, cols:] = edges[2]

    lane = iota((8, LANES), 1)
    sub = iota((8, width), 0)
    is_south = me == 0
    is_north = me == parts - 1

    def substep(here, there, weight, last):
        low = 0 if last or parts > 2 else 3
        south = (lane >= low) & (lane < RIM) & is_south
        north = (lane >= LANES - RIM) & (lane < LANES - low) & is_north
        tiles = rows // 8 if last else ring // 8

        def one_level(level, carry):
            ch = coefs[0, level]
            cv = coefs[1, level]
            centre = 1.0 - 4.0 * ch - 2.0 * cv

            def row_tile(t):
                t = t % (ring // 8)
                return here[level + 1, 8 * t : 8 * t + 8, :]

            now = row_tile(-1)
            down_before = pltpu.roll(now, 1, 0)
            now = row_tile(0)
            up_now = pltpu.roll(now, 7, 0)
            for t in range(tiles):
                following = row_tile(t + 1)
                down_now = pltpu.roll(now, 1, 0)
                up_next = pltpu.roll(following, 7, 0)
                around = jnp.where(sub == 0, down_before, down_now) + jnp.where(
                    sub == 7, up_next, up_now
                )
                around = around + (pltpu.roll(now, 1, 1) + pltpu.roll(now, width - 1, 1))
                span = slice(8 * t, 8 * t + 8)
                stacked = here[level, span, :] + here[level + 2, span, :]
                value = centre * now + ch * around + (cv * stacked + src[level, span, :])
                rim = rim_old[level, span, :] + weight * rim_diff[level, span, :]
                if last:
                    store, at, stop = there, level, pieces
                else:
                    store, at, stop = there, level + 1, width // LANES
                for piece in range(stop):
                    part = value[:, piece * LANES : (piece + 1) * LANES]
                    if piece == 0:
                        part = jnp.where(south, rim, part)
                    if piece == pieces - 1:
                        part = jnp.where(north, rim, part)
                    store[at, span, piece * LANES : (piece + 1) * LANES] = part
                down_before, now, up_now = down_now, following, up_next
            return carry

        lax.fori_loop(0, levels, one_level, 0)

    substep(ping, pong, 1.0 / 3.0, False)
    substep(pong, ping, 2.0 / 3.0, False)
    substep(ping, result, 1.0, True)
    store = pltpu.make_async_copy(result, nest_out, sems.at[2])
    store.start()
    foot = cols // RATIO
    offset = iota((cols, foot), 0) - RATIO * iota((cols, foot), 1)
    gather = ((offset >= 0) & (offset < RATIO)).astype(jnp.float32)
    flat = result[...].reshape(levels * rows, cols)
    thin[...] = jnp.dot(
        flat, gather, precision=HIGHEST, preferred_element_type=jnp.float32
    )
    total = levels * rows // RATIO
    means = (
        thin[pl.ds(0, total, RATIO), :]
        + thin[pl.ds(1, total, RATIO), :]
        + thin[pl.ds(2, total, RATIO), :]
    ) * (1.0 / 9.0)
    coarse_out[...] = means.reshape(coarse_out.shape)
    store.wait()


def parent_step(parts, coefs, parent, source, before, after, y_left, y_right, out):
    levels, rows, cols = parent.shape
    me = lax.axis_index("gy")
    row = iota((rows, cols), 0)
    lane = iota((rows, cols), 1)
    has_left = me > 0
    has_right = me < parts - 1
    left = y_left[:rows, :]
    right = y_right[:rows, :]
    zero = jnp.zeros((rows, cols), jnp.float32)
    for level in range(levels):
        now = parent[level]
        from_left = left[:, PARENT_LANE + level : PARENT_LANE + level + 1]
        from_right = right[:, PARENT_LANE + level : PARENT_LANE + level + 1]
        top = before[TAIL_ROW + level : TAIL_ROW + level + 1, :cols]
        end = after[TAIL_ROW + level : TAIL_ROW + level + 1, :cols]
        around = (
            jnp.where(row == 0, top, pltpu.roll(now, 1, 0))
            + jnp.where(row == rows - 1, end, pltpu.roll(now, rows - 1, 0))
            + jnp.where(
                lane == 0, jnp.where(has_left, from_left, 0.0), pltpu.roll(now, 1, 1)
            )
            + jnp.where(
                lane == cols - 1,
                jnp.where(has_right, from_right, 0.0),
                pltpu.roll(now, cols - 1, 1),
            )
        )
        stacked = (parent[level - 1] if level > 0 else zero) + (
            parent[level + 1] if level < levels - 1 else zero
        )
        ch = coefs[0, level]
        cv = coefs[1, level]
        out[level] = (
            (1.0 - 4.0 * ch - 2.0 * cv) * now + ch * around + (cv * stacked + source[level])
        )


def merge(parts, band, ox_ref, oy_ref, step, *rest):
    own, previous, out, joined = (
        rest[:parts],
        rest[parts : 2 * parts],
        rest[2 * parts],
        rest[2 * parts + 1],
    )
    levels, rows, cols = step.shape
    foot = own[0].shape[2]
    me = lax.axis_index("gy")
    ox = ox_ref[0]
    oy = oy_ref[0]
    for k in range(parts):
        joined[k, :, :rows, :] = previous[k][...]
        joined[k, :, rows:, :] = own[k][...]
    lane = iota((rows, LANES), 1)
    for level in range(levels):
        values = [tile(step, level, piece) for piece in range(cols // LANES)]
        for k in range(parts):
            source = lax.rem(me + parts - k, parts)
            block = joined[k, level, pl.ds(rows - ox, rows), :]
            begin = oy + source * foot - me * cols
            block = pltpu.roll(block, (16384 + begin) & (LANES - 1), 1)
            low = jnp.maximum(source * foot, 2)
            high = jnp.minimum((source + 1) * foot, band - 2)
            for piece in range(cols // LANES):
                at = lane + (piece * LANES + me * cols - oy)
                values[piece] = jnp.where((at >= low) & (at < high), block, values[piece])
        for piece, value in enumerate(values):
            out[level, :, piece * LANES : (piece + 1) * LANES] = value


def shifted(value, axis, steps):
    count = lax.axis_size(axis)
    pairs = [(source, (source + steps) % count) for source in range(count)]
    return lax.ppermute(value, axis, pairs)


def shards(
    parent_old, parent_source, parent_coefs, nest_old, nest_source, nest_coefs, offset_x, offset_y
):
    parts = lax.axis_size("gy")
    along = ("gx", "gz")
    levels, parent_rows, parent_cols = parent_old.shape
    _, rows, cols = nest_old.shape
    foot = cols // RATIO
    band = foot * parts
    width = cols if parts == 2 else cols + LANES
    ring = rows + 8
    f32 = jnp.float32
    shape = jax.ShapeDtypeStruct
    sides = 1 if parts == 2 else 2
    messages = [shape((parent_rows, LANES), f32)] + [
        shape((rows if k in (1, parts - 1) else parent_rows, LANES), f32)
        for k in range(1, parts)
    ]
    anywhere = pl.BlockSpec(memory_space=pl.ANY)
    packed = pl.pallas_call(
        functools.partial(pack_columns, parts, band),
        out_shape=messages,
        in_specs=[scalars(), anywhere, anywhere, whole(), whole()],
        out_specs=[whole()] * parts,
        scratch_shapes=[
            VMEM((sides, levels, rows, LANES), f32),
            VMEM((sides, levels, rows, LANES), f32),
            pltpu.SemaphoreType.DMA((sides, 2)),
        ],
        compiler_params=params(),
        cost_estimate=cost(200000, 1000000),
        name="pack_columns",
    )(offset_y, nest_old, nest_source, parent_old, parent_source)
    columns = [shifted(packed[k], "gy", k) for k in range(1, parts)]

    def block(ref, last):
        count = ref.shape[1] // 8 - 1 if last else 0
        return pl.BlockSpec((levels, 8, ref.shape[2]), lambda i, c=count: (0, c, 0))

    def full(extent):
        return pl.BlockSpec(extent, lambda i: (0,) * len(extent))

    outs = [
        shape((TAIL_ROW + 8, width), f32),
        shape((TAIL_ROW + 16, width), f32),
        shape((8, LANES), f32),
        shape((parent_rows, LANES), f32),
    ]
    up, down, far, strips = pl.pallas_call(
        functools.partial(pack_rows, parts),
        out_shape=outs,
        grid=(1,),
        in_specs=[
            block(nest_old, False),
            block(nest_old, True),
            block(nest_old, False),
            block(nest_old, True),
            block(parent_old, False),
            block(parent_old, True),
            full(packed[0].shape),
        ]
        + [full(message.shape) for message in columns],
        out_specs=[full(out.shape) for out in outs],
        compiler_params=params(),
        cost_estimate=cost(100000, 700000),
        name="pack_rows",
    )(nest_old, nest_old, nest_source, nest_source, parent_old, parent_old, packed[0], *columns)
    before = shifted(up, along, 1)
    after = shifted(down, along, -1)
    beyond = shifted(far, along, -2)
    nest_new, coarse = pl.pallas_call(
        functools.partial(nest_steps, parts, parent_cols),
        out_shape=[
            shape(nest_old.shape, f32),
            shape((levels, parent_rows, foot), f32),
        ],
        in_specs=[scalars()] * 3 + [anywhere] * 2 + [whole()] * 6,
        out_specs=[anywhere, whole()],
        scratch_shapes=[
            VMEM((levels + 2, ring, width), f32),
            VMEM((levels + 2, ring, width), f32),
            VMEM((levels, ring, width), f32),
            VMEM((levels, ring, LANES), f32),
            VMEM((levels, ring, LANES), f32),
            VMEM((levels, rows, cols), f32),
            VMEM((levels * rows, foot), f32),
            pltpu.SemaphoreType.DMA((3,)),
        ],
        compiler_params=params(),
        cost_estimate=cost(10000000, 3000000),
        name="nest_steps",
    )(
        offset_x,
        parent_coefs,
        nest_coefs,
        nest_old,
        nest_source,
        strips,
        before,
        after,
        beyond,
        columns[0],
        columns[-1],
    )
    own = [coarse] + [shifted(coarse, "gy", k) for k in range(1, parts)]
    previous = [shifted(coarse, along, 1)] + [
        shifted_both(coarse, k) for k in range(1, parts)
    ]
    step = pl.pallas_call(
        functools.partial(parent_step, parts),
        out_shape=shape(parent_old.shape, f32),
        in_specs=[scalars()] + [whole()] * 6,
        out_specs=whole(),
        compiler_params=params(),
        cost_estimate=cost(800000, 800000),
        name="parent_step",
    )(parent_coefs, parent_old, parent_source, before, after, columns[0], columns[-1])
    parent_new = pl.pallas_call(
        functools.partial(merge, parts, band),
        out_shape=shape(parent_old.shape, f32),
        in_specs=[scalars()] * 2 + [whole()] * (1 + 2 * parts),
        out_specs=whole(),
        scratch_shapes=[VMEM((parts, levels, 2 * parent_rows, foot), f32)],
        compiler_params=params(),
        cost_estimate=cost(200000, 800000),
        name="merge",
    )(offset_x, offset_y, step, *own, *previous)
    return (parent_new, nest_new)


def shifted_both(value, steps):
    sizes = [lax.axis_size(axis) for axis in ("gx", "gy", "gz")]
    gx, gy, gz = sizes
    pairs = []
    for x in range(gx):
        for y in range(gy):
            for z in range(gz):
                place = (x * gz + z + 1) % (gx * gz)
                target = (place // gz * gy + (y + steps) % gy) * gz + place % gz
                pairs.append(((x * gy + y) * gz + z, target))
    return lax.ppermute(value, ("gx", "gy", "gz"), pairs)


def solution(mesh):
    return jax.shard_map(
        shards,
        mesh=mesh,
        in_specs=(
            P(None, ("grp", "gx", "gz"), "gy"),
            P(None, ("grp", "gx", "gz"), "gy"),
            P(),
            P(None, ("grp", "gx", "gz"), "gy"),
            P(None, ("grp", "gx", "gz"), "gy"),
            P(),
            P("grp"),
            P("grp"),
        ),
        out_specs=(P(None, ("grp", "gx", "gz"), "gy"), P(None, ("grp", "gx", "gz"), "gy")),
        check_vma=False,
    )
```

```python
import functools

import jax
import jax.numpy as jnp
from jax import lax
from jax.experimental import pallas as pl
from jax.experimental.pallas import tpu as pltpu
from jax.sharding import PartitionSpec as P

RATIO = 3
SUBSTEPS = 3
RIM = 6
LANES = 128
PARENT_LANE = 48
STRIP_LANE = 64
STRIP_SOURCE = 96
SOURCE_ROW = 24
TAIL_ROW = 40
VMEM = pltpu.VMEM
LIMIT = 24 * 1024 * 1024
HIGHEST = lax.Precision.HIGHEST


def iota(shape, dim):
    return lax.broadcasted_iota(jnp.int32, shape, dim)


def whole():
    return pl.BlockSpec(memory_space=VMEM)


def scalars():
    return pl.BlockSpec(memory_space=pltpu.SMEM)


def params():
    return pltpu.CompilerParams(vmem_limit_bytes=LIMIT)


def cost(flops, moved):
    return pl.CostEstimate(flops=flops, bytes_accessed=moved, transcendentals=0)


def tile(ref, level, index):
    return ref[level, :, index * LANES : (index + 1) * LANES]


def pack_columns(parts, band, oy_hbm, nest, source, parent_hbm, parent_source_hbm, *rest):
    outs = rest[:parts]
    old_buf, src_buf, parent, parent_source, oy_ref, sems, field_sems = rest[parts:]
    levels, rows, cols = nest.shape
    parent_cols = parent.shape[2]
    me = lax.axis_index("gy")
    sides = [1] if parts == 2 else [1, parts - 1]
    fields = [
        pltpu.make_async_copy(ref, buf, field_sems.at[at])
        for at, (ref, buf) in enumerate(
            ((oy_hbm, oy_ref), (parent_hbm, parent), (parent_source_hbm, parent_source))
        )
    ]
    for copy in fields:
        copy.start()
    copies = []
    for at, step in enumerate(sides):
        right = (me == 0) if parts == 2 else jnp.bool_(step == 1)
        start = pl.multiple_of(jnp.where(right, cols - LANES, 0), LANES)
        pair = [
            pltpu.make_async_copy(
                ref.at[:, :, pl.ds(start, LANES)], buf.at[at], sems.at[at, which]
            )
            for which, (ref, buf) in enumerate(((nest, old_buf), (source, src_buf)))
        ]
        for copy in pair:
            copy.start()
        copies.append((right, pair))
    lane = iota((parent.shape[1], LANES), 1)
    for copy in fields:
        copy.wait()
    oy = oy_ref[0]

    def strip(dest):
        base = jnp.where(dest == 0, oy - 1, oy + band - 3) - me * parent_cols
        total = jnp.zeros(lane.shape, jnp.float32)
        for ref, first in ((parent, STRIP_LANE), (parent_source, STRIP_SOURCE)):
            for level in range(levels):
                found = jnp.zeros(lane.shape, jnp.float32)
                for at in range(parent_cols // LANES):
                    place = lane + (at * LANES - base)
                    found = jnp.where(
                        (place >= 0) & (place < 4), tile(ref, level, at), found
                    )
                turn = (16384 + first + 4 * level - base) & (LANES - 1)
                total = total + pltpu.roll(found, turn, 1)
        return total

    outs[0][...] = strip(me)
    for step in range(1, parts):
        out = outs[step]
        part = strip(lax.rem(me + step, parts))
        if step not in sides:
            out[...] = part
            continue
        at = sides.index(step)
        right, pair = copies[at]
        first = jnp.where(right, LANES - 3, 0)
        for level in range(levels):
            edge = jnp.where(
                right, tile(parent, level, parent_cols // LANES - 1), tile(parent, level, 0)
            )
            edge = jnp.where(lane == jnp.where(right, LANES - 1, 0), edge, 0.0)
            turn = (LANES + PARENT_LANE + level - jnp.where(right, LANES - 1, 0)) & (LANES - 1)
            part = part + pltpu.roll(edge, turn, 1)
        for copy in pair:
            copy.wait()
        fine = iota((rows, LANES), 1) - first
        wanted = (fine >= 0) & (fine < 3)
        total = jnp.zeros((rows, LANES), jnp.float32)
        for level in range(levels):
            for buf, shift in ((old_buf, 0), (src_buf, 3)):
                value = jnp.where(wanted, buf[at, level], 0.0)
                turn = (LANES + 6 * level + shift - first) & (LANES - 1)
                total = total + pltpu.roll(value, turn, 1)
        out[...] = total
        out[: part.shape[0], :] += part


def with_columns(tiles, left, right, me, parts, place):
    lane = iota(left.shape, 1)
    from_right = pltpu.roll(right, (LANES - place) % LANES, 1)
    from_left = pltpu.roll(left, (2 * LANES - 3 - place) % LANES, 1)
    if parts == 2:
        tiles[0] = jnp.where((lane < 3) & (me == 0), from_right, tiles[0])
        tiles[-1] = jnp.where((lane >= LANES - 3) & (me == 1), from_left, tiles[-1])
        return tiles
    extra = jnp.where(lane < 3, from_right, jnp.where(lane >= LANES - 3, from_left, 0.0))
    return tiles + [extra]


def pack_rows(
    parts, old_top, old_end, src_top, src_end, par_top, par_end, own_strip, *rest
):
    columns = rest[: parts - 1]
    within, across, far, strip_out, both = rest[parts - 1 :]
    core = lax.axis_index("gz")
    up, down = both.at[core], both.at[1 - core]
    levels, _, cols = old_top.shape
    me = lax.axis_index("gy")
    left, right = columns[0], columns[-1]
    rows = left.shape[0]
    strip_rows = own_strip.shape[0]
    lane = iota((strip_rows, LANES), 1)
    strips = own_strip[...]
    for message in columns:
        strips = strips + message[:strip_rows, :]
    strips = jnp.where(lane >= STRIP_LANE, strips, 0.0)
    strip_out[...] = strips
    far[...] = strips[:8]
    pieces = cols // LANES
    for out, old, src, first, at, src_at in (
        (up, old_end, src_end, rows - 8, 5, 6),
        (down, old_top, src_top, 0, 0, 0),
    ):
        y_left = left[first : first + 8, :]
        y_right = right[first : first + 8, :]
        for level in range(levels):
            for ref, shift, row, count, base in (
                (old, 0, at, 3, 0),
                (src, 3, src_at, 2, SOURCE_ROW),
            ):
                tiles = [tile(ref, level, piece) for piece in range(pieces)]
                tiles = with_columns(tiles, y_left, y_right, me, parts, 6 * level + shift)
                for piece, value in enumerate(tiles):
                    out[
                        base + count * level : base + count * (level + 1),
                        piece * LANES : (piece + 1) * LANES,
                    ] = value[row : row + count]
    parent_cols = par_top.shape[2]
    for level in range(levels):
        up[TAIL_ROW + level : TAIL_ROW + level + 1, :parent_cols] = par_end[level, 7:8, :]
        down[TAIL_ROW + level : TAIL_ROW + level + 1, :parent_cols] = par_top[level, 0:1, :]
    up[TAIL_ROW : TAIL_ROW + 8, parent_cols : parent_cols + LANES] = strips[strip_rows - 8 :]
    down[TAIL_ROW : TAIL_ROW + 8, parent_cols : parent_cols + LANES] = strips[:8]
    down[TAIL_ROW + 8 : TAIL_ROW + 16, :LANES] = strips[8:16]
    down[TAIL_ROW + 8 : TAIL_ROW + 16, LANES : 2 * LANES] = strips[16:24]
    within[...] = both[0]
    across[...] = both[1]


def nest_steps(
    parts,
    parent_cols,
    ox_ref,
    parent_coefs,
    coefs,
    nest,
    source,
    strips,
    within,
    across,
    beyond,
    y_left,
    y_right,
    nest_out,
    coarse_out,
    ping,
    pong,
    src,
    rim_old,
    rim_diff,
    result,
    thin,
    both,
    sems,
):
    core = lax.axis_index("gz")
    both[0] = within[...]
    both[1] = across[...]
    before, after = both.at[1 - core], both.at[core]
    levels, rows, cols = nest.shape
    ring = ping.shape[1]
    width = ping.shape[2]
    pieces = cols // LANES
    strip_rows = strips.shape[0]
    me = lax.axis_index("gy")
    ox = ox_ref[0]
    loads = [
        pltpu.make_async_copy(nest, ping.at[1 : levels + 1, :rows, :cols], sems.at[0]),
        pltpu.make_async_copy(source, src.at[:, :rows, :cols], sems.at[1]),
    ]
    for copy in loads:
        copy.start()

    old = jnp.concatenate(
        [
            strips[...],
            after[TAIL_ROW : TAIL_ROW + 8, parent_cols : parent_cols + LANES],
            after[TAIL_ROW + 8 : TAIL_ROW + 16, :LANES],
            after[TAIL_ROW + 8 : TAIL_ROW + 16, LANES : 2 * LANES],
            jnp.where(
                iota((8, LANES), 0) == 0,
                beyond[...],
                jnp.where(
                    iota((8, LANES), 0) == 7,
                    before[TAIL_ROW : TAIL_ROW + 8, parent_cols : parent_cols + LANES],
                    0.0,
                ),
            ),
        ],
        axis=0,
    )
    count = old.shape[0]
    lane = iota(old.shape, 1)
    coef_h = jnp.zeros(old.shape, jnp.float32)
    coef_v = jnp.zeros(old.shape, jnp.float32)
    for level in range(levels):
        here = lane >= STRIP_LANE + 4 * level
        coef_h = jnp.where(here, parent_coefs[0, level], coef_h)
        coef_v = jnp.where(here, parent_coefs[1, level], coef_v)
    lateral = (
        pltpu.roll(old, 1, 0)
        + pltpu.roll(old, count - 1, 0)
        + pltpu.roll(old, 1, 1)
        + pltpu.roll(old, LANES - 1, 1)
        - 4.0 * old
    )
    higher = jnp.where(lane < STRIP_SOURCE - 4, pltpu.roll(old, LANES - 4, 1), 0.0)
    vertical = pltpu.roll(old, 4, 1) + higher - 2.0 * old
    forcing = pltpu.roll(old, LANES - (STRIP_SOURCE - STRIP_LANE), 1)
    diff = coef_h * lateral + coef_v * vertical + forcing
    index = iota((ring, count), 0)
    parent_row = jnp.where(index < rows + 3, (index * 171) >> 9, -1) + ox
    pick = (iota((ring, count), 1) == parent_row).astype(jnp.float32)
    picked = jnp.dot(
        pick,
        jnp.concatenate([old, diff], axis=1),
        precision=HIGHEST,
        preferred_element_type=jnp.float32,
    )
    lane = iota((ring, LANES), 1)
    first = jnp.where(me == 0, 0, LANES - RIM)
    column = jnp.where((lane >= first + 3) & (lane < first + RIM), 2, 1)
    for level in range(levels):
        at = column + (STRIP_LANE + 4 * level)
        rim_old[level] = jnp.take_along_axis(picked[:, :LANES], at, axis=1)
        rim_diff[level] = jnp.take_along_axis(picked[:, LANES:], at, axis=1)

    zero = jnp.zeros((ring, width), jnp.float32)
    for buf in (ping, pong):
        buf[0] = zero
        buf[levels + 1] = zero
    for level in range(levels):
        for buf, lead, base, n in ((ping, 1, 0, 3), (src, 0, SOURCE_ROW, 2)):
            rest = slice(base + n * level, base + n * (level + 1))
            buf[level + lead, rows : rows + n, :] = after[rest, :]
            buf[level + lead, ring - n : ring, :] = before[rest, :]
    for copy in loads:
        copy.wait()
    left = y_left[...]
    right = y_right[...]
    for level in range(levels):
        for buf, lead, shift in ((ping, 1, 0), (src, 0, 3)):
            edges = [
                buf[level + lead, :rows, :LANES],
                buf[level + lead, :rows, cols - LANES : cols],
            ]
            edges = with_columns(edges, left, right, me, parts, 6 * level + shift)
            if parts == 2:
                buf[level + lead, :rows, :LANES] = edges[0]
                buf[level + lead, :rows, cols - LANES : cols] = edges[1]
            else:
                buf[level + lead, :rows, cols:] = edges[2]

    lane = iota((8, LANES), 1)
    sub = iota((8, width), 0)
    is_south = me == 0
    is_north = me == parts - 1

    def substep(here, there, weight, last):
        low = 0 if last or parts > 2 else 3
        south = (lane >= low) & (lane < RIM) & is_south
        north = (lane >= LANES - RIM) & (lane < LANES - low) & is_north
        tiles = rows // 8 if last else ring // 8

        def one_level(level, carry):
            ch = coefs[0, level]
            cv = coefs[1, level]
            centre = 1.0 - 4.0 * ch - 2.0 * cv

            def row_tile(t):
                t = t % (ring // 8)
                return here[level + 1, 8 * t : 8 * t + 8, :]

            now = row_tile(-1)
            down_before = pltpu.roll(now, 1, 0)
            now = row_tile(0)
            up_now = pltpu.roll(now, 7, 0)
            for t in range(tiles):
                following = row_tile(t + 1)
                down_now = pltpu.roll(now, 1, 0)
                up_next = pltpu.roll(following, 7, 0)
                around = jnp.where(sub == 0, down_before, down_now) + jnp.where(
                    sub == 7, up_next, up_now
                )
                around = around + (pltpu.roll(now, 1, 1) + pltpu.roll(now, width - 1, 1))
                span = slice(8 * t, 8 * t + 8)
                stacked = here[level, span, :] + here[level + 2, span, :]
                value = centre * now + ch * around + (cv * stacked + src[level, span, :])
                rim = rim_old[level, span, :] + weight * rim_diff[level, span, :]
                if last:
                    store, at, stop = there, level, pieces
                else:
                    store, at, stop = there, level + 1, width // LANES
                for piece in range(stop):
                    part = value[:, piece * LANES : (piece + 1) * LANES]
                    if piece == 0:
                        part = jnp.where(south, rim, part)
                    if piece == pieces - 1:
                        part = jnp.where(north, rim, part)
                    store[at, span, piece * LANES : (piece + 1) * LANES] = part
                down_before, now, up_now = down_now, following, up_next
            return carry

        lax.fori_loop(0, levels, one_level, 0)

    substep(ping, pong, 1.0 / 3.0, False)
    substep(pong, ping, 2.0 / 3.0, False)
    substep(ping, result, 1.0, True)
    store = pltpu.make_async_copy(result, nest_out, sems.at[2])
    store.start()
    foot = cols // RATIO
    offset = iota((cols, foot), 0) - RATIO * iota((cols, foot), 1)
    gather = ((offset >= 0) & (offset < RATIO)).astype(jnp.float32)
    flat = result[...].reshape(levels * rows, cols)
    thin[...] = jnp.dot(
        flat, gather, precision=HIGHEST, preferred_element_type=jnp.float32
    )
    total = levels * rows // RATIO
    means = (
        thin[pl.ds(0, total, RATIO), :]
        + thin[pl.ds(1, total, RATIO), :]
        + thin[pl.ds(2, total, RATIO), :]
    ) * (1.0 / 9.0)
    coarse_out[...] = means.reshape(coarse_out.shape)
    store.wait()


def parent_step(parts, coefs, parent, source, within, across, y_left, y_right, out, tail):
    core = lax.axis_index("gz")
    levels, rows, cols = parent.shape
    tail[0] = within[TAIL_ROW : TAIL_ROW + levels, :cols]
    tail[1] = across[TAIL_ROW : TAIL_ROW + levels, :cols]
    me = lax.axis_index("gy")
    row = iota((rows, cols), 0)
    lane = iota((rows, cols), 1)
    has_left = me > 0
    has_right = me < parts - 1
    left = y_left[:rows, :]
    right = y_right[:rows, :]
    zero = jnp.zeros((rows, cols), jnp.float32)
    for level in range(levels):
        now = parent[level]
        from_left = left[:, PARENT_LANE + level : PARENT_LANE + level + 1]
        from_right = right[:, PARENT_LANE + level : PARENT_LANE + level + 1]
        top = tail[1 - core, level : level + 1, :]
        end = tail[core, level : level + 1, :]
        around = (
            jnp.where(row == 0, top, pltpu.roll(now, 1, 0))
            + jnp.where(row == rows - 1, end, pltpu.roll(now, rows - 1, 0))
            + jnp.where(
                lane == 0, jnp.where(has_left, from_left, 0.0), pltpu.roll(now, 1, 1)
            )
            + jnp.where(
                lane == cols - 1,
                jnp.where(has_right, from_right, 0.0),
                pltpu.roll(now, cols - 1, 1),
            )
        )
        stacked = (parent[level - 1] if level > 0 else zero) + (
            parent[level + 1] if level < levels - 1 else zero
        )
        ch = coefs[0, level]
        cv = coefs[1, level]
        out[level] = (
            (1.0 - 4.0 * ch - 2.0 * cv) * now + ch * around + (cv * stacked + source[level])
        )


def merge(parts, band, ox_ref, oy_ref, step, *rest):
    own, previous, out, joined = (
        rest[:parts],
        rest[parts : 2 * parts],
        rest[2 * parts],
        rest[2 * parts + 1],
    )
    levels, rows, cols = step.shape
    foot = own[0].shape[2]
    me = lax.axis_index("gy")
    ox = ox_ref[0]
    oy = oy_ref[0]
    for k in range(parts):
        joined[k, :, :rows, :] = previous[k][...]
        joined[k, :, rows:, :] = own[k][...]
    lane = iota((rows, LANES), 1)
    for level in range(levels):
        values = [tile(step, level, piece) for piece in range(cols // LANES)]
        for k in range(parts):
            source = lax.rem(me + parts - k, parts)
            block = joined[k, level, pl.ds(rows - ox, rows), :]
            begin = oy + source * foot - me * cols
            block = pltpu.roll(block, (16384 + begin) & (LANES - 1), 1)
            low = jnp.maximum(source * foot, 2)
            high = jnp.minimum((source + 1) * foot, band - 2)
            for piece in range(cols // LANES):
                at = lane + (piece * LANES + me * cols - oy)
                values[piece] = jnp.where((at >= low) & (at < high), block, values[piece])
        for piece, value in enumerate(values):
            out[level, :, piece * LANES : (piece + 1) * LANES] = value


def shifted(value, axis, steps):
    count = lax.axis_size(axis)
    pairs = [(source, (source + steps) % count) for source in range(count)]
    return lax.ppermute(value, axis, pairs)


def shards(
    parent_old, parent_source, parent_coefs, nest_old, nest_source, nest_coefs, offset_x, offset_y
):
    parts = lax.axis_size("gy")
    along = ("gx", "gz")
    levels, parent_rows, parent_cols = parent_old.shape
    _, rows, cols = nest_old.shape
    foot = cols // RATIO
    band = foot * parts
    width = cols if parts == 2 else cols + LANES
    ring = rows + 8
    f32 = jnp.float32
    shape = jax.ShapeDtypeStruct
    sides = 1 if parts == 2 else 2
    messages = [shape((parent_rows, LANES), f32)] + [
        shape((rows if k in (1, parts - 1) else parent_rows, LANES), f32)
        for k in range(1, parts)
    ]
    anywhere = pl.BlockSpec(memory_space=pl.ANY)
    in_hbm = pl.BlockSpec(memory_space=pltpu.HBM)
    packed = pl.pallas_call(
        functools.partial(pack_columns, parts, band),
        out_shape=messages,
        in_specs=[in_hbm] * 5,
        out_specs=[whole()] * parts,
        scratch_shapes=[
            VMEM((sides, levels, rows, LANES), f32),
            VMEM((sides, levels, rows, LANES), f32),
            VMEM(parent_old.shape, f32),
            VMEM(parent_old.shape, f32),
            pltpu.SMEM(offset_y.shape, jnp.int32),
            pltpu.SemaphoreType.DMA((sides, 2)),
            pltpu.SemaphoreType.DMA((3,)),
        ],
        compiler_params=params(),
        cost_estimate=cost(200000, 1000000),
        name="pack_columns",
    )(offset_y, nest_old, nest_source, parent_old, parent_source)
    columns = [shifted(packed[k], "gy", k) for k in range(1, parts)]

    def block(ref, last):
        count = ref.shape[1] // 8 - 1 if last else 0
        return pl.BlockSpec((levels, 8, ref.shape[2]), lambda i, c=count: (0, c, 0))

    def full(extent):
        return pl.BlockSpec(extent, lambda i: (0,) * len(extent))

    height = TAIL_ROW + 16
    outs = [
        shape((height, width), f32),
        shape((height, width), f32),
        shape((8, LANES), f32),
        shape((parent_rows, LANES), f32),
    ]
    within, across, far, strips = pl.pallas_call(
        functools.partial(pack_rows, parts),
        out_shape=outs,
        grid=(1,),
        in_specs=[
            block(nest_old, False),
            block(nest_old, True),
            block(nest_old, False),
            block(nest_old, True),
            block(parent_old, False),
            block(parent_old, True),
            full(packed[0].shape),
        ]
        + [full(message.shape) for message in columns],
        out_specs=[full(out.shape) for out in outs],
        scratch_shapes=[VMEM((2, height, width), f32)],
        compiler_params=params(),
        cost_estimate=cost(100000, 700000),
        name="pack_rows",
    )(nest_old, nest_old, nest_source, nest_source, parent_old, parent_old, packed[0], *columns)
    across = swapped(across, 1)
    within = swapped(within, 0)
    beyond = shifted(far, along, -2)
    nest_new, coarse = pl.pallas_call(
        functools.partial(nest_steps, parts, parent_cols),
        out_shape=[
            shape(nest_old.shape, f32),
            shape((levels, parent_rows, foot), f32),
        ],
        in_specs=[scalars()] * 3 + [anywhere] * 2 + [whole()] * 6,
        out_specs=[anywhere, whole()],
        scratch_shapes=[
            VMEM((levels + 2, ring, width), f32),
            VMEM((levels + 2, ring, width), f32),
            VMEM((levels, ring, width), f32),
            VMEM((levels, ring, LANES), f32),
            VMEM((levels, ring, LANES), f32),
            VMEM((levels, rows, cols), f32),
            VMEM((levels * rows, foot), f32),
            VMEM((2, height, width), f32),
            pltpu.SemaphoreType.DMA((3,)),
        ],
        compiler_params=params(),
        cost_estimate=cost(10000000, 3000000),
        name="nest_steps",
    )(
        offset_x,
        parent_coefs,
        nest_coefs,
        nest_old,
        nest_source,
        strips,
        within,
        across,
        beyond,
        columns[0],
        columns[-1],
    )
    own = [coarse] + [shifted(coarse, "gy", k) for k in range(1, parts)]
    previous = [shifted(coarse, along, 1)] + [
        shifted_both(coarse, k) for k in range(1, parts)
    ]
    step = pl.pallas_call(
        functools.partial(parent_step, parts),
        out_shape=shape(parent_old.shape, f32),
        in_specs=[scalars()] + [whole()] * 6,
        out_specs=whole(),
        scratch_shapes=[VMEM((2, levels, parent_cols), f32)],
        compiler_params=params(),
        cost_estimate=cost(800000, 800000),
        name="parent_step",
    )(parent_coefs, parent_old, parent_source, within, across, columns[0], columns[-1])
    parent_new = pl.pallas_call(
        functools.partial(merge, parts, band),
        out_shape=shape(parent_old.shape, f32),
        in_specs=[scalars()] * 2 + [whole()] * (1 + 2 * parts),
        out_specs=whole(),
        scratch_shapes=[VMEM((parts, levels, 2 * parent_rows, foot), f32)],
        compiler_params=params(),
        cost_estimate=cost(200000, 800000),
        name="merge",
    )(offset_x, offset_y, step, *own, *previous)
    return (parent_new, nest_new)


def swapped(value, first):
    along = ("gx", "gz")
    count = lax.axis_size(along)
    pairs = []
    for at in range(first, count, 2):
        pairs += [(at, (at + 1) % count), ((at + 1) % count, at)]
    return lax.ppermute(value, along, pairs)


def shifted_both(value, steps):
    sizes = [lax.axis_size(axis) for axis in ("gx", "gy", "gz")]
    gx, gy, gz = sizes
    pairs = []
    for x in range(gx):
        for y in range(gy):
            for z in range(gz):
                place = (x * gz + z + 1) % (gx * gz)
                target = (place // gz * gy + (y + steps) % gy) * gz + place % gz
                pairs.append(((x * gy + y) * gz + z, target))
    return lax.ppermute(value, ("gx", "gy", "gz"), pairs)


def solution(mesh):
    return jax.shard_map(
        shards,
        mesh=mesh,
        in_specs=(
            P(None, ("grp", "gx", "gz"), "gy"),
            P(None, ("grp", "gx", "gz"), "gy"),
            P(),
            P(None, ("grp", "gx", "gz"), "gy"),
            P(None, ("grp", "gx", "gz"), "gy"),
            P(),
            P("grp"),
            P("grp"),
        ),
        out_specs=(P(None, ("grp", "gx", "gz"), "gy"), P(None, ("grp", "gx", "gz"), "gy")),
        check_vma=False,
    )
```

```python
import functools

import jax
import jax.numpy as jnp
from jax import lax
from jax.experimental import pallas as pl
from jax.experimental.pallas import tpu as pltpu
from jax.sharding import PartitionSpec as P

RATIO = 3
SUBSTEPS = 3
RIM = 6
LANES = 128
STRIDE = 16
SOURCE_AT = 3
PARENT_AT = 6
STRIP_AT = 8
STRIP_SOURCE_AT = 12
SOURCE_ROW = 24
TAIL_ROW = 40
FIXED = 8
LEFT_AT = 3
RIGHT_OWN = STRIDE - 3
VMEM = pltpu.VMEM
LIMIT = 24 * 1024 * 1024
MOST = 54 * 1024 * 1024
HIGHEST = lax.Precision.HIGHEST


def iota(shape, dim):
    return lax.broadcasted_iota(jnp.int32, shape, dim)


def whole():
    return pl.BlockSpec(memory_space=VMEM)


def scalars():
    return pl.BlockSpec(memory_space=pltpu.SMEM)


def params(limit=LIMIT):
    return pltpu.CompilerParams(vmem_limit_bytes=limit)


def cost(flops, moved):
    return pl.CostEstimate(flops=flops, bytes_accessed=moved, transcendentals=0)


def tile(ref, level, index):
    return ref[level, :, index * LANES : (index + 1) * LANES]


def turned(value, lanes):
    lanes = lanes % LANES
    return pltpu.roll(value, lanes, 1) if lanes else value


def edge_strip(dest, band, oy, parent, parent_source):
    levels, rows, cols = parent.shape
    lane = iota((rows, LANES), 1)
    base = jnp.where(dest == 0, oy - 1, oy + band - 3) - lax.axis_index("gy") * cols
    total = jnp.zeros(lane.shape, jnp.float32)
    for ref, first in ((parent, STRIP_AT), (parent_source, STRIP_SOURCE_AT)):
        for level in range(levels):
            found = jnp.zeros(lane.shape, jnp.float32)
            for at in range(cols // LANES):
                place = lane + (at * LANES - base)
                found = jnp.where((place >= 0) & (place < 4), tile(ref, level, at), found)
            turn = (16384 + first + STRIDE * level - base) & (LANES - 1)
            total = total + pltpu.roll(found, turn, 1)
    return total


def pack_columns(parts, band, oy_hbm, nest, source, parent_hbm, parent_source_hbm, *rest):
    outs = rest[: parts - 1]
    old_buf, src_buf, parent, parent_source, oy_ref, sems, field_sems = rest[parts - 1 :]
    levels, rows, cols = nest.shape
    parent_cols = parent.shape[2]
    me = lax.axis_index("gy")
    sides = [1] if parts == 2 else [1, parts - 1]
    fields = [
        pltpu.make_async_copy(ref, buf, field_sems.at[at])
        for at, (ref, buf) in enumerate(
            ((oy_hbm, oy_ref), (parent_hbm, parent), (parent_source_hbm, parent_source))
        )
    ]
    for copy in fields:
        copy.start()
    copies = []
    for at, step in enumerate(sides):
        right = (me == 0) if parts == 2 else jnp.bool_(step == 1)
        start = pl.multiple_of(jnp.where(right, cols - LANES, 0), LANES)
        pair = [
            pltpu.make_async_copy(
                ref.at[:, :, pl.ds(start, LANES)], buf.at[at], sems.at[at, which]
            )
            for which, (ref, buf) in enumerate(((nest, old_buf), (source, src_buf)))
        ]
        for copy in pair:
            copy.start()
        copies.append((right, pair))
    for copy in fields:
        copy.wait()
    oy = oy_ref[0]
    lane = iota((parent.shape[1], LANES), 1)
    for step in range(1, parts):
        out = outs[step - 1]
        part = edge_strip(lax.rem(me + step, parts), band, oy, parent, parent_source)
        if step not in sides:
            out[...] = part
            continue
        at = sides.index(step)
        right, pair = copies[at]
        first = jnp.where(right, LANES - 3, 0)
        outer = jnp.where(right, LANES - 1, 0)
        for level in range(levels):
            edge = jnp.where(
                right, tile(parent, level, parent_cols // LANES - 1), tile(parent, level, 0)
            )
            edge = jnp.where(lane == outer, edge, 0.0)
            turn = (LANES + PARENT_AT + STRIDE * level - outer) & (LANES - 1)
            part = part + pltpu.roll(edge, turn, 1)
        for copy in pair:
            copy.wait()
        fine = iota((rows, LANES), 1) - first
        wanted = (fine >= 0) & (fine < 3)
        total = jnp.zeros((rows, LANES), jnp.float32)
        for level in range(levels):
            for buf, shift in ((old_buf, 0), (src_buf, SOURCE_AT)):
                value = jnp.where(wanted, buf[at, level], 0.0)
                turn = (LANES + STRIDE * level + shift - first) & (LANES - 1)
                total = total + pltpu.roll(value, turn, 1)
        out[...] = total
        out[: part.shape[0], :] += part


def inner_substep(coefs, here, source, there):
    levels, rows, cols = here.shape
    sub = iota((8, cols), 0)
    tiles = rows // 8

    def one_level(level):
        ch = coefs[0, level]
        cv = coefs[1, level]
        centre = 1.0 - 4.0 * ch - 2.0 * cv
        below = jnp.maximum(level - 1, 0)
        above = jnp.minimum(level + 1, levels - 1)
        cv_below = jnp.where(level > 0, cv, 0.0)
        cv_above = jnp.where(level < levels - 1, cv, 0.0)

        def row_tile(t):
            t = t % tiles
            return here[level, 8 * t : 8 * t + 8, :]

        down_before = pltpu.roll(row_tile(-1), 1, 0)
        now = row_tile(0)
        up_now = pltpu.roll(now, 7, 0)
        for t in range(tiles):
            following = row_tile(t + 1)
            down_now = pltpu.roll(now, 1, 0)
            up_next = pltpu.roll(following, 7, 0)
            around = jnp.where(sub == 0, down_before, down_now) + jnp.where(
                sub == 7, up_next, up_now
            )
            around = around + (pltpu.roll(now, 1, 1) + pltpu.roll(now, cols - 1, 1))
            span = slice(8 * t, 8 * t + 8)
            stacked = cv_below * here[below, span, :] + cv_above * here[above, span, :]
            there[level, span, :] = centre * now + ch * around + (stacked + source[level, span, :])
            down_before, now, up_now = down_now, following, up_next

    def two_levels(pair, carry):
        one_level(2 * pair)
        one_level(2 * pair + 1)
        return carry

    lax.fori_loop(0, levels // 2, two_levels, 0)


def inner_first(
    band, oy_ref, coefs, nest, source, parent, parent_source, strip, first, packs
):
    levels, rows, cols = nest.shape
    strip[...] = edge_strip(lax.axis_index("gy"), band, oy_ref[0], parent, parent_source)
    lane = iota((rows, LANES), 1)
    for at, ref in enumerate((nest, source)):
        left = jnp.zeros(lane.shape, jnp.float32)
        right = jnp.zeros(lane.shape, jnp.float32)
        for level in range(levels):
            value = jnp.where(lane < RIGHT_OWN, tile(ref, level, 0), 0.0)
            left = left + turned(value, STRIDE * level + LEFT_AT)
            value = jnp.where(lane >= LANES - RIGHT_OWN, tile(ref, level, cols // LANES - 1), 0.0)
            right = right + turned(value, STRIDE * level + RIGHT_OWN)
        packs[2 * at] = left
        packs[2 * at + 1] = right
    inner_substep(coefs, nest, source, first)


def inner_rest(coefs, first, source, after_pack, third, second):
    inner_substep(coefs, first, source, second)
    inner_substep(coefs, second, source, third)


def with_columns(tiles, left, right, me, parts, place):
    lane = iota(left.shape, 1)
    from_right = turned(right, -place)
    from_left = turned(left, -3 - place)
    if parts == 2:
        tiles[0] = jnp.where((lane < 3) & (me == 0), from_right, tiles[0])
        tiles[-1] = jnp.where((lane >= LANES - 3) & (me == 1), from_left, tiles[-1])
        return tiles
    extra = jnp.where(lane < 3, from_right, jnp.where(lane >= LANES - 3, from_left, 0.0))
    return tiles + [extra]


def pack_rows(
    parts, old_top, old_end, src_top, src_end, par_top, par_end, own_strip, *rest
):
    columns = rest[: parts - 1]
    within, across, far, strip_out, both = rest[parts - 1 :]
    core = lax.axis_index("gz")
    up, down = both.at[core], both.at[1 - core]
    levels, _, cols = old_top.shape
    me = lax.axis_index("gy")
    left, right = columns[0], columns[-1]
    rows = left.shape[0]
    strip_rows = own_strip.shape[0]
    lane = iota((strip_rows, LANES), 1)
    strips = own_strip[...]
    for message in columns:
        strips = strips + message[:strip_rows, :]
    strips = jnp.where((lane & (STRIDE - 1)) >= STRIP_AT, strips, 0.0)
    strip_out[...] = strips
    far[...] = strips[:8]
    pieces = cols // LANES
    for out, old, src, first, at, src_at in (
        (up, old_end, src_end, rows - 8, 5, 6),
        (down, old_top, src_top, 0, 0, 0),
    ):
        y_left = left[first : first + 8, :]
        y_right = right[first : first + 8, :]
        for level in range(levels):
            for ref, shift, row, count, base in (
                (old, 0, at, 3, 0),
                (src, SOURCE_AT, src_at, 2, SOURCE_ROW),
            ):
                tiles = [tile(ref, level, piece) for piece in range(pieces)]
                tiles = with_columns(
                    tiles, y_left, y_right, me, parts, STRIDE * level + shift
                )
                for piece, value in enumerate(tiles):
                    out[
                        base + count * level : base + count * (level + 1),
                        piece * LANES : (piece + 1) * LANES,
                    ] = value[row : row + count]
    parent_cols = par_top.shape[2]
    for level in range(levels):
        up[TAIL_ROW + level : TAIL_ROW + level + 1, :parent_cols] = par_end[level, 7:8, :]
        down[TAIL_ROW + level : TAIL_ROW + level + 1, :parent_cols] = par_top[level, 0:1, :]
    up[TAIL_ROW : TAIL_ROW + 8, parent_cols : parent_cols + LANES] = strips[strip_rows - 8 :]
    down[TAIL_ROW : TAIL_ROW + 8, parent_cols : parent_cols + LANES] = strips[:8]
    down[TAIL_ROW + 8 : TAIL_ROW + 16, :LANES] = strips[8:16]
    down[TAIL_ROW + 8 : TAIL_ROW + 16, LANES : 2 * LANES] = strips[16:24]
    within[...] = both[0]
    across[...] = both[1]


def edges(
    parts,
    parent_cols,
    ox_ref,
    parent_coefs,
    coefs,
    nest,
    source,
    third,
    packs,
    strips,
    within,
    across,
    beyond,
    y_left,
    y_right,
    result,
    coarse_out,
    both,
    ping,
    pong,
    src,
    split,
):
    levels, rows, cols = nest.shape
    width = ping.shape[3]
    pieces = cols // LANES
    me = lax.axis_index("gy")
    core = lax.axis_index("gz")
    both[0] = within[...]
    both[1] = across[...]
    before, after = both.at[1 - core], both.at[core]
    ox = ox_ref[0]
    is_south = me == 0
    is_north = me == parts - 1

    sub = iota((8, LANES), 0)
    old = jnp.concatenate(
        [
            strips[...],
            after[TAIL_ROW : TAIL_ROW + 8, parent_cols : parent_cols + LANES],
            after[TAIL_ROW + 8 : TAIL_ROW + 16, :LANES],
            after[TAIL_ROW + 8 : TAIL_ROW + 16, LANES : 2 * LANES],
            jnp.where(
                sub == 0,
                beyond[...],
                jnp.where(
                    sub == 7,
                    before[TAIL_ROW : TAIL_ROW + 8, parent_cols : parent_cols + LANES],
                    0.0,
                ),
            ),
        ],
        axis=0,
    )
    count = old.shape[0]

    def per_level(ref, which, shape):
        lane = iota(shape, 1)
        total = jnp.full(shape, ref[which, 0], jnp.float32)
        for level in range(1, levels):
            total = jnp.where(lane >= STRIDE * level, ref[which, level], total)
        return total

    def stacked(value):
        lane = iota(value.shape, 1)
        below = jnp.where(lane >= STRIDE, turned(value, STRIDE), 0.0)
        return below + jnp.where(lane < STRIDE * (levels - 1), turned(value, -STRIDE), 0.0)

    def around(value):
        return (
            pltpu.roll(value, 1, 0)
            + pltpu.roll(value, value.shape[0] - 1, 0)
            + turned(value, 1)
            + turned(value, -1)
        )

    diff = (
        per_level(parent_coefs, 0, old.shape) * (around(old) - 4.0 * old)
        + per_level(parent_coefs, 1, old.shape) * (stacked(old) - 2.0 * old)
        + turned(old, STRIP_AT - STRIP_SOURCE_AT)
    )
    index = iota((rows + 16, count), 0)
    nest_row = jnp.where(index < rows, index, jnp.where(index < rows + 8, index - rows - 3, index - 13))
    parent_row = ((nest_row + 3) * 171 >> 9) - 1 + ox
    pick = (iota((rows + 16, count), 1) == parent_row).astype(jnp.float32)
    picked = jnp.dot(
        pick,
        jnp.concatenate([old, diff], axis=1),
        precision=HIGHEST,
        preferred_element_type=jnp.float32,
    )
    picked_old, picked_diff = picked[:, :LANES], picked[:, LANES:]

    lane = iota((rows, LANES), 1)
    c = lane & (STRIDE - 1)
    rim_first = jnp.where(is_south, LEFT_AT, RIGHT_OWN - RIM)
    in_rim = (c >= rim_first) & (c < rim_first + RIM)
    at = lane - c + STRIP_AT + jnp.where(c >= rim_first + 3, 2, 1)
    rim_old = jnp.take_along_axis(picked_old[:rows], at, axis=1)
    rim_diff = jnp.take_along_axis(picked_diff[:rows], at, axis=1)
    ch = per_level(coefs, 0, lane.shape)
    cv = per_level(coefs, 1, lane.shape)
    centre = 1.0 - 4.0 * ch - 2.0 * cv
    left = jnp.where(c < 3, y_left[...], packs[0])
    left_src = jnp.where(c < 3, turned(y_left[...], -SOURCE_AT), packs[2])
    right = jnp.where(c >= RIGHT_OWN, turned(y_right[...], RIGHT_OWN), packs[1])
    right_src = jnp.where(c >= RIGHT_OWN, turned(y_right[...], RIGHT_OWN - SOURCE_AT), packs[3])
    sides = []
    for value, forcing, rim in (
        (left, left_src, in_rim & is_south),
        (right, right_src, in_rim & is_north),
    ):
        for substep in range(1, SUBSTEPS + 1):
            value = centre * value + ch * around(value) + (cv * stacked(value) + forcing)
            value = jnp.where(rim, rim_old + (substep / SUBSTEPS) * rim_diff, value)
        sides.append(value)

    sub = iota((8, width), 0)
    lane = iota((8, LANES), 1)
    for level in range(levels):
        for buf, field, shift, n, base in (
            (ping, nest, 0, 3, 0),
            (src, source, SOURCE_AT, 2, SOURCE_ROW),
        ):
            for window, first, turn, at, message in (
                (0, 0, 3, 3 - n, before),
                (1, rows - 8, 5, 5, after),
            ):
                tiles = [
                    field[level, first : first + 8, piece * LANES : (piece + 1) * LANES]
                    for piece in range(pieces)
                ]
                tiles = with_columns(
                    tiles,
                    y_left[first : first + 8, :],
                    y_right[first : first + 8, :],
                    me,
                    parts,
                    STRIDE * level + shift,
                )
                for piece, value in enumerate(tiles):
                    value = pltpu.roll(value, turn, 0)
                    span = slice(piece * LANES, (piece + 1) * LANES)
                    buf[level, window, :, span] = value
                    if n == 3:
                        pong[level, window, :, span] = value
                buf[level, window, at : at + n, :] = message[
                    base + n * level : base + n * (level + 1), :
                ]
    rim_first = jnp.where(is_south, 0, LANES - RIM)
    column = STRIP_AT + jnp.where((lane >= rim_first + 3) & (lane < rim_first + RIM), 2, 1)
    rims = {}
    for level in range(levels):
        for window in range(2):
            span = slice(rows + 8 * window, rows + 8 * window + 8)
            at = column + STRIDE * level
            rims[level, window] = (
                jnp.take_along_axis(picked_old[span], at, axis=1),
                jnp.take_along_axis(picked_diff[span], at, axis=1),
            )
    for substep in range(1, SUBSTEPS + 1):
        here, there = (ping, pong) if substep % 2 else (pong, ping)
        low = 0 if substep == SUBSTEPS or parts > 2 else 3
        south = (lane >= low) & (lane < RIM) & is_south
        north = (lane >= LANES - RIM) & (lane < LANES - low) & is_north
        weight = substep / SUBSTEPS
        for level in range(levels):
            c_h = coefs[0, level]
            c_v = coefs[1, level]
            c_0 = 1.0 - 4.0 * c_h - 2.0 * c_v
            for window in range(2):
                now = here[level, window]
                up = pltpu.roll(now, 1, 0)
                down = pltpu.roll(now, 7, 0)
                if substep == 1:
                    beyond_row = pong[level, window]
                    if window == 0:
                        down = jnp.where(sub == 7, pltpu.roll(beyond_row, 7, 0), down)
                    else:
                        up = jnp.where(sub == 0, pltpu.roll(beyond_row, 1, 0), up)
                beside = pltpu.roll(now, 1, 1) + pltpu.roll(now, width - 1, 1)
                value = c_0 * now + c_h * ((up + down) + beside) + src[level, window]
                if level > 0:
                    value = value + c_v * here[level - 1, window]
                if level < levels - 1:
                    value = value + c_v * here[level + 1, window]
                rim_o, rim_d = rims[level, window]
                rim = rim_o + weight * rim_d
                for piece in range(width // LANES):
                    span = slice(piece * LANES, (piece + 1) * LANES)
                    part = value[:, span]
                    if piece == 0:
                        part = jnp.where(south, rim, part)
                    if piece == pieces - 1:
                        part = jnp.where(north, rim, part)
                    there[level, window, :, span] = part

    lane = iota((rows, LANES), 1)
    sub = iota((8, cols), 0)
    for level in range(levels):
        fixed = turned(sides[0], -STRIDE * level - LEFT_AT)
        result[level, :, :LANES] = jnp.where(lane < FIXED, fixed, tile(third, level, 0))
        for piece in range(1, pieces - 1):
            result[level, :, piece * LANES : (piece + 1) * LANES] = tile(third, level, piece)
        fixed = turned(sides[1], -STRIDE * level - RIGHT_OWN)
        result[level, :, cols - LANES :] = jnp.where(
            lane >= LANES - FIXED, fixed, tile(third, level, pieces - 1)
        )
        top = pltpu.roll(there[level, 0, :, :cols], 5, 0)
        result[level, :8, :] = jnp.where(sub < 3, top, result[level, :8, :])
        end = pltpu.roll(there[level, 1, :, :cols], 3, 0)
        result[level, rows - 8 :, :] = jnp.where(sub >= 5, end, result[level, rows - 8 :, :])

    foot = cols // RATIO
    offset = iota((cols, foot), 0) - RATIO * iota((cols, foot), 1)
    gather = ((offset >= 0) & (offset < RATIO)).astype(jnp.float32)
    parent_rows = rows // RATIO
    for level in range(levels):
        for piece in range(pieces):
            split[piece, level * rows : (level + 1) * rows, :] = tile(result, level, piece)
    total = levels * parent_rows
    sums = [
        split[piece, pl.ds(0, total, RATIO), :]
        + split[piece, pl.ds(1, total, RATIO), :]
        + split[piece, pl.ds(2, total, RATIO), :]
        for piece in range(pieces)
    ]
    means = jnp.dot(
        jnp.concatenate(sums, axis=1),
        gather,
        precision=HIGHEST,
        preferred_element_type=jnp.float32,
    ) * (1.0 / 9.0)
    coarse_out[...] = means.reshape(coarse_out.shape)


def parent_step(
    parts, coefs, nest, parent, source, within, across, y_left, y_right, out, nest_out, tail, sem
):
    store = pltpu.make_async_copy(nest, nest_out, sem)
    store.start()
    core = lax.axis_index("gz")
    levels, rows, cols = parent.shape
    tail[0] = within[TAIL_ROW : TAIL_ROW + levels, :cols]
    tail[1] = across[TAIL_ROW : TAIL_ROW + levels, :cols]
    me = lax.axis_index("gy")
    row = iota((rows, cols), 0)
    lane = iota((rows, cols), 1)
    has_left = me > 0
    has_right = me < parts - 1
    left = y_left[:rows, :]
    right = y_right[:rows, :]
    zero = jnp.zeros((rows, cols), jnp.float32)
    for level in range(levels):
        now = parent[level]
        at = STRIDE * level + PARENT_AT
        from_left = left[:, at : at + 1]
        from_right = right[:, at : at + 1]
        top = tail[1 - core, level : level + 1, :]
        end = tail[core, level : level + 1, :]
        around = (
            jnp.where(row == 0, top, pltpu.roll(now, 1, 0))
            + jnp.where(row == rows - 1, end, pltpu.roll(now, rows - 1, 0))
            + jnp.where(
                lane == 0, jnp.where(has_left, from_left, 0.0), pltpu.roll(now, 1, 1)
            )
            + jnp.where(
                lane == cols - 1,
                jnp.where(has_right, from_right, 0.0),
                pltpu.roll(now, cols - 1, 1),
            )
        )
        stacked = (parent[level - 1] if level > 0 else zero) + (
            parent[level + 1] if level < levels - 1 else zero
        )
        ch = coefs[0, level]
        cv = coefs[1, level]
        out[level] = (
            (1.0 - 4.0 * ch - 2.0 * cv) * now + ch * around + (cv * stacked + source[level])
        )
    store.wait()


def merge(parts, band, ox_ref, oy_ref, step, *rest):
    own, previous, out, joined = (
        rest[:parts],
        rest[parts : 2 * parts],
        rest[2 * parts],
        rest[2 * parts + 1],
    )
    levels, rows, cols = step.shape
    foot = own[0].shape[2]
    me = lax.axis_index("gy")
    ox = ox_ref[0]
    oy = oy_ref[0]
    for k in range(parts):
        joined[k, :, :rows, :] = previous[k][...]
        joined[k, :, rows:, :] = own[k][...]
    lane = iota((rows, LANES), 1)
    for level in range(levels):
        values = [tile(step, level, piece) for piece in range(cols // LANES)]
        for k in range(parts):
            source = lax.rem(me + parts - k, parts)
            block = joined[k, level, pl.ds(rows - ox, rows), :]
            begin = oy + source * foot - me * cols
            block = pltpu.roll(block, (16384 + begin) & (LANES - 1), 1)
            low = jnp.maximum(source * foot, 2)
            high = jnp.minimum((source + 1) * foot, band - 2)
            for piece in range(cols // LANES):
                at = lane + (piece * LANES + me * cols - oy)
                values[piece] = jnp.where((at >= low) & (at < high), block, values[piece])
        for piece, value in enumerate(values):
            out[level, :, piece * LANES : (piece + 1) * LANES] = value


def shifted(value, axis, steps):
    count = lax.axis_size(axis)
    pairs = [(source, (source + steps) % count) for source in range(count)]
    return lax.ppermute(value, axis, pairs)


def shards(
    parent_old, parent_source, parent_coefs, nest_old, nest_source, nest_coefs, offset_x, offset_y
):
    parts = lax.axis_size("gy")
    along = ("gx", "gz")
    levels, parent_rows, parent_cols = parent_old.shape
    _, rows, cols = nest_old.shape
    foot = cols // RATIO
    band = foot * parts
    width = cols if parts == 2 else cols + LANES
    height = TAIL_ROW + 16
    f32 = jnp.float32
    shape = jax.ShapeDtypeStruct
    anywhere = pl.BlockSpec(memory_space=pl.ANY)
    in_hbm = pl.BlockSpec(memory_space=pltpu.HBM)
    sides = 1 if parts == 2 else 2
    packed = pl.pallas_call(
        functools.partial(pack_columns, parts, band),
        out_shape=[
            shape((rows if k in (1, parts - 1) else parent_rows, LANES), f32)
            for k in range(1, parts)
        ],
        in_specs=[in_hbm] * 5,
        out_specs=[whole()] * (parts - 1),
        scratch_shapes=[
            VMEM((sides, levels, rows, LANES), f32),
            VMEM((sides, levels, rows, LANES), f32),
            VMEM(parent_old.shape, f32),
            VMEM(parent_old.shape, f32),
            pltpu.SMEM(offset_y.shape, jnp.int32),
            pltpu.SemaphoreType.DMA((sides, 2)),
            pltpu.SemaphoreType.DMA((3,)),
        ],
        compiler_params=params(MOST),
        cost_estimate=cost(200000, 1000000),
        name="pack_columns",
    )(offset_y, nest_old, nest_source, parent_old, parent_source)
    columns = [shifted(packed[k - 1], "gy", k) for k in range(1, parts)]
    own_strip, first, packs = pl.pallas_call(
        functools.partial(inner_first, band),
        out_shape=[
            shape((parent_rows, LANES), f32),
            shape(nest_old.shape, f32),
            shape((4, rows, LANES), f32),
        ],
        in_specs=[scalars()] * 2 + [whole()] * 4,
        out_specs=[whole()] * 3,
        compiler_params=params(),
        cost_estimate=cost(4000000, 3000000),
        name="inner_first",
    )(offset_y, nest_coefs, nest_old, nest_source, parent_old, parent_source)

    def block(ref, last):
        count = ref.shape[1] // 8 - 1 if last else 0
        return pl.BlockSpec((levels, 8, ref.shape[2]), lambda i, c=count: (0, c, 0))

    def full(extent):
        return pl.BlockSpec(extent, lambda i: (0,) * len(extent))

    outs = [
        shape((height, width), f32),
        shape((height, width), f32),
        shape((8, LANES), f32),
        shape((parent_rows, LANES), f32),
    ]
    within, across, far, strips = pl.pallas_call(
        functools.partial(pack_rows, parts),
        out_shape=outs,
        grid=(1,),
        in_specs=[
            block(nest_old, False),
            block(nest_old, True),
            block(nest_old, False),
            block(nest_old, True),
            block(parent_old, False),
            block(parent_old, True),
            full(own_strip.shape),
        ]
        + [full(message.shape) for message in columns],
        out_specs=[full(out.shape) for out in outs],
        scratch_shapes=[VMEM((2, height, width), f32)],
        compiler_params=params(),
        cost_estimate=cost(100000, 700000),
        name="pack_rows",
    )(nest_old, nest_old, nest_source, nest_source, parent_old, parent_old, own_strip, *columns)
    across = swapped(across, 1)
    within = swapped(within, 0)
    beyond = shifted(far, along, -2)
    third = pl.pallas_call(
        inner_rest,
        out_shape=shape(nest_old.shape, f32),
        in_specs=[scalars()] + [whole()] * 2 + [anywhere],
        out_specs=whole(),
        scratch_shapes=[VMEM(nest_old.shape, f32)],
        compiler_params=params(),
        cost_estimate=cost(8000000, 6000000),
        name="inner_rest",
    )(nest_coefs, first, nest_source, strips)
    nest_done, coarse = pl.pallas_call(
        functools.partial(edges, parts, parent_cols),
        out_shape=[
            shape(nest_old.shape, f32),
            shape((levels, parent_rows, foot), f32),
        ],
        in_specs=[scalars()] * 3 + [whole()] * 10,
        out_specs=[whole(), whole()],
        scratch_shapes=[
            VMEM((2, height, width), f32),
            VMEM((levels, 2, 8, width), f32),
            VMEM((levels, 2, 8, width), f32),
            VMEM((levels, 2, 8, width), f32),
            VMEM((cols // LANES, levels * rows, LANES), f32),
        ],
        compiler_params=params(),
        cost_estimate=cost(4000000, 3000000),
        name="edges",
    )(
        offset_x,
        parent_coefs,
        nest_coefs,
        nest_old,
        nest_source,
        third,
        packs,
        strips,
        within,
        across,
        beyond,
        columns[0],
        columns[-1],
    )
    own = [coarse] + [shifted(coarse, "gy", k) for k in range(1, parts)]
    previous = [shifted(coarse, along, 1)] + [
        shifted_both(coarse, k) for k in range(1, parts)
    ]
    step, nest_new = pl.pallas_call(
        functools.partial(parent_step, parts),
        out_shape=[shape(parent_old.shape, f32), shape(nest_old.shape, f32)],
        in_specs=[scalars(), anywhere] + [whole()] * 6,
        out_specs=[whole(), in_hbm],
        scratch_shapes=[VMEM((2, levels, parent_cols), f32), pltpu.SemaphoreType.DMA],
        compiler_params=params(),
        cost_estimate=cost(800000, 2500000),
        name="parent_step",
    )(
        parent_coefs,
        nest_done,
        parent_old,
        parent_source,
        within,
        across,
        columns[0],
        columns[-1],
    )
    parent_new = pl.pallas_call(
        functools.partial(merge, parts, band),
        out_shape=shape(parent_old.shape, f32),
        in_specs=[scalars()] * 2 + [whole()] * (1 + 2 * parts),
        out_specs=whole(),
        scratch_shapes=[VMEM((parts, levels, 2 * parent_rows, foot), f32)],
        compiler_params=params(),
        cost_estimate=cost(200000, 800000),
        name="merge",
    )(offset_x, offset_y, step, *own, *previous)
    return (parent_new, nest_new)


def swapped(value, first):
    along = ("gx", "gz")
    count = lax.axis_size(along)
    pairs = []
    for at in range(first, count, 2):
        pairs += [(at, (at + 1) % count), ((at + 1) % count, at)]
    return lax.ppermute(value, along, pairs)


def shifted_both(value, steps):
    sizes = [lax.axis_size(axis) for axis in ("gx", "gy", "gz")]
    gx, gy, gz = sizes
    pairs = []
    for x in range(gx):
        for y in range(gy):
            for z in range(gz):
                place = (x * gz + z + 1) % (gx * gz)
                target = (place // gz * gy + (y + steps) % gy) * gz + place % gz
                pairs.append(((x * gy + y) * gz + z, target))
    return lax.ppermute(value, ("gx", "gy", "gz"), pairs)


def solution(mesh):
    return jax.shard_map(
        shards,
        mesh=mesh,
        in_specs=(
            P(None, ("grp", "gx", "gz"), "gy"),
            P(None, ("grp", "gx", "gz"), "gy"),
            P(),
            P(None, ("grp", "gx", "gz"), "gy"),
            P(None, ("grp", "gx", "gz"), "gy"),
            P(),
            P("grp"),
            P("grp"),
        ),
        out_specs=(P(None, ("grp", "gx", "gz"), "gy"), P(None, ("grp", "gx", "gz"), "gy")),
        check_vma=False,
    )
```

```python
import functools

import jax
import jax.numpy as jnp
from jax import lax
from jax.experimental import pallas as pl
from jax.experimental.pallas import tpu as pltpu
from jax.sharding import PartitionSpec as P

RATIO = 3
SUBSTEPS = 3
RIM = 6
LANES = 128
STRIDE = 16
SOURCE_AT = 3
PARENT_AT = 6
STRIP_AT = 8
STRIP_SOURCE_AT = 12
SOURCE_ROW = 24
TAIL_ROW = 40
FIXED = 8
LEFT_AT = 3
RIGHT_OWN = STRIDE - 3
VMEM = pltpu.VMEM
LIMIT = 24 * 1024 * 1024
MOST = 54 * 1024 * 1024
HIGHEST = lax.Precision.HIGHEST


def iota(shape, dim):
    return lax.broadcasted_iota(jnp.int32, shape, dim)


def whole():
    return pl.BlockSpec(memory_space=VMEM)


def scalars():
    return pl.BlockSpec(memory_space=pltpu.SMEM)


def params(limit=LIMIT):
    return pltpu.CompilerParams(vmem_limit_bytes=limit)


def cost(flops, moved):
    return pl.CostEstimate(flops=flops, bytes_accessed=moved, transcendentals=0)


def tile(ref, level, index):
    return ref[level, :, index * LANES : (index + 1) * LANES]


def turned(value, lanes):
    lanes = lanes % LANES
    return pltpu.roll(value, lanes, 1) if lanes else value


def edge_strip(dest, band, oy, parent, parent_source):
    levels, rows, cols = parent.shape
    lane = iota((rows, LANES), 1)
    base = jnp.where(dest == 0, oy - 1, oy + band - 3) - lax.axis_index("gy") * cols
    total = jnp.zeros(lane.shape, jnp.float32)
    for ref, first in ((parent, STRIP_AT), (parent_source, STRIP_SOURCE_AT)):
        for level in range(levels):
            found = jnp.zeros(lane.shape, jnp.float32)
            for at in range(cols // LANES):
                place = lane + (at * LANES - base)
                found = jnp.where((place >= 0) & (place < 4), tile(ref, level, at), found)
            turn = (16384 + first + STRIDE * level - base) & (LANES - 1)
            total = total + pltpu.roll(found, turn, 1)
    return total


def pack_pair(nest, source, parent, parent_source, out, fine_buf, coarse_buf, sems):
    levels, rows, cols = nest.shape
    parent_rows, parent_cols = parent.shape[1:]
    right = lax.axis_index("gy") == 0
    loads = []
    for at, (ref, buf) in enumerate(
        (
            (parent, coarse_buf.at[0]),
            (parent_source, coarse_buf.at[1]),
            (nest, fine_buf.at[0]),
            (source, fine_buf.at[1]),
        )
    ):
        start = pl.multiple_of(jnp.where(right, ref.shape[2] - LANES, 0), LANES)
        loads.append(pltpu.make_async_copy(ref.at[:, :, pl.ds(start, LANES)], buf, sems.at[at]))
    for copy in loads:
        copy.start()

    def columns(value, count, to):
        first = jnp.where(right, LANES - count, 0)
        place = iota(value.shape, 1) - first
        value = jnp.where((place >= 0) & (place < count), value, 0.0)
        return pltpu.roll(value, (LANES + to - first) & (LANES - 1), 1)

    part = jnp.zeros((parent_rows, LANES), jnp.float32)
    loads[0].wait()
    loads[1].wait()
    for level in range(levels):
        base = STRIDE * level
        part = part + columns(coarse_buf[0, level], 1, base + PARENT_AT)
        part = part + columns(coarse_buf[0, level], 2, base + STRIP_AT)
        part = part + columns(coarse_buf[1, level], 2, base + STRIP_SOURCE_AT)
    total = jnp.zeros((rows, LANES), jnp.float32)
    loads[2].wait()
    loads[3].wait()
    for level in range(levels):
        base = STRIDE * level
        total = total + columns(fine_buf[0, level], 3, base)
        total = total + columns(fine_buf[1, level], 3, base + SOURCE_AT)
    out[...] = total
    out[:parent_rows, :] += part


def across_border(message, oy, parent_cols, me):
    c = iota(message.shape, 1) & (STRIDE - 1)
    place = jnp.where(me == 0, parent_cols + 1, 1) - oy
    total = jnp.zeros(message.shape, jnp.float32)
    for turn in (-1, 0, 2, 3):
        at = jnp.where(c >= STRIP_SOURCE_AT, c - STRIP_SOURCE_AT, c - STRIP_AT) - turn
        fits = (c >= STRIP_AT) & (at >= 0) & (at < 2) & (place == turn)
        total = total + jnp.where(fits, turned(message, turn), 0.0)
    return total


def pack_columns(parts, band, oy_hbm, nest, source, parent_hbm, parent_source_hbm, *rest):
    outs = rest[: parts - 1]
    old_buf, src_buf, parent, parent_source, oy_ref, sems, field_sems = rest[parts - 1 :]
    levels, rows, cols = nest.shape
    parent_cols = parent.shape[2]
    me = lax.axis_index("gy")
    sides = [1] if parts == 2 else [1, parts - 1]
    fields = [
        pltpu.make_async_copy(ref, buf, field_sems.at[at])
        for at, (ref, buf) in enumerate(
            ((oy_hbm, oy_ref), (parent_hbm, parent), (parent_source_hbm, parent_source))
        )
    ]
    for copy in fields:
        copy.start()
    copies = []
    for at, step in enumerate(sides):
        right = (me == 0) if parts == 2 else jnp.bool_(step == 1)
        start = pl.multiple_of(jnp.where(right, cols - LANES, 0), LANES)
        pair = [
            pltpu.make_async_copy(
                ref.at[:, :, pl.ds(start, LANES)], buf.at[at], sems.at[at, which]
            )
            for which, (ref, buf) in enumerate(((nest, old_buf), (source, src_buf)))
        ]
        for copy in pair:
            copy.start()
        copies.append((right, pair))
    for copy in fields:
        copy.wait()
    oy = oy_ref[0]
    lane = iota((parent.shape[1], LANES), 1)
    for step in range(1, parts):
        out = outs[step - 1]
        part = edge_strip(lax.rem(me + step, parts), band, oy, parent, parent_source)
        if step not in sides:
            out[...] = part
            continue
        at = sides.index(step)
        right, pair = copies[at]
        first = jnp.where(right, LANES - 3, 0)
        outer = jnp.where(right, LANES - 1, 0)
        for level in range(levels):
            edge = jnp.where(
                right, tile(parent, level, parent_cols // LANES - 1), tile(parent, level, 0)
            )
            edge = jnp.where(lane == outer, edge, 0.0)
            turn = (LANES + PARENT_AT + STRIDE * level - outer) & (LANES - 1)
            part = part + pltpu.roll(edge, turn, 1)
        for copy in pair:
            copy.wait()
        fine = iota((rows, LANES), 1) - first
        wanted = (fine >= 0) & (fine < 3)
        total = jnp.zeros((rows, LANES), jnp.float32)
        for level in range(levels):
            for buf, shift in ((old_buf, 0), (src_buf, SOURCE_AT)):
                value = jnp.where(wanted, buf[at, level], 0.0)
                turn = (LANES + STRIDE * level + shift - first) & (LANES - 1)
                total = total + pltpu.roll(value, turn, 1)
        out[...] = total
        out[: part.shape[0], :] += part


def inner_substep(coefs, here, source, there):
    levels, rows, cols = here.shape
    sub = iota((8, cols), 0)
    tiles = rows // 8

    def one_level(level):
        ch = coefs[0, level]
        cv = coefs[1, level]
        centre = 1.0 - 4.0 * ch - 2.0 * cv
        below = jnp.maximum(level - 1, 0)
        above = jnp.minimum(level + 1, levels - 1)
        cv_below = jnp.where(level > 0, cv, 0.0)
        cv_above = jnp.where(level < levels - 1, cv, 0.0)

        def row_tile(t):
            t = t % tiles
            return here[level, 8 * t : 8 * t + 8, :]

        down_before = pltpu.roll(row_tile(-1), 1, 0)
        now = row_tile(0)
        up_now = pltpu.roll(now, 7, 0)
        for t in range(tiles):
            following = row_tile(t + 1)
            down_now = pltpu.roll(now, 1, 0)
            up_next = pltpu.roll(following, 7, 0)
            around = jnp.where(sub == 0, down_before, down_now) + jnp.where(
                sub == 7, up_next, up_now
            )
            around = around + (pltpu.roll(now, 1, 1) + pltpu.roll(now, cols - 1, 1))
            span = slice(8 * t, 8 * t + 8)
            stacked = cv_below * here[below, span, :] + cv_above * here[above, span, :]
            there[level, span, :] = centre * now + ch * around + (stacked + source[level, span, :])
            down_before, now, up_now = down_now, following, up_next

    def two_levels(pair, carry):
        one_level(2 * pair)
        one_level(2 * pair + 1)
        return carry

    lax.fori_loop(0, levels // 2, two_levels, 0)


def spread_coefs(parent_coefs, coefs, out):
    levels = out.shape[2]
    lane = iota((levels, LANES), 1)
    row = iota((levels, LANES), 0)
    for at, ref in enumerate((parent_coefs, coefs)):
        for which in range(2):
            packed = jnp.full(lane.shape, ref[which, 0], jnp.float32)
            rows = packed
            for level in range(1, levels):
                packed = jnp.where(lane >= STRIDE * level, ref[which, level], packed)
                rows = jnp.where(row == level, ref[which, level], rows)
            out[0, 2 * at + which] = packed
            out[1, 2 * at + which] = rows


def inner_first(
    band,
    ox_hbm,
    oy_hbm,
    parent_coefs,
    coefs,
    nest,
    source,
    parent,
    parent_source,
    strip,
    first,
    packs,
    spread,
    rows_out,
    offsets_out,
    ox_ref,
    oy_ref,
    sems,
):
    levels, rows, cols = nest.shape
    loads = [
        pltpu.make_async_copy(ref, to, sems.at[at])
        for at, (ref, to) in enumerate(((ox_hbm, ox_ref), (oy_hbm, oy_ref)))
    ]
    for copy in loads:
        copy.start()
    spread_coefs(parent_coefs, coefs, spread)
    for copy in loads:
        copy.wait()
    ox, oy = ox_ref[0], oy_ref[0]
    rows_out[0] = jnp.full(rows_out.shape[1:], ox, jnp.int32)
    rows_out[1] = jnp.full(rows_out.shape[1:], oy, jnp.int32)
    offsets_out[0] = ox
    offsets_out[1] = oy
    strip[...] = edge_strip(lax.axis_index("gy"), band, oy, parent, parent_source)
    lane = iota((rows, LANES), 1)
    for at, ref in enumerate((nest, source)):
        left = jnp.zeros(lane.shape, jnp.float32)
        right = jnp.zeros(lane.shape, jnp.float32)
        for level in range(levels):
            value = jnp.where(lane < RIGHT_OWN, tile(ref, level, 0), 0.0)
            left = left + turned(value, STRIDE * level + LEFT_AT)
            value = jnp.where(lane >= LANES - RIGHT_OWN, tile(ref, level, cols // LANES - 1), 0.0)
            right = right + turned(value, STRIDE * level + RIGHT_OWN)
        packs[2 * at] = left
        packs[2 * at + 1] = right
    inner_substep(coefs, nest, source, first)


def inner_rest(coefs, first, source, after_pack, third, second):
    inner_substep(coefs, first, source, second)
    inner_substep(coefs, second, source, third)


def with_columns(tiles, left, right, me, parts, place):
    lane = iota(left.shape, 1)
    from_right = turned(right, -place)
    from_left = turned(left, -3 - place)
    if parts == 2:
        tiles[0] = jnp.where((lane < 3) & (me == 0), from_right, tiles[0])
        tiles[-1] = jnp.where((lane >= LANES - 3) & (me == 1), from_left, tiles[-1])
        return tiles
    extra = jnp.where(lane < 3, from_right, jnp.where(lane >= LANES - 3, from_left, 0.0))
    return tiles + [extra]


def pack_rows(
    parts, old_top, old_end, src_top, src_end, par_top, par_end, own_strip, offset_rows, *rest
):
    columns = rest[: parts - 1]
    across, within, far, strip_out, both = rest[parts - 1 :]
    core = lax.axis_index("gz")
    up, down = both.at[core], both.at[1 - core]
    levels, _, cols = old_top.shape
    me = lax.axis_index("gy")
    left, right = columns[0], columns[-1]
    rows = left.shape[0]
    strip_rows = own_strip.shape[0]
    lane = iota((strip_rows, LANES), 1)
    strips = own_strip[...]
    if parts == 2:
        oy = jnp.concatenate([offset_rows[1]] * (strip_rows // 8), axis=0)
        strips = strips + across_border(left[:strip_rows, :], oy, par_top.shape[2], me)
    else:
        for message in columns:
            strips = strips + message[:strip_rows, :]
        strips = jnp.where((lane & (STRIDE - 1)) >= STRIP_AT, strips, 0.0)
    strip_out[...] = strips
    far[...] = strips[:8]
    pieces = cols // LANES
    for out, old, src, first, at, src_at in (
        (up, old_end, src_end, rows - 8, 5, 6),
        (down, old_top, src_top, 0, 0, 0),
    ):
        y_left = left[first : first + 8, :]
        y_right = right[first : first + 8, :]
        for level in range(levels):
            for ref, shift, row, count, base in (
                (old, 0, at, 3, 0),
                (src, SOURCE_AT, src_at, 2, SOURCE_ROW),
            ):
                tiles = [tile(ref, level, piece) for piece in range(pieces)]
                tiles = with_columns(
                    tiles, y_left, y_right, me, parts, STRIDE * level + shift
                )
                for piece, value in enumerate(tiles):
                    out[
                        base + count * level : base + count * (level + 1),
                        piece * LANES : (piece + 1) * LANES,
                    ] = value[row : row + count]
    parent_cols = par_top.shape[2]
    for level in range(levels):
        up[TAIL_ROW + level : TAIL_ROW + level + 1, :parent_cols] = par_end[level, 7:8, :]
        down[TAIL_ROW + level : TAIL_ROW + level + 1, :parent_cols] = par_top[level, 0:1, :]
    up[TAIL_ROW : TAIL_ROW + 8, parent_cols : parent_cols + LANES] = strips[strip_rows - 8 :]
    down[TAIL_ROW : TAIL_ROW + 8, parent_cols : parent_cols + LANES] = strips[:8]
    down[TAIL_ROW + 8 : TAIL_ROW + 16, :LANES] = strips[8:16]
    down[TAIL_ROW + 8 : TAIL_ROW + 16, LANES : 2 * LANES] = strips[16:24]
    within[...] = both[0]
    across[...] = both[1]


def edges(
    parts,
    parent_cols,
    offset_rows,
    spread,
    nest,
    source,
    third,
    packs,
    strips,
    across,
    within,
    beyond,
    y_left,
    y_right,
    result,
    coarse_out,
    both,
    ping,
    pong,
    src,
    split,
):
    levels, rows, cols = nest.shape
    width = ping.shape[3]
    pieces = cols // LANES
    me = lax.axis_index("gy")
    core = lax.axis_index("gz")
    both[0] = within[...]
    both[1] = across[...]
    before, after = both.at[1 - core], both.at[core]
    is_south = me == 0
    is_north = me == parts - 1

    sub = iota((8, LANES), 0)
    old = jnp.concatenate(
        [
            strips[...],
            after[TAIL_ROW : TAIL_ROW + 8, parent_cols : parent_cols + LANES],
            after[TAIL_ROW + 8 : TAIL_ROW + 16, :LANES],
            after[TAIL_ROW + 8 : TAIL_ROW + 16, LANES : 2 * LANES],
            jnp.where(
                sub == 0,
                beyond[...],
                jnp.where(
                    sub == 7,
                    before[TAIL_ROW : TAIL_ROW + 8, parent_cols : parent_cols + LANES],
                    0.0,
                ),
            ),
        ],
        axis=0,
    )
    count = old.shape[0]

    def packed_coef(which, height):
        return jnp.concatenate([spread[0, which]] * (height // 8), axis=0)

    def stacked(value):
        lane = iota(value.shape, 1)
        below = jnp.where(lane >= STRIDE, turned(value, STRIDE), 0.0)
        return below + jnp.where(lane < STRIDE * (levels - 1), turned(value, -STRIDE), 0.0)

    def around(value):
        return (
            pltpu.roll(value, 1, 0)
            + pltpu.roll(value, value.shape[0] - 1, 0)
            + turned(value, 1)
            + turned(value, -1)
        )

    diff = (
        packed_coef(0, count) * (around(old) - 4.0 * old)
        + packed_coef(1, count) * (stacked(old) - 2.0 * old)
        + turned(old, STRIP_AT - STRIP_SOURCE_AT)
    )
    index = iota((rows + 16, count), 0)
    nest_row = jnp.where(index < rows, index, jnp.where(index < rows + 8, index - rows - 3, index - 13))
    parent_row = ((nest_row + 3) * 171 >> 9) - 1 + offset_rows[0, 0:1, :count]
    pick = (iota((rows + 16, count), 1) == parent_row).astype(jnp.float32)
    picked = jnp.dot(
        pick,
        jnp.concatenate([old, diff], axis=1),
        precision=HIGHEST,
        preferred_element_type=jnp.float32,
    )
    picked_old, picked_diff = picked[:, :LANES], picked[:, LANES:]

    lane = iota((rows, LANES), 1)
    c = lane & (STRIDE - 1)
    rim_first = jnp.where(is_south, LEFT_AT, RIGHT_OWN - RIM)
    in_rim = (c >= rim_first) & (c < rim_first + RIM)
    at = lane - c + STRIP_AT + jnp.where(c >= rim_first + 3, 2, 1)
    rim_old = jnp.take_along_axis(picked_old[:rows], at, axis=1)
    rim_diff = jnp.take_along_axis(picked_diff[:rows], at, axis=1)
    ch = packed_coef(2, rows)
    cv = packed_coef(3, rows)
    centre = 1.0 - 4.0 * ch - 2.0 * cv
    left = jnp.where(c < 3, y_left[...], packs[0])
    left_src = jnp.where(c < 3, turned(y_left[...], -SOURCE_AT), packs[2])
    right = jnp.where(c >= RIGHT_OWN, turned(y_right[...], RIGHT_OWN), packs[1])
    right_src = jnp.where(c >= RIGHT_OWN, turned(y_right[...], RIGHT_OWN - SOURCE_AT), packs[3])
    sides = []
    for value, forcing, rim in (
        (left, left_src, in_rim & is_south),
        (right, right_src, in_rim & is_north),
    ):
        for substep in range(1, SUBSTEPS + 1):
            value = centre * value + ch * around(value) + (cv * stacked(value) + forcing)
            value = jnp.where(rim, rim_old + (substep / SUBSTEPS) * rim_diff, value)
        sides.append(value)

    sub = iota((8, width), 0)
    lane = iota((8, LANES), 1)
    for level in range(levels):
        for buf, field, shift, n, base in (
            (ping, nest, 0, 3, 0),
            (src, source, SOURCE_AT, 2, SOURCE_ROW),
        ):
            for window, first, turn, at, message in (
                (0, 0, 3, 3 - n, before),
                (1, rows - 8, 5, 5, after),
            ):
                tiles = [
                    field[level, first : first + 8, piece * LANES : (piece + 1) * LANES]
                    for piece in range(pieces)
                ]
                tiles = with_columns(
                    tiles,
                    y_left[first : first + 8, :],
                    y_right[first : first + 8, :],
                    me,
                    parts,
                    STRIDE * level + shift,
                )
                for piece, value in enumerate(tiles):
                    value = pltpu.roll(value, turn, 0)
                    span = slice(piece * LANES, (piece + 1) * LANES)
                    buf[level, window, :, span] = value
                    if n == 3:
                        pong[level, window, :, span] = value
                buf[level, window, at : at + n, :] = message[
                    base + n * level : base + n * (level + 1), :
                ]
    rim_first = jnp.where(is_south, 0, LANES - RIM)
    column = STRIP_AT + jnp.where((lane >= rim_first + 3) & (lane < rim_first + RIM), 2, 1)
    rims = {}
    for level in range(levels):
        for window in range(2):
            span = slice(rows + 8 * window, rows + 8 * window + 8)
            at = column + STRIDE * level
            rims[level, window] = (
                jnp.take_along_axis(picked_old[span], at, axis=1),
                jnp.take_along_axis(picked_diff[span], at, axis=1),
            )
    for substep in range(1, SUBSTEPS + 1):
        here, there = (ping, pong) if substep % 2 else (pong, ping)
        low = 0 if substep == SUBSTEPS or parts > 2 else 3
        south = (lane >= low) & (lane < RIM) & is_south
        north = (lane >= LANES - RIM) & (lane < LANES - low) & is_north
        weight = substep / SUBSTEPS
        for level in range(levels):
            c_h, c_v = (
                jnp.concatenate([spread[1, which, level : level + 1, :]] * (width // LANES), axis=1)
                for which in (2, 3)
            )
            c_0 = 1.0 - 4.0 * c_h - 2.0 * c_v
            for window in range(2):
                now = here[level, window]
                up = pltpu.roll(now, 1, 0)
                down = pltpu.roll(now, 7, 0)
                if substep == 1:
                    beyond_row = pong[level, window]
                    if window == 0:
                        down = jnp.where(sub == 7, pltpu.roll(beyond_row, 7, 0), down)
                    else:
                        up = jnp.where(sub == 0, pltpu.roll(beyond_row, 1, 0), up)
                beside = pltpu.roll(now, 1, 1) + pltpu.roll(now, width - 1, 1)
                value = c_0 * now + c_h * ((up + down) + beside) + src[level, window]
                if level > 0:
                    value = value + c_v * here[level - 1, window]
                if level < levels - 1:
                    value = value + c_v * here[level + 1, window]
                rim_o, rim_d = rims[level, window]
                rim = rim_o + weight * rim_d
                for piece in range(width // LANES):
                    span = slice(piece * LANES, (piece + 1) * LANES)
                    part = value[:, span]
                    if piece == 0:
                        part = jnp.where(south, rim, part)
                    if piece == pieces - 1:
                        part = jnp.where(north, rim, part)
                    there[level, window, :, span] = part

    lane = iota((rows, LANES), 1)
    sub = iota((8, cols), 0)
    for level in range(levels):
        fixed = turned(sides[0], -STRIDE * level - LEFT_AT)
        result[level, :, :LANES] = jnp.where(lane < FIXED, fixed, tile(third, level, 0))
        for piece in range(1, pieces - 1):
            result[level, :, piece * LANES : (piece + 1) * LANES] = tile(third, level, piece)
        fixed = turned(sides[1], -STRIDE * level - RIGHT_OWN)
        result[level, :, cols - LANES :] = jnp.where(
            lane >= LANES - FIXED, fixed, tile(third, level, pieces - 1)
        )
        top = pltpu.roll(there[level, 0, :, :cols], 5, 0)
        result[level, :8, :] = jnp.where(sub < 3, top, result[level, :8, :])
        end = pltpu.roll(there[level, 1, :, :cols], 3, 0)
        result[level, rows - 8 :, :] = jnp.where(sub >= 5, end, result[level, rows - 8 :, :])

    foot = cols // RATIO
    offset = iota((cols, foot), 0) - RATIO * iota((cols, foot), 1)
    gather = ((offset >= 0) & (offset < RATIO)).astype(jnp.float32)
    parent_rows = rows // RATIO
    for level in range(levels):
        for piece in range(pieces):
            split[piece, level * rows : (level + 1) * rows, :] = tile(result, level, piece)
    total = levels * parent_rows
    sums = [
        split[piece, pl.ds(0, total, RATIO), :]
        + split[piece, pl.ds(1, total, RATIO), :]
        + split[piece, pl.ds(2, total, RATIO), :]
        for piece in range(pieces)
    ]
    means = jnp.dot(
        jnp.concatenate(sums, axis=1),
        gather,
        precision=HIGHEST,
        preferred_element_type=jnp.float32,
    ) * (1.0 / 9.0)
    coarse_out[...] = means.reshape(coarse_out.shape)


def parent_step(
    parts, spread, nest, parent, source, within, across, y_left, y_right, out, nest_out, tail, sem
):
    store = pltpu.make_async_copy(nest, nest_out, sem)
    store.start()
    core = lax.axis_index("gz")
    levels, rows, cols = parent.shape
    tail[0] = within[TAIL_ROW : TAIL_ROW + levels, :cols]
    tail[1] = across[TAIL_ROW : TAIL_ROW + levels, :cols]
    me = lax.axis_index("gy")
    row = iota((rows, cols), 0)
    lane = iota((rows, cols), 1)
    has_left = me > 0
    has_right = me < parts - 1
    left = y_left[:rows, :]
    right = y_right[:rows, :]
    zero = jnp.zeros((rows, cols), jnp.float32)
    for level in range(levels):
        now = parent[level]
        at = STRIDE * level + PARENT_AT
        from_left = left[:, at : at + 1]
        from_right = right[:, at : at + 1]
        top = tail[1 - core, level : level + 1, :]
        end = tail[core, level : level + 1, :]
        around = (
            jnp.where(row == 0, top, pltpu.roll(now, 1, 0))
            + jnp.where(row == rows - 1, end, pltpu.roll(now, rows - 1, 0))
            + jnp.where(
                lane == 0, jnp.where(has_left, from_left, 0.0), pltpu.roll(now, 1, 1)
            )
            + jnp.where(
                lane == cols - 1,
                jnp.where(has_right, from_right, 0.0),
                pltpu.roll(now, cols - 1, 1),
            )
        )
        stacked = (parent[level - 1] if level > 0 else zero) + (
            parent[level + 1] if level < levels - 1 else zero
        )
        ch, cv = (
            jnp.concatenate([spread[1, which, level : level + 1, :]] * (cols // LANES), axis=1)
            for which in (0, 1)
        )
        out[level] = (
            (1.0 - 4.0 * ch - 2.0 * cv) * now + ch * around + (cv * stacked + source[level])
        )
    store.wait()


def merge(parts, band, offsets, step, *rest):
    previous, own, out, joined = (
        rest[:parts],
        rest[parts : 2 * parts],
        rest[2 * parts],
        rest[2 * parts + 1],
    )
    levels, rows, cols = step.shape
    foot = own[0].shape[2]
    me = lax.axis_index("gy")
    ox = offsets[0]
    oy = offsets[1]
    for k in range(parts):
        joined[k, :, :rows, :] = previous[k][...]
        joined[k, :, rows:, :] = own[k][...]
    lane = iota((rows, LANES), 1)
    for level in range(levels):
        values = [tile(step, level, piece) for piece in range(cols // LANES)]
        for k in range(parts):
            source = lax.rem(me + parts - k, parts)
            block = joined[k, level, pl.ds(rows - ox, rows), :]
            begin = oy + source * foot - me * cols
            block = pltpu.roll(block, (16384 + begin) & (LANES - 1), 1)
            low = jnp.maximum(source * foot, 2)
            high = jnp.minimum((source + 1) * foot, band - 2)
            for piece in range(cols // LANES):
                at = lane + (piece * LANES + me * cols - oy)
                values[piece] = jnp.where((at >= low) & (at < high), block, values[piece])
        for piece, value in enumerate(values):
            out[level, :, piece * LANES : (piece + 1) * LANES] = value


def shifted(value, axis, steps):
    count = lax.axis_size(axis)
    pairs = [(source, (source + steps) % count) for source in range(count)]
    return lax.ppermute(value, axis, pairs)


def shards(
    parent_old, parent_source, parent_coefs, nest_old, nest_source, nest_coefs, offset_x, offset_y
):
    parts = lax.axis_size("gy")
    along = ("gx", "gz")
    levels, parent_rows, parent_cols = parent_old.shape
    _, rows, cols = nest_old.shape
    foot = cols // RATIO
    band = foot * parts
    width = cols if parts == 2 else cols + LANES
    height = TAIL_ROW + 16
    f32 = jnp.float32
    shape = jax.ShapeDtypeStruct
    anywhere = pl.BlockSpec(memory_space=pl.ANY)
    in_hbm = pl.BlockSpec(memory_space=pltpu.HBM)
    sides = 1 if parts == 2 else 2
    if parts == 2:
        packed = [
            pl.pallas_call(
                pack_pair,
                out_shape=shape((rows, LANES), f32),
                in_specs=[in_hbm] * 4,
                out_specs=whole(),
                scratch_shapes=[
                    VMEM((2, levels, rows, LANES), f32),
                    VMEM((2, levels, parent_rows, LANES), f32),
                    pltpu.SemaphoreType.DMA((4,)),
                ],
                compiler_params=params(MOST),
                cost_estimate=cost(200000, 800000),
                name="pack_pair",
            )(nest_old, nest_source, parent_old, parent_source)
        ]
    else:
        packed = pl.pallas_call(
            functools.partial(pack_columns, parts, band),
            out_shape=[
                shape((rows if k in (1, parts - 1) else parent_rows, LANES), f32)
                for k in range(1, parts)
            ],
            in_specs=[in_hbm] * 5,
            out_specs=[whole()] * (parts - 1),
            scratch_shapes=[
                VMEM((sides, levels, rows, LANES), f32),
                VMEM((sides, levels, rows, LANES), f32),
                VMEM(parent_old.shape, f32),
                VMEM(parent_old.shape, f32),
                pltpu.SMEM(offset_y.shape, jnp.int32),
                pltpu.SemaphoreType.DMA((sides, 2)),
                pltpu.SemaphoreType.DMA((3,)),
            ],
            compiler_params=params(MOST),
            cost_estimate=cost(200000, 1000000),
            name="pack_columns",
        )(offset_y, nest_old, nest_source, parent_old, parent_source)
    columns = [shifted(packed[k - 1], "gy", k) for k in range(1, parts)]
    own_strip, first, packs, spread, offset_rows, offsets = pl.pallas_call(
        functools.partial(inner_first, band),
        out_shape=[
            shape((parent_rows, LANES), f32),
            shape(nest_old.shape, f32),
            shape((4, rows, LANES), f32),
            shape((2, 4, levels, LANES), f32),
            shape((2, 8, LANES), jnp.int32),
            shape((2,), jnp.int32),
        ],
        in_specs=[in_hbm] * 2 + [scalars()] * 2 + [whole()] * 4,
        out_specs=[whole()] * 5 + [scalars()],
        scratch_shapes=[
            pltpu.SMEM(offset_x.shape, jnp.int32),
            pltpu.SMEM(offset_y.shape, jnp.int32),
            pltpu.SemaphoreType.DMA((2,)),
        ],
        compiler_params=params(),
        cost_estimate=cost(4000000, 3000000),
        name="inner_first",
    )(
        offset_x,
        offset_y,
        parent_coefs,
        nest_coefs,
        nest_old,
        nest_source,
        parent_old,
        parent_source,
    )

    def block(ref, last):
        count = ref.shape[1] // 8 - 1 if last else 0
        return pl.BlockSpec((levels, 8, ref.shape[2]), lambda i, c=count: (0, c, 0))

    def full(extent):
        return pl.BlockSpec(extent, lambda i: (0,) * len(extent))

    outs = [
        shape((height, width), f32),
        shape((height, width), f32),
        shape((8, LANES), f32),
        shape((parent_rows, LANES), f32),
    ]
    across, within, far, strips = pl.pallas_call(
        functools.partial(pack_rows, parts),
        out_shape=outs,
        grid=(1,),
        in_specs=[
            block(nest_old, False),
            block(nest_old, True),
            block(nest_old, False),
            block(nest_old, True),
            block(parent_old, False),
            block(parent_old, True),
            full(own_strip.shape),
            full(offset_rows.shape),
        ]
        + [full(message.shape) for message in columns],
        out_specs=[full(out.shape) for out in outs],
        scratch_shapes=[VMEM((2, height, width), f32)],
        compiler_params=params(),
        cost_estimate=cost(100000, 700000),
        name="pack_rows",
    )(nest_old, nest_old, nest_source, nest_source, parent_old, parent_old, own_strip, offset_rows, *columns)
    across = swapped(across, 1)
    within = swapped(within, 0)
    beyond = shifted(far, along, -2)
    third = pl.pallas_call(
        inner_rest,
        out_shape=shape(nest_old.shape, f32),
        in_specs=[scalars()] + [whole()] * 2 + [anywhere],
        out_specs=whole(),
        scratch_shapes=[VMEM(nest_old.shape, f32)],
        compiler_params=params(),
        cost_estimate=cost(8000000, 6000000),
        name="inner_rest",
    )(nest_coefs, first, nest_source, strips)
    nest_done, coarse = pl.pallas_call(
        functools.partial(edges, parts, parent_cols),
        out_shape=[
            shape(nest_old.shape, f32),
            shape((levels, parent_rows, foot), f32),
        ],
        in_specs=[whole()] * 12,
        out_specs=[whole(), whole()],
        scratch_shapes=[
            VMEM((2, height, width), f32),
            VMEM((levels, 2, 8, width), f32),
            VMEM((levels, 2, 8, width), f32),
            VMEM((levels, 2, 8, width), f32),
            VMEM((cols // LANES, levels * rows, LANES), f32),
        ],
        compiler_params=params(),
        cost_estimate=cost(4000000, 3000000),
        name="edges",
    )(
        offset_rows,
        spread,
        nest_old,
        nest_source,
        third,
        packs,
        strips,
        across,
        within,
        beyond,
        columns[0],
        columns[-1],
    )
    previous = [shifted(coarse, along, 1)] + [
        shifted_both(coarse, k) for k in range(1, parts)
    ]
    own = [coarse] + [shifted(coarse, "gy", k) for k in range(1, parts)]
    step, nest_new = pl.pallas_call(
        functools.partial(parent_step, parts),
        out_shape=[shape(parent_old.shape, f32), shape(nest_old.shape, f32)],
        in_specs=[whole(), anywhere] + [whole()] * 6,
        out_specs=[whole(), in_hbm],
        scratch_shapes=[VMEM((2, levels, parent_cols), f32), pltpu.SemaphoreType.DMA],
        compiler_params=params(),
        cost_estimate=cost(800000, 2500000),
        name="parent_step",
    )(
        spread,
        nest_done,
        parent_old,
        parent_source,
        within,
        across,
        columns[0],
        columns[-1],
    )
    parent_new = pl.pallas_call(
        functools.partial(merge, parts, band),
        out_shape=shape(parent_old.shape, f32),
        in_specs=[scalars()] + [whole()] * (1 + 2 * parts),
        out_specs=whole(),
        scratch_shapes=[VMEM((parts, levels, 2 * parent_rows, foot), f32)],
        compiler_params=params(),
        cost_estimate=cost(200000, 800000),
        name="merge",
    )(offsets, step, *previous, *own)
    return (parent_new, nest_new)


def swapped(value, first):
    along = ("gx", "gz")
    count = lax.axis_size(along)
    pairs = []
    for at in range(first, count, 2):
        pairs += [(at, (at + 1) % count), ((at + 1) % count, at)]
    return lax.ppermute(value, along, pairs)


def shifted_both(value, steps):
    sizes = [lax.axis_size(axis) for axis in ("gx", "gy", "gz")]
    gx, gy, gz = sizes
    pairs = []
    for x in range(gx):
        for y in range(gy):
            for z in range(gz):
                place = (x * gz + z + 1) % (gx * gz)
                target = (place // gz * gy + (y + steps) % gy) * gz + place % gz
                pairs.append(((x * gy + y) * gz + z, target))
    return lax.ppermute(value, ("gx", "gy", "gz"), pairs)


def solution(mesh):
    return jax.shard_map(
        shards,
        mesh=mesh,
        in_specs=(
            P(None, ("grp", "gx", "gz"), "gy"),
            P(None, ("grp", "gx", "gz"), "gy"),
            P(),
            P(None, ("grp", "gx", "gz"), "gy"),
            P(None, ("grp", "gx", "gz"), "gy"),
            P(),
            P("grp"),
            P("grp"),
        ),
        out_specs=(P(None, ("grp", "gx", "gz"), "gy"), P(None, ("grp", "gx", "gz"), "gy")),
        check_vma=False,
    )
```

```python
import functools

import jax
import jax.numpy as jnp
from jax import lax
from jax.experimental import pallas as pl
from jax.experimental.pallas import tpu as pltpu
from jax.sharding import PartitionSpec as P

RATIO = 3
SUBSTEPS = 3
RIM = 6
LANES = 128
STRIDE = 16
SOURCE_AT = 3
PARENT_AT = 6
STRIP_AT = 8
STRIP_SOURCE_AT = 12
SOURCE_ROW = 24
TAIL_ROW = 40
FIXED = 8
LEFT_AT = 3
RIGHT_OWN = STRIDE - 3
VMEM = pltpu.VMEM
LIMIT = 24 * 1024 * 1024
MOST = 54 * 1024 * 1024
HIGHEST = lax.Precision.HIGHEST


def iota(shape, dim):
    return lax.broadcasted_iota(jnp.int32, shape, dim)


def whole():
    return pl.BlockSpec(memory_space=VMEM)


def scalars():
    return pl.BlockSpec(memory_space=pltpu.SMEM)


def params(limit=LIMIT):
    return pltpu.CompilerParams(vmem_limit_bytes=limit)


def cost(flops, moved):
    return pl.CostEstimate(flops=flops, bytes_accessed=moved, transcendentals=0)


def tile(ref, level, index):
    return ref[level, :, index * LANES : (index + 1) * LANES]


def turned(value, lanes):
    lanes = lanes % LANES
    return pltpu.roll(value, lanes, 1) if lanes else value


def edge_strip(dest, band, oy, parent, parent_source):
    levels, rows, cols = parent.shape
    lane = iota((rows, LANES), 1)
    base = jnp.where(dest == 0, oy - 1, oy + band - 3) - lax.axis_index("gy") * cols
    total = jnp.zeros(lane.shape, jnp.float32)
    for ref, first in ((parent, STRIP_AT), (parent_source, STRIP_SOURCE_AT)):
        for level in range(levels):
            found = jnp.zeros(lane.shape, jnp.float32)
            for at in range(cols // LANES):
                place = lane + (at * LANES - base)
                found = jnp.where((place >= 0) & (place < 4), tile(ref, level, at), found)
            turn = (16384 + first + STRIDE * level - base) & (LANES - 1)
            total = total + pltpu.roll(found, turn, 1)
    return total


def pack_pair(nest, source, parent, parent_source, out, fine_buf, coarse_buf, sems):
    levels, rows, cols = nest.shape
    parent_rows, parent_cols = parent.shape[1:]
    right = lax.axis_index("gy") == 0
    loads = []
    for at, (ref, buf) in enumerate(
        (
            (parent, coarse_buf.at[0]),
            (parent_source, coarse_buf.at[1]),
            (nest, fine_buf.at[0]),
            (source, fine_buf.at[1]),
        )
    ):
        start = pl.multiple_of(jnp.where(right, ref.shape[2] - LANES, 0), LANES)
        loads.append(pltpu.make_async_copy(ref.at[:, :, pl.ds(start, LANES)], buf, sems.at[at]))
    for copy in loads:
        copy.start()

    def columns(value, count, to):
        first = jnp.where(right, LANES - count, 0)
        place = iota(value.shape, 1) - first
        value = jnp.where((place >= 0) & (place < count), value, 0.0)
        return pltpu.roll(value, (LANES + to - first) & (LANES - 1), 1)

    part = jnp.zeros((parent_rows, LANES), jnp.float32)
    loads[0].wait()
    loads[1].wait()
    for level in range(levels):
        base = STRIDE * level
        part = part + columns(coarse_buf[0, level], 1, base + PARENT_AT)
        part = part + columns(coarse_buf[0, level], 2, base + STRIP_AT)
        part = part + columns(coarse_buf[1, level], 2, base + STRIP_SOURCE_AT)
    total = jnp.zeros((rows, LANES), jnp.float32)
    loads[2].wait()
    loads[3].wait()
    for level in range(levels):
        base = STRIDE * level
        total = total + columns(fine_buf[0, level], 3, base)
        total = total + columns(fine_buf[1, level], 3, base + SOURCE_AT)
    out[...] = total
    out[:parent_rows, :] += part


def across_border(message, oy, parent_cols, me):
    c = iota(message.shape, 1) & (STRIDE - 1)
    place = jnp.where(me == 0, parent_cols + 1, 1) - oy
    total = jnp.zeros(message.shape, jnp.float32)
    for turn in (-1, 0, 2, 3):
        at = jnp.where(c >= STRIP_SOURCE_AT, c - STRIP_SOURCE_AT, c - STRIP_AT) - turn
        fits = (c >= STRIP_AT) & (at >= 0) & (at < 2) & (place == turn)
        total = total + jnp.where(fits, turned(message, turn), 0.0)
    return total


def pack_columns(parts, band, oy_hbm, nest, source, parent_hbm, parent_source_hbm, *rest):
    outs = rest[: parts - 1]
    old_buf, src_buf, parent, parent_source, oy_ref, sems, field_sems = rest[parts - 1 :]
    levels, rows, cols = nest.shape
    parent_cols = parent.shape[2]
    me = lax.axis_index("gy")
    sides = [1] if parts == 2 else [1, parts - 1]
    fields = [
        pltpu.make_async_copy(ref, buf, field_sems.at[at])
        for at, (ref, buf) in enumerate(
            ((oy_hbm, oy_ref), (parent_hbm, parent), (parent_source_hbm, parent_source))
        )
    ]
    for copy in fields:
        copy.start()
    copies = []
    for at, step in enumerate(sides):
        right = (me == 0) if parts == 2 else jnp.bool_(step == 1)
        start = pl.multiple_of(jnp.where(right, cols - LANES, 0), LANES)
        pair = [
            pltpu.make_async_copy(
                ref.at[:, :, pl.ds(start, LANES)], buf.at[at], sems.at[at, which]
            )
            for which, (ref, buf) in enumerate(((nest, old_buf), (source, src_buf)))
        ]
        for copy in pair:
            copy.start()
        copies.append((right, pair))
    for copy in fields:
        copy.wait()
    oy = oy_ref[0]
    lane = iota((parent.shape[1], LANES), 1)
    for step in range(1, parts):
        out = outs[step - 1]
        part = edge_strip(lax.rem(me + step, parts), band, oy, parent, parent_source)
        if step not in sides:
            out[...] = part
            continue
        at = sides.index(step)
        right, pair = copies[at]
        first = jnp.where(right, LANES - 3, 0)
        outer = jnp.where(right, LANES - 1, 0)
        for level in range(levels):
            edge = jnp.where(
                right, tile(parent, level, parent_cols // LANES - 1), tile(parent, level, 0)
            )
            edge = jnp.where(lane == outer, edge, 0.0)
            turn = (LANES + PARENT_AT + STRIDE * level - outer) & (LANES - 1)
            part = part + pltpu.roll(edge, turn, 1)
        for copy in pair:
            copy.wait()
        fine = iota((rows, LANES), 1) - first
        wanted = (fine >= 0) & (fine < 3)
        total = jnp.zeros((rows, LANES), jnp.float32)
        for level in range(levels):
            for buf, shift in ((old_buf, 0), (src_buf, SOURCE_AT)):
                value = jnp.where(wanted, buf[at, level], 0.0)
                turn = (LANES + STRIDE * level + shift - first) & (LANES - 1)
                total = total + pltpu.roll(value, turn, 1)
        out[...] = total
        out[: part.shape[0], :] += part


def inner_substep(coefs, here, source, there):
    levels, rows, cols = here.shape
    sub = iota((8, cols), 0)
    tiles = rows // 8

    def one_level(level):
        ch = coefs[0, level]
        cv = coefs[1, level]
        centre = 1.0 - 4.0 * ch - 2.0 * cv
        below = jnp.maximum(level - 1, 0)
        above = jnp.minimum(level + 1, levels - 1)
        cv_below = jnp.where(level > 0, cv, 0.0)
        cv_above = jnp.where(level < levels - 1, cv, 0.0)

        def row_tile(t):
            t = t % tiles
            return here[level, 8 * t : 8 * t + 8, :]

        down_before = pltpu.roll(row_tile(-1), 1, 0)
        now = row_tile(0)
        up_now = pltpu.roll(now, 7, 0)
        for t in range(tiles):
            following = row_tile(t + 1)
            down_now = pltpu.roll(now, 1, 0)
            up_next = pltpu.roll(following, 7, 0)
            around = jnp.where(sub == 0, down_before, down_now) + jnp.where(
                sub == 7, up_next, up_now
            )
            around = around + (pltpu.roll(now, 1, 1) + pltpu.roll(now, cols - 1, 1))
            span = slice(8 * t, 8 * t + 8)
            stacked = cv_below * here[below, span, :] + cv_above * here[above, span, :]
            there[level, span, :] = centre * now + ch * around + (stacked + source[level, span, :])
            down_before, now, up_now = down_now, following, up_next

    def two_levels(pair, carry):
        one_level(2 * pair)
        one_level(2 * pair + 1)
        return carry

    lax.fori_loop(0, levels // 2, two_levels, 0)


def spread_coefs(parent_coefs, coefs, out):
    levels = out.shape[2]
    lane = iota((levels, LANES), 1)
    row = iota((levels, LANES), 0)
    for at, ref in enumerate((parent_coefs, coefs)):
        for which in range(2):
            packed = jnp.full(lane.shape, ref[which, 0], jnp.float32)
            rows = packed
            for level in range(1, levels):
                packed = jnp.where(lane >= STRIDE * level, ref[which, level], packed)
                rows = jnp.where(row == level, ref[which, level], rows)
            out[0, 2 * at + which] = packed
            out[1, 2 * at + which] = rows


def inner_first(
    band,
    oy_ref,
    parent_coefs,
    coefs,
    nest,
    source,
    parent,
    parent_source,
    strip,
    first,
    packs,
    spread,
    oy_rows,
):
    levels, rows, cols = nest.shape
    oy = oy_ref[0]
    oy_rows[...] = jnp.full(oy_rows.shape, oy, jnp.int32)
    spread_coefs(parent_coefs, coefs, spread)
    strip[...] = edge_strip(lax.axis_index("gy"), band, oy, parent, parent_source)
    lane = iota((rows, LANES), 1)
    for at, ref in enumerate((nest, source)):
        left = jnp.zeros(lane.shape, jnp.float32)
        right = jnp.zeros(lane.shape, jnp.float32)
        for level in range(levels):
            value = jnp.where(lane < RIGHT_OWN, tile(ref, level, 0), 0.0)
            left = left + turned(value, STRIDE * level + LEFT_AT)
            value = jnp.where(lane >= LANES - RIGHT_OWN, tile(ref, level, cols // LANES - 1), 0.0)
            right = right + turned(value, STRIDE * level + RIGHT_OWN)
        packs[2 * at] = left
        packs[2 * at + 1] = right
    inner_substep(coefs, nest, source, first)


def inner_rest(coefs, first, source, after_pack, third, second):
    inner_substep(coefs, first, source, second)
    inner_substep(coefs, second, source, third)


def with_columns(tiles, left, right, me, parts, place):
    lane = iota(left.shape, 1)
    from_right = turned(right, -place)
    from_left = turned(left, -3 - place)
    if parts == 2:
        tiles[0] = jnp.where((lane < 3) & (me == 0), from_right, tiles[0])
        tiles[-1] = jnp.where((lane >= LANES - 3) & (me == 1), from_left, tiles[-1])
        return tiles
    extra = jnp.where(lane < 3, from_right, jnp.where(lane >= LANES - 3, from_left, 0.0))
    return tiles + [extra]


def pack_rows(
    parts, old_top, old_end, src_top, src_end, par_top, par_end, own_strip, oy_rows, *rest
):
    columns = rest[: parts - 1]
    across, within, far, strip_out, both = rest[parts - 1 :]
    core = lax.axis_index("gz")
    up, down = both.at[core], both.at[1 - core]
    levels, _, cols = old_top.shape
    me = lax.axis_index("gy")
    left, right = columns[0], columns[-1]
    rows = left.shape[0]
    strip_rows = own_strip.shape[0]
    lane = iota((strip_rows, LANES), 1)
    strips = own_strip[...]
    if parts == 2:
        oy = jnp.concatenate([oy_rows[...]] * (strip_rows // 8), axis=0)
        strips = strips + across_border(left[:strip_rows, :], oy, par_top.shape[2], me)
    else:
        for message in columns:
            strips = strips + message[:strip_rows, :]
    c = lane & (STRIDE - 1)
    strips = jnp.where(c >= STRIP_AT, strips, 0.0)
    strips = jnp.where(c == PARENT_AT, left[:strip_rows, :], strips)
    strips = jnp.where(c == PARENT_AT + 1, turned(right[:strip_rows, :], 1), strips)
    strip_out[...] = strips
    far[...] = strips[:8]
    pieces = cols // LANES
    for out, old, src, first, at, src_at in (
        (up, old_end, src_end, rows - 8, 5, 6),
        (down, old_top, src_top, 0, 0, 0),
    ):
        y_left = left[first : first + 8, :]
        y_right = right[first : first + 8, :]
        for level in range(levels):
            for ref, shift, row, count, base in (
                (old, 0, at, 3, 0),
                (src, SOURCE_AT, src_at, 2, SOURCE_ROW),
            ):
                tiles = [tile(ref, level, piece) for piece in range(pieces)]
                tiles = with_columns(
                    tiles, y_left, y_right, me, parts, STRIDE * level + shift
                )
                for piece, value in enumerate(tiles):
                    out[
                        base + count * level : base + count * (level + 1),
                        piece * LANES : (piece + 1) * LANES,
                    ] = value[row : row + count]
    parent_cols = par_top.shape[2]
    for level in range(levels):
        up[TAIL_ROW + level : TAIL_ROW + level + 1, :parent_cols] = par_end[level, 7:8, :]
        down[TAIL_ROW + level : TAIL_ROW + level + 1, :parent_cols] = par_top[level, 0:1, :]
    up[TAIL_ROW : TAIL_ROW + 8, parent_cols : parent_cols + LANES] = strips[strip_rows - 8 :]
    down[TAIL_ROW : TAIL_ROW + 8, parent_cols : parent_cols + LANES] = strips[:8]
    down[TAIL_ROW + 8 : TAIL_ROW + 16, :LANES] = strips[8:16]
    down[TAIL_ROW + 8 : TAIL_ROW + 16, LANES : 2 * LANES] = strips[16:24]
    within[...] = both[0]
    across[...] = both[1]


def edges(
    parts,
    parent_cols,
    ox_ref,
    spread,
    nest,
    source,
    third,
    packs,
    strips,
    across,
    within,
    far,
    y_left,
    y_right,
    result,
    coarse_out,
    far_out,
    both,
    ping,
    pong,
    src,
    split,
):
    levels, rows, cols = nest.shape
    width = ping.shape[3]
    pieces = cols // LANES
    me = lax.axis_index("gy")
    core = lax.axis_index("gz")
    both[0] = within[...]
    both[1] = across[...]
    before, after = both.at[1 - core], both.at[core]
    is_south = me == 0
    is_north = me == parts - 1

    far_out[...] = far[...]
    sub = iota((8, LANES), 0)
    old = jnp.concatenate(
        [
            strips[...],
            after[TAIL_ROW : TAIL_ROW + 8, parent_cols : parent_cols + LANES],
            after[TAIL_ROW + 8 : TAIL_ROW + 16, :LANES],
            after[TAIL_ROW + 8 : TAIL_ROW + 16, LANES : 2 * LANES],
            jnp.where(
                sub == 7,
                before[TAIL_ROW : TAIL_ROW + 8, parent_cols : parent_cols + LANES],
                0.0,
            ),
        ],
        axis=0,
    )
    count = old.shape[0]

    def packed_coef(which, height):
        return jnp.concatenate([spread[0, which]] * (height // 8), axis=0)

    def stacked(value):
        lane = iota(value.shape, 1)
        below = jnp.where(lane >= STRIDE, turned(value, STRIDE), 0.0)
        return below + jnp.where(lane < STRIDE * (levels - 1), turned(value, -STRIDE), 0.0)

    def around(value):
        return (
            pltpu.roll(value, 1, 0)
            + pltpu.roll(value, value.shape[0] - 1, 0)
            + turned(value, 1)
            + turned(value, -1)
        )

    diff = (
        packed_coef(0, count) * (around(old) - 4.0 * old)
        + packed_coef(1, count) * (stacked(old) - 2.0 * old)
        + turned(old, STRIP_AT - STRIP_SOURCE_AT)
    )
    index = iota((rows + 16, count), 0)
    nest_row = jnp.where(index < rows, index, jnp.where(index < rows + 8, index - rows - 3, index - 13))
    parent_row = ((nest_row + 3) * 171 >> 9) - 1 + ox_ref[0]
    pick = (iota((rows + 16, count), 1) == parent_row).astype(jnp.float32)
    picked = jnp.dot(
        pick,
        jnp.concatenate([old, diff], axis=1),
        precision=HIGHEST,
        preferred_element_type=jnp.float32,
    )
    picked_old, picked_diff = picked[:, :LANES], picked[:, LANES:]

    lane = iota((rows, LANES), 1)
    c = lane & (STRIDE - 1)
    rim_first = jnp.where(is_south, LEFT_AT, RIGHT_OWN - RIM)
    in_rim = (c >= rim_first) & (c < rim_first + RIM)
    at = lane - c + STRIP_AT + jnp.where(c >= rim_first + 3, 2, 1)
    rim_old = jnp.take_along_axis(picked_old[:rows], at, axis=1)
    rim_diff = jnp.take_along_axis(picked_diff[:rows], at, axis=1)
    ch = packed_coef(2, rows)
    cv = packed_coef(3, rows)
    centre = 1.0 - 4.0 * ch - 2.0 * cv
    left = jnp.where(c < 3, y_left[...], packs[0])
    left_src = jnp.where(c < 3, turned(y_left[...], -SOURCE_AT), packs[2])
    right = jnp.where(c >= RIGHT_OWN, turned(y_right[...], RIGHT_OWN), packs[1])
    right_src = jnp.where(c >= RIGHT_OWN, turned(y_right[...], RIGHT_OWN - SOURCE_AT), packs[3])
    sides = []
    for value, forcing, rim in (
        (left, left_src, in_rim & is_south),
        (right, right_src, in_rim & is_north),
    ):
        for substep in range(1, SUBSTEPS + 1):
            value = centre * value + ch * around(value) + (cv * stacked(value) + forcing)
            value = jnp.where(rim, rim_old + (substep / SUBSTEPS) * rim_diff, value)
        sides.append(value)

    sub = iota((8, width), 0)
    lane = iota((8, LANES), 1)
    for level in range(levels):
        for buf, field, shift, n, base in (
            (ping, nest, 0, 3, 0),
            (src, source, SOURCE_AT, 2, SOURCE_ROW),
        ):
            for window, first, turn, at, message in (
                (0, 0, 3, 3 - n, before),
                (1, rows - 8, 5, 5, after),
            ):
                tiles = [
                    field[level, first : first + 8, piece * LANES : (piece + 1) * LANES]
                    for piece in range(pieces)
                ]
                tiles = with_columns(
                    tiles,
                    y_left[first : first + 8, :],
                    y_right[first : first + 8, :],
                    me,
                    parts,
                    STRIDE * level + shift,
                )
                for piece, value in enumerate(tiles):
                    value = pltpu.roll(value, turn, 0)
                    span = slice(piece * LANES, (piece + 1) * LANES)
                    buf[level, window, :, span] = value
                    if n == 3:
                        pong[level, window, :, span] = value
                buf[level, window, at : at + n, :] = message[
                    base + n * level : base + n * (level + 1), :
                ]
    rim_first = jnp.where(is_south, 0, LANES - RIM)
    column = STRIP_AT + jnp.where((lane >= rim_first + 3) & (lane < rim_first + RIM), 2, 1)
    rims = {}
    for level in range(levels):
        for window in range(2):
            span = slice(rows + 8 * window, rows + 8 * window + 8)
            at = column + STRIDE * level
            rims[level, window] = (
                jnp.take_along_axis(picked_old[span], at, axis=1),
                jnp.take_along_axis(picked_diff[span], at, axis=1),
            )
    for substep in range(1, SUBSTEPS + 1):
        here, there = (ping, pong) if substep % 2 else (pong, ping)
        low = 0 if substep == SUBSTEPS or parts > 2 else 3
        south = (lane >= low) & (lane < RIM) & is_south
        north = (lane >= LANES - RIM) & (lane < LANES - low) & is_north
        weight = substep / SUBSTEPS
        for level in range(levels):
            c_h, c_v = (
                jnp.concatenate([spread[1, which, level : level + 1, :]] * (width // LANES), axis=1)
                for which in (2, 3)
            )
            c_0 = 1.0 - 4.0 * c_h - 2.0 * c_v
            for window in range(2):
                now = here[level, window]
                up = pltpu.roll(now, 1, 0)
                down = pltpu.roll(now, 7, 0)
                if substep == 1:
                    beyond_row = pong[level, window]
                    if window == 0:
                        down = jnp.where(sub == 7, pltpu.roll(beyond_row, 7, 0), down)
                    else:
                        up = jnp.where(sub == 0, pltpu.roll(beyond_row, 1, 0), up)
                beside = pltpu.roll(now, 1, 1) + pltpu.roll(now, width - 1, 1)
                value = c_0 * now + c_h * ((up + down) + beside) + src[level, window]
                if level > 0:
                    value = value + c_v * here[level - 1, window]
                if level < levels - 1:
                    value = value + c_v * here[level + 1, window]
                rim_o, rim_d = rims[level, window]
                rim = rim_o + weight * rim_d
                for piece in range(width // LANES):
                    span = slice(piece * LANES, (piece + 1) * LANES)
                    part = value[:, span]
                    if piece == 0:
                        part = jnp.where(south, rim, part)
                    if piece == pieces - 1:
                        part = jnp.where(north, rim, part)
                    there[level, window, :, span] = part

    lane = iota((rows, LANES), 1)
    sub = iota((8, cols), 0)
    for level in range(levels):
        fixed = turned(sides[0], -STRIDE * level - LEFT_AT)
        result[level, :, :LANES] = jnp.where(lane < FIXED, fixed, tile(third, level, 0))
        for piece in range(1, pieces - 1):
            result[level, :, piece * LANES : (piece + 1) * LANES] = tile(third, level, piece)
        fixed = turned(sides[1], -STRIDE * level - RIGHT_OWN)
        result[level, :, cols - LANES :] = jnp.where(
            lane >= LANES - FIXED, fixed, tile(third, level, pieces - 1)
        )
        top = pltpu.roll(there[level, 0, :, :cols], 5, 0)
        result[level, :8, :] = jnp.where(sub < 3, top, result[level, :8, :])
        end = pltpu.roll(there[level, 1, :, :cols], 3, 0)
        result[level, rows - 8 :, :] = jnp.where(sub >= 5, end, result[level, rows - 8 :, :])

    foot = cols // RATIO
    offset = iota((cols, foot), 0) - RATIO * iota((cols, foot), 1)
    gather = ((offset >= 0) & (offset < RATIO)).astype(jnp.float32)
    parent_rows = rows // RATIO
    for level in range(levels):
        for piece in range(pieces):
            split[piece, level * rows : (level + 1) * rows, :] = tile(result, level, piece)
    total = levels * parent_rows
    sums = [
        split[piece, pl.ds(0, total, RATIO), :]
        + split[piece, pl.ds(1, total, RATIO), :]
        + split[piece, pl.ds(2, total, RATIO), :]
        for piece in range(pieces)
    ]
    means = jnp.dot(
        jnp.concatenate(sums, axis=1),
        gather,
        precision=HIGHEST,
        preferred_element_type=jnp.float32,
    ) * (1.0 / 9.0)
    coarse_out[...] = means.reshape(coarse_out.shape)


def parent_step(
    parts,
    band,
    ox_ref,
    oy_ref,
    spread,
    nest,
    parent,
    source,
    within,
    across,
    beyond,
    y_left,
    y_right,
    out,
    nest_out,
    late,
    tail,
    corner,
    sem,
):
    store = pltpu.make_async_copy(nest, nest_out, sem)
    store.start()
    core = lax.axis_index("gz")
    levels, rows, cols = parent.shape
    tail[0] = within[TAIL_ROW : TAIL_ROW + levels, : cols + LANES]
    tail[1] = across[TAIL_ROW : TAIL_ROW + levels, : cols + LANES]
    me = lax.axis_index("gy")
    is_last = ox_ref[0] == rows - 1
    wide = iota((1, cols), 1)
    south = (wide == oy_ref[0] + 2 - me * cols) & is_last
    north = (wide == oy_ref[0] + band - 3 - me * cols) & is_last
    row = iota((rows, cols), 0)
    lane = iota((rows, cols), 1)
    has_left = me > 0
    has_right = me < parts - 1
    left = y_left[:rows, :]
    right = y_right[:rows, :]
    zero = jnp.zeros((rows, cols), jnp.float32)
    for level in range(levels):
        now = parent[level]
        at = STRIDE * level + PARENT_AT
        from_left = left[:, at : at + 1]
        from_right = right[:, at : at + 1]
        top = tail[1 - core, level : level + 1, :cols]
        end = tail[core, level : level + 1, :cols]
        around = (
            jnp.where(row == 0, top, pltpu.roll(now, 1, 0))
            + jnp.where(row == rows - 1, end, pltpu.roll(now, rows - 1, 0))
            + jnp.where(
                lane == 0, jnp.where(has_left, from_left, 0.0), pltpu.roll(now, 1, 1)
            )
            + jnp.where(
                lane == cols - 1,
                jnp.where(has_right, from_right, 0.0),
                pltpu.roll(now, cols - 1, 1),
            )
        )
        stacked = (parent[level - 1] if level > 0 else zero) + (
            parent[level + 1] if level < levels - 1 else zero
        )
        ch, cv = (
            jnp.concatenate([spread[1, which, level : level + 1, :]] * (cols // LANES), axis=1)
            for which in (0, 1)
        )
        out[level] = (
            (1.0 - 4.0 * ch - 2.0 * cv) * now + ch * around + (cv * stacked + source[level])
        )
        at = cols + STRIDE * level + PARENT_AT
        before_end = jnp.where(
            wide == 0, tail[core, 0:1, at : at + 1], pltpu.roll(end, 1, 1)
        )
        after_end = jnp.where(
            wide == cols - 1, tail[core, 0:1, at + 1 : at + 2], pltpu.roll(end, cols - 1, 1)
        )
        nest_ch = spread[1, 2, level : level + 1, :]
        nest_ch = jnp.concatenate([nest_ch] * (cols // LANES), axis=1)
        share = nest_ch * nest_ch * ch * (1.0 / SUBSTEPS)
        late[level : level + 1, :] = (share * (1.0 / (RATIO * RATIO))) * (
            jnp.where(south, before_end, 0.0) + jnp.where(north, after_end, 0.0)
        )
    store.wait()

    @pl.when(is_last & ((me == 0) | (me == parts - 1)))
    def _():
        nest_rows, nest_cols = nest.shape[1:]
        first = pl.multiple_of(jnp.where(me == 0, 0, nest_cols - LANES), LANES)
        place = (slice(None), pl.ds(nest_rows - 8, 8), pl.ds(first, LANES))
        load = pltpu.make_async_copy(nest.at[place], corner, sem)
        load.start()
        load.wait()
        sub = iota((8, LANES), 0)
        lane = iota((8, LANES), 1)
        cell = (sub == 7) & (lane == jnp.where(me == 0, RIM, LANES - RIM - 1))
        for level in range(levels):
            at = STRIDE * level + STRIP_AT
            value = jnp.where(me == 0, beyond[0:1, at + 2 : at + 3], beyond[0:1, at + 1 : at + 2])
            nest_ch = spread[1, 2, level : level + 1, :]
            share = nest_ch * nest_ch * spread[1, 0, level : level + 1, :] * (1.0 / SUBSTEPS)
            corner[level] += jnp.where(cell, share * value, 0.0)
        again = pltpu.make_async_copy(corner, nest_out.at[place], sem)
        again.start()
        again.wait()


def merge(parts, band, ox_ref, oy_ref, late, step, *rest):
    previous, own, out, joined = (
        rest[:parts],
        rest[parts : 2 * parts],
        rest[2 * parts],
        rest[2 * parts + 1],
    )
    levels, rows, cols = step.shape
    foot = own[0].shape[2]
    me = lax.axis_index("gy")
    ox = ox_ref[0]
    oy = oy_ref[0]
    for k in range(parts):
        joined[k, :, :rows, :] = previous[k][...]
        joined[k, :, rows:, :] = own[k][...]
    lane = iota((rows, LANES), 1)
    row = iota((rows, LANES), 0)
    for level in range(levels):
        values = [tile(step, level, piece) for piece in range(cols // LANES)]
        for k in range(parts):
            source = lax.rem(me + parts - k, parts)
            block = joined[k, level, pl.ds(rows - ox, rows), :]
            begin = oy + source * foot - me * cols
            block = pltpu.roll(block, (16384 + begin) & (LANES - 1), 1)
            low = jnp.maximum(source * foot, 2)
            high = jnp.minimum((source + 1) * foot, band - 2)
            for piece in range(cols // LANES):
                at = lane + (piece * LANES + me * cols - oy)
                values[piece] = jnp.where((at >= low) & (at < high), block, values[piece])
        for piece, value in enumerate(values):
            term = late[level : level + 1, piece * LANES : (piece + 1) * LANES]
            value = value + jnp.where(row == rows - 2, term, 0.0)
            out[level, :, piece * LANES : (piece + 1) * LANES] = value


def shifted(value, axis, steps):
    count = lax.axis_size(axis)
    pairs = [(source, (source + steps) % count) for source in range(count)]
    return lax.ppermute(value, axis, pairs)


def shards(
    parent_old, parent_source, parent_coefs, nest_old, nest_source, nest_coefs, offset_x, offset_y
):
    parts = lax.axis_size("gy")
    along = ("gx", "gz")
    levels, parent_rows, parent_cols = parent_old.shape
    _, rows, cols = nest_old.shape
    foot = cols // RATIO
    band = foot * parts
    width = cols if parts == 2 else cols + LANES
    height = TAIL_ROW + 16
    f32 = jnp.float32
    shape = jax.ShapeDtypeStruct
    anywhere = pl.BlockSpec(memory_space=pl.ANY)
    in_hbm = pl.BlockSpec(memory_space=pltpu.HBM)
    sides = 1 if parts == 2 else 2
    if parts == 2:
        packed = [
            pl.pallas_call(
                pack_pair,
                out_shape=shape((rows, LANES), f32),
                in_specs=[in_hbm] * 4,
                out_specs=whole(),
                scratch_shapes=[
                    VMEM((2, levels, rows, LANES), f32),
                    VMEM((2, levels, parent_rows, LANES), f32),
                    pltpu.SemaphoreType.DMA((4,)),
                ],
                compiler_params=params(MOST),
                cost_estimate=cost(200000, 800000),
                name="pack_pair",
            )(nest_old, nest_source, parent_old, parent_source)
        ]
    else:
        packed = pl.pallas_call(
            functools.partial(pack_columns, parts, band),
            out_shape=[
                shape((rows if k in (1, parts - 1) else parent_rows, LANES), f32)
                for k in range(1, parts)
            ],
            in_specs=[in_hbm] * 5,
            out_specs=[whole()] * (parts - 1),
            scratch_shapes=[
                VMEM((sides, levels, rows, LANES), f32),
                VMEM((sides, levels, rows, LANES), f32),
                VMEM(parent_old.shape, f32),
                VMEM(parent_old.shape, f32),
                pltpu.SMEM(offset_y.shape, jnp.int32),
                pltpu.SemaphoreType.DMA((sides, 2)),
                pltpu.SemaphoreType.DMA((3,)),
            ],
            compiler_params=params(MOST),
            cost_estimate=cost(200000, 1000000),
            name="pack_columns",
        )(offset_y, nest_old, nest_source, parent_old, parent_source)
    columns = [shifted(packed[k - 1], "gy", k) for k in range(1, parts)]
    own_strip, first, packs, spread, oy_rows = pl.pallas_call(
        functools.partial(inner_first, band),
        out_shape=[
            shape((parent_rows, LANES), f32),
            shape(nest_old.shape, f32),
            shape((4, rows, LANES), f32),
            shape((2, 4, levels, LANES), f32),
            shape((8, LANES), jnp.int32),
        ],
        in_specs=[scalars()] * 3 + [whole()] * 4,
        out_specs=[whole()] * 5,
        compiler_params=params(),
        cost_estimate=cost(4000000, 3000000),
        name="inner_first",
    )(
        offset_y,
        parent_coefs,
        nest_coefs,
        nest_old,
        nest_source,
        parent_old,
        parent_source,
    )

    def block(ref, last):
        count = ref.shape[1] // 8 - 1 if last else 0
        return pl.BlockSpec((levels, 8, ref.shape[2]), lambda i, c=count: (0, c, 0))

    def full(extent):
        return pl.BlockSpec(extent, lambda i: (0,) * len(extent))

    outs = [
        shape((height, width), f32),
        shape((height, width), f32),
        shape((8, LANES), f32),
        shape((parent_rows, LANES), f32),
    ]
    across, within, far, strips = pl.pallas_call(
        functools.partial(pack_rows, parts),
        out_shape=outs,
        grid=(1,),
        in_specs=[
            block(nest_old, False),
            block(nest_old, True),
            block(nest_old, False),
            block(nest_old, True),
            block(parent_old, False),
            block(parent_old, True),
            full(own_strip.shape),
            full(oy_rows.shape),
        ]
        + [full(message.shape) for message in columns],
        out_specs=[full(out.shape) for out in outs],
        scratch_shapes=[VMEM((2, height, width), f32)],
        compiler_params=params(),
        cost_estimate=cost(100000, 700000),
        name="pack_rows",
    )(nest_old, nest_old, nest_source, nest_source, parent_old, parent_old, own_strip, oy_rows, *columns)
    across = swapped(across, 1)
    within = swapped(within, 0)
    third = pl.pallas_call(
        inner_rest,
        out_shape=shape(nest_old.shape, f32),
        in_specs=[scalars()] + [whole()] * 2 + [anywhere],
        out_specs=whole(),
        scratch_shapes=[VMEM(nest_old.shape, f32)],
        compiler_params=params(),
        cost_estimate=cost(8000000, 6000000),
        name="inner_rest",
    )(nest_coefs, first, nest_source, strips)
    nest_done, coarse, far = pl.pallas_call(
        functools.partial(edges, parts, parent_cols),
        out_shape=[
            shape(nest_old.shape, f32),
            shape((levels, parent_rows, foot), f32),
            shape((8, LANES), f32),
        ],
        in_specs=[scalars()] + [whole()] * 11,
        out_specs=[whole()] * 3,
        scratch_shapes=[
            VMEM((2, height, width), f32),
            VMEM((levels, 2, 8, width), f32),
            VMEM((levels, 2, 8, width), f32),
            VMEM((levels, 2, 8, width), f32),
            VMEM((cols // LANES, levels * rows, LANES), f32),
        ],
        compiler_params=params(),
        cost_estimate=cost(4000000, 3000000),
        name="edges",
    )(
        offset_x,
        spread,
        nest_old,
        nest_source,
        third,
        packs,
        strips,
        across,
        within,
        far,
        columns[0],
        columns[-1],
    )
    previous = [shifted(coarse, along, 1)] + [
        shifted_both(coarse, k) for k in range(1, parts)
    ]
    own = [coarse] + [shifted(coarse, "gy", k) for k in range(1, parts)]
    beyond = shifted(far, along, -2)
    step, nest_new, late = pl.pallas_call(
        functools.partial(parent_step, parts, band),
        out_shape=[
            shape(parent_old.shape, f32),
            shape(nest_old.shape, f32),
            shape((levels, parent_cols), f32),
        ],
        in_specs=[scalars()] * 2 + [whole(), anywhere] + [whole()] * 7,
        out_specs=[whole(), in_hbm, whole()],
        scratch_shapes=[
            VMEM((2, levels, parent_cols + LANES), f32),
            VMEM((levels, 8, LANES), f32),
            pltpu.SemaphoreType.DMA,
        ],
        compiler_params=params(),
        cost_estimate=cost(800000, 2500000),
        name="parent_step",
    )(
        offset_x,
        offset_y,
        spread,
        nest_done,
        parent_old,
        parent_source,
        within,
        across,
        beyond,
        columns[0],
        columns[-1],
    )
    parent_new = pl.pallas_call(
        functools.partial(merge, parts, band),
        out_shape=shape(parent_old.shape, f32),
        in_specs=[scalars()] * 2 + [whole()] * (2 + 2 * parts),
        out_specs=whole(),
        scratch_shapes=[VMEM((parts, levels, 2 * parent_rows, foot), f32)],
        compiler_params=params(),
        cost_estimate=cost(200000, 800000),
        name="merge",
    )(offset_x, offset_y, late, step, *previous, *own)
    return (parent_new, nest_new)


def swapped(value, first):
    along = ("gx", "gz")
    count = lax.axis_size(along)
    pairs = []
    for at in range(first, count, 2):
        pairs += [(at, (at + 1) % count), ((at + 1) % count, at)]
    return lax.ppermute(value, along, pairs)


def shifted_both(value, steps):
    sizes = [lax.axis_size(axis) for axis in ("gx", "gy", "gz")]
    gx, gy, gz = sizes
    pairs = []
    for x in range(gx):
        for y in range(gy):
            for z in range(gz):
                place = (x * gz + z + 1) % (gx * gz)
                target = (place // gz * gy + (y + steps) % gy) * gz + place % gz
                pairs.append(((x * gy + y) * gz + z, target))
    return lax.ppermute(value, ("gx", "gy", "gz"), pairs)


def solution(mesh):
    return jax.shard_map(
        shards,
        mesh=mesh,
        in_specs=(
            P(None, ("grp", "gx", "gz"), "gy"),
            P(None, ("grp", "gx", "gz"), "gy"),
            P(),
            P(None, ("grp", "gx", "gz"), "gy"),
            P(None, ("grp", "gx", "gz"), "gy"),
            P(),
            P("grp"),
            P("grp"),
        ),
        out_specs=(P(None, ("grp", "gx", "gz"), "gy"), P(None, ("grp", "gx", "gz"), "gy")),
        check_vma=False,
    )
```

```python
import functools

import jax
import jax.numpy as jnp
from jax import lax
from jax.experimental import pallas as pl
from jax.experimental.pallas import tpu as pltpu
from jax.sharding import PartitionSpec as P

RATIO = 3
SUBSTEPS = 3
RIM = 6
LANES = 128
STRIDE = 16
SOURCE_AT = 3
PARENT_AT = 6
STRIP_AT = 8
STRIP_SOURCE_AT = 12
SOURCE_ROW = 24
TAIL_ROW = 40
FIXED = 8
LEFT_AT = 3
RIGHT_OWN = STRIDE - 3
VMEM = pltpu.VMEM
LIMIT = 24 * 1024 * 1024
MOST = 54 * 1024 * 1024
HIGHEST = lax.Precision.HIGHEST


def iota(shape, dim):
    return lax.broadcasted_iota(jnp.int32, shape, dim)


def whole():
    return pl.BlockSpec(memory_space=VMEM)


def scalars():
    return pl.BlockSpec(memory_space=pltpu.SMEM)


def params(limit=LIMIT):
    return pltpu.CompilerParams(vmem_limit_bytes=limit)


def cost(flops, moved):
    return pl.CostEstimate(flops=flops, bytes_accessed=moved, transcendentals=0)


def tile(ref, level, index):
    return ref[level, :, index * LANES : (index + 1) * LANES]


def turned(value, lanes):
    lanes = lanes % LANES
    return pltpu.roll(value, lanes, 1) if lanes else value


def edge_strip(dest, band, oy, parent, parent_source):
    levels, rows, cols = parent.shape
    lane = iota((rows, LANES), 1)
    base = jnp.where(dest == 0, oy - 1, oy + band - 3) - lax.axis_index("gy") * cols
    total = jnp.zeros(lane.shape, jnp.float32)
    for ref, first in ((parent, STRIP_AT), (parent_source, STRIP_SOURCE_AT)):
        for level in range(levels):
            found = jnp.zeros(lane.shape, jnp.float32)
            for at in range(cols // LANES):
                place = lane + (at * LANES - base)
                found = jnp.where((place >= 0) & (place < 4), tile(ref, level, at), found)
            turn = (16384 + first + STRIDE * level - base) & (LANES - 1)
            total = total + pltpu.roll(found, turn, 1)
    return total


def pack_pair(nest, source, parent, parent_source, out, fine_buf, coarse_buf, sems):
    levels, rows, cols = nest.shape
    parent_rows, parent_cols = parent.shape[1:]
    right = lax.axis_index("gy") == 0
    loads = []
    for at, (ref, buf) in enumerate(
        (
            (parent, coarse_buf.at[0]),
            (parent_source, coarse_buf.at[1]),
            (nest, fine_buf.at[0]),
            (source, fine_buf.at[1]),
        )
    ):
        start = pl.multiple_of(jnp.where(right, ref.shape[2] - LANES, 0), LANES)
        loads.append(pltpu.make_async_copy(ref.at[:, :, pl.ds(start, LANES)], buf, sems.at[at]))
    for copy in loads:
        copy.start()

    def columns(value, count, to):
        first = jnp.where(right, LANES - count, 0)
        place = iota(value.shape, 1) - first
        value = jnp.where((place >= 0) & (place < count), value, 0.0)
        return pltpu.roll(value, (LANES + to - first) & (LANES - 1), 1)

    part = jnp.zeros((parent_rows, LANES), jnp.float32)
    loads[0].wait()
    loads[1].wait()
    for level in range(levels):
        base = STRIDE * level
        part = part + columns(coarse_buf[0, level], 1, base + PARENT_AT)
        part = part + columns(coarse_buf[0, level], 2, base + STRIP_AT)
        part = part + columns(coarse_buf[1, level], 2, base + STRIP_SOURCE_AT)
    total = jnp.zeros((rows, LANES), jnp.float32)
    loads[2].wait()
    loads[3].wait()
    for level in range(levels):
        base = STRIDE * level
        total = total + columns(fine_buf[0, level], 3, base)
        total = total + columns(fine_buf[1, level], 3, base + SOURCE_AT)
    out[...] = total
    out[:parent_rows, :] += part


def across_border(message, oy, parent_cols, me):
    c = iota(message.shape, 1) & (STRIDE - 1)
    place = jnp.where(me == 0, parent_cols + 1, 1) - oy
    total = jnp.zeros(message.shape, jnp.float32)
    for turn in (-1, 0, 2, 3):
        at = jnp.where(c >= STRIP_SOURCE_AT, c - STRIP_SOURCE_AT, c - STRIP_AT) - turn
        fits = (c >= STRIP_AT) & (at >= 0) & (at < 2) & (place == turn)
        total = total + jnp.where(fits, turned(message, turn), 0.0)
    return total


def pack_columns(parts, band, oy_hbm, nest, source, parent_hbm, parent_source_hbm, *rest):
    outs = rest[: parts - 1]
    old_buf, src_buf, parent, parent_source, oy_ref, sems, field_sems = rest[parts - 1 :]
    levels, rows, cols = nest.shape
    parent_cols = parent.shape[2]
    me = lax.axis_index("gy")
    sides = [1] if parts == 2 else [1, parts - 1]
    fields = [
        pltpu.make_async_copy(ref, buf, field_sems.at[at])
        for at, (ref, buf) in enumerate(
            ((oy_hbm, oy_ref), (parent_hbm, parent), (parent_source_hbm, parent_source))
        )
    ]
    for copy in fields:
        copy.start()
    copies = []
    for at, step in enumerate(sides):
        right = (me == 0) if parts == 2 else jnp.bool_(step == 1)
        start = pl.multiple_of(jnp.where(right, cols - LANES, 0), LANES)
        pair = [
            pltpu.make_async_copy(
                ref.at[:, :, pl.ds(start, LANES)], buf.at[at], sems.at[at, which]
            )
            for which, (ref, buf) in enumerate(((nest, old_buf), (source, src_buf)))
        ]
        for copy in pair:
            copy.start()
        copies.append((right, pair))
    for copy in fields:
        copy.wait()
    oy = oy_ref[0]
    lane = iota((parent.shape[1], LANES), 1)
    for step in range(1, parts):
        out = outs[step - 1]
        part = edge_strip(lax.rem(me + step, parts), band, oy, parent, parent_source)
        if step not in sides:
            out[...] = part
            continue
        at = sides.index(step)
        right, pair = copies[at]
        first = jnp.where(right, LANES - 3, 0)
        outer = jnp.where(right, LANES - 1, 0)
        for level in range(levels):
            edge = jnp.where(
                right, tile(parent, level, parent_cols // LANES - 1), tile(parent, level, 0)
            )
            edge = jnp.where(lane == outer, edge, 0.0)
            turn = (LANES + PARENT_AT + STRIDE * level - outer) & (LANES - 1)
            part = part + pltpu.roll(edge, turn, 1)
        for copy in pair:
            copy.wait()
        fine = iota((rows, LANES), 1) - first
        wanted = (fine >= 0) & (fine < 3)
        total = jnp.zeros((rows, LANES), jnp.float32)
        for level in range(levels):
            for buf, shift in ((old_buf, 0), (src_buf, SOURCE_AT)):
                value = jnp.where(wanted, buf[at, level], 0.0)
                turn = (LANES + STRIDE * level + shift - first) & (LANES - 1)
                total = total + pltpu.roll(value, turn, 1)
        out[...] = total
        out[: part.shape[0], :] += part


def inner_substep(coefs, here, source, there):
    levels, rows, cols = here.shape
    sub = iota((8, cols), 0)
    tiles = rows // 8

    def one_level(level):
        ch = coefs[0, level]
        cv = coefs[1, level]
        centre = 1.0 - 4.0 * ch - 2.0 * cv
        below = jnp.maximum(level - 1, 0)
        above = jnp.minimum(level + 1, levels - 1)
        cv_below = jnp.where(level > 0, cv, 0.0)
        cv_above = jnp.where(level < levels - 1, cv, 0.0)

        def row_tile(t):
            t = t % tiles
            return here[level, 8 * t : 8 * t + 8, :]

        down_before = pltpu.roll(row_tile(-1), 1, 0)
        now = row_tile(0)
        up_now = pltpu.roll(now, 7, 0)
        for t in range(tiles):
            following = row_tile(t + 1)
            down_now = pltpu.roll(now, 1, 0)
            up_next = pltpu.roll(following, 7, 0)
            around = jnp.where(sub == 0, down_before, down_now) + jnp.where(
                sub == 7, up_next, up_now
            )
            around = around + (pltpu.roll(now, 1, 1) + pltpu.roll(now, cols - 1, 1))
            span = slice(8 * t, 8 * t + 8)
            stacked = cv_below * here[below, span, :] + cv_above * here[above, span, :]
            there[level, span, :] = centre * now + ch * around + (stacked + source[level, span, :])
            down_before, now, up_now = down_now, following, up_next

    def two_levels(pair, carry):
        one_level(2 * pair)
        one_level(2 * pair + 1)
        return carry

    lax.fori_loop(0, levels // 2, two_levels, 0)


def spread_coefs(parent_coefs, coefs, out):
    levels = out.shape[2]
    lane = iota((levels, LANES), 1)
    row = iota((levels, LANES), 0)
    for at, ref in enumerate((parent_coefs, coefs)):
        for which in range(2):
            packed = jnp.full(lane.shape, ref[which, 0], jnp.float32)
            rows = packed
            for level in range(1, levels):
                packed = jnp.where(lane >= STRIDE * level, ref[which, level], packed)
                rows = jnp.where(row == level, ref[which, level], rows)
            out[0, 2 * at + which] = packed
            out[1, 2 * at + which] = rows


def inner_first(
    band,
    oy_ref,
    parent_coefs,
    coefs,
    nest,
    source,
    parent,
    parent_source,
    strip,
    first,
    packs,
    spread,
    oy_rows,
):
    levels, rows, cols = nest.shape
    oy = oy_ref[0]
    oy_rows[...] = jnp.full(oy_rows.shape, oy, jnp.int32)
    spread_coefs(parent_coefs, coefs, spread)
    strip[...] = edge_strip(lax.axis_index("gy"), band, oy, parent, parent_source)
    lane = iota((rows, LANES), 1)
    for at, ref in enumerate((nest, source)):
        left = jnp.zeros(lane.shape, jnp.float32)
        right = jnp.zeros(lane.shape, jnp.float32)
        for level in range(levels):
            value = jnp.where(lane < RIGHT_OWN, tile(ref, level, 0), 0.0)
            left = left + turned(value, STRIDE * level + LEFT_AT)
            value = jnp.where(lane >= LANES - RIGHT_OWN, tile(ref, level, cols // LANES - 1), 0.0)
            right = right + turned(value, STRIDE * level + RIGHT_OWN)
        packs[2 * at] = left
        packs[2 * at + 1] = right
    inner_substep(coefs, nest, source, first)


def inner_rest(coefs, first, source, after_pack, third, second):
    inner_substep(coefs, first, source, second)
    inner_substep(coefs, second, source, third)


def with_columns(tiles, left, right, me, parts, place):
    lane = iota(left.shape, 1)
    from_right = turned(right, -place)
    from_left = turned(left, -3 - place)
    if parts == 2:
        tiles[0] = jnp.where((lane < 3) & (me == 0), from_right, tiles[0])
        tiles[-1] = jnp.where((lane >= LANES - 3) & (me == 1), from_left, tiles[-1])
        return tiles
    extra = jnp.where(lane < 3, from_right, jnp.where(lane >= LANES - 3, from_left, 0.0))
    return tiles + [extra]


def pack_rows(
    parts, old_top, old_end, src_top, src_end, par_top, par_end, own_strip, oy_rows, *rest
):
    columns = rest[: parts - 1]
    across, within, far, strip_out, both = rest[parts - 1 :]
    core = lax.axis_index("gz")
    up, down = both.at[core], both.at[1 - core]
    levels, _, cols = old_top.shape
    me = lax.axis_index("gy")
    left, right = columns[0], columns[-1]
    rows = left.shape[0]
    strip_rows = own_strip.shape[0]
    lane = iota((strip_rows, LANES), 1)
    strips = own_strip[...]
    if parts == 2:
        oy = jnp.concatenate([oy_rows[...]] * (strip_rows // 8), axis=0)
        strips = strips + across_border(left[:strip_rows, :], oy, par_top.shape[2], me)
    else:
        for message in columns:
            strips = strips + message[:strip_rows, :]
    c = lane & (STRIDE - 1)
    strips = jnp.where(c >= STRIP_AT, strips, 0.0)
    strips = jnp.where(c == PARENT_AT, left[:strip_rows, :], strips)
    strips = jnp.where(c == PARENT_AT + 1, turned(right[:strip_rows, :], 1), strips)
    strip_out[...] = strips
    far[...] = strips[:8]
    pieces = cols // LANES
    for out, old, src, first, at, src_at in (
        (up, old_end, src_end, rows - 8, 5, 6),
        (down, old_top, src_top, 0, 0, 0),
    ):
        y_left = left[first : first + 8, :]
        y_right = right[first : first + 8, :]
        for level in range(levels):
            for ref, shift, row, count, base in (
                (old, 0, at, 3, 0),
                (src, SOURCE_AT, src_at, 2, SOURCE_ROW),
            ):
                tiles = [tile(ref, level, piece) for piece in range(pieces)]
                tiles = with_columns(
                    tiles, y_left, y_right, me, parts, STRIDE * level + shift
                )
                for piece, value in enumerate(tiles):
                    out[
                        base + count * level : base + count * (level + 1),
                        piece * LANES : (piece + 1) * LANES,
                    ] = value[row : row + count]
    parent_cols = par_top.shape[2]
    for level in range(levels):
        up[TAIL_ROW + level : TAIL_ROW + level + 1, :parent_cols] = par_end[level, 7:8, :]
        down[TAIL_ROW + level : TAIL_ROW + level + 1, :parent_cols] = par_top[level, 0:1, :]
    up[TAIL_ROW : TAIL_ROW + 8, parent_cols : parent_cols + LANES] = strips[strip_rows - 8 :]
    down[TAIL_ROW : TAIL_ROW + 8, parent_cols : parent_cols + LANES] = strips[:8]
    down[TAIL_ROW + 8 : TAIL_ROW + 16, :LANES] = strips[8:16]
    down[TAIL_ROW + 8 : TAIL_ROW + 16, LANES : 2 * LANES] = strips[16:24]
    within[...] = both[0]
    across[...] = both[1]


def edges(
    parts,
    parent_cols,
    ox_ref,
    spread,
    nest,
    source,
    third,
    packs,
    strips,
    across,
    within,
    far,
    y_left,
    y_right,
    result,
    coarse_out,
    far_out,
    both,
    ping,
    pong,
    src,
    split,
):
    levels, rows, cols = nest.shape
    width = ping.shape[3]
    pieces = cols // LANES
    me = lax.axis_index("gy")
    core = lax.axis_index("gz")
    both[0] = within[...]
    both[1] = across[...]
    before, after = both.at[1 - core], both.at[core]
    is_south = me == 0
    is_north = me == parts - 1

    far_out[...] = far[...]
    sub = iota((8, LANES), 0)
    old = jnp.concatenate(
        [
            strips[...],
            after[TAIL_ROW : TAIL_ROW + 8, parent_cols : parent_cols + LANES],
            after[TAIL_ROW + 8 : TAIL_ROW + 16, :LANES],
            after[TAIL_ROW + 8 : TAIL_ROW + 16, LANES : 2 * LANES],
            jnp.where(
                sub == 7,
                before[TAIL_ROW : TAIL_ROW + 8, parent_cols : parent_cols + LANES],
                0.0,
            ),
        ],
        axis=0,
    )
    count = old.shape[0]

    def packed_coef(which, height):
        return jnp.concatenate([spread[0, which]] * (height // 8), axis=0)

    def stacked(value):
        lane = iota(value.shape, 1)
        below = jnp.where(lane >= STRIDE, turned(value, STRIDE), 0.0)
        return below + jnp.where(lane < STRIDE * (levels - 1), turned(value, -STRIDE), 0.0)

    def around(value):
        return (
            pltpu.roll(value, 1, 0)
            + pltpu.roll(value, value.shape[0] - 1, 0)
            + turned(value, 1)
            + turned(value, -1)
        )

    diff = (
        packed_coef(0, count) * (around(old) - 4.0 * old)
        + packed_coef(1, count) * (stacked(old) - 2.0 * old)
        + turned(old, STRIP_AT - STRIP_SOURCE_AT)
    )
    index = iota((rows + 16, count), 0)
    nest_row = jnp.where(index < rows, index, jnp.where(index < rows + 8, index - rows - 3, index - 13))
    parent_row = ((nest_row + 3) * 171 >> 9) - 1 + ox_ref[0]
    pick = (iota((rows + 16, count), 1) == parent_row).astype(jnp.float32)
    picked = jnp.dot(
        pick,
        jnp.concatenate([old, diff], axis=1),
        precision=HIGHEST,
        preferred_element_type=jnp.float32,
    )
    picked_old, picked_diff = picked[:, :LANES], picked[:, LANES:]

    lane = iota((rows, LANES), 1)
    c = lane & (STRIDE - 1)
    rim_first = jnp.where(is_south, LEFT_AT, RIGHT_OWN - RIM)
    in_rim = (c >= rim_first) & (c < rim_first + RIM)
    at = lane - c + STRIP_AT + jnp.where(c >= rim_first + 3, 2, 1)
    rim_old = jnp.take_along_axis(picked_old[:rows], at, axis=1)
    rim_diff = jnp.take_along_axis(picked_diff[:rows], at, axis=1)
    ch = packed_coef(2, rows)
    cv = packed_coef(3, rows)
    centre = 1.0 - 4.0 * ch - 2.0 * cv
    left = jnp.where(c < 3, y_left[...], packs[0])
    left_src = jnp.where(c < 3, turned(y_left[...], -SOURCE_AT), packs[2])
    right = jnp.where(c >= RIGHT_OWN, turned(y_right[...], RIGHT_OWN), packs[1])
    right_src = jnp.where(c >= RIGHT_OWN, turned(y_right[...], RIGHT_OWN - SOURCE_AT), packs[3])
    sides = []
    for value, forcing, rim in (
        (left, left_src, in_rim & is_south),
        (right, right_src, in_rim & is_north),
    ):
        for substep in range(1, SUBSTEPS + 1):
            value = centre * value + ch * around(value) + (cv * stacked(value) + forcing)
            value = jnp.where(rim, rim_old + (substep / SUBSTEPS) * rim_diff, value)
        sides.append(value)

    sub = iota((8, width), 0)
    lane = iota((8, LANES), 1)
    for level in range(levels):
        for buf, field, shift, n, base in (
            (ping, nest, 0, 3, 0),
            (src, source, SOURCE_AT, 2, SOURCE_ROW),
        ):
            for window, first, turn, at, message in (
                (0, 0, 3, 3 - n, before),
                (1, rows - 8, 5, 5, after),
            ):
                tiles = [
                    field[level, first : first + 8, piece * LANES : (piece + 1) * LANES]
                    for piece in range(pieces)
                ]
                tiles = with_columns(
                    tiles,
                    y_left[first : first + 8, :],
                    y_right[first : first + 8, :],
                    me,
                    parts,
                    STRIDE * level + shift,
                )
                for piece, value in enumerate(tiles):
                    value = pltpu.roll(value, turn, 0)
                    span = slice(piece * LANES, (piece + 1) * LANES)
                    buf[level, window, :, span] = value
                    if n == 3:
                        pong[level, window, :, span] = value
                buf[level, window, at : at + n, :] = message[
                    base + n * level : base + n * (level + 1), :
                ]
    rim_first = jnp.where(is_south, 0, LANES - RIM)
    column = STRIP_AT + jnp.where((lane >= rim_first + 3) & (lane < rim_first + RIM), 2, 1)
    rims = {}
    for level in range(levels):
        for window in range(2):
            span = slice(rows + 8 * window, rows + 8 * window + 8)
            at = column + STRIDE * level
            rims[level, window] = (
                jnp.take_along_axis(picked_old[span], at, axis=1),
                jnp.take_along_axis(picked_diff[span], at, axis=1),
            )
    for substep in range(1, SUBSTEPS + 1):
        here, there = (ping, pong) if substep % 2 else (pong, ping)
        low = 0 if substep == SUBSTEPS or parts > 2 else 3
        south = (lane >= low) & (lane < RIM) & is_south
        north = (lane >= LANES - RIM) & (lane < LANES - low) & is_north
        weight = substep / SUBSTEPS
        for level in range(levels):
            c_h, c_v = (
                jnp.concatenate([spread[1, which, level : level + 1, :]] * (width // LANES), axis=1)
                for which in (2, 3)
            )
            c_0 = 1.0 - 4.0 * c_h - 2.0 * c_v
            for window in range(2):
                now = here[level, window]
                up = pltpu.roll(now, 1, 0)
                down = pltpu.roll(now, 7, 0)
                if substep == 1:
                    beyond_row = pong[level, window]
                    if window == 0:
                        down = jnp.where(sub == 7, pltpu.roll(beyond_row, 7, 0), down)
                    else:
                        up = jnp.where(sub == 0, pltpu.roll(beyond_row, 1, 0), up)
                beside = pltpu.roll(now, 1, 1) + pltpu.roll(now, width - 1, 1)
                value = c_0 * now + c_h * ((up + down) + beside) + src[level, window]
                if level > 0:
                    value = value + c_v * here[level - 1, window]
                if level < levels - 1:
                    value = value + c_v * here[level + 1, window]
                rim_o, rim_d = rims[level, window]
                rim = rim_o + weight * rim_d
                for piece in range(width // LANES):
                    span = slice(piece * LANES, (piece + 1) * LANES)
                    part = value[:, span]
                    if piece == 0:
                        part = jnp.where(south, rim, part)
                    if piece == pieces - 1:
                        part = jnp.where(north, rim, part)
                    there[level, window, :, span] = part

    lane = iota((rows, LANES), 1)
    sub = iota((8, cols), 0)
    for level in range(levels):
        fixed = turned(sides[0], -STRIDE * level - LEFT_AT)
        result[level, :, :LANES] = jnp.where(lane < FIXED, fixed, tile(third, level, 0))
        for piece in range(1, pieces - 1):
            result[level, :, piece * LANES : (piece + 1) * LANES] = tile(third, level, piece)
        fixed = turned(sides[1], -STRIDE * level - RIGHT_OWN)
        result[level, :, cols - LANES :] = jnp.where(
            lane >= LANES - FIXED, fixed, tile(third, level, pieces - 1)
        )
        top = pltpu.roll(there[level, 0, :, :cols], 5, 0)
        result[level, :8, :] = jnp.where(sub < 3, top, result[level, :8, :])
        end = pltpu.roll(there[level, 1, :, :cols], 3, 0)
        result[level, rows - 8 :, :] = jnp.where(sub >= 5, end, result[level, rows - 8 :, :])

    foot = cols // RATIO
    offset = iota((cols, foot), 0) - RATIO * iota((cols, foot), 1)
    gather = ((offset >= 0) & (offset < RATIO)).astype(jnp.float32)
    parent_rows = rows // RATIO
    for level in range(levels):
        for piece in range(pieces):
            split[piece, level * rows : (level + 1) * rows, :] = tile(result, level, piece)
    total = levels * parent_rows
    sums = [
        split[piece, pl.ds(0, total, RATIO), :]
        + split[piece, pl.ds(1, total, RATIO), :]
        + split[piece, pl.ds(2, total, RATIO), :]
        for piece in range(pieces)
    ]
    means = jnp.dot(
        jnp.concatenate(sums, axis=1),
        gather,
        precision=HIGHEST,
        preferred_element_type=jnp.float32,
    ) * (1.0 / 9.0)
    coarse_out[...] = means.reshape(coarse_out.shape)


def parent_step(
    parts,
    band,
    ox_ref,
    oy_ref,
    spread,
    nest,
    parent,
    source,
    within,
    across,
    y_left,
    y_right,
    out,
    nest_out,
    late,
    tail,
    sem,
):
    store = pltpu.make_async_copy(nest, nest_out, sem)
    store.start()
    core = lax.axis_index("gz")
    levels, rows, cols = parent.shape
    tail[0] = within[TAIL_ROW : TAIL_ROW + levels, : cols + LANES]
    tail[1] = across[TAIL_ROW : TAIL_ROW + levels, : cols + LANES]
    me = lax.axis_index("gy")
    is_last = ox_ref[0] == rows - 1
    wide = iota((1, cols), 1)
    south = (wide == oy_ref[0] + 2 - me * cols) & is_last
    north = (wide == oy_ref[0] + band - 3 - me * cols) & is_last
    row = iota((rows, cols), 0)
    lane = iota((rows, cols), 1)
    has_left = me > 0
    has_right = me < parts - 1
    left = y_left[:rows, :]
    right = y_right[:rows, :]
    zero = jnp.zeros((rows, cols), jnp.float32)
    for level in range(levels):
        now = parent[level]
        at = STRIDE * level + PARENT_AT
        from_left = left[:, at : at + 1]
        from_right = right[:, at : at + 1]
        top = tail[1 - core, level : level + 1, :cols]
        end = tail[core, level : level + 1, :cols]
        around = (
            jnp.where(row == 0, top, pltpu.roll(now, 1, 0))
            + jnp.where(row == rows - 1, end, pltpu.roll(now, rows - 1, 0))
            + jnp.where(
                lane == 0, jnp.where(has_left, from_left, 0.0), pltpu.roll(now, 1, 1)
            )
            + jnp.where(
                lane == cols - 1,
                jnp.where(has_right, from_right, 0.0),
                pltpu.roll(now, cols - 1, 1),
            )
        )
        stacked = (parent[level - 1] if level > 0 else zero) + (
            parent[level + 1] if level < levels - 1 else zero
        )
        ch, cv = (
            jnp.concatenate([spread[1, which, level : level + 1, :]] * (cols // LANES), axis=1)
            for which in (0, 1)
        )
        out[level] = (
            (1.0 - 4.0 * ch - 2.0 * cv) * now + ch * around + (cv * stacked + source[level])
        )
        at = cols + STRIDE * level + PARENT_AT
        before_end = jnp.where(
            wide == 0, tail[core, 0:1, at : at + 1], pltpu.roll(end, 1, 1)
        )
        after_end = jnp.where(
            wide == cols - 1, tail[core, 0:1, at + 1 : at + 2], pltpu.roll(end, cols - 1, 1)
        )
        nest_ch = spread[1, 2, level : level + 1, :]
        nest_ch = jnp.concatenate([nest_ch] * (cols // LANES), axis=1)
        share = nest_ch * nest_ch * ch * (1.0 / SUBSTEPS)
        late[level : level + 1, :] = (share * (1.0 / (RATIO * RATIO))) * (
            jnp.where(south, before_end, 0.0) + jnp.where(north, after_end, 0.0)
        )
    store.wait()


def merge(parts, band, ox_ref, oy_ref, late, step, nest, spread, beyond, *rest):
    own, previous = rest[:parts], rest[parts : 2 * parts]
    out, nest_out, joined, corner, sem = rest[2 * parts :]
    levels, rows, cols = step.shape
    foot = own[0].shape[2]
    me = lax.axis_index("gy")

    @pl.when((ox_ref[0] == rows - 1) & ((me == 0) | (me == parts - 1)))
    def _():
        nest_rows, nest_cols = nest.shape[1:]
        first = pl.multiple_of(jnp.where(me == 0, 0, nest_cols - LANES), LANES)
        place = (slice(None), pl.ds(nest_rows - 8, 8), pl.ds(first, LANES))
        load = pltpu.make_async_copy(nest_out.at[place], corner, sem)
        load.start()
        load.wait()
        sub = iota((8, LANES), 0)
        lane = iota((8, LANES), 1)
        cell = (sub == 7) & (lane == jnp.where(me == 0, RIM, LANES - RIM - 1))
        for level in range(levels):
            at = STRIDE * level + STRIP_AT
            value = jnp.where(me == 0, beyond[0:1, at + 2 : at + 3], beyond[0:1, at + 1 : at + 2])
            nest_ch = spread[1, 2, level : level + 1, :]
            share = nest_ch * nest_ch * spread[1, 0, level : level + 1, :] * (1.0 / SUBSTEPS)
            corner[level] += jnp.where(cell, share * value, 0.0)
        again = pltpu.make_async_copy(corner, nest_out.at[place], sem)
        again.start()
        again.wait()

    ox = ox_ref[0]
    oy = oy_ref[0]
    for k in range(parts):
        joined[k, :, :rows, :] = previous[k][...]
        joined[k, :, rows:, :] = own[k][...]
    lane = iota((rows, LANES), 1)
    row = iota((rows, LANES), 0)
    for level in range(levels):
        values = [tile(step, level, piece) for piece in range(cols // LANES)]
        for k in range(parts):
            source = lax.rem(me + parts - k, parts)
            block = joined[k, level, pl.ds(rows - ox, rows), :]
            begin = oy + source * foot - me * cols
            block = pltpu.roll(block, (16384 + begin) & (LANES - 1), 1)
            low = jnp.maximum(source * foot, 2)
            high = jnp.minimum((source + 1) * foot, band - 2)
            for piece in range(cols // LANES):
                at = lane + (piece * LANES + me * cols - oy)
                values[piece] = jnp.where((at >= low) & (at < high), block, values[piece])
        for piece, value in enumerate(values):
            term = late[level : level + 1, piece * LANES : (piece + 1) * LANES]
            value = value + jnp.where(row == rows - 2, term, 0.0)
            out[level, :, piece * LANES : (piece + 1) * LANES] = value


def shifted(value, axis, steps):
    count = lax.axis_size(axis)
    pairs = [(source, (source + steps) % count) for source in range(count)]
    return lax.ppermute(value, axis, pairs)


def shards(
    parent_old, parent_source, parent_coefs, nest_old, nest_source, nest_coefs, offset_x, offset_y
):
    parts = lax.axis_size("gy")
    along = ("gx", "gz")
    levels, parent_rows, parent_cols = parent_old.shape
    _, rows, cols = nest_old.shape
    foot = cols // RATIO
    band = foot * parts
    width = cols if parts == 2 else cols + LANES
    height = TAIL_ROW + 16
    f32 = jnp.float32
    shape = jax.ShapeDtypeStruct
    anywhere = pl.BlockSpec(memory_space=pl.ANY)
    in_hbm = pl.BlockSpec(memory_space=pltpu.HBM)
    sides = 1 if parts == 2 else 2
    if parts == 2:
        packed = [
            pl.pallas_call(
                pack_pair,
                out_shape=shape((rows, LANES), f32),
                in_specs=[in_hbm] * 4,
                out_specs=whole(),
                scratch_shapes=[
                    VMEM((2, levels, rows, LANES), f32),
                    VMEM((2, levels, parent_rows, LANES), f32),
                    pltpu.SemaphoreType.DMA((4,)),
                ],
                compiler_params=params(MOST),
                cost_estimate=cost(200000, 800000),
                name="pack_pair",
            )(nest_old, nest_source, parent_old, parent_source)
        ]
    else:
        packed = pl.pallas_call(
            functools.partial(pack_columns, parts, band),
            out_shape=[
                shape((rows if k in (1, parts - 1) else parent_rows, LANES), f32)
                for k in range(1, parts)
            ],
            in_specs=[in_hbm] * 5,
            out_specs=[whole()] * (parts - 1),
            scratch_shapes=[
                VMEM((sides, levels, rows, LANES), f32),
                VMEM((sides, levels, rows, LANES), f32),
                VMEM(parent_old.shape, f32),
                VMEM(parent_old.shape, f32),
                pltpu.SMEM(offset_y.shape, jnp.int32),
                pltpu.SemaphoreType.DMA((sides, 2)),
                pltpu.SemaphoreType.DMA((3,)),
            ],
            compiler_params=params(MOST),
            cost_estimate=cost(200000, 1000000),
            name="pack_columns",
        )(offset_y, nest_old, nest_source, parent_old, parent_source)
    columns = [shifted(packed[k - 1], "gy", k) for k in range(1, parts)]
    own_strip, first, packs, spread, oy_rows = pl.pallas_call(
        functools.partial(inner_first, band),
        out_shape=[
            shape((parent_rows, LANES), f32),
            shape(nest_old.shape, f32),
            shape((4, rows, LANES), f32),
            shape((2, 4, levels, LANES), f32),
            shape((8, LANES), jnp.int32),
        ],
        in_specs=[scalars()] * 3 + [whole()] * 4,
        out_specs=[whole()] * 5,
        compiler_params=params(),
        cost_estimate=cost(4000000, 3000000),
        name="inner_first",
    )(
        offset_y,
        parent_coefs,
        nest_coefs,
        nest_old,
        nest_source,
        parent_old,
        parent_source,
    )

    def block(ref, last):
        count = ref.shape[1] // 8 - 1 if last else 0
        return pl.BlockSpec((levels, 8, ref.shape[2]), lambda i, c=count: (0, c, 0))

    def full(extent):
        return pl.BlockSpec(extent, lambda i: (0,) * len(extent))

    outs = [
        shape((height, width), f32),
        shape((height, width), f32),
        shape((8, LANES), f32),
        shape((parent_rows, LANES), f32),
    ]
    across, within, far, strips = pl.pallas_call(
        functools.partial(pack_rows, parts),
        out_shape=outs,
        grid=(1,),
        in_specs=[
            block(nest_old, False),
            block(nest_old, True),
            block(nest_old, False),
            block(nest_old, True),
            block(parent_old, False),
            block(parent_old, True),
            full(own_strip.shape),
            full(oy_rows.shape),
        ]
        + [full(message.shape) for message in columns],
        out_specs=[full(out.shape) for out in outs],
        scratch_shapes=[VMEM((2, height, width), f32)],
        compiler_params=params(),
        cost_estimate=cost(100000, 700000),
        name="pack_rows",
    )(nest_old, nest_old, nest_source, nest_source, parent_old, parent_old, own_strip, oy_rows, *columns)
    across = swapped(across, 1)
    within = swapped(within, 0)
    third = pl.pallas_call(
        inner_rest,
        out_shape=shape(nest_old.shape, f32),
        in_specs=[scalars()] + [whole()] * 2 + [anywhere],
        out_specs=whole(),
        scratch_shapes=[VMEM(nest_old.shape, f32)],
        compiler_params=params(),
        cost_estimate=cost(8000000, 6000000),
        name="inner_rest",
    )(nest_coefs, first, nest_source, strips)
    nest_done, coarse, far = pl.pallas_call(
        functools.partial(edges, parts, parent_cols),
        out_shape=[
            shape(nest_old.shape, f32),
            shape((levels, parent_rows, foot), f32),
            shape((8, LANES), f32),
        ],
        in_specs=[scalars()] + [whole()] * 11,
        out_specs=[whole()] * 3,
        scratch_shapes=[
            VMEM((2, height, width), f32),
            VMEM((levels, 2, 8, width), f32),
            VMEM((levels, 2, 8, width), f32),
            VMEM((levels, 2, 8, width), f32),
            VMEM((cols // LANES, levels * rows, LANES), f32),
        ],
        compiler_params=params(),
        cost_estimate=cost(4000000, 3000000),
        name="edges",
    )(
        offset_x,
        spread,
        nest_old,
        nest_source,
        third,
        packs,
        strips,
        across,
        within,
        far,
        columns[0],
        columns[-1],
    )
    previous = [shifted(coarse, along, 1)] + [
        shifted_both(coarse, k) for k in range(1, parts)
    ]
    own = [coarse] + [shifted(coarse, "gy", k) for k in range(1, parts)]
    beyond = shifted(far, along, -2)
    step, nest_stored, late = pl.pallas_call(
        functools.partial(parent_step, parts, band),
        out_shape=[
            shape(parent_old.shape, f32),
            shape(nest_old.shape, f32),
            shape((levels, parent_cols), f32),
        ],
        in_specs=[scalars()] * 2 + [whole(), anywhere] + [whole()] * 6,
        out_specs=[whole(), in_hbm, whole()],
        scratch_shapes=[
            VMEM((2, levels, parent_cols + LANES), f32),
            pltpu.SemaphoreType.DMA,
        ],
        compiler_params=params(),
        cost_estimate=cost(800000, 2500000),
        name="parent_step",
    )(
        offset_x,
        offset_y,
        spread,
        nest_done,
        parent_old,
        parent_source,
        within,
        across,
        columns[0],
        columns[-1],
    )
    parent_new, nest_new = pl.pallas_call(
        functools.partial(merge, parts, band),
        out_shape=[shape(parent_old.shape, f32), shape(nest_old.shape, f32)],
        in_specs=[scalars()] * 2 + [whole()] * 2 + [in_hbm] + [whole()] * (2 + 2 * parts),
        out_specs=[whole(), in_hbm],
        scratch_shapes=[
            VMEM((parts, levels, 2 * parent_rows, foot), f32),
            VMEM((levels, 8, LANES), f32),
            pltpu.SemaphoreType.DMA,
        ],
        input_output_aliases={4: 1},
        compiler_params=params(),
        cost_estimate=cost(200000, 800000),
        name="merge",
    )(offset_x, offset_y, late, step, nest_stored, spread, beyond, *own, *previous)
    return (parent_new, nest_new)


def swapped(value, first):
    along = ("gx", "gz")
    count = lax.axis_size(along)
    pairs = []
    for at in range(first, count, 2):
        pairs += [(at, (at + 1) % count), ((at + 1) % count, at)]
    return lax.ppermute(value, along, pairs)


def shifted_both(value, steps):
    sizes = [lax.axis_size(axis) for axis in ("gx", "gy", "gz")]
    gx, gy, gz = sizes
    pairs = []
    for x in range(gx):
        for y in range(gy):
            for z in range(gz):
                place = (x * gz + z + 1) % (gx * gz)
                target = (place // gz * gy + (y + steps) % gy) * gz + place % gz
                pairs.append(((x * gy + y) * gz + z, target))
    return lax.ppermute(value, ("gx", "gy", "gz"), pairs)


def solution(mesh):
    return jax.shard_map(
        shards,
        mesh=mesh,
        in_specs=(
            P(None, ("grp", "gx", "gz"), "gy"),
            P(None, ("grp", "gx", "gz"), "gy"),
            P(),
            P(None, ("grp", "gx", "gz"), "gy"),
            P(None, ("grp", "gx", "gz"), "gy"),
            P(),
            P("grp"),
            P("grp"),
        ),
        out_specs=(P(None, ("grp", "gx", "gz"), "gy"), P(None, ("grp", "gx", "gz"), "gy")),
        check_vma=False,
    )
```

```python
import functools

import jax
import jax.numpy as jnp
from jax import lax
from jax.experimental import pallas as pl
from jax.experimental.pallas import tpu as pltpu
from jax.sharding import PartitionSpec as P

RATIO = 3
SUBSTEPS = 3
RIM = 6
LANES = 128
STRIDE = 16
SOURCE_AT = 3
PARENT_AT = 6
STRIP_AT = 8
STRIP_SOURCE_AT = 12
SOURCE_ROW = 24
TAIL_ROW = 40
FIXED = 8
LEFT_AT = 3
RIGHT_OWN = STRIDE - 3
VMEM = pltpu.VMEM
LIMIT = 24 * 1024 * 1024
MOST = 54 * 1024 * 1024
HIGHEST = lax.Precision.HIGHEST


def iota(shape, dim):
    return lax.broadcasted_iota(jnp.int32, shape, dim)


def whole():
    return pl.BlockSpec(memory_space=VMEM)


def scalars():
    return pl.BlockSpec(memory_space=pltpu.SMEM)


def params(limit=LIMIT):
    return pltpu.CompilerParams(vmem_limit_bytes=limit)


def cost(flops, moved):
    return pl.CostEstimate(flops=flops, bytes_accessed=moved, transcendentals=0)


def tile(ref, level, index):
    return ref[level, :, index * LANES : (index + 1) * LANES]


def turned(value, lanes):
    lanes = lanes % LANES
    return pltpu.roll(value, lanes, 1) if lanes else value


def edge_strip(dest, band, oy, parent, parent_source):
    levels, rows, cols = parent.shape
    lane = iota((rows, LANES), 1)
    base = jnp.where(dest == 0, oy - 1, oy + band - 3) - lax.axis_index("gy") * cols
    total = jnp.zeros(lane.shape, jnp.float32)
    for ref, first in ((parent, STRIP_AT), (parent_source, STRIP_SOURCE_AT)):
        for level in range(levels):
            found = jnp.zeros(lane.shape, jnp.float32)
            for at in range(cols // LANES):
                place = lane + (at * LANES - base)
                found = jnp.where((place >= 0) & (place < 4), tile(ref, level, at), found)
            turn = (16384 + first + STRIDE * level - base) & (LANES - 1)
            total = total + pltpu.roll(found, turn, 1)
    return total


def pack_pair(nest, source, parent, parent_source, out, fine_buf, coarse_buf, sems):
    levels, rows, cols = nest.shape
    parent_rows, parent_cols = parent.shape[1:]
    right = lax.axis_index("gy") == 0
    loads = []
    for at, (ref, buf) in enumerate(
        (
            (parent, coarse_buf.at[0]),
            (parent_source, coarse_buf.at[1]),
            (nest, fine_buf.at[0]),
            (source, fine_buf.at[1]),
        )
    ):
        start = pl.multiple_of(jnp.where(right, ref.shape[2] - LANES, 0), LANES)
        loads.append(pltpu.make_async_copy(ref.at[:, :, pl.ds(start, LANES)], buf, sems.at[at]))
    for copy in loads:
        copy.start()

    def columns(value, count, to):
        first = jnp.where(right, LANES - count, 0)
        place = iota(value.shape, 1) - first
        value = jnp.where((place >= 0) & (place < count), value, 0.0)
        return pltpu.roll(value, (LANES + to - first) & (LANES - 1), 1)

    part = jnp.zeros((parent_rows, LANES), jnp.float32)
    loads[0].wait()
    loads[1].wait()
    for level in range(levels):
        base = STRIDE * level
        part = part + columns(coarse_buf[0, level], 1, base + PARENT_AT)
        part = part + columns(coarse_buf[0, level], 2, base + STRIP_AT)
        part = part + columns(coarse_buf[1, level], 2, base + STRIP_SOURCE_AT)
    total = jnp.zeros((rows, LANES), jnp.float32)
    loads[2].wait()
    loads[3].wait()
    for level in range(levels):
        base = STRIDE * level
        total = total + columns(fine_buf[0, level], 3, base)
        total = total + columns(fine_buf[1, level], 3, base + SOURCE_AT)
    out[...] = total
    out[:parent_rows, :] += part


def across_border(message, oy, parent_cols, me):
    c = iota(message.shape, 1) & (STRIDE - 1)
    place = jnp.where(me == 0, parent_cols + 1, 1) - oy
    total = jnp.zeros(message.shape, jnp.float32)
    for turn in (-1, 0, 2, 3):
        at = jnp.where(c >= STRIP_SOURCE_AT, c - STRIP_SOURCE_AT, c - STRIP_AT) - turn
        fits = (c >= STRIP_AT) & (at >= 0) & (at < 2) & (place == turn)
        total = total + jnp.where(fits, turned(message, turn), 0.0)
    return total


def pack_columns(parts, band, oy_hbm, nest, source, parent_hbm, parent_source_hbm, *rest):
    outs = rest[: parts - 1]
    old_buf, src_buf, parent, parent_source, oy_ref, sems, field_sems = rest[parts - 1 :]
    levels, rows, cols = nest.shape
    parent_cols = parent.shape[2]
    me = lax.axis_index("gy")
    sides = [1] if parts == 2 else [1, parts - 1]
    fields = [
        pltpu.make_async_copy(ref, buf, field_sems.at[at])
        for at, (ref, buf) in enumerate(
            ((oy_hbm, oy_ref), (parent_hbm, parent), (parent_source_hbm, parent_source))
        )
    ]
    for copy in fields:
        copy.start()
    copies = []
    for at, step in enumerate(sides):
        right = (me == 0) if parts == 2 else jnp.bool_(step == 1)
        start = pl.multiple_of(jnp.where(right, cols - LANES, 0), LANES)
        pair = [
            pltpu.make_async_copy(
                ref.at[:, :, pl.ds(start, LANES)], buf.at[at], sems.at[at, which]
            )
            for which, (ref, buf) in enumerate(((nest, old_buf), (source, src_buf)))
        ]
        for copy in pair:
            copy.start()
        copies.append((right, pair))
    for copy in fields:
        copy.wait()
    oy = oy_ref[0]
    lane = iota((parent.shape[1], LANES), 1)
    for step in range(1, parts):
        out = outs[step - 1]
        part = edge_strip(lax.rem(me + step, parts), band, oy, parent, parent_source)
        if step not in sides:
            out[...] = part
            continue
        at = sides.index(step)
        right, pair = copies[at]
        first = jnp.where(right, LANES - 3, 0)
        outer = jnp.where(right, LANES - 1, 0)
        for level in range(levels):
            edge = jnp.where(
                right, tile(parent, level, parent_cols // LANES - 1), tile(parent, level, 0)
            )
            edge = jnp.where(lane == outer, edge, 0.0)
            turn = (LANES + PARENT_AT + STRIDE * level - outer) & (LANES - 1)
            part = part + pltpu.roll(edge, turn, 1)
        for copy in pair:
            copy.wait()
        fine = iota((rows, LANES), 1) - first
        wanted = (fine >= 0) & (fine < 3)
        total = jnp.zeros((rows, LANES), jnp.float32)
        for level in range(levels):
            for buf, shift in ((old_buf, 0), (src_buf, SOURCE_AT)):
                value = jnp.where(wanted, buf[at, level], 0.0)
                turn = (LANES + STRIDE * level + shift - first) & (LANES - 1)
                total = total + pltpu.roll(value, turn, 1)
        out[...] = total
        out[: part.shape[0], :] += part


def sum_rows(ref):
    count = ref.shape[0] // RATIO
    first, second, third = (ref[pl.ds(at, count, RATIO), :] for at in range(RATIO))
    return first + second + third


def inner_substep(coefs, here, source, there):
    levels, rows, cols = here.shape
    sub = iota((8, cols), 0)
    tiles = rows // 8

    def one_level(level):
        ch = coefs[0, level]
        cv = coefs[1, level]
        centre = 1.0 - 4.0 * ch - 2.0 * cv
        below = jnp.maximum(level - 1, 0)
        above = jnp.minimum(level + 1, levels - 1)
        cv_below = jnp.where(level > 0, cv, 0.0)
        cv_above = jnp.where(level < levels - 1, cv, 0.0)

        def row_tile(t):
            t = t % tiles
            return here[level, 8 * t : 8 * t + 8, :]

        down_before = pltpu.roll(row_tile(-1), 1, 0)
        now = row_tile(0)
        up_now = pltpu.roll(now, 7, 0)
        for t in range(tiles):
            following = row_tile(t + 1)
            down_now = pltpu.roll(now, 1, 0)
            up_next = pltpu.roll(following, 7, 0)
            around = jnp.where(sub == 0, down_before, down_now) + jnp.where(
                sub == 7, up_next, up_now
            )
            around = around + (pltpu.roll(now, 1, 1) + pltpu.roll(now, cols - 1, 1))
            span = slice(8 * t, 8 * t + 8)
            stacked = cv_below * here[below, span, :] + cv_above * here[above, span, :]
            there[level, span, :] = centre * now + ch * around + (stacked + source[level, span, :])
            down_before, now, up_now = down_now, following, up_next

    def two_levels(pair, carry):
        one_level(2 * pair)
        one_level(2 * pair + 1)
        return carry

    lax.fori_loop(0, levels // 2, two_levels, 0)


def spread_coefs(parent_coefs, coefs, out):
    levels = out.shape[2]
    lane = iota((levels, LANES), 1)
    row = iota((levels, LANES), 0)
    for at, ref in enumerate((parent_coefs, coefs)):
        for which in range(2):
            packed = jnp.full(lane.shape, ref[which, 0], jnp.float32)
            rows = packed
            for level in range(1, levels):
                packed = jnp.where(lane >= STRIDE * level, ref[which, level], packed)
                rows = jnp.where(row == level, ref[which, level], rows)
            out[0, 2 * at + which] = packed
            out[1, 2 * at + which] = rows


def inner_first(
    band,
    oy_ref,
    parent_coefs,
    coefs,
    nest,
    source,
    parent,
    parent_source,
    strip,
    first,
    spread,
    oy_rows,
):
    oy = oy_ref[0]
    oy_rows[...] = jnp.full(oy_rows.shape, oy, jnp.int32)
    spread_coefs(parent_coefs, coefs, spread)
    strip[...] = edge_strip(lax.axis_index("gy"), band, oy, parent, parent_source)
    inner_substep(coefs, nest, source, first)


def inner_rest(coefs, nest, first, source, after_pack, third, packs, sums, second, split):
    levels, rows, cols = nest.shape
    lane = iota((rows, LANES), 1)
    for at, ref in enumerate((nest, source)):
        left = jnp.zeros(lane.shape, jnp.float32)
        right = jnp.zeros(lane.shape, jnp.float32)
        for level in range(levels):
            value = jnp.where(lane < RIGHT_OWN, tile(ref, level, 0), 0.0)
            left = left + turned(value, STRIDE * level + LEFT_AT)
            value = jnp.where(lane >= LANES - RIGHT_OWN, tile(ref, level, cols // LANES - 1), 0.0)
            right = right + turned(value, STRIDE * level + RIGHT_OWN)
        packs[2 * at] = left
        packs[2 * at + 1] = right
    inner_substep(coefs, first, source, second)
    inner_substep(coefs, second, source, third)
    for level in range(levels):
        for piece in range(cols // LANES):
            split[piece, level * rows : (level + 1) * rows, :] = tile(third, level, piece)
    for piece in range(cols // LANES):
        sums[piece] = sum_rows(split.at[piece])


def with_columns(tiles, left, right, me, parts, place):
    lane = iota(left.shape, 1)
    from_right = turned(right, -place)
    from_left = turned(left, -3 - place)
    if parts == 2:
        tiles[0] = jnp.where((lane < 3) & (me == 0), from_right, tiles[0])
        tiles[-1] = jnp.where((lane >= LANES - 3) & (me == 1), from_left, tiles[-1])
        return tiles
    extra = jnp.where(lane < 3, from_right, jnp.where(lane >= LANES - 3, from_left, 0.0))
    return tiles + [extra]


def pack_rows(
    parts, old_top, old_end, src_top, src_end, par_top, par_end, own_strip, oy_rows, *rest
):
    columns = rest[: parts - 1]
    across, within, far, strip_out, both = rest[parts - 1 :]
    core = lax.axis_index("gz")
    up, down = both.at[core], both.at[1 - core]
    levels, _, cols = old_top.shape
    me = lax.axis_index("gy")
    left, right = columns[0], columns[-1]
    rows = left.shape[0]
    strip_rows = own_strip.shape[0]
    lane = iota((strip_rows, LANES), 1)
    strips = own_strip[...]
    if parts == 2:
        oy = jnp.concatenate([oy_rows[...]] * (strip_rows // 8), axis=0)
        strips = strips + across_border(left[:strip_rows, :], oy, par_top.shape[2], me)
    else:
        for message in columns:
            strips = strips + message[:strip_rows, :]
    c = lane & (STRIDE - 1)
    strips = jnp.where(c >= STRIP_AT, strips, 0.0)
    strips = jnp.where(c == PARENT_AT, left[:strip_rows, :], strips)
    strips = jnp.where(c == PARENT_AT + 1, turned(right[:strip_rows, :], 1), strips)
    strip_out[...] = strips
    far[...] = strips[:8]
    pieces = cols // LANES
    for out, old, src, first, at, src_at in (
        (up, old_end, src_end, rows - 8, 5, 6),
        (down, old_top, src_top, 0, 0, 0),
    ):
        y_left = left[first : first + 8, :]
        y_right = right[first : first + 8, :]
        for level in range(levels):
            for ref, shift, row, count, base in (
                (old, 0, at, 3, 0),
                (src, SOURCE_AT, src_at, 2, SOURCE_ROW),
            ):
                tiles = [tile(ref, level, piece) for piece in range(pieces)]
                tiles = with_columns(
                    tiles, y_left, y_right, me, parts, STRIDE * level + shift
                )
                for piece, value in enumerate(tiles):
                    out[
                        base + count * level : base + count * (level + 1),
                        piece * LANES : (piece + 1) * LANES,
                    ] = value[row : row + count]
    parent_cols = par_top.shape[2]
    for level in range(levels):
        up[TAIL_ROW + level : TAIL_ROW + level + 1, :parent_cols] = par_end[level, 7:8, :]
        down[TAIL_ROW + level : TAIL_ROW + level + 1, :parent_cols] = par_top[level, 0:1, :]
    up[TAIL_ROW : TAIL_ROW + 8, parent_cols : parent_cols + LANES] = strips[strip_rows - 8 :]
    down[TAIL_ROW : TAIL_ROW + 8, parent_cols : parent_cols + LANES] = strips[:8]
    down[TAIL_ROW + 8 : TAIL_ROW + 16, :LANES] = strips[8:16]
    down[TAIL_ROW + 8 : TAIL_ROW + 16, LANES : 2 * LANES] = strips[16:24]
    within[...] = both[0]
    across[...] = both[1]


def edges(
    parts,
    parent_cols,
    ox_ref,
    spread,
    nest,
    source,
    sums,
    packs,
    strips,
    across,
    within,
    far,
    y_left,
    y_right,
    sides,
    windows,
    coarse_out,
    far_out,
    both,
    ping,
    pong,
    src,
):
    levels, rows, cols = nest.shape
    width = ping.shape[3]
    pieces = cols // LANES
    me = lax.axis_index("gy")
    core = lax.axis_index("gz")
    both[0] = within[...]
    both[1] = across[...]
    before, after = both.at[1 - core], both.at[core]
    is_south = me == 0
    is_north = me == parts - 1

    far_out[...] = far[...]
    sub = iota((8, LANES), 0)
    old = jnp.concatenate(
        [
            strips[...],
            after[TAIL_ROW : TAIL_ROW + 8, parent_cols : parent_cols + LANES],
            after[TAIL_ROW + 8 : TAIL_ROW + 16, :LANES],
            after[TAIL_ROW + 8 : TAIL_ROW + 16, LANES : 2 * LANES],
            jnp.where(
                sub == 7,
                before[TAIL_ROW : TAIL_ROW + 8, parent_cols : parent_cols + LANES],
                0.0,
            ),
        ],
        axis=0,
    )
    count = old.shape[0]

    def packed_coef(which, height):
        return jnp.concatenate([spread[0, which]] * (height // 8), axis=0)

    def stacked(value):
        lane = iota(value.shape, 1)
        below = jnp.where(lane >= STRIDE, turned(value, STRIDE), 0.0)
        return below + jnp.where(lane < STRIDE * (levels - 1), turned(value, -STRIDE), 0.0)

    def around(value):
        return (
            pltpu.roll(value, 1, 0)
            + pltpu.roll(value, value.shape[0] - 1, 0)
            + turned(value, 1)
            + turned(value, -1)
        )

    diff = (
        packed_coef(0, count) * (around(old) - 4.0 * old)
        + packed_coef(1, count) * (stacked(old) - 2.0 * old)
        + turned(old, STRIP_AT - STRIP_SOURCE_AT)
    )
    index = iota((rows + 16, count), 0)
    nest_row = jnp.where(index < rows, index, jnp.where(index < rows + 8, index - rows - 3, index - 13))
    parent_row = ((nest_row + 3) * 171 >> 9) - 1 + ox_ref[0]
    pick = (iota((rows + 16, count), 1) == parent_row).astype(jnp.float32)
    picked = jnp.dot(
        pick,
        jnp.concatenate([old, diff], axis=1),
        precision=HIGHEST,
        preferred_element_type=jnp.float32,
    )
    picked_old, picked_diff = picked[:, :LANES], picked[:, LANES:]

    lane = iota((rows, LANES), 1)
    c = lane & (STRIDE - 1)
    rim_first = jnp.where(is_south, LEFT_AT, RIGHT_OWN - RIM)
    in_rim = (c >= rim_first) & (c < rim_first + RIM)
    at = lane - c + STRIP_AT + jnp.where(c >= rim_first + 3, 2, 1)
    rim_old = jnp.take_along_axis(picked_old[:rows], at, axis=1)
    rim_diff = jnp.take_along_axis(picked_diff[:rows], at, axis=1)
    ch = packed_coef(2, rows)
    cv = packed_coef(3, rows)
    centre = 1.0 - 4.0 * ch - 2.0 * cv
    left = jnp.where(c < 3, y_left[...], packs[0])
    left_src = jnp.where(c < 3, turned(y_left[...], -SOURCE_AT), packs[2])
    right = jnp.where(c >= RIGHT_OWN, turned(y_right[...], RIGHT_OWN), packs[1])
    right_src = jnp.where(c >= RIGHT_OWN, turned(y_right[...], RIGHT_OWN - SOURCE_AT), packs[3])
    for side, (value, forcing, rim) in enumerate(
        (
            (left, left_src, in_rim & is_south),
            (right, right_src, in_rim & is_north),
        )
    ):
        for substep in range(1, SUBSTEPS + 1):
            value = centre * value + ch * around(value) + (cv * stacked(value) + forcing)
            value = jnp.where(rim, rim_old + (substep / SUBSTEPS) * rim_diff, value)
        sides[side] = value

    sub = iota((8, width), 0)
    lane = iota((8, LANES), 1)
    for level in range(levels):
        for buf, field, shift, n, base in (
            (ping, nest, 0, 3, 0),
            (src, source, SOURCE_AT, 2, SOURCE_ROW),
        ):
            for window, first, turn, at, message in (
                (0, 0, 3, 3 - n, before),
                (1, rows - 8, 5, 5, after),
            ):
                tiles = [
                    field[level, first : first + 8, piece * LANES : (piece + 1) * LANES]
                    for piece in range(pieces)
                ]
                tiles = with_columns(
                    tiles,
                    y_left[first : first + 8, :],
                    y_right[first : first + 8, :],
                    me,
                    parts,
                    STRIDE * level + shift,
                )
                for piece, value in enumerate(tiles):
                    value = pltpu.roll(value, turn, 0)
                    span = slice(piece * LANES, (piece + 1) * LANES)
                    buf[level, window, :, span] = value
                    if n == 3:
                        pong[level, window, :, span] = value
                buf[level, window, at : at + n, :] = message[
                    base + n * level : base + n * (level + 1), :
                ]
    rim_first = jnp.where(is_south, 0, LANES - RIM)
    column = STRIP_AT + jnp.where((lane >= rim_first + 3) & (lane < rim_first + RIM), 2, 1)
    rims = {}
    for level in range(levels):
        for window in range(2):
            span = slice(rows + 8 * window, rows + 8 * window + 8)
            at = column + STRIDE * level
            rims[level, window] = (
                jnp.take_along_axis(picked_old[span], at, axis=1),
                jnp.take_along_axis(picked_diff[span], at, axis=1),
            )
    for substep in range(1, SUBSTEPS + 1):
        here, there = (ping, pong) if substep % 2 else (pong, ping)
        there = windows if substep == SUBSTEPS else there
        low = 0 if substep == SUBSTEPS or parts > 2 else 3
        south = (lane >= low) & (lane < RIM) & is_south
        north = (lane >= LANES - RIM) & (lane < LANES - low) & is_north
        weight = substep / SUBSTEPS
        for level in range(levels):
            c_h, c_v = (
                jnp.concatenate([spread[1, which, level : level + 1, :]] * (width // LANES), axis=1)
                for which in (2, 3)
            )
            c_0 = 1.0 - 4.0 * c_h - 2.0 * c_v
            for window in range(2):
                now = here[level, window]
                up = pltpu.roll(now, 1, 0)
                down = pltpu.roll(now, 7, 0)
                if substep == 1:
                    beyond_row = pong[level, window]
                    if window == 0:
                        down = jnp.where(sub == 7, pltpu.roll(beyond_row, 7, 0), down)
                    else:
                        up = jnp.where(sub == 0, pltpu.roll(beyond_row, 1, 0), up)
                beside = pltpu.roll(now, 1, 1) + pltpu.roll(now, width - 1, 1)
                value = c_0 * now + c_h * ((up + down) + beside) + src[level, window]
                if level > 0:
                    value = value + c_v * here[level - 1, window]
                if level < levels - 1:
                    value = value + c_v * here[level + 1, window]
                rim_o, rim_d = rims[level, window]
                rim = rim_o + weight * rim_d
                for piece in range(width // LANES):
                    span = slice(piece * LANES, (piece + 1) * LANES)
                    part = value[:, span]
                    if piece == 0:
                        part = jnp.where(south, rim, part)
                    if piece == pieces - 1:
                        part = jnp.where(north, rim, part)
                    there[level, window, :, span] = part

    parent_rows = rows // RATIO
    lane = iota((parent_rows, LANES), 1)
    row = iota((parent_rows, LANES), 0)
    side_sums = [sum_rows(sides.at[side]) for side in range(2)]
    replaced = [[] for _ in range(pieces)]
    for level in range(levels):
        span = slice(level * parent_rows, (level + 1) * parent_rows)
        top = windows[level, 0, 3:4, :] + windows[level, 0, 4:5, :] + windows[level, 0, 5:6, :]
        end = windows[level, 1, 2:3, :] + windows[level, 1, 3:4, :] + windows[level, 1, 4:5, :]
        for piece in range(pieces):
            value = sums[piece, span, :]
            if piece == 0:
                fixed = turned(side_sums[0], -STRIDE * level - LEFT_AT)
                value = jnp.where(lane < FIXED, fixed, value)
            if piece == pieces - 1:
                fixed = turned(side_sums[1], -STRIDE * level - RIGHT_OWN)
                value = jnp.where(lane >= LANES - FIXED, fixed, value)
            across_piece = slice(piece * LANES, (piece + 1) * LANES)
            value = jnp.where(row == 0, top[:, across_piece], value)
            value = jnp.where(row == parent_rows - 1, end[:, across_piece], value)
            replaced[piece].append(value)
    foot = cols // RATIO
    offset = iota((cols, foot), 0) - RATIO * iota((cols, foot), 1)
    gather = ((offset >= 0) & (offset < RATIO)).astype(jnp.float32)
    means = jnp.dot(
        jnp.concatenate([jnp.concatenate(values, axis=0) for values in replaced], axis=1),
        gather,
        precision=HIGHEST,
        preferred_element_type=jnp.float32,
    ) * (1.0 / 9.0)
    coarse_out[...] = means.reshape(coarse_out.shape)


def put_together(third, sides, windows, result):
    levels, rows, cols = third.shape
    pieces = cols // LANES
    lane = iota((rows, LANES), 1)
    sub = iota((8, cols), 0)
    for level in range(levels):
        fixed = turned(sides[0], -STRIDE * level - LEFT_AT)
        result[level, :, :LANES] = jnp.where(lane < FIXED, fixed, tile(third, level, 0))
        for piece in range(1, pieces - 1):
            result[level, :, piece * LANES : (piece + 1) * LANES] = tile(third, level, piece)
        fixed = turned(sides[1], -STRIDE * level - RIGHT_OWN)
        result[level, :, cols - LANES :] = jnp.where(
            lane >= LANES - FIXED, fixed, tile(third, level, pieces - 1)
        )
        top = pltpu.roll(windows[level, 0, :, :cols], 5, 0)
        result[level, :8, :] = jnp.where(sub < 3, top, result[level, :8, :])
        end = pltpu.roll(windows[level, 1, :, :cols], 3, 0)
        result[level, rows - 8 :, :] = jnp.where(sub >= 5, end, result[level, rows - 8 :, :])


def parent_step(
    parts,
    band,
    ox_ref,
    oy_ref,
    spread,
    third,
    sides,
    windows,
    parent,
    source,
    within,
    across,
    y_left,
    y_right,
    out,
    nest_out,
    late,
    tail,
    result,
    sem,
):
    put_together(third, sides, windows, result)
    store = pltpu.make_async_copy(result, nest_out, sem)
    store.start()
    core = lax.axis_index("gz")
    levels, rows, cols = parent.shape
    tail[0] = within[TAIL_ROW : TAIL_ROW + levels, : cols + LANES]
    tail[1] = across[TAIL_ROW : TAIL_ROW + levels, : cols + LANES]
    me = lax.axis_index("gy")
    is_last = ox_ref[0] == rows - 1
    wide = iota((1, cols), 1)
    south = (wide == oy_ref[0] + 2 - me * cols) & is_last
    north = (wide == oy_ref[0] + band - 3 - me * cols) & is_last
    row = iota((rows, cols), 0)
    lane = iota((rows, cols), 1)
    has_left = me > 0
    has_right = me < parts - 1
    left = y_left[:rows, :]
    right = y_right[:rows, :]
    zero = jnp.zeros((rows, cols), jnp.float32)
    for level in range(levels):
        now = parent[level]
        at = STRIDE * level + PARENT_AT
        from_left = left[:, at : at + 1]
        from_right = right[:, at : at + 1]
        top = tail[1 - core, level : level + 1, :cols]
        end = tail[core, level : level + 1, :cols]
        around = (
            jnp.where(row == 0, top, pltpu.roll(now, 1, 0))
            + jnp.where(row == rows - 1, end, pltpu.roll(now, rows - 1, 0))
            + jnp.where(
                lane == 0, jnp.where(has_left, from_left, 0.0), pltpu.roll(now, 1, 1)
            )
            + jnp.where(
                lane == cols - 1,
                jnp.where(has_right, from_right, 0.0),
                pltpu.roll(now, cols - 1, 1),
            )
        )
        stacked = (parent[level - 1] if level > 0 else zero) + (
            parent[level + 1] if level < levels - 1 else zero
        )
        ch, cv = (
            jnp.concatenate([spread[1, which, level : level + 1, :]] * (cols // LANES), axis=1)
            for which in (0, 1)
        )
        out[level] = (
            (1.0 - 4.0 * ch - 2.0 * cv) * now + ch * around + (cv * stacked + source[level])
        )
        at = cols + STRIDE * level + PARENT_AT
        before_end = jnp.where(
            wide == 0, tail[core, 0:1, at : at + 1], pltpu.roll(end, 1, 1)
        )
        after_end = jnp.where(
            wide == cols - 1, tail[core, 0:1, at + 1 : at + 2], pltpu.roll(end, cols - 1, 1)
        )
        nest_ch = spread[1, 2, level : level + 1, :]
        nest_ch = jnp.concatenate([nest_ch] * (cols // LANES), axis=1)
        share = nest_ch * nest_ch * ch * (1.0 / SUBSTEPS)
        late[level : level + 1, :] = (share * (1.0 / (RATIO * RATIO))) * (
            jnp.where(south, before_end, 0.0) + jnp.where(north, after_end, 0.0)
        )
    store.wait()


def merge(parts, band, ox_ref, oy_ref, late, step, nest, spread, beyond, *rest):
    own, previous = rest[:parts], rest[parts : 2 * parts]
    out, nest_out, joined, corner, sem = rest[2 * parts :]
    levels, rows, cols = step.shape
    foot = own[0].shape[2]
    me = lax.axis_index("gy")

    @pl.when((ox_ref[0] == rows - 1) & ((me == 0) | (me == parts - 1)))
    def _():
        nest_rows, nest_cols = nest.shape[1:]
        first = pl.multiple_of(jnp.where(me == 0, 0, nest_cols - LANES), LANES)
        place = (slice(None), pl.ds(nest_rows - 8, 8), pl.ds(first, LANES))
        load = pltpu.make_async_copy(nest_out.at[place], corner, sem)
        load.start()
        load.wait()
        sub = iota((8, LANES), 0)
        lane = iota((8, LANES), 1)
        cell = (sub == 7) & (lane == jnp.where(me == 0, RIM, LANES - RIM - 1))
        for level in range(levels):
            at = STRIDE * level + STRIP_AT
            value = jnp.where(me == 0, beyond[0:1, at + 2 : at + 3], beyond[0:1, at + 1 : at + 2])
            nest_ch = spread[1, 2, level : level + 1, :]
            share = nest_ch * nest_ch * spread[1, 0, level : level + 1, :] * (1.0 / SUBSTEPS)
            corner[level] += jnp.where(cell, share * value, 0.0)
        again = pltpu.make_async_copy(corner, nest_out.at[place], sem)
        again.start()
        again.wait()

    ox = ox_ref[0]
    oy = oy_ref[0]
    for k in range(parts):
        joined[k, :, :rows, :] = previous[k][...]
        joined[k, :, rows:, :] = own[k][...]
    lane = iota((rows, LANES), 1)
    row = iota((rows, LANES), 0)
    for level in range(levels):
        values = [tile(step, level, piece) for piece in range(cols // LANES)]
        for k in range(parts):
            source = lax.rem(me + parts - k, parts)
            block = joined[k, level, pl.ds(rows - ox, rows), :]
            begin = oy + source * foot - me * cols
            block = pltpu.roll(block, (16384 + begin) & (LANES - 1), 1)
            low = jnp.maximum(source * foot, 2)
            high = jnp.minimum((source + 1) * foot, band - 2)
            for piece in range(cols // LANES):
                at = lane + (piece * LANES + me * cols - oy)
                values[piece] = jnp.where((at >= low) & (at < high), block, values[piece])
        for piece, value in enumerate(values):
            term = late[level : level + 1, piece * LANES : (piece + 1) * LANES]
            value = value + jnp.where(row == rows - 2, term, 0.0)
            out[level, :, piece * LANES : (piece + 1) * LANES] = value


def shifted(value, axis, steps):
    count = lax.axis_size(axis)
    pairs = [(source, (source + steps) % count) for source in range(count)]
    return lax.ppermute(value, axis, pairs)


def shards(
    parent_old, parent_source, parent_coefs, nest_old, nest_source, nest_coefs, offset_x, offset_y
):
    parts = lax.axis_size("gy")
    along = ("gx", "gz")
    levels, parent_rows, parent_cols = parent_old.shape
    _, rows, cols = nest_old.shape
    foot = cols // RATIO
    band = foot * parts
    width = cols if parts == 2 else cols + LANES
    height = TAIL_ROW + 16
    f32 = jnp.float32
    shape = jax.ShapeDtypeStruct
    anywhere = pl.BlockSpec(memory_space=pl.ANY)
    in_hbm = pl.BlockSpec(memory_space=pltpu.HBM)
    sides = 1 if parts == 2 else 2
    if parts == 2:
        packed = [
            pl.pallas_call(
                pack_pair,
                out_shape=VMEM((rows, LANES), f32),
                in_specs=[in_hbm] * 4,
                out_specs=whole(),
                scratch_shapes=[
                    VMEM((2, levels, rows, LANES), f32),
                    VMEM((2, levels, parent_rows, LANES), f32),
                    pltpu.SemaphoreType.DMA((4,)),
                ],
                compiler_params=params(MOST),
                cost_estimate=cost(200000, 800000),
                name="pack_pair",
            )(nest_old, nest_source, parent_old, parent_source)
        ]
    else:
        packed = pl.pallas_call(
            functools.partial(pack_columns, parts, band),
            out_shape=[
                shape((rows if k in (1, parts - 1) else parent_rows, LANES), f32)
                for k in range(1, parts)
            ],
            in_specs=[in_hbm] * 5,
            out_specs=[whole()] * (parts - 1),
            scratch_shapes=[
                VMEM((sides, levels, rows, LANES), f32),
                VMEM((sides, levels, rows, LANES), f32),
                VMEM(parent_old.shape, f32),
                VMEM(parent_old.shape, f32),
                pltpu.SMEM(offset_y.shape, jnp.int32),
                pltpu.SemaphoreType.DMA((sides, 2)),
                pltpu.SemaphoreType.DMA((3,)),
            ],
            compiler_params=params(MOST),
            cost_estimate=cost(200000, 1000000),
            name="pack_columns",
        )(offset_y, nest_old, nest_source, parent_old, parent_source)
    columns = [shifted(packed[k - 1], "gy", k) for k in range(1, parts)]
    own_strip, first, spread, oy_rows = pl.pallas_call(
        functools.partial(inner_first, band),
        out_shape=[
            shape((parent_rows, LANES), f32),
            shape(nest_old.shape, f32),
            shape((2, 4, levels, LANES), f32),
            shape((8, LANES), jnp.int32),
        ],
        in_specs=[scalars()] * 3 + [whole()] * 4,
        out_specs=[whole()] * 4,
        compiler_params=params(),
        cost_estimate=cost(4000000, 3000000),
        name="inner_first",
    )(
        offset_y,
        parent_coefs,
        nest_coefs,
        nest_old,
        nest_source,
        parent_old,
        parent_source,
    )

    def block(ref, last):
        count = ref.shape[1] // 8 - 1 if last else 0
        return pl.BlockSpec((levels, 8, ref.shape[2]), lambda i, c=count: (0, c, 0))

    def full(extent):
        return pl.BlockSpec(extent, lambda i: (0,) * len(extent))

    outs = [
        shape((height, width), f32),
        shape((height, width), f32),
        shape((8, LANES), f32),
        shape((parent_rows, LANES), f32),
    ]
    across, within, far, strips = pl.pallas_call(
        functools.partial(pack_rows, parts),
        out_shape=outs,
        grid=(1,),
        in_specs=[
            block(nest_old, False),
            block(nest_old, True),
            block(nest_old, False),
            block(nest_old, True),
            block(parent_old, False),
            block(parent_old, True),
            full(own_strip.shape),
            full(oy_rows.shape),
        ]
        + [full(message.shape) for message in columns],
        out_specs=[full(out.shape) for out in outs],
        scratch_shapes=[VMEM((2, height, width), f32)],
        compiler_params=params(),
        cost_estimate=cost(100000, 700000),
        name="pack_rows",
    )(nest_old, nest_old, nest_source, nest_source, parent_old, parent_old, own_strip, oy_rows, *columns)
    across = swapped(across, 1)
    within = swapped(within, 0)
    third, packs, sums = pl.pallas_call(
        inner_rest,
        out_shape=[
            shape(nest_old.shape, f32),
            shape((4, rows, LANES), f32),
            shape((cols // LANES, levels * parent_rows, LANES), f32),
        ],
        in_specs=[scalars()] + [whole()] * 3 + [anywhere],
        out_specs=[whole()] * 3,
        scratch_shapes=[
            VMEM(nest_old.shape, f32),
            VMEM((cols // LANES, levels * rows, LANES), f32),
        ],
        compiler_params=params(),
        cost_estimate=cost(8000000, 6000000),
        name="inner_rest",
    )(nest_coefs, nest_old, first, nest_source, strips)
    sides, windows, coarse, far = pl.pallas_call(
        functools.partial(edges, parts, parent_cols),
        out_shape=[
            shape((2, rows, LANES), f32),
            shape((levels, 2, 8, width), f32),
            shape((levels, parent_rows, foot), f32),
            shape((8, LANES), f32),
        ],
        in_specs=[scalars()] + [whole()] * 11,
        out_specs=[whole()] * 4,
        scratch_shapes=[
            VMEM((2, height, width), f32),
            VMEM((levels, 2, 8, width), f32),
            VMEM((levels, 2, 8, width), f32),
            VMEM((levels, 2, 8, width), f32),
        ],
        compiler_params=params(),
        cost_estimate=cost(4000000, 3000000),
        name="edges",
    )(
        offset_x,
        spread,
        nest_old,
        nest_source,
        sums,
        packs,
        strips,
        across,
        within,
        far,
        columns[0],
        columns[-1],
    )
    previous = [shifted(coarse, along, 1)] + [
        shifted_both(coarse, k) for k in range(1, parts)
    ]
    own = [coarse] + [shifted(coarse, "gy", k) for k in range(1, parts)]
    beyond = shifted(far, along, -2)
    step, nest_stored, late = pl.pallas_call(
        functools.partial(parent_step, parts, band),
        out_shape=[
            shape(parent_old.shape, f32),
            shape(nest_old.shape, f32),
            shape((levels, parent_cols), f32),
        ],
        in_specs=[scalars()] * 2 + [whole()] * 10,
        out_specs=[whole(), in_hbm, whole()],
        scratch_shapes=[
            VMEM((2, levels, parent_cols + LANES), f32),
            VMEM(nest_old.shape, f32),
            pltpu.SemaphoreType.DMA,
        ],
        compiler_params=params(),
        cost_estimate=cost(800000, 2500000),
        name="parent_step",
    )(
        offset_x,
        offset_y,
        spread,
        third,
        sides,
        windows,
        parent_old,
        parent_source,
        within,
        across,
        columns[0],
        columns[-1],
    )
    parent_new, nest_new = pl.pallas_call(
        functools.partial(merge, parts, band),
        out_shape=[shape(parent_old.shape, f32), shape(nest_old.shape, f32)],
        in_specs=[scalars()] * 2 + [whole()] * 2 + [in_hbm] + [whole()] * (2 + 2 * parts),
        out_specs=[whole(), in_hbm],
        scratch_shapes=[
            VMEM((parts, levels, 2 * parent_rows, foot), f32),
            VMEM((levels, 8, LANES), f32),
            pltpu.SemaphoreType.DMA,
        ],
        input_output_aliases={4: 1},
        compiler_params=params(),
        cost_estimate=cost(200000, 800000),
        name="merge",
    )(offset_x, offset_y, late, step, nest_stored, spread, beyond, *own, *previous)
    return (parent_new, nest_new)


def swapped(value, first):
    along = ("gx", "gz")
    count = lax.axis_size(along)
    pairs = []
    for at in range(first, count, 2):
        pairs += [(at, (at + 1) % count), ((at + 1) % count, at)]
    return lax.ppermute(value, along, pairs)


def shifted_both(value, steps):
    sizes = [lax.axis_size(axis) for axis in ("gx", "gy", "gz")]
    gx, gy, gz = sizes
    pairs = []
    for x in range(gx):
        for y in range(gy):
            for z in range(gz):
                place = (x * gz + z + 1) % (gx * gz)
                target = (place // gz * gy + (y + steps) % gy) * gz + place % gz
                pairs.append(((x * gy + y) * gz + z, target))
    return lax.ppermute(value, ("gx", "gy", "gz"), pairs)


def solution(mesh):
    return jax.shard_map(
        shards,
        mesh=mesh,
        in_specs=(
            P(None, ("grp", "gx", "gz"), "gy"),
            P(None, ("grp", "gx", "gz"), "gy"),
            P(),
            P(None, ("grp", "gx", "gz"), "gy"),
            P(None, ("grp", "gx", "gz"), "gy"),
            P(),
            P("grp"),
            P("grp"),
        ),
        out_specs=(P(None, ("grp", "gx", "gz"), "gy"), P(None, ("grp", "gx", "gz"), "gy")),
        check_vma=False,
    )
```

```python
import functools

import jax
import jax.numpy as jnp
from jax import lax
from jax.experimental import pallas as pl
from jax.experimental.pallas import tpu as pltpu
from jax.sharding import PartitionSpec as P

RATIO = 3
SUBSTEPS = 3
RIM = 6
LANES = 128
STRIDE = 16
SOURCE_AT = 3
PARENT_AT = 6
STRIP_AT = 8
STRIP_SOURCE_AT = 12
SOURCE_ROW = 24
TAIL_ROW = 40
FIXED = 8
LEFT_AT = 3
RIGHT_OWN = STRIDE - 3
VMEM = pltpu.VMEM
LIMIT = 24 * 1024 * 1024
MOST = 54 * 1024 * 1024


def iota(shape, dim):
    return lax.broadcasted_iota(jnp.int32, shape, dim)


def whole():
    return pl.BlockSpec(memory_space=VMEM)


def scalars():
    return pl.BlockSpec(memory_space=pltpu.SMEM)


def params(limit=LIMIT):
    return pltpu.CompilerParams(vmem_limit_bytes=limit)


def cost(flops, moved):
    return pl.CostEstimate(flops=flops, bytes_accessed=moved, transcendentals=0)


def tile(ref, level, index):
    return ref[level, :, index * LANES : (index + 1) * LANES]


def turned(value, lanes):
    lanes = lanes % LANES
    return pltpu.roll(value, lanes, 1) if lanes else value


def edge_strip(dest, band, oy, parent, parent_source):
    levels, rows, cols = parent.shape
    lane = iota((rows, LANES), 1)
    base = jnp.where(dest == 0, oy - 1, oy + band - 3) - lax.axis_index("gy") * cols
    total = jnp.zeros(lane.shape, jnp.float32)
    for ref, first in ((parent, STRIP_AT), (parent_source, STRIP_SOURCE_AT)):
        for level in range(levels):
            found = jnp.zeros(lane.shape, jnp.float32)
            for at in range(cols // LANES):
                place = lane + (at * LANES - base)
                found = jnp.where((place >= 0) & (place < 4), tile(ref, level, at), found)
            turn = (16384 + first + STRIDE * level - base) & (LANES - 1)
            total = total + pltpu.roll(found, turn, 1)
    return total


def pack_pair(nest, source, parent, parent_source, out, fine_buf, coarse_buf, sems):
    levels, rows, cols = nest.shape
    parent_rows, parent_cols = parent.shape[1:]
    right = lax.axis_index("gy") == 0
    loads = []
    for at, (ref, buf) in enumerate(
        (
            (parent, coarse_buf.at[0]),
            (parent_source, coarse_buf.at[1]),
            (nest, fine_buf.at[0]),
            (source, fine_buf.at[1]),
        )
    ):
        start = pl.multiple_of(jnp.where(right, ref.shape[2] - LANES, 0), LANES)
        loads.append(pltpu.make_async_copy(ref.at[:, :, pl.ds(start, LANES)], buf, sems.at[at]))
    for copy in loads:
        copy.start()

    def columns(value, count, to):
        first = jnp.where(right, LANES - count, 0)
        place = iota(value.shape, 1) - first
        value = jnp.where((place >= 0) & (place < count), value, 0.0)
        return pltpu.roll(value, (LANES + to - first) & (LANES - 1), 1)

    part = jnp.zeros((parent_rows, LANES), jnp.float32)
    loads[0].wait()
    loads[1].wait()
    for level in range(levels):
        base = STRIDE * level
        part = part + columns(coarse_buf[0, level], 1, base + PARENT_AT)
        part = part + columns(coarse_buf[0, level], 2, base + STRIP_AT)
        part = part + columns(coarse_buf[1, level], 2, base + STRIP_SOURCE_AT)
    total = jnp.zeros((rows, LANES), jnp.float32)
    loads[2].wait()
    loads[3].wait()
    for level in range(levels):
        base = STRIDE * level
        total = total + columns(fine_buf[0, level], 3, base)
        total = total + columns(fine_buf[1, level], 3, base + SOURCE_AT)
    out[...] = total
    out[:parent_rows, :] += part


def across_border(message, oy, parent_cols, me):
    c = iota(message.shape, 1) & (STRIDE - 1)
    place = jnp.where(me == 0, parent_cols + 1, 1) - oy
    total = jnp.zeros(message.shape, jnp.float32)
    for turn in (-1, 0, 2, 3):
        at = jnp.where(c >= STRIP_SOURCE_AT, c - STRIP_SOURCE_AT, c - STRIP_AT) - turn
        fits = (c >= STRIP_AT) & (at >= 0) & (at < 2) & (place == turn)
        total = total + jnp.where(fits, turned(message, turn), 0.0)
    return total


def pack_columns(parts, band, oy_hbm, nest, source, parent_hbm, parent_source_hbm, *rest):
    outs = rest[: parts - 1]
    old_buf, src_buf, parent, parent_source, oy_ref, sems, field_sems = rest[parts - 1 :]
    levels, rows, cols = nest.shape
    parent_cols = parent.shape[2]
    me = lax.axis_index("gy")
    sides = [1] if parts == 2 else [1, parts - 1]
    fields = [
        pltpu.make_async_copy(ref, buf, field_sems.at[at])
        for at, (ref, buf) in enumerate(
            ((oy_hbm, oy_ref), (parent_hbm, parent), (parent_source_hbm, parent_source))
        )
    ]
    for copy in fields:
        copy.start()
    copies = []
    for at, step in enumerate(sides):
        right = (me == 0) if parts == 2 else jnp.bool_(step == 1)
        start = pl.multiple_of(jnp.where(right, cols - LANES, 0), LANES)
        pair = [
            pltpu.make_async_copy(
                ref.at[:, :, pl.ds(start, LANES)], buf.at[at], sems.at[at, which]
            )
            for which, (ref, buf) in enumerate(((nest, old_buf), (source, src_buf)))
        ]
        for copy in pair:
            copy.start()
        copies.append((right, pair))
    for copy in fields:
        copy.wait()
    oy = oy_ref[0]
    lane = iota((parent.shape[1], LANES), 1)
    for step in range(1, parts):
        out = outs[step - 1]
        part = edge_strip(lax.rem(me + step, parts), band, oy, parent, parent_source)
        if step not in sides:
            out[...] = part
            continue
        at = sides.index(step)
        right, pair = copies[at]
        first = jnp.where(right, LANES - 3, 0)
        outer = jnp.where(right, LANES - 1, 0)
        for level in range(levels):
            edge = jnp.where(
                right, tile(parent, level, parent_cols // LANES - 1), tile(parent, level, 0)
            )
            edge = jnp.where(lane == outer, edge, 0.0)
            turn = (LANES + PARENT_AT + STRIDE * level - outer) & (LANES - 1)
            part = part + pltpu.roll(edge, turn, 1)
        for copy in pair:
            copy.wait()
        fine = iota((rows, LANES), 1) - first
        wanted = (fine >= 0) & (fine < 3)
        total = jnp.zeros((rows, LANES), jnp.float32)
        for level in range(levels):
            for buf, shift in ((old_buf, 0), (src_buf, SOURCE_AT)):
                value = jnp.where(wanted, buf[at, level], 0.0)
                turn = (LANES + STRIDE * level + shift - first) & (LANES - 1)
                total = total + pltpu.roll(value, turn, 1)
        out[...] = total
        out[: part.shape[0], :] += part


def three_terms(value):
    terms = []
    for _ in range(3):
        term = value.astype(jnp.bfloat16)
        terms.append(term)
        value = value - term.astype(jnp.float32)
    return terms


def select_rows(selector, value):
    selector = selector.astype(jnp.bfloat16)
    high, middle, low = (
        jnp.dot(selector, term, preferred_element_type=jnp.float32)
        for term in three_terms(value)
    )
    return high + (middle + low)


def select_columns(value, selector):
    selector = selector.astype(jnp.bfloat16)
    high, middle, low = (
        jnp.dot(term, selector, preferred_element_type=jnp.float32)
        for term in three_terms(value)
    )
    return high + (middle + low)


def sum_rows(ref):
    count = ref.shape[0] // RATIO
    first, second, third = (ref[pl.ds(at, count, RATIO), :] for at in range(RATIO))
    return first + second + third


def inner_substep(coefs, here, source, there):
    levels, rows, cols = here.shape
    sub = iota((8, cols), 0)
    tiles = rows // 8

    def one_level(level):
        ch = coefs[0, level]
        cv = coefs[1, level]
        centre = 1.0 - 4.0 * ch - 2.0 * cv
        below = jnp.maximum(level - 1, 0)
        above = jnp.minimum(level + 1, levels - 1)
        cv_below = jnp.where(level > 0, cv, 0.0)
        cv_above = jnp.where(level < levels - 1, cv, 0.0)

        def row_tile(t):
            t = t % tiles
            return here[level, 8 * t : 8 * t + 8, :]

        down_before = pltpu.roll(row_tile(-1), 1, 0)
        now = row_tile(0)
        up_now = pltpu.roll(now, 7, 0)
        for t in range(tiles):
            following = row_tile(t + 1)
            down_now = pltpu.roll(now, 1, 0)
            up_next = pltpu.roll(following, 7, 0)
            around = jnp.where(sub == 0, down_before, down_now) + jnp.where(
                sub == 7, up_next, up_now
            )
            around = around + (pltpu.roll(now, 1, 1) + pltpu.roll(now, cols - 1, 1))
            span = slice(8 * t, 8 * t + 8)
            stacked = cv_below * here[below, span, :] + cv_above * here[above, span, :]
            there[level, span, :] = centre * now + ch * around + (stacked + source[level, span, :])
            down_before, now, up_now = down_now, following, up_next

    def two_levels(pair, carry):
        one_level(2 * pair)
        one_level(2 * pair + 1)
        return carry

    lax.fori_loop(0, levels // 2, two_levels, 0)


def spread_coefs(parent_coefs, coefs, out):
    levels = out.shape[2]
    lane = iota((levels, LANES), 1)
    row = iota((levels, LANES), 0)
    for at, ref in enumerate((parent_coefs, coefs)):
        for which in range(2):
            packed = jnp.full(lane.shape, ref[which, 0], jnp.float32)
            rows = packed
            for level in range(1, levels):
                packed = jnp.where(lane >= STRIDE * level, ref[which, level], packed)
                rows = jnp.where(row == level, ref[which, level], rows)
            out[0, 2 * at + which] = packed
            out[1, 2 * at + which] = rows


def inner_first(
    band,
    oy_ref,
    parent_coefs,
    coefs,
    nest,
    source,
    parent,
    parent_source,
    strip,
    first,
    spread,
    oy_rows,
):
    oy = oy_ref[0]
    oy_rows[...] = jnp.full(oy_rows.shape, oy, jnp.int32)
    spread_coefs(parent_coefs, coefs, spread)
    strip[...] = edge_strip(lax.axis_index("gy"), band, oy, parent, parent_source)
    inner_substep(coefs, nest, source, first)


def inner_rest(coefs, nest, first, source, after_pack, third, packs, sums, second, split):
    levels, rows, cols = nest.shape
    lane = iota((rows, LANES), 1)
    for at, ref in enumerate((nest, source)):
        left = jnp.zeros(lane.shape, jnp.float32)
        right = jnp.zeros(lane.shape, jnp.float32)
        for level in range(levels):
            value = jnp.where(lane < RIGHT_OWN, tile(ref, level, 0), 0.0)
            left = left + turned(value, STRIDE * level + LEFT_AT)
            value = jnp.where(lane >= LANES - RIGHT_OWN, tile(ref, level, cols // LANES - 1), 0.0)
            right = right + turned(value, STRIDE * level + RIGHT_OWN)
        packs[2 * at] = left
        packs[2 * at + 1] = right
    inner_substep(coefs, first, source, second)
    inner_substep(coefs, second, source, third)
    for level in range(levels):
        for piece in range(cols // LANES):
            split[piece, level * rows : (level + 1) * rows, :] = tile(third, level, piece)
    for piece in range(cols // LANES):
        sums[piece] = sum_rows(split.at[piece])


def with_columns(tiles, left, right, me, parts, place):
    lane = iota(left.shape, 1)
    from_right = turned(right, -place)
    from_left = turned(left, -3 - place)
    if parts == 2:
        tiles[0] = jnp.where((lane < 3) & (me == 0), from_right, tiles[0])
        tiles[-1] = jnp.where((lane >= LANES - 3) & (me == 1), from_left, tiles[-1])
        return tiles
    extra = jnp.where(lane < 3, from_right, jnp.where(lane >= LANES - 3, from_left, 0.0))
    return tiles + [extra]


def pack_rows(
    parts, old_top, old_end, src_top, src_end, par_top, par_end, own_strip, oy_rows, *rest
):
    columns = rest[: parts - 1]
    across, within, far, strip_out, both = rest[parts - 1 :]
    core = lax.axis_index("gz")
    up, down = both.at[core], both.at[1 - core]
    levels, _, cols = old_top.shape
    me = lax.axis_index("gy")
    left, right = columns[0], columns[-1]
    rows = left.shape[0]
    strip_rows = own_strip.shape[0]
    lane = iota((strip_rows, LANES), 1)
    strips = own_strip[...]
    if parts == 2:
        oy = jnp.concatenate([oy_rows[...]] * (strip_rows // 8), axis=0)
        strips = strips + across_border(left[:strip_rows, :], oy, par_top.shape[2], me)
    else:
        for message in columns:
            strips = strips + message[:strip_rows, :]
    c = lane & (STRIDE - 1)
    strips = jnp.where(c >= STRIP_AT, strips, 0.0)
    strips = jnp.where(c == PARENT_AT, left[:strip_rows, :], strips)
    strips = jnp.where(c == PARENT_AT + 1, turned(right[:strip_rows, :], 1), strips)
    strip_out[...] = strips
    far[...] = strips[:8]
    pieces = cols // LANES
    for out, old, src, first, at, src_at in (
        (up, old_end, src_end, rows - 8, 5, 6),
        (down, old_top, src_top, 0, 0, 0),
    ):
        y_left = left[first : first + 8, :]
        y_right = right[first : first + 8, :]
        for level in range(levels):
            for ref, shift, row, count, base in (
                (old, 0, at, 3, 0),
                (src, SOURCE_AT, src_at, 2, SOURCE_ROW),
            ):
                tiles = [tile(ref, level, piece) for piece in range(pieces)]
                tiles = with_columns(
                    tiles, y_left, y_right, me, parts, STRIDE * level + shift
                )
                for piece, value in enumerate(tiles):
                    out[
                        base + count * level : base + count * (level + 1),
                        piece * LANES : (piece + 1) * LANES,
                    ] = value[row : row + count]
    parent_cols = par_top.shape[2]
    for level in range(levels):
        up[TAIL_ROW + level : TAIL_ROW + level + 1, :parent_cols] = par_end[level, 7:8, :]
        down[TAIL_ROW + level : TAIL_ROW + level + 1, :parent_cols] = par_top[level, 0:1, :]
    up[TAIL_ROW : TAIL_ROW + 8, parent_cols : parent_cols + LANES] = strips[strip_rows - 8 :]
    down[TAIL_ROW : TAIL_ROW + 8, parent_cols : parent_cols + LANES] = strips[:8]
    down[TAIL_ROW + 8 : TAIL_ROW + 16, :LANES] = strips[8:16]
    down[TAIL_ROW + 8 : TAIL_ROW + 16, LANES : 2 * LANES] = strips[16:24]
    within[...] = both[0]
    across[...] = both[1]


def edges(
    parts,
    parent_cols,
    ox_ref,
    spread,
    nest,
    source,
    sums,
    packs,
    strips,
    across,
    within,
    far,
    y_left,
    y_right,
    sides,
    windows,
    coarse_out,
    far_out,
    both,
    ping,
    pong,
    src,
):
    levels, rows, cols = nest.shape
    width = ping.shape[3]
    pieces = cols // LANES
    me = lax.axis_index("gy")
    core = lax.axis_index("gz")
    both[0] = within[...]
    both[1] = across[...]
    before, after = both.at[1 - core], both.at[core]
    is_south = me == 0
    is_north = me == parts - 1

    far_out[...] = far[...]
    sub = iota((8, LANES), 0)
    old = jnp.concatenate(
        [
            strips[...],
            after[TAIL_ROW : TAIL_ROW + 8, parent_cols : parent_cols + LANES],
            after[TAIL_ROW + 8 : TAIL_ROW + 16, :LANES],
            after[TAIL_ROW + 8 : TAIL_ROW + 16, LANES : 2 * LANES],
            jnp.where(
                sub == 7,
                before[TAIL_ROW : TAIL_ROW + 8, parent_cols : parent_cols + LANES],
                0.0,
            ),
        ],
        axis=0,
    )
    count = old.shape[0]

    def packed_coef(which, height):
        return jnp.concatenate([spread[0, which]] * (height // 8), axis=0)

    def stacked(value):
        lane = iota(value.shape, 1)
        below = jnp.where(lane >= STRIDE, turned(value, STRIDE), 0.0)
        return below + jnp.where(lane < STRIDE * (levels - 1), turned(value, -STRIDE), 0.0)

    def around(value):
        return (
            pltpu.roll(value, 1, 0)
            + pltpu.roll(value, value.shape[0] - 1, 0)
            + turned(value, 1)
            + turned(value, -1)
        )

    diff = (
        packed_coef(0, count) * (around(old) - 4.0 * old)
        + packed_coef(1, count) * (stacked(old) - 2.0 * old)
        + turned(old, STRIP_AT - STRIP_SOURCE_AT)
    )
    index = iota((rows + 16, count), 0)
    nest_row = jnp.where(index < rows, index, jnp.where(index < rows + 8, index - rows - 3, index - 13))
    parent_row = ((nest_row + 3) * 171 >> 9) - 1 + ox_ref[0]
    pick = (iota((rows + 16, count), 1) == parent_row).astype(jnp.float32)
    picked = select_rows(pick, jnp.concatenate([old, diff], axis=1))
    picked_old, picked_diff = picked[:, :LANES], picked[:, LANES:]

    lane = iota((rows, LANES), 1)
    c = lane & (STRIDE - 1)
    rim_first = jnp.where(is_south, LEFT_AT, RIGHT_OWN - RIM)
    in_rim = (c >= rim_first) & (c < rim_first + RIM)
    at = lane - c + STRIP_AT + jnp.where(c >= rim_first + 3, 2, 1)
    rim_old = jnp.take_along_axis(picked_old[:rows], at, axis=1)
    rim_diff = jnp.take_along_axis(picked_diff[:rows], at, axis=1)
    ch = packed_coef(2, rows)
    cv = packed_coef(3, rows)
    centre = 1.0 - 4.0 * ch - 2.0 * cv
    left = jnp.where(c < 3, y_left[...], packs[0])
    left_src = jnp.where(c < 3, turned(y_left[...], -SOURCE_AT), packs[2])
    right = jnp.where(c >= RIGHT_OWN, turned(y_right[...], RIGHT_OWN), packs[1])
    right_src = jnp.where(c >= RIGHT_OWN, turned(y_right[...], RIGHT_OWN - SOURCE_AT), packs[3])
    for side, (value, forcing, rim) in enumerate(
        (
            (left, left_src, in_rim & is_south),
            (right, right_src, in_rim & is_north),
        )
    ):
        for substep in range(1, SUBSTEPS + 1):
            value = centre * value + ch * around(value) + (cv * stacked(value) + forcing)
            value = jnp.where(rim, rim_old + (substep / SUBSTEPS) * rim_diff, value)
        sides[side] = value

    sub = iota((8, width), 0)
    lane = iota((8, LANES), 1)
    for level in range(levels):
        for buf, field, shift, n, base in (
            (ping, nest, 0, 3, 0),
            (src, source, SOURCE_AT, 2, SOURCE_ROW),
        ):
            for window, first, turn, at, message in (
                (0, 0, 3, 3 - n, before),
                (1, rows - 8, 5, 5, after),
            ):
                tiles = [
                    field[level, first : first + 8, piece * LANES : (piece + 1) * LANES]
                    for piece in range(pieces)
                ]
                tiles = with_columns(
                    tiles,
                    y_left[first : first + 8, :],
                    y_right[first : first + 8, :],
                    me,
                    parts,
                    STRIDE * level + shift,
                )
                for piece, value in enumerate(tiles):
                    value = pltpu.roll(value, turn, 0)
                    span = slice(piece * LANES, (piece + 1) * LANES)
                    buf[level, window, :, span] = value
                    if n == 3:
                        pong[level, window, :, span] = value
                buf[level, window, at : at + n, :] = message[
                    base + n * level : base + n * (level + 1), :
                ]
    rim_first = jnp.where(is_south, 0, LANES - RIM)
    column = STRIP_AT + jnp.where((lane >= rim_first + 3) & (lane < rim_first + RIM), 2, 1)
    rims = {}
    for level in range(levels):
        for window in range(2):
            span = slice(rows + 8 * window, rows + 8 * window + 8)
            at = column + STRIDE * level
            rims[level, window] = (
                jnp.take_along_axis(picked_old[span], at, axis=1),
                jnp.take_along_axis(picked_diff[span], at, axis=1),
            )
    for substep in range(1, SUBSTEPS + 1):
        here, there = (ping, pong) if substep % 2 else (pong, ping)
        there = windows if substep == SUBSTEPS else there
        low = 0 if substep == SUBSTEPS or parts > 2 else 3
        south = (lane >= low) & (lane < RIM) & is_south
        north = (lane >= LANES - RIM) & (lane < LANES - low) & is_north
        weight = substep / SUBSTEPS
        for level in range(levels):
            c_h, c_v = (
                jnp.concatenate([spread[1, which, level : level + 1, :]] * (width // LANES), axis=1)
                for which in (2, 3)
            )
            c_0 = 1.0 - 4.0 * c_h - 2.0 * c_v
            for window in range(2):
                now = here[level, window]
                up = pltpu.roll(now, 1, 0)
                down = pltpu.roll(now, 7, 0)
                if substep == 1:
                    beyond_row = pong[level, window]
                    if window == 0:
                        down = jnp.where(sub == 7, pltpu.roll(beyond_row, 7, 0), down)
                    else:
                        up = jnp.where(sub == 0, pltpu.roll(beyond_row, 1, 0), up)
                beside = pltpu.roll(now, 1, 1) + pltpu.roll(now, width - 1, 1)
                value = c_0 * now + c_h * ((up + down) + beside) + src[level, window]
                if level > 0:
                    value = value + c_v * here[level - 1, window]
                if level < levels - 1:
                    value = value + c_v * here[level + 1, window]
                rim_o, rim_d = rims[level, window]
                rim = rim_o + weight * rim_d
                for piece in range(width // LANES):
                    span = slice(piece * LANES, (piece + 1) * LANES)
                    part = value[:, span]
                    if piece == 0:
                        part = jnp.where(south, rim, part)
                    if piece == pieces - 1:
                        part = jnp.where(north, rim, part)
                    there[level, window, :, span] = part

    parent_rows = rows // RATIO
    lane = iota((parent_rows, LANES), 1)
    row = iota((parent_rows, LANES), 0)
    side_sums = [sum_rows(sides.at[side]) for side in range(2)]
    replaced = [[] for _ in range(pieces)]
    for level in range(levels):
        span = slice(level * parent_rows, (level + 1) * parent_rows)
        top = windows[level, 0, 3:4, :] + windows[level, 0, 4:5, :] + windows[level, 0, 5:6, :]
        end = windows[level, 1, 2:3, :] + windows[level, 1, 3:4, :] + windows[level, 1, 4:5, :]
        for piece in range(pieces):
            value = sums[piece, span, :]
            if piece == 0:
                fixed = turned(side_sums[0], -STRIDE * level - LEFT_AT)
                value = jnp.where(lane < FIXED, fixed, value)
            if piece == pieces - 1:
                fixed = turned(side_sums[1], -STRIDE * level - RIGHT_OWN)
                value = jnp.where(lane >= LANES - FIXED, fixed, value)
            across_piece = slice(piece * LANES, (piece + 1) * LANES)
            value = jnp.where(row == 0, top[:, across_piece], value)
            value = jnp.where(row == parent_rows - 1, end[:, across_piece], value)
            replaced[piece].append(value)
    foot = cols // RATIO
    offset = iota((cols, foot), 0) - RATIO * iota((cols, foot), 1)
    gather = ((offset >= 0) & (offset < RATIO)).astype(jnp.float32)
    means = select_columns(
        jnp.concatenate([jnp.concatenate(values, axis=0) for values in replaced], axis=1), gather
    ) * (1.0 / 9.0)
    coarse_out[...] = means.reshape(coarse_out.shape)


def put_together(third, sides, windows, result):
    levels, rows, cols = third.shape
    pieces = cols // LANES
    lane = iota((rows, LANES), 1)
    sub = iota((8, cols), 0)
    for level in range(levels):
        fixed = turned(sides[0], -STRIDE * level - LEFT_AT)
        result[level, :, :LANES] = jnp.where(lane < FIXED, fixed, tile(third, level, 0))
        for piece in range(1, pieces - 1):
            result[level, :, piece * LANES : (piece + 1) * LANES] = tile(third, level, piece)
        fixed = turned(sides[1], -STRIDE * level - RIGHT_OWN)
        result[level, :, cols - LANES :] = jnp.where(
            lane >= LANES - FIXED, fixed, tile(third, level, pieces - 1)
        )
        top = pltpu.roll(windows[level, 0, :, :cols], 5, 0)
        result[level, :8, :] = jnp.where(sub < 3, top, result[level, :8, :])
        end = pltpu.roll(windows[level, 1, :, :cols], 3, 0)
        result[level, rows - 8 :, :] = jnp.where(sub >= 5, end, result[level, rows - 8 :, :])


def parent_step(
    parts,
    band,
    ox_ref,
    oy_ref,
    spread,
    third,
    sides,
    windows,
    parent,
    source,
    within,
    across,
    y_left,
    y_right,
    out,
    nest_out,
    late,
    tail,
    result,
    sem,
):
    put_together(third, sides, windows, result)
    store = pltpu.make_async_copy(result, nest_out, sem)
    store.start()
    core = lax.axis_index("gz")
    levels, rows, cols = parent.shape
    tail[0] = within[TAIL_ROW : TAIL_ROW + levels, : cols + LANES]
    tail[1] = across[TAIL_ROW : TAIL_ROW + levels, : cols + LANES]
    me = lax.axis_index("gy")
    is_last = ox_ref[0] == rows - 1
    wide = iota((1, cols), 1)
    south = (wide == oy_ref[0] + 2 - me * cols) & is_last
    north = (wide == oy_ref[0] + band - 3 - me * cols) & is_last
    row = iota((rows, cols), 0)
    lane = iota((rows, cols), 1)
    has_left = me > 0
    has_right = me < parts - 1
    left = y_left[:rows, :]
    right = y_right[:rows, :]
    zero = jnp.zeros((rows, cols), jnp.float32)
    for level in range(levels):
        now = parent[level]
        at = STRIDE * level + PARENT_AT
        from_left = left[:, at : at + 1]
        from_right = right[:, at : at + 1]
        top = tail[1 - core, level : level + 1, :cols]
        end = tail[core, level : level + 1, :cols]
        around = (
            jnp.where(row == 0, top, pltpu.roll(now, 1, 0))
            + jnp.where(row == rows - 1, end, pltpu.roll(now, rows - 1, 0))
            + jnp.where(
                lane == 0, jnp.where(has_left, from_left, 0.0), pltpu.roll(now, 1, 1)
            )
            + jnp.where(
                lane == cols - 1,
                jnp.where(has_right, from_right, 0.0),
                pltpu.roll(now, cols - 1, 1),
            )
        )
        stacked = (parent[level - 1] if level > 0 else zero) + (
            parent[level + 1] if level < levels - 1 else zero
        )
        ch, cv = (
            jnp.concatenate([spread[1, which, level : level + 1, :]] * (cols // LANES), axis=1)
            for which in (0, 1)
        )
        out[level] = (
            (1.0 - 4.0 * ch - 2.0 * cv) * now + ch * around + (cv * stacked + source[level])
        )
        at = cols + STRIDE * level + PARENT_AT
        before_end = jnp.where(
            wide == 0, tail[core, 0:1, at : at + 1], pltpu.roll(end, 1, 1)
        )
        after_end = jnp.where(
            wide == cols - 1, tail[core, 0:1, at + 1 : at + 2], pltpu.roll(end, cols - 1, 1)
        )
        nest_ch = spread[1, 2, level : level + 1, :]
        nest_ch = jnp.concatenate([nest_ch] * (cols // LANES), axis=1)
        share = nest_ch * nest_ch * ch * (1.0 / SUBSTEPS)
        late[level : level + 1, :] = (share * (1.0 / (RATIO * RATIO))) * (
            jnp.where(south, before_end, 0.0) + jnp.where(north, after_end, 0.0)
        )
    store.wait()


def merge(parts, band, ox_ref, oy_ref, late, step, nest, spread, beyond, *rest):
    own = rest[:parts]
    previous = rest[2 * parts - 1 : 2 * parts] + rest[parts : 2 * parts - 1]
    out, nest_out, joined, corner, sem = rest[2 * parts :]
    levels, rows, cols = step.shape
    foot = own[0].shape[2]
    me = lax.axis_index("gy")

    @pl.when((ox_ref[0] == rows - 1) & ((me == 0) | (me == parts - 1)))
    def _():
        nest_rows, nest_cols = nest.shape[1:]
        first = pl.multiple_of(jnp.where(me == 0, 0, nest_cols - LANES), LANES)
        place = (slice(None), pl.ds(nest_rows - 8, 8), pl.ds(first, LANES))
        load = pltpu.make_async_copy(nest_out.at[place], corner, sem)
        load.start()
        load.wait()
        sub = iota((8, LANES), 0)
        lane = iota((8, LANES), 1)
        cell = (sub == 7) & (lane == jnp.where(me == 0, RIM, LANES - RIM - 1))
        for level in range(levels):
            at = STRIDE * level + STRIP_AT
            value = jnp.where(me == 0, beyond[0:1, at + 2 : at + 3], beyond[0:1, at + 1 : at + 2])
            nest_ch = spread[1, 2, level : level + 1, :]
            share = nest_ch * nest_ch * spread[1, 0, level : level + 1, :] * (1.0 / SUBSTEPS)
            corner[level] += jnp.where(cell, share * value, 0.0)
        again = pltpu.make_async_copy(corner, nest_out.at[place], sem)
        again.start()
        again.wait()

    ox = ox_ref[0]
    oy = oy_ref[0]
    for k in range(parts):
        joined[k, :, :rows, :] = previous[k][...]
        joined[k, :, rows:, :] = own[k][...]
    lane = iota((rows, LANES), 1)
    row = iota((rows, LANES), 0)
    for level in range(levels):
        values = [tile(step, level, piece) for piece in range(cols // LANES)]
        for k in range(parts):
            source = lax.rem(me + parts - k, parts)
            block = joined[k, level, pl.ds(rows - ox, rows), :]
            begin = oy + source * foot - me * cols
            block = pltpu.roll(block, (16384 + begin) & (LANES - 1), 1)
            low = jnp.maximum(source * foot, 2)
            high = jnp.minimum((source + 1) * foot, band - 2)
            for piece in range(cols // LANES):
                at = lane + (piece * LANES + me * cols - oy)
                values[piece] = jnp.where((at >= low) & (at < high), block, values[piece])
        for piece, value in enumerate(values):
            term = late[level : level + 1, piece * LANES : (piece + 1) * LANES]
            value = value + jnp.where(row == rows - 2, term, 0.0)
            out[level, :, piece * LANES : (piece + 1) * LANES] = value


def shifted(value, axis, steps):
    count = lax.axis_size(axis)
    pairs = [(source, (source + steps) % count) for source in range(count)]
    return lax.ppermute(value, axis, pairs)


def shards(
    parent_old, parent_source, parent_coefs, nest_old, nest_source, nest_coefs, offset_x, offset_y
):
    parts = lax.axis_size("gy")
    along = ("gx", "gz")
    levels, parent_rows, parent_cols = parent_old.shape
    _, rows, cols = nest_old.shape
    foot = cols // RATIO
    band = foot * parts
    width = cols if parts == 2 else cols + LANES
    height = TAIL_ROW + 16
    f32 = jnp.float32
    shape = jax.ShapeDtypeStruct
    anywhere = pl.BlockSpec(memory_space=pl.ANY)
    in_hbm = pl.BlockSpec(memory_space=pltpu.HBM)
    sides = 1 if parts == 2 else 2
    if parts == 2:
        packed = [
            pl.pallas_call(
                pack_pair,
                out_shape=VMEM((rows, LANES), f32),
                in_specs=[in_hbm] * 4,
                out_specs=whole(),
                scratch_shapes=[
                    VMEM((2, levels, rows, LANES), f32),
                    VMEM((2, levels, parent_rows, LANES), f32),
                    pltpu.SemaphoreType.DMA((4,)),
                ],
                compiler_params=params(MOST),
                cost_estimate=cost(200000, 800000),
                name="pack_pair",
            )(nest_old, nest_source, parent_old, parent_source)
        ]
    else:
        packed = pl.pallas_call(
            functools.partial(pack_columns, parts, band),
            out_shape=[
                shape((rows if k in (1, parts - 1) else parent_rows, LANES), f32)
                for k in range(1, parts)
            ],
            in_specs=[in_hbm] * 5,
            out_specs=[whole()] * (parts - 1),
            scratch_shapes=[
                VMEM((sides, levels, rows, LANES), f32),
                VMEM((sides, levels, rows, LANES), f32),
                VMEM(parent_old.shape, f32),
                VMEM(parent_old.shape, f32),
                pltpu.SMEM(offset_y.shape, jnp.int32),
                pltpu.SemaphoreType.DMA((sides, 2)),
                pltpu.SemaphoreType.DMA((3,)),
            ],
            compiler_params=params(MOST),
            cost_estimate=cost(200000, 1000000),
            name="pack_columns",
        )(offset_y, nest_old, nest_source, parent_old, parent_source)
    columns = [shifted(packed[k - 1], "gy", k) for k in range(1, parts)]
    own_strip, first, spread, oy_rows = pl.pallas_call(
        functools.partial(inner_first, band),
        out_shape=[
            shape((parent_rows, LANES), f32),
            shape(nest_old.shape, f32),
            shape((2, 4, levels, LANES), f32),
            shape((8, LANES), jnp.int32),
        ],
        in_specs=[scalars()] * 3 + [whole()] * 4,
        out_specs=[whole()] * 4,
        compiler_params=params(),
        cost_estimate=cost(4000000, 3000000),
        name="inner_first",
    )(
        offset_y,
        parent_coefs,
        nest_coefs,
        nest_old,
        nest_source,
        parent_old,
        parent_source,
    )

    def block(ref, last):
        count = ref.shape[1] // 8 - 1 if last else 0
        return pl.BlockSpec((levels, 8, ref.shape[2]), lambda i, c=count: (0, c, 0))

    def full(extent):
        return pl.BlockSpec(extent, lambda i: (0,) * len(extent))

    outs = [
        shape((height, width), f32),
        shape((height, width), f32),
        shape((8, LANES), f32),
        shape((parent_rows, LANES), f32),
    ]
    across, within, far, strips = pl.pallas_call(
        functools.partial(pack_rows, parts),
        out_shape=outs,
        grid=(1,),
        in_specs=[
            block(nest_old, False),
            block(nest_old, True),
            block(nest_old, False),
            block(nest_old, True),
            block(parent_old, False),
            block(parent_old, True),
            full(own_strip.shape),
            full(oy_rows.shape),
        ]
        + [full(message.shape) for message in columns],
        out_specs=[full(out.shape) for out in outs],
        scratch_shapes=[VMEM((2, height, width), f32)],
        compiler_params=params(),
        cost_estimate=cost(100000, 700000),
        name="pack_rows",
    )(nest_old, nest_old, nest_source, nest_source, parent_old, parent_old, own_strip, oy_rows, *columns)
    across = swapped(across, 1)
    within = swapped(within, 0)
    third, packs, sums = pl.pallas_call(
        inner_rest,
        out_shape=[
            shape(nest_old.shape, f32),
            shape((4, rows, LANES), f32),
            shape((cols // LANES, levels * parent_rows, LANES), f32),
        ],
        in_specs=[scalars()] + [whole()] * 3 + [anywhere],
        out_specs=[whole()] * 3,
        scratch_shapes=[
            VMEM(nest_old.shape, f32),
            VMEM((cols // LANES, levels * rows, LANES), f32),
        ],
        compiler_params=params(),
        cost_estimate=cost(8000000, 6000000),
        name="inner_rest",
    )(nest_coefs, nest_old, first, nest_source, strips)
    sides, windows, coarse, far = pl.pallas_call(
        functools.partial(edges, parts, parent_cols),
        out_shape=[
            shape((2, rows, LANES), f32),
            shape((levels, 2, 8, width), f32),
            shape((levels, parent_rows, foot), f32),
            shape((8, LANES), f32),
        ],
        in_specs=[scalars()] + [whole()] * 11,
        out_specs=[whole()] * 4,
        scratch_shapes=[
            VMEM((2, height, width), f32),
            VMEM((levels, 2, 8, width), f32),
            VMEM((levels, 2, 8, width), f32),
            VMEM((levels, 2, 8, width), f32),
        ],
        compiler_params=params(),
        cost_estimate=cost(4000000, 3000000),
        name="edges",
    )(
        offset_x,
        spread,
        nest_old,
        nest_source,
        sums,
        packs,
        strips,
        across,
        within,
        far,
        columns[0],
        columns[-1],
    )
    previous = [shifted_both(coarse, k) for k in range(1, parts)] + [shifted(coarse, along, 1)]
    own = [coarse] + [shifted(coarse, "gy", k) for k in range(1, parts)]
    beyond = shifted(far, along, -2)
    step, nest_stored, late = pl.pallas_call(
        functools.partial(parent_step, parts, band),
        out_shape=[
            shape(parent_old.shape, f32),
            shape(nest_old.shape, f32),
            shape((levels, parent_cols), f32),
        ],
        in_specs=[scalars()] * 2 + [whole()] * 10,
        out_specs=[whole(), in_hbm, whole()],
        scratch_shapes=[
            VMEM((2, levels, parent_cols + LANES), f32),
            VMEM(nest_old.shape, f32),
            pltpu.SemaphoreType.DMA,
        ],
        compiler_params=params(),
        cost_estimate=cost(800000, 2500000),
        name="parent_step",
    )(
        offset_x,
        offset_y,
        spread,
        third,
        sides,
        windows,
        parent_old,
        parent_source,
        within,
        across,
        columns[0],
        columns[-1],
    )
    parent_new, nest_new = pl.pallas_call(
        functools.partial(merge, parts, band),
        out_shape=[shape(parent_old.shape, f32), shape(nest_old.shape, f32)],
        in_specs=[scalars()] * 2 + [whole()] * 2 + [in_hbm] + [whole()] * (2 + 2 * parts),
        out_specs=[whole(), in_hbm],
        scratch_shapes=[
            VMEM((parts, levels, 2 * parent_rows, foot), f32),
            VMEM((levels, 8, LANES), f32),
            pltpu.SemaphoreType.DMA,
        ],
        input_output_aliases={4: 1},
        compiler_params=params(),
        cost_estimate=cost(200000, 800000),
        name="merge",
    )(offset_x, offset_y, late, step, nest_stored, spread, beyond, *own, *previous)
    return (parent_new, nest_new)


def swapped(value, first):
    along = ("gx", "gz")
    count = lax.axis_size(along)
    pairs = []
    for at in range(first, count, 2):
        pairs += [(at, (at + 1) % count), ((at + 1) % count, at)]
    return lax.ppermute(value, along, pairs)


def shifted_both(value, steps):
    sizes = [lax.axis_size(axis) for axis in ("gx", "gy", "gz")]
    gx, gy, gz = sizes
    pairs = []
    for x in range(gx):
        for y in range(gy):
            for z in range(gz):
                place = (x * gz + z + 1) % (gx * gz)
                target = (place // gz * gy + (y + steps) % gy) * gz + place % gz
                pairs.append(((x * gy + y) * gz + z, target))
    return lax.ppermute(value, ("gx", "gy", "gz"), pairs)


def solution(mesh):
    return jax.shard_map(
        shards,
        mesh=mesh,
        in_specs=(
            P(None, ("grp", "gx", "gz"), "gy"),
            P(None, ("grp", "gx", "gz"), "gy"),
            P(),
            P(None, ("grp", "gx", "gz"), "gy"),
            P(None, ("grp", "gx", "gz"), "gy"),
            P(),
            P("grp"),
            P("grp"),
        ),
        out_specs=(P(None, ("grp", "gx", "gz"), "gy"), P(None, ("grp", "gx", "gz"), "gy")),
        check_vma=False,
    )
```

```python
import functools

import jax
import jax.numpy as jnp
from jax import lax
from jax.experimental import pallas as pl
from jax.experimental.pallas import tpu as pltpu
from jax.sharding import PartitionSpec as P

RATIO = 3
SUBSTEPS = 3
RIM = 6
LANES = 128
STRIDE = 16
SOURCE_AT = 3
PARENT_AT = 6
STRIP_AT = 8
STRIP_SOURCE_AT = 12
SOURCE_ROW = 24
TAIL_ROW = 40
FIXED = 8
LEFT_AT = 3
RIGHT_OWN = STRIDE - 3
VMEM = pltpu.VMEM
LIMIT = 24 * 1024 * 1024
MOST = 54 * 1024 * 1024


def iota(shape, dim):
    return lax.broadcasted_iota(jnp.int32, shape, dim)


def whole():
    return pl.BlockSpec(memory_space=VMEM)


def scalars():
    return pl.BlockSpec(memory_space=pltpu.SMEM)


def params(limit=LIMIT):
    return pltpu.CompilerParams(vmem_limit_bytes=limit)


def cost(flops, moved):
    return pl.CostEstimate(flops=flops, bytes_accessed=moved, transcendentals=0)


def tile(ref, level, index):
    return ref[level, :, index * LANES : (index + 1) * LANES]


def turned(value, lanes):
    lanes = lanes % LANES
    return pltpu.roll(value, lanes, 1) if lanes else value


def edge_strip(dest, band, oy, parent, parent_source):
    levels, rows, cols = parent.shape
    lane = iota((rows, LANES), 1)
    base = jnp.where(dest == 0, oy - 1, oy + band - 3) - lax.axis_index("gy") * cols
    total = jnp.zeros(lane.shape, jnp.float32)
    for ref, first in ((parent, STRIP_AT), (parent_source, STRIP_SOURCE_AT)):
        for level in range(levels):
            found = jnp.zeros(lane.shape, jnp.float32)
            for at in range(cols // LANES):
                place = lane + (at * LANES - base)
                found = jnp.where((place >= 0) & (place < 4), tile(ref, level, at), found)
            turn = (16384 + first + STRIDE * level - base) & (LANES - 1)
            total = total + pltpu.roll(found, turn, 1)
    return total


def pack_pair(nest, source, parent, parent_source, out, fine_buf, coarse_buf, sems):
    levels, rows, cols = nest.shape
    parent_rows, parent_cols = parent.shape[1:]
    right = lax.axis_index("gy") == 0
    loads = []
    for at, (ref, buf) in enumerate(
        (
            (parent, coarse_buf.at[0]),
            (parent_source, coarse_buf.at[1]),
            (nest, fine_buf.at[0]),
            (source, fine_buf.at[1]),
        )
    ):
        start = pl.multiple_of(jnp.where(right, ref.shape[2] - LANES, 0), LANES)
        loads.append(pltpu.make_async_copy(ref.at[:, :, pl.ds(start, LANES)], buf, sems.at[at]))
    for copy in loads:
        copy.start()

    def columns(value, count, to):
        first = jnp.where(right, LANES - count, 0)
        place = iota(value.shape, 1) - first
        value = jnp.where((place >= 0) & (place < count), value, 0.0)
        return pltpu.roll(value, (LANES + to - first) & (LANES - 1), 1)

    part = jnp.zeros((parent_rows, LANES), jnp.float32)
    loads[0].wait()
    loads[1].wait()
    for level in range(levels):
        base = STRIDE * level
        part = part + columns(coarse_buf[0, level], 1, base + PARENT_AT)
        part = part + columns(coarse_buf[0, level], 2, base + STRIP_AT)
        part = part + columns(coarse_buf[1, level], 2, base + STRIP_SOURCE_AT)
    total = jnp.zeros((rows, LANES), jnp.float32)
    loads[2].wait()
    loads[3].wait()
    for level in range(levels):
        base = STRIDE * level
        total = total + columns(fine_buf[0, level], 3, base)
        total = total + columns(fine_buf[1, level], 3, base + SOURCE_AT)
    out[...] = total
    out[:parent_rows, :] += part


def across_border(message, oy, parent_cols, me):
    c = iota(message.shape, 1) & (STRIDE - 1)
    place = jnp.where(me == 0, parent_cols + 1, 1) - oy
    total = jnp.zeros(message.shape, jnp.float32)
    for turn in (-1, 0, 2, 3):
        at = jnp.where(c >= STRIP_SOURCE_AT, c - STRIP_SOURCE_AT, c - STRIP_AT) - turn
        fits = (c >= STRIP_AT) & (at >= 0) & (at < 2) & (place == turn)
        total = total + jnp.where(fits, turned(message, turn), 0.0)
    return total


def pack_columns(parts, band, oy_hbm, nest, source, parent_hbm, parent_source_hbm, *rest):
    outs = rest[: parts - 1]
    old_buf, src_buf, parent, parent_source, oy_ref, sems, field_sems = rest[parts - 1 :]
    levels, rows, cols = nest.shape
    parent_cols = parent.shape[2]
    me = lax.axis_index("gy")
    sides = [1] if parts == 2 else [1, parts - 1]
    fields = [
        pltpu.make_async_copy(ref, buf, field_sems.at[at])
        for at, (ref, buf) in enumerate(
            ((oy_hbm, oy_ref), (parent_hbm, parent), (parent_source_hbm, parent_source))
        )
    ]
    for copy in fields:
        copy.start()
    copies = []
    for at, step in enumerate(sides):
        right = (me == 0) if parts == 2 else jnp.bool_(step == 1)
        start = pl.multiple_of(jnp.where(right, cols - LANES, 0), LANES)
        pair = [
            pltpu.make_async_copy(
                ref.at[:, :, pl.ds(start, LANES)], buf.at[at], sems.at[at, which]
            )
            for which, (ref, buf) in enumerate(((nest, old_buf), (source, src_buf)))
        ]
        for copy in pair:
            copy.start()
        copies.append((right, pair))
    for copy in fields:
        copy.wait()
    oy = oy_ref[0]
    lane = iota((parent.shape[1], LANES), 1)
    for step in range(1, parts):
        out = outs[step - 1]
        part = edge_strip(lax.rem(me + step, parts), band, oy, parent, parent_source)
        if step not in sides:
            out[...] = part
            continue
        at = sides.index(step)
        right, pair = copies[at]
        first = jnp.where(right, LANES - 3, 0)
        outer = jnp.where(right, LANES - 1, 0)
        for level in range(levels):
            edge = jnp.where(
                right, tile(parent, level, parent_cols // LANES - 1), tile(parent, level, 0)
            )
            edge = jnp.where(lane == outer, edge, 0.0)
            turn = (LANES + PARENT_AT + STRIDE * level - outer) & (LANES - 1)
            part = part + pltpu.roll(edge, turn, 1)
        for copy in pair:
            copy.wait()
        fine = iota((rows, LANES), 1) - first
        wanted = (fine >= 0) & (fine < 3)
        total = jnp.zeros((rows, LANES), jnp.float32)
        for level in range(levels):
            for buf, shift in ((old_buf, 0), (src_buf, SOURCE_AT)):
                value = jnp.where(wanted, buf[at, level], 0.0)
                turn = (LANES + STRIDE * level + shift - first) & (LANES - 1)
                total = total + pltpu.roll(value, turn, 1)
        out[...] = total
        out[: part.shape[0], :] += part


def three_terms(value):
    terms = []
    for _ in range(3):
        term = value.astype(jnp.bfloat16)
        terms.append(term)
        value = value - term.astype(jnp.float32)
    return terms


def select_rows(selector, value):
    selector = selector.astype(jnp.bfloat16)
    high, middle, low = (
        jnp.dot(selector, term, preferred_element_type=jnp.float32)
        for term in three_terms(value)
    )
    return high + (middle + low)


def select_columns(value, selector):
    selector = selector.astype(jnp.bfloat16)
    high, middle, low = (
        jnp.dot(term, selector, preferred_element_type=jnp.float32)
        for term in three_terms(value)
    )
    return high + (middle + low)


def sum_rows(ref):
    count = ref.shape[0] // RATIO
    first, second, third = (ref[pl.ds(at, count, RATIO), :] for at in range(RATIO))
    return first + second + third


def inner_substep(coefs, here, source, there):
    levels, rows, cols = here.shape
    sub = iota((8, cols), 0)
    tiles = rows // 8

    def one_level(level):
        ch = coefs[0, level]
        cv = coefs[1, level]
        centre = 1.0 - 4.0 * ch - 2.0 * cv
        below = jnp.maximum(level - 1, 0)
        above = jnp.minimum(level + 1, levels - 1)
        cv_below = jnp.where(level > 0, cv, 0.0)
        cv_above = jnp.where(level < levels - 1, cv, 0.0)

        def row_tile(t):
            t = t % tiles
            return here[level, 8 * t : 8 * t + 8, :]

        down_before = pltpu.roll(row_tile(-1), 1, 0)
        now = row_tile(0)
        up_now = pltpu.roll(now, 7, 0)
        for t in range(tiles):
            following = row_tile(t + 1)
            down_now = pltpu.roll(now, 1, 0)
            up_next = pltpu.roll(following, 7, 0)
            around = jnp.where(sub == 0, down_before, down_now) + jnp.where(
                sub == 7, up_next, up_now
            )
            around = around + (pltpu.roll(now, 1, 1) + pltpu.roll(now, cols - 1, 1))
            span = slice(8 * t, 8 * t + 8)
            stacked = cv_below * here[below, span, :] + cv_above * here[above, span, :]
            there[level, span, :] = centre * now + ch * around + (stacked + source[level, span, :])
            down_before, now, up_now = down_now, following, up_next

    def two_levels(pair, carry):
        one_level(2 * pair)
        one_level(2 * pair + 1)
        return carry

    lax.fori_loop(0, levels // 2, two_levels, 0)


def spread_coefs(parent_coefs, coefs, out):
    levels = out.shape[2]
    lane = iota((levels, LANES), 1)
    row = iota((levels, LANES), 0)
    for at, ref in enumerate((parent_coefs, coefs)):
        for which in range(2):
            packed = jnp.full(lane.shape, ref[which, 0], jnp.float32)
            rows = packed
            for level in range(1, levels):
                packed = jnp.where(lane >= STRIDE * level, ref[which, level], packed)
                rows = jnp.where(row == level, ref[which, level], rows)
            out[0, 2 * at + which] = packed
            out[1, 2 * at + which] = rows


def inner_first(
    band,
    oy_ref,
    parent_coefs,
    coefs,
    nest,
    source,
    parent,
    parent_source,
    strip,
    first,
    spread,
    oy_rows,
):
    oy = oy_ref[0]
    oy_rows[...] = jnp.full(oy_rows.shape, oy, jnp.int32)
    spread_coefs(parent_coefs, coefs, spread)
    strip[...] = edge_strip(lax.axis_index("gy"), band, oy, parent, parent_source)
    inner_substep(coefs, nest, source, first)


def inner_rest(coefs, nest, first, source, after_pack, third, packs, sums, second, split):
    levels, rows, cols = nest.shape
    lane = iota((rows, LANES), 1)
    for at, ref in enumerate((nest, source)):
        left = jnp.zeros(lane.shape, jnp.float32)
        right = jnp.zeros(lane.shape, jnp.float32)
        for level in range(levels):
            value = jnp.where(lane < RIGHT_OWN, tile(ref, level, 0), 0.0)
            left = left + turned(value, STRIDE * level + LEFT_AT)
            value = jnp.where(lane >= LANES - RIGHT_OWN, tile(ref, level, cols // LANES - 1), 0.0)
            right = right + turned(value, STRIDE * level + RIGHT_OWN)
        packs[2 * at] = left
        packs[2 * at + 1] = right
    inner_substep(coefs, first, source, second)
    inner_substep(coefs, second, source, third)
    for level in range(levels):
        for piece in range(cols // LANES):
            split[piece, level * rows : (level + 1) * rows, :] = tile(third, level, piece)
    for piece in range(cols // LANES):
        sums[piece] = sum_rows(split.at[piece])


def with_columns(tiles, left, right, me, parts, place):
    lane = iota(left.shape, 1)
    from_right = turned(right, -place)
    from_left = turned(left, -3 - place)
    if parts == 2:
        tiles[0] = jnp.where((lane < 3) & (me == 0), from_right, tiles[0])
        tiles[-1] = jnp.where((lane >= LANES - 3) & (me == 1), from_left, tiles[-1])
        return tiles
    extra = jnp.where(lane < 3, from_right, jnp.where(lane >= LANES - 3, from_left, 0.0))
    return tiles + [extra]


def pack_rows(
    parts, old_top, old_end, src_top, src_end, par_top, par_end, own_strip, oy_rows, *rest
):
    columns = rest[: parts - 1]
    across, within, far, strip_out, both = rest[parts - 1 :]
    core = lax.axis_index("gz")
    up, down = both.at[core], both.at[1 - core]
    levels, _, cols = old_top.shape
    me = lax.axis_index("gy")
    left, right = columns[0], columns[-1]
    rows = left.shape[0]
    strip_rows = own_strip.shape[0]
    lane = iota((strip_rows, LANES), 1)
    strips = own_strip[...]
    if parts == 2:
        oy = jnp.concatenate([oy_rows[...]] * (strip_rows // 8), axis=0)
        strips = strips + across_border(left[:strip_rows, :], oy, par_top.shape[2], me)
    else:
        for message in columns:
            strips = strips + message[:strip_rows, :]
    c = lane & (STRIDE - 1)
    strips = jnp.where(c >= STRIP_AT, strips, 0.0)
    strips = jnp.where(c == PARENT_AT, left[:strip_rows, :], strips)
    strips = jnp.where(c == PARENT_AT + 1, turned(right[:strip_rows, :], 1), strips)
    strip_out[...] = strips
    far[...] = strips[:8]
    pieces = cols // LANES
    for out, old, src, first, at, src_at in (
        (up, old_end, src_end, rows - 8, 5, 6),
        (down, old_top, src_top, 0, 0, 0),
    ):
        y_left = left[first : first + 8, :]
        y_right = right[first : first + 8, :]
        for level in range(levels):
            for ref, shift, row, count, base in (
                (old, 0, at, 3, 0),
                (src, SOURCE_AT, src_at, 2, SOURCE_ROW),
            ):
                tiles = [tile(ref, level, piece) for piece in range(pieces)]
                tiles = with_columns(
                    tiles, y_left, y_right, me, parts, STRIDE * level + shift
                )
                for piece, value in enumerate(tiles):
                    out[
                        base + count * level : base + count * (level + 1),
                        piece * LANES : (piece + 1) * LANES,
                    ] = value[row : row + count]
    parent_cols = par_top.shape[2]
    for level in range(levels):
        up[TAIL_ROW + level : TAIL_ROW + level + 1, :parent_cols] = par_end[level, 7:8, :]
        down[TAIL_ROW + level : TAIL_ROW + level + 1, :parent_cols] = par_top[level, 0:1, :]
    up[TAIL_ROW : TAIL_ROW + 8, parent_cols : parent_cols + LANES] = strips[strip_rows - 8 :]
    down[TAIL_ROW : TAIL_ROW + 8, parent_cols : parent_cols + LANES] = strips[:8]
    down[TAIL_ROW + 8 : TAIL_ROW + 16, :LANES] = strips[8:16]
    down[TAIL_ROW + 8 : TAIL_ROW + 16, LANES : 2 * LANES] = strips[16:24]
    within[...] = both[0]
    across[...] = both[1]


def edges(
    parts,
    parent_cols,
    ox_ref,
    spread,
    nest,
    source,
    sums,
    packs,
    strips,
    across,
    within,
    far,
    y_left,
    y_right,
    sides,
    windows,
    coarse_out,
    far_out,
    both,
    ping,
    pong,
    src,
):
    levels, rows, cols = nest.shape
    width = ping.shape[3]
    pieces = cols // LANES
    me = lax.axis_index("gy")
    core = lax.axis_index("gz")
    both[0] = within[...]
    both[1] = across[...]
    before, after = both.at[1 - core], both.at[core]
    is_south = me == 0
    is_north = me == parts - 1

    far_out[...] = far[...]
    sub = iota((8, LANES), 0)
    old = jnp.concatenate(
        [
            strips[...],
            after[TAIL_ROW : TAIL_ROW + 8, parent_cols : parent_cols + LANES],
            after[TAIL_ROW + 8 : TAIL_ROW + 16, :LANES],
            after[TAIL_ROW + 8 : TAIL_ROW + 16, LANES : 2 * LANES],
            jnp.where(
                sub == 7,
                before[TAIL_ROW : TAIL_ROW + 8, parent_cols : parent_cols + LANES],
                0.0,
            ),
        ],
        axis=0,
    )
    count = old.shape[0]

    def packed_coef(which, height):
        return jnp.concatenate([spread[0, which]] * (height // 8), axis=0)

    def stacked(value):
        lane = iota(value.shape, 1)
        below = jnp.where(lane >= STRIDE, turned(value, STRIDE), 0.0)
        return below + jnp.where(lane < STRIDE * (levels - 1), turned(value, -STRIDE), 0.0)

    def around(value):
        return (
            pltpu.roll(value, 1, 0)
            + pltpu.roll(value, value.shape[0] - 1, 0)
            + turned(value, 1)
            + turned(value, -1)
        )

    diff = (
        packed_coef(0, count) * (around(old) - 4.0 * old)
        + packed_coef(1, count) * (stacked(old) - 2.0 * old)
        + turned(old, STRIP_AT - STRIP_SOURCE_AT)
    )
    index = iota((rows + 16, count), 0)
    nest_row = jnp.where(index < rows, index, jnp.where(index < rows + 8, index - rows - 3, index - 13))
    parent_row = ((nest_row + 3) * 171 >> 9) - 1 + ox_ref[0]
    pick = (iota((rows + 16, count), 1) == parent_row).astype(jnp.float32)
    picked = select_rows(pick, jnp.concatenate([old, diff], axis=1))
    picked_old, picked_diff = picked[:, :LANES], picked[:, LANES:]

    lane = iota((rows, LANES), 1)
    c = lane & (STRIDE - 1)
    rim_first = jnp.where(is_south, LEFT_AT, RIGHT_OWN - RIM)
    in_rim = (c >= rim_first) & (c < rim_first + RIM)
    at = lane - c + STRIP_AT + jnp.where(c >= rim_first + 3, 2, 1)
    rim_old = jnp.take_along_axis(picked_old[:rows], at, axis=1)
    rim_diff = jnp.take_along_axis(picked_diff[:rows], at, axis=1)
    ch = packed_coef(2, rows)
    cv = packed_coef(3, rows)
    centre = 1.0 - 4.0 * ch - 2.0 * cv
    left = jnp.where(c < 3, y_left[...], packs[0])
    left_src = jnp.where(c < 3, turned(y_left[...], -SOURCE_AT), packs[2])
    right = jnp.where(c >= RIGHT_OWN, turned(y_right[...], RIGHT_OWN), packs[1])
    right_src = jnp.where(c >= RIGHT_OWN, turned(y_right[...], RIGHT_OWN - SOURCE_AT), packs[3])
    for side, (value, forcing, rim) in enumerate(
        (
            (left, left_src, in_rim & is_south),
            (right, right_src, in_rim & is_north),
        )
    ):
        for substep in range(1, SUBSTEPS + 1):
            value = centre * value + ch * around(value) + (cv * stacked(value) + forcing)
            value = jnp.where(rim, rim_old + (substep / SUBSTEPS) * rim_diff, value)
        sides[side] = value

    sub = iota((8, width), 0)
    lane = iota((8, LANES), 1)
    for level in range(levels):
        for buf, field, shift, n, base in (
            (ping, nest, 0, 3, 0),
            (src, source, SOURCE_AT, 2, SOURCE_ROW),
        ):
            for window, first, turn, at, message in (
                (0, 0, 3, 3 - n, before),
                (1, rows - 8, 5, 5, after),
            ):
                tiles = [
                    field[level, first : first + 8, piece * LANES : (piece + 1) * LANES]
                    for piece in range(pieces)
                ]
                tiles = with_columns(
                    tiles,
                    y_left[first : first + 8, :],
                    y_right[first : first + 8, :],
                    me,
                    parts,
                    STRIDE * level + shift,
                )
                for piece, value in enumerate(tiles):
                    value = pltpu.roll(value, turn, 0)
                    span = slice(piece * LANES, (piece + 1) * LANES)
                    buf[level, window, :, span] = value
                    if n == 3:
                        pong[level, window, :, span] = value
                buf[level, window, at : at + n, :] = message[
                    base + n * level : base + n * (level + 1), :
                ]
    rim_first = jnp.where(is_south, 0, LANES - RIM)
    column = STRIP_AT + jnp.where((lane >= rim_first + 3) & (lane < rim_first + RIM), 2, 1)
    rims = {}
    for level in range(levels):
        for window in range(2):
            span = slice(rows + 8 * window, rows + 8 * window + 8)
            at = column + STRIDE * level
            rims[level, window] = (
                jnp.take_along_axis(picked_old[span], at, axis=1),
                jnp.take_along_axis(picked_diff[span], at, axis=1),
            )
    for substep in range(1, SUBSTEPS + 1):
        here, there = (ping, pong) if substep % 2 else (pong, ping)
        there = windows if substep == SUBSTEPS else there
        low = 0 if substep == SUBSTEPS or parts > 2 else 3
        south = (lane >= low) & (lane < RIM) & is_south
        north = (lane >= LANES - RIM) & (lane < LANES - low) & is_north
        weight = substep / SUBSTEPS
        for level in range(levels):
            c_h, c_v = (
                jnp.concatenate([spread[1, which, level : level + 1, :]] * (width // LANES), axis=1)
                for which in (2, 3)
            )
            c_0 = 1.0 - 4.0 * c_h - 2.0 * c_v
            for window in range(2):
                now = here[level, window]
                up = pltpu.roll(now, 1, 0)
                down = pltpu.roll(now, 7, 0)
                if substep == 1:
                    beyond_row = pong[level, window]
                    if window == 0:
                        down = jnp.where(sub == 7, pltpu.roll(beyond_row, 7, 0), down)
                    else:
                        up = jnp.where(sub == 0, pltpu.roll(beyond_row, 1, 0), up)
                beside = pltpu.roll(now, 1, 1) + pltpu.roll(now, width - 1, 1)
                value = c_0 * now + c_h * ((up + down) + beside) + src[level, window]
                if level > 0:
                    value = value + c_v * here[level - 1, window]
                if level < levels - 1:
                    value = value + c_v * here[level + 1, window]
                rim_o, rim_d = rims[level, window]
                rim = rim_o + weight * rim_d
                for piece in range(width // LANES):
                    span = slice(piece * LANES, (piece + 1) * LANES)
                    part = value[:, span]
                    if piece == 0:
                        part = jnp.where(south, rim, part)
                    if piece == pieces - 1:
                        part = jnp.where(north, rim, part)
                    there[level, window, :, span] = part

    parent_rows = rows // RATIO
    lane = iota((parent_rows, LANES), 1)
    row = iota((parent_rows, LANES), 0)
    side_sums = [sum_rows(sides.at[side]) for side in range(2)]
    replaced = [[] for _ in range(pieces)]
    for level in range(levels):
        span = slice(level * parent_rows, (level + 1) * parent_rows)
        top = windows[level, 0, 3:4, :] + windows[level, 0, 4:5, :] + windows[level, 0, 5:6, :]
        end = windows[level, 1, 2:3, :] + windows[level, 1, 3:4, :] + windows[level, 1, 4:5, :]
        for piece in range(pieces):
            value = sums[piece, span, :]
            if piece == 0:
                fixed = turned(side_sums[0], -STRIDE * level - LEFT_AT)
                value = jnp.where(lane < FIXED, fixed, value)
            if piece == pieces - 1:
                fixed = turned(side_sums[1], -STRIDE * level - RIGHT_OWN)
                value = jnp.where(lane >= LANES - FIXED, fixed, value)
            across_piece = slice(piece * LANES, (piece + 1) * LANES)
            value = jnp.where(row == 0, top[:, across_piece], value)
            value = jnp.where(row == parent_rows - 1, end[:, across_piece], value)
            replaced[piece].append(value)
    foot = cols // RATIO
    offset = iota((cols, foot), 0) - RATIO * iota((cols, foot), 1)
    gather = ((offset >= 0) & (offset < RATIO)).astype(jnp.float32)
    means = select_columns(
        jnp.concatenate([jnp.concatenate(values, axis=0) for values in replaced], axis=1), gather
    ) * (1.0 / 9.0)
    coarse_out[...] = means.reshape(coarse_out.shape)


def put_together(third, sides, windows, result):
    levels, rows, cols = third.shape
    pieces = cols // LANES
    lane = iota((rows, LANES), 1)
    sub = iota((8, cols), 0)
    for level in range(levels):
        fixed = turned(sides[0], -STRIDE * level - LEFT_AT)
        result[level, :, :LANES] = jnp.where(lane < FIXED, fixed, tile(third, level, 0))
        for piece in range(1, pieces - 1):
            result[level, :, piece * LANES : (piece + 1) * LANES] = tile(third, level, piece)
        fixed = turned(sides[1], -STRIDE * level - RIGHT_OWN)
        result[level, :, cols - LANES :] = jnp.where(
            lane >= LANES - FIXED, fixed, tile(third, level, pieces - 1)
        )
        top = pltpu.roll(windows[level, 0, :, :cols], 5, 0)
        result[level, :8, :] = jnp.where(sub < 3, top, result[level, :8, :])
        end = pltpu.roll(windows[level, 1, :, :cols], 3, 0)
        result[level, rows - 8 :, :] = jnp.where(sub >= 5, end, result[level, rows - 8 :, :])


def parent_step(
    parts,
    band,
    ox_ref,
    oy_ref,
    spread,
    third,
    sides,
    windows,
    parent,
    source,
    within,
    across,
    y_left,
    y_right,
    out,
    nest_out,
    late,
    tail,
    result,
    sem,
):
    put_together(third, sides, windows, result)
    store = pltpu.make_async_copy(result, nest_out, sem)
    store.start()
    core = lax.axis_index("gz")
    levels, rows, cols = parent.shape
    tail[0] = within[TAIL_ROW : TAIL_ROW + levels, : cols + LANES]
    tail[1] = across[TAIL_ROW : TAIL_ROW + levels, : cols + LANES]
    me = lax.axis_index("gy")
    is_last = ox_ref[0] == rows - 1
    wide = iota((1, cols), 1)
    south = (wide == oy_ref[0] + 2 - me * cols) & is_last
    north = (wide == oy_ref[0] + band - 3 - me * cols) & is_last
    row = iota((rows, cols), 0)
    lane = iota((rows, cols), 1)
    has_left = me > 0
    has_right = me < parts - 1
    left = y_left[:rows, :]
    right = y_right[:rows, :]
    zero = jnp.zeros((rows, cols), jnp.float32)
    for level in range(levels):
        now = parent[level]
        at = STRIDE * level + PARENT_AT
        from_left = left[:, at : at + 1]
        from_right = right[:, at : at + 1]
        top = tail[1 - core, level : level + 1, :cols]
        end = tail[core, level : level + 1, :cols]
        around = (
            jnp.where(row == 0, top, pltpu.roll(now, 1, 0))
            + jnp.where(row == rows - 1, end, pltpu.roll(now, rows - 1, 0))
            + jnp.where(
                lane == 0, jnp.where(has_left, from_left, 0.0), pltpu.roll(now, 1, 1)
            )
            + jnp.where(
                lane == cols - 1,
                jnp.where(has_right, from_right, 0.0),
                pltpu.roll(now, cols - 1, 1),
            )
        )
        stacked = (parent[level - 1] if level > 0 else zero) + (
            parent[level + 1] if level < levels - 1 else zero
        )
        ch, cv = (
            jnp.concatenate([spread[1, which, level : level + 1, :]] * (cols // LANES), axis=1)
            for which in (0, 1)
        )
        out[level] = (
            (1.0 - 4.0 * ch - 2.0 * cv) * now + ch * around + (cv * stacked + source[level])
        )
        at = cols + STRIDE * level + PARENT_AT
        before_end = jnp.where(
            wide == 0, tail[core, 0:1, at : at + 1], pltpu.roll(end, 1, 1)
        )
        after_end = jnp.where(
            wide == cols - 1, tail[core, 0:1, at + 1 : at + 2], pltpu.roll(end, cols - 1, 1)
        )
        nest_ch = spread[1, 2, level : level + 1, :]
        nest_ch = jnp.concatenate([nest_ch] * (cols // LANES), axis=1)
        share = nest_ch * nest_ch * ch * (1.0 / SUBSTEPS)
        late[level : level + 1, :] = (share * (1.0 / (RATIO * RATIO))) * (
            jnp.where(south, before_end, 0.0) + jnp.where(north, after_end, 0.0)
        )
    store.wait()


def merge(parts, band, ox_ref, oy_ref, late, step, nest, spread, beyond, *rest):
    own, arrived = rest[:parts], rest[parts:-5]
    out, nest_out, joined, corner, sem = rest[-5:]
    levels, rows, cols = step.shape
    foot = own[0].shape[2]
    me = lax.axis_index("gy")

    @pl.when((ox_ref[0] == rows - 1) & ((me == 0) | (me == parts - 1)))
    def _():
        nest_rows, nest_cols = nest.shape[1:]
        first = pl.multiple_of(jnp.where(me == 0, 0, nest_cols - LANES), LANES)
        place = (slice(None), pl.ds(nest_rows - 8, 8), pl.ds(first, LANES))
        load = pltpu.make_async_copy(nest_out.at[place], corner, sem)
        load.start()
        load.wait()
        sub = iota((8, LANES), 0)
        lane = iota((8, LANES), 1)
        cell = (sub == 7) & (lane == jnp.where(me == 0, RIM, LANES - RIM - 1))
        for level in range(levels):
            at = STRIDE * level + STRIP_AT
            value = jnp.where(me == 0, beyond[0:1, at + 2 : at + 3], beyond[0:1, at + 1 : at + 2])
            nest_ch = spread[1, 2, level : level + 1, :]
            share = nest_ch * nest_ch * spread[1, 0, level : level + 1, :] * (1.0 / SUBSTEPS)
            corner[level] += jnp.where(cell, share * value, 0.0)
        again = pltpu.make_async_copy(corner, nest_out.at[place], sem)
        again.start()
        again.wait()

    ox = ox_ref[0]
    oy = oy_ref[0]
    for k in range(parts):
        if parts == 2 and k == 1:
            to_north, to_south = arrived[0], arrived[2]
            joined[k, :, :rows, :] = jnp.where(me == 0, to_south[...], to_north[...])
        else:
            joined[k, :, :rows, :] = arrived[1 if parts == 2 else k][...]
        joined[k, :, rows:, :] = own[k][...]
    lane = iota((rows, LANES), 1)
    row = iota((rows, LANES), 0)
    for level in range(levels):
        values = [tile(step, level, piece) for piece in range(cols // LANES)]
        for k in range(parts):
            source = lax.rem(me + parts - k, parts)
            block = joined[k, level, pl.ds(rows - ox, rows), :]
            begin = oy + source * foot - me * cols
            block = pltpu.roll(block, (16384 + begin) & (LANES - 1), 1)
            low = jnp.maximum(source * foot, 2)
            high = jnp.minimum((source + 1) * foot, band - 2)
            for piece in range(cols // LANES):
                at = lane + (piece * LANES + me * cols - oy)
                values[piece] = jnp.where((at >= low) & (at < high), block, values[piece])
        for piece, value in enumerate(values):
            term = late[level : level + 1, piece * LANES : (piece + 1) * LANES]
            value = value + jnp.where(row == rows - 2, term, 0.0)
            out[level, :, piece * LANES : (piece + 1) * LANES] = value


def shifted(value, axis, steps):
    count = lax.axis_size(axis)
    pairs = [(source, (source + steps) % count) for source in range(count)]
    return lax.ppermute(value, axis, pairs)


def shards(
    parent_old, parent_source, parent_coefs, nest_old, nest_source, nest_coefs, offset_x, offset_y
):
    parts = lax.axis_size("gy")
    along = ("gx", "gz")
    levels, parent_rows, parent_cols = parent_old.shape
    _, rows, cols = nest_old.shape
    foot = cols // RATIO
    band = foot * parts
    width = cols if parts == 2 else cols + LANES
    height = TAIL_ROW + 16
    f32 = jnp.float32
    shape = jax.ShapeDtypeStruct
    anywhere = pl.BlockSpec(memory_space=pl.ANY)
    in_hbm = pl.BlockSpec(memory_space=pltpu.HBM)
    sides = 1 if parts == 2 else 2
    if parts == 2:
        packed = [
            pl.pallas_call(
                pack_pair,
                out_shape=VMEM((rows, LANES), f32),
                in_specs=[in_hbm] * 4,
                out_specs=whole(),
                scratch_shapes=[
                    VMEM((2, levels, rows, LANES), f32),
                    VMEM((2, levels, parent_rows, LANES), f32),
                    pltpu.SemaphoreType.DMA((4,)),
                ],
                compiler_params=params(MOST),
                cost_estimate=cost(200000, 800000),
                name="pack_pair",
            )(nest_old, nest_source, parent_old, parent_source)
        ]
    else:
        packed = pl.pallas_call(
            functools.partial(pack_columns, parts, band),
            out_shape=[
                shape((rows if k in (1, parts - 1) else parent_rows, LANES), f32)
                for k in range(1, parts)
            ],
            in_specs=[in_hbm] * 5,
            out_specs=[whole()] * (parts - 1),
            scratch_shapes=[
                VMEM((sides, levels, rows, LANES), f32),
                VMEM((sides, levels, rows, LANES), f32),
                VMEM(parent_old.shape, f32),
                VMEM(parent_old.shape, f32),
                pltpu.SMEM(offset_y.shape, jnp.int32),
                pltpu.SemaphoreType.DMA((sides, 2)),
                pltpu.SemaphoreType.DMA((3,)),
            ],
            compiler_params=params(MOST),
            cost_estimate=cost(200000, 1000000),
            name="pack_columns",
        )(offset_y, nest_old, nest_source, parent_old, parent_source)
    columns = [shifted(packed[k - 1], "gy", k) for k in range(1, parts)]
    own_strip, first, spread, oy_rows = pl.pallas_call(
        functools.partial(inner_first, band),
        out_shape=[
            shape((parent_rows, LANES), f32),
            shape(nest_old.shape, f32),
            shape((2, 4, levels, LANES), f32),
            shape((8, LANES), jnp.int32),
        ],
        in_specs=[scalars()] * 3 + [whole()] * 4,
        out_specs=[whole()] * 4,
        compiler_params=params(),
        cost_estimate=cost(4000000, 3000000),
        name="inner_first",
    )(
        offset_y,
        parent_coefs,
        nest_coefs,
        nest_old,
        nest_source,
        parent_old,
        parent_source,
    )

    def block(ref, last):
        count = ref.shape[1] // 8 - 1 if last else 0
        return pl.BlockSpec((levels, 8, ref.shape[2]), lambda i, c=count: (0, c, 0))

    def full(extent):
        return pl.BlockSpec(extent, lambda i: (0,) * len(extent))

    outs = [
        shape((height, width), f32),
        shape((height, width), f32),
        shape((8, LANES), f32),
        shape((parent_rows, LANES), f32),
    ]
    across, within, far, strips = pl.pallas_call(
        functools.partial(pack_rows, parts),
        out_shape=outs,
        grid=(1,),
        in_specs=[
            block(nest_old, False),
            block(nest_old, True),
            block(nest_old, False),
            block(nest_old, True),
            block(parent_old, False),
            block(parent_old, True),
            full(own_strip.shape),
            full(oy_rows.shape),
        ]
        + [full(message.shape) for message in columns],
        out_specs=[full(out.shape) for out in outs],
        scratch_shapes=[VMEM((2, height, width), f32)],
        compiler_params=params(),
        cost_estimate=cost(100000, 700000),
        name="pack_rows",
    )(nest_old, nest_old, nest_source, nest_source, parent_old, parent_old, own_strip, oy_rows, *columns)
    across = swapped(across, 1)
    within = swapped(within, 0)
    third, packs, sums = pl.pallas_call(
        inner_rest,
        out_shape=[
            shape(nest_old.shape, f32),
            shape((4, rows, LANES), f32),
            shape((cols // LANES, levels * parent_rows, LANES), f32),
        ],
        in_specs=[scalars()] + [whole()] * 3 + [anywhere],
        out_specs=[whole()] * 3,
        scratch_shapes=[
            VMEM(nest_old.shape, f32),
            VMEM((cols // LANES, levels * rows, LANES), f32),
        ],
        compiler_params=params(),
        cost_estimate=cost(8000000, 6000000),
        name="inner_rest",
    )(nest_coefs, nest_old, first, nest_source, strips)
    sides, windows, coarse, far = pl.pallas_call(
        functools.partial(edges, parts, parent_cols),
        out_shape=[
            shape((2, rows, LANES), f32),
            shape((levels, 2, 8, width), f32),
            shape((levels, parent_rows, foot), f32),
            shape((8, LANES), f32),
        ],
        in_specs=[scalars()] + [whole()] * 11,
        out_specs=[whole()] * 4,
        scratch_shapes=[
            VMEM((2, height, width), f32),
            VMEM((levels, 2, 8, width), f32),
            VMEM((levels, 2, 8, width), f32),
            VMEM((levels, 2, 8, width), f32),
        ],
        compiler_params=params(),
        cost_estimate=cost(4000000, 3000000),
        name="edges",
    )(
        offset_x,
        spread,
        nest_old,
        nest_source,
        sums,
        packs,
        strips,
        across,
        within,
        far,
        columns[0],
        columns[-1],
    )
    if parts == 2:
        arrived = [
            shifted_both(coarse, 1, 1),
            shifted(coarse, along, 1),
            shifted_both(coarse, 1, 0),
        ]
    else:
        arrived = [shifted_both(coarse, k) for k in range(parts)]
    own = [coarse] + [shifted(coarse, "gy", k) for k in range(1, parts)]
    beyond = shifted(far, along, -2)
    step, nest_stored, late = pl.pallas_call(
        functools.partial(parent_step, parts, band),
        out_shape=[
            shape(parent_old.shape, f32),
            shape(nest_old.shape, f32),
            shape((levels, parent_cols), f32),
        ],
        in_specs=[scalars()] * 2 + [whole()] * 10,
        out_specs=[whole(), in_hbm, whole()],
        scratch_shapes=[
            VMEM((2, levels, parent_cols + LANES), f32),
            VMEM(nest_old.shape, f32),
            pltpu.SemaphoreType.DMA,
        ],
        compiler_params=params(),
        cost_estimate=cost(800000, 2500000),
        name="parent_step",
    )(
        offset_x,
        offset_y,
        spread,
        third,
        sides,
        windows,
        parent_old,
        parent_source,
        within,
        across,
        columns[0],
        columns[-1],
    )
    parent_new, nest_new = pl.pallas_call(
        functools.partial(merge, parts, band),
        out_shape=[shape(parent_old.shape, f32), shape(nest_old.shape, f32)],
        in_specs=[scalars()] * 2 + [whole()] * 2 + [in_hbm] + [whole()] * (2 + parts + len(arrived)),
        out_specs=[whole(), in_hbm],
        scratch_shapes=[
            VMEM((parts, levels, 2 * parent_rows, foot), f32),
            VMEM((levels, 8, LANES), f32),
            pltpu.SemaphoreType.DMA,
        ],
        input_output_aliases={4: 1},
        compiler_params=params(),
        cost_estimate=cost(200000, 800000),
        name="merge",
    )(offset_x, offset_y, late, step, nest_stored, spread, beyond, *own, *arrived)
    return (parent_new, nest_new)


def swapped(value, first):
    along = ("gx", "gz")
    count = lax.axis_size(along)
    pairs = []
    for at in range(first, count, 2):
        pairs += [(at, (at + 1) % count), ((at + 1) % count, at)]
    return lax.ppermute(value, along, pairs)


def shifted_both(value, steps, only=None):
    sizes = [lax.axis_size(axis) for axis in ("gx", "gy", "gz")]
    gx, gy, gz = sizes
    pairs = []
    for x in range(gx):
        for y in range(gy):
            for z in range(gz):
                place = (x * gz + z + 1) % (gx * gz)
                target = (place // gz * gy + (y + steps) % gy) * gz + place % gz
                if only is not None and (y + steps) % gy != only:
                    continue
                pairs.append(((x * gy + y) * gz + z, target))
    return lax.ppermute(value, ("gx", "gy", "gz"), pairs)


def solution(mesh):
    return jax.shard_map(
        shards,
        mesh=mesh,
        in_specs=(
            P(None, ("grp", "gx", "gz"), "gy"),
            P(None, ("grp", "gx", "gz"), "gy"),
            P(),
            P(None, ("grp", "gx", "gz"), "gy"),
            P(None, ("grp", "gx", "gz"), "gy"),
            P(),
            P("grp"),
            P("grp"),
        ),
        out_specs=(P(None, ("grp", "gx", "gz"), "gy"), P(None, ("grp", "gx", "gz"), "gy")),
        check_vma=False,
    )
```

```python
import functools

import jax
import jax.numpy as jnp
from jax import lax
from jax.experimental import pallas as pl
from jax.experimental.pallas import tpu as pltpu
from jax.sharding import PartitionSpec as P

RATIO = 3
SUBSTEPS = 3
RIM = 6
LANES = 128
STRIDE = 16
SOURCE_AT = 3
PARENT_AT = 6
STRIP_AT = 8
STRIP_SOURCE_AT = 12
SOURCE_ROW = 24
TAIL_ROW = 40
FIXED = 8
LEFT_AT = 3
RIGHT_OWN = STRIDE - 3
VMEM = pltpu.VMEM
LIMIT = 24 * 1024 * 1024
MOST = 54 * 1024 * 1024


def iota(shape, dim):
    return lax.broadcasted_iota(jnp.int32, shape, dim)


def whole():
    return pl.BlockSpec(memory_space=VMEM)


def scalars():
    return pl.BlockSpec(memory_space=pltpu.SMEM)


def params(limit=LIMIT):
    return pltpu.CompilerParams(vmem_limit_bytes=limit)


def cost(flops, moved):
    return pl.CostEstimate(flops=flops, bytes_accessed=moved, transcendentals=0)


def tile(ref, level, index):
    return ref[level, :, index * LANES : (index + 1) * LANES]


def turned(value, lanes):
    lanes = lanes % LANES
    return pltpu.roll(value, lanes, 1) if lanes else value


def edge_strip(dest, band, oy, parent, parent_source):
    levels, rows, cols = parent.shape
    lane = iota((rows, LANES), 1)
    base = jnp.where(dest == 0, oy - 1, oy + band - 3) - lax.axis_index("gy") * cols
    total = jnp.zeros(lane.shape, jnp.float32)
    for ref, first in ((parent, STRIP_AT), (parent_source, STRIP_SOURCE_AT)):
        for level in range(levels):
            found = jnp.zeros(lane.shape, jnp.float32)
            for at in range(cols // LANES):
                place = lane + (at * LANES - base)
                found = jnp.where((place >= 0) & (place < 4), tile(ref, level, at), found)
            turn = (16384 + first + STRIDE * level - base) & (LANES - 1)
            total = total + pltpu.roll(found, turn, 1)
    return total


def pack_pair(nest, source, parent, parent_source, out, fine_buf, coarse_buf, sems):
    levels, rows, cols = nest.shape
    parent_rows, parent_cols = parent.shape[1:]
    right = lax.axis_index("gy") == 0
    loads = []
    for at, (ref, buf) in enumerate(
        (
            (parent, coarse_buf.at[0]),
            (parent_source, coarse_buf.at[1]),
            (nest, fine_buf.at[0]),
            (source, fine_buf.at[1]),
        )
    ):
        start = pl.multiple_of(jnp.where(right, ref.shape[2] - LANES, 0), LANES)
        loads.append(pltpu.make_async_copy(ref.at[:, :, pl.ds(start, LANES)], buf, sems.at[at]))
    for copy in loads:
        copy.start()

    def columns(value, count, to):
        first = jnp.where(right, LANES - count, 0)
        place = iota(value.shape, 1) - first
        value = jnp.where((place >= 0) & (place < count), value, 0.0)
        return pltpu.roll(value, (LANES + to - first) & (LANES - 1), 1)

    part = jnp.zeros((parent_rows, LANES), jnp.float32)
    loads[0].wait()
    loads[1].wait()
    for level in range(levels):
        base = STRIDE * level
        part = part + columns(coarse_buf[0, level], 1, base + PARENT_AT)
        part = part + columns(coarse_buf[0, level], 2, base + STRIP_AT)
        part = part + columns(coarse_buf[1, level], 2, base + STRIP_SOURCE_AT)
    total = jnp.zeros((rows, LANES), jnp.float32)
    loads[2].wait()
    loads[3].wait()
    for level in range(levels):
        base = STRIDE * level
        total = total + columns(fine_buf[0, level], 3, base)
        total = total + columns(fine_buf[1, level], 3, base + SOURCE_AT)
    out[...] = total
    out[:parent_rows, :] += part


def across_border(message, oy, parent_cols, me):
    c = iota(message.shape, 1) & (STRIDE - 1)
    place = jnp.where(me == 0, parent_cols + 1, 1) - oy
    total = jnp.zeros(message.shape, jnp.float32)
    for turn in (-1, 0, 2, 3):
        at = jnp.where(c >= STRIP_SOURCE_AT, c - STRIP_SOURCE_AT, c - STRIP_AT) - turn
        fits = (c >= STRIP_AT) & (at >= 0) & (at < 2) & (place == turn)
        total = total + jnp.where(fits, turned(message, turn), 0.0)
    return total


def pack_columns(parts, band, oy_hbm, nest, source, parent_hbm, parent_source_hbm, *rest):
    outs = rest[: parts - 1]
    old_buf, src_buf, parent, parent_source, oy_ref, sems, field_sems = rest[parts - 1 :]
    levels, rows, cols = nest.shape
    parent_cols = parent.shape[2]
    me = lax.axis_index("gy")
    sides = [1] if parts == 2 else [1, parts - 1]
    fields = [
        pltpu.make_async_copy(ref, buf, field_sems.at[at])
        for at, (ref, buf) in enumerate(
            ((oy_hbm, oy_ref), (parent_hbm, parent), (parent_source_hbm, parent_source))
        )
    ]
    for copy in fields:
        copy.start()
    copies = []
    for at, step in enumerate(sides):
        right = (me == 0) if parts == 2 else jnp.bool_(step == 1)
        start = pl.multiple_of(jnp.where(right, cols - LANES, 0), LANES)
        pair = [
            pltpu.make_async_copy(
                ref.at[:, :, pl.ds(start, LANES)], buf.at[at], sems.at[at, which]
            )
            for which, (ref, buf) in enumerate(((nest, old_buf), (source, src_buf)))
        ]
        for copy in pair:
            copy.start()
        copies.append((right, pair))
    for copy in fields:
        copy.wait()
    oy = oy_ref[0]
    lane = iota((parent.shape[1], LANES), 1)
    for step in range(1, parts):
        out = outs[step - 1]
        part = edge_strip(lax.rem(me + step, parts), band, oy, parent, parent_source)
        if step not in sides:
            out[...] = part
            continue
        at = sides.index(step)
        right, pair = copies[at]
        first = jnp.where(right, LANES - 3, 0)
        outer = jnp.where(right, LANES - 1, 0)
        for level in range(levels):
            edge = jnp.where(
                right, tile(parent, level, parent_cols // LANES - 1), tile(parent, level, 0)
            )
            edge = jnp.where(lane == outer, edge, 0.0)
            turn = (LANES + PARENT_AT + STRIDE * level - outer) & (LANES - 1)
            part = part + pltpu.roll(edge, turn, 1)
        for copy in pair:
            copy.wait()
        fine = iota((rows, LANES), 1) - first
        wanted = (fine >= 0) & (fine < 3)
        total = jnp.zeros((rows, LANES), jnp.float32)
        for level in range(levels):
            for buf, shift in ((old_buf, 0), (src_buf, SOURCE_AT)):
                value = jnp.where(wanted, buf[at, level], 0.0)
                turn = (LANES + STRIDE * level + shift - first) & (LANES - 1)
                total = total + pltpu.roll(value, turn, 1)
        out[...] = total
        out[: part.shape[0], :] += part


def three_terms(value):
    terms = []
    for _ in range(3):
        term = value.astype(jnp.bfloat16)
        terms.append(term)
        value = value - term.astype(jnp.float32)
    return terms


def select_rows(selector, value):
    selector = selector.astype(jnp.bfloat16)
    high, middle, low = (
        jnp.dot(selector, term, preferred_element_type=jnp.float32)
        for term in three_terms(value)
    )
    return high + (middle + low)


def select_columns(value, selector):
    selector = selector.astype(jnp.bfloat16)
    high, middle, low = (
        jnp.dot(term, selector, preferred_element_type=jnp.float32)
        for term in three_terms(value)
    )
    return high + (middle + low)


def sum_rows(ref):
    count = ref.shape[0] // RATIO
    first, second, third = (ref[pl.ds(at, count, RATIO), :] for at in range(RATIO))
    return first + second + third


def inner_substep(coefs, here, source, there):
    levels, rows, cols = here.shape
    sub = iota((8, cols), 0)
    tiles = rows // 8

    def one_level(level):
        ch = coefs[0, level]
        cv = coefs[1, level]
        centre = 1.0 - 4.0 * ch - 2.0 * cv
        below = jnp.maximum(level - 1, 0)
        above = jnp.minimum(level + 1, levels - 1)
        cv_below = jnp.where(level > 0, cv, 0.0)
        cv_above = jnp.where(level < levels - 1, cv, 0.0)

        def row_tile(t):
            t = t % tiles
            return here[level, 8 * t : 8 * t + 8, :]

        down_before = pltpu.roll(row_tile(-1), 1, 0)
        now = row_tile(0)
        up_now = pltpu.roll(now, 7, 0)
        for t in range(tiles):
            following = row_tile(t + 1)
            down_now = pltpu.roll(now, 1, 0)
            up_next = pltpu.roll(following, 7, 0)
            around = jnp.where(sub == 0, down_before, down_now) + jnp.where(
                sub == 7, up_next, up_now
            )
            around = around + (pltpu.roll(now, 1, 1) + pltpu.roll(now, cols - 1, 1))
            span = slice(8 * t, 8 * t + 8)
            stacked = cv_below * here[below, span, :] + cv_above * here[above, span, :]
            there[level, span, :] = centre * now + ch * around + (stacked + source[level, span, :])
            down_before, now, up_now = down_now, following, up_next

    def two_levels(pair, carry):
        one_level(2 * pair)
        one_level(2 * pair + 1)
        return carry

    lax.fori_loop(0, levels // 2, two_levels, 0)


def spread_coefs(parent_coefs, coefs, out):
    levels = out.shape[2]
    lane = iota((levels, LANES), 1)
    row = iota((levels, LANES), 0)
    for at, ref in enumerate((parent_coefs, coefs)):
        for which in range(2):
            packed = jnp.full(lane.shape, ref[which, 0], jnp.float32)
            rows = packed
            for level in range(1, levels):
                packed = jnp.where(lane >= STRIDE * level, ref[which, level], packed)
                rows = jnp.where(row == level, ref[which, level], rows)
            out[0, 2 * at + which] = packed
            out[1, 2 * at + which] = rows


def inner_first(
    band,
    oy_ref,
    parent_coefs,
    coefs,
    nest,
    source,
    parent,
    parent_source,
    strip,
    first,
    spread,
    oy_rows,
):
    oy = oy_ref[0]
    oy_rows[...] = jnp.full(oy_rows.shape, oy, jnp.int32)
    spread_coefs(parent_coefs, coefs, spread)
    strip[...] = edge_strip(lax.axis_index("gy"), band, oy, parent, parent_source)
    inner_substep(coefs, nest, source, first)


def own_windows(parts, nest, source, y_left, y_right, window_old, window_src):
    levels, rows, cols = nest.shape
    pieces = cols // LANES
    me = lax.axis_index("gy")
    for level in range(levels):
        for buf, field, shift in ((window_old, nest, 0), (window_src, source, SOURCE_AT)):
            for window, first, turn in ((0, 0, 3), (1, rows - 8, 5)):
                tiles = [
                    field[level, first : first + 8, piece * LANES : (piece + 1) * LANES]
                    for piece in range(pieces)
                ]
                tiles = with_columns(
                    tiles,
                    y_left[first : first + 8, :],
                    y_right[first : first + 8, :],
                    me,
                    parts,
                    STRIDE * level + shift,
                )
                for piece, value in enumerate(tiles):
                    buf[level, window, :, piece * LANES : (piece + 1) * LANES] = pltpu.roll(
                        value, turn, 0
                    )


def inner_rest(
    parts,
    coefs,
    nest,
    first,
    source,
    y_left,
    y_right,
    after_pack,
    third,
    packs,
    window_old,
    window_src,
    sums,
    second,
    split,
):
    levels, rows, cols = nest.shape
    own_windows(parts, nest, source, y_left, y_right, window_old, window_src)
    lane = iota((rows, LANES), 1)
    for at, ref in enumerate((nest, source)):
        left = jnp.zeros(lane.shape, jnp.float32)
        right = jnp.zeros(lane.shape, jnp.float32)
        for level in range(levels):
            value = jnp.where(lane < RIGHT_OWN, tile(ref, level, 0), 0.0)
            left = left + turned(value, STRIDE * level + LEFT_AT)
            value = jnp.where(lane >= LANES - RIGHT_OWN, tile(ref, level, cols // LANES - 1), 0.0)
            right = right + turned(value, STRIDE * level + RIGHT_OWN)
        packs[2 * at] = left
        packs[2 * at + 1] = right
    inner_substep(coefs, first, source, second)
    inner_substep(coefs, second, source, third)
    for level in range(levels):
        for piece in range(cols // LANES):
            split[piece, level * rows : (level + 1) * rows, :] = tile(third, level, piece)
    for piece in range(cols // LANES):
        sums[piece] = sum_rows(split.at[piece])


def with_columns(tiles, left, right, me, parts, place):
    lane = iota(left.shape, 1)
    from_right = turned(right, -place)
    from_left = turned(left, -3 - place)
    if parts == 2:
        tiles[0] = jnp.where((lane < 3) & (me == 0), from_right, tiles[0])
        tiles[-1] = jnp.where((lane >= LANES - 3) & (me == 1), from_left, tiles[-1])
        return tiles
    extra = jnp.where(lane < 3, from_right, jnp.where(lane >= LANES - 3, from_left, 0.0))
    return tiles + [extra]


def pack_rows(
    parts, old_top, old_end, src_top, src_end, par_top, par_end, own_strip, oy_rows, *rest
):
    columns = rest[: parts - 1]
    across, within, far, strip_out, both = rest[parts - 1 :]
    core = lax.axis_index("gz")
    up, down = both.at[core], both.at[1 - core]
    levels, _, cols = old_top.shape
    me = lax.axis_index("gy")
    left, right = columns[0], columns[-1]
    rows = left.shape[0]
    strip_rows = own_strip.shape[0]
    lane = iota((strip_rows, LANES), 1)
    strips = own_strip[...]
    if parts == 2:
        oy = jnp.concatenate([oy_rows[...]] * (strip_rows // 8), axis=0)
        strips = strips + across_border(left[:strip_rows, :], oy, par_top.shape[2], me)
    else:
        for message in columns:
            strips = strips + message[:strip_rows, :]
    c = lane & (STRIDE - 1)
    strips = jnp.where(c >= STRIP_AT, strips, 0.0)
    strips = jnp.where(c == PARENT_AT, left[:strip_rows, :], strips)
    strips = jnp.where(c == PARENT_AT + 1, turned(right[:strip_rows, :], 1), strips)
    strip_out[...] = strips
    far[...] = strips[:8]
    pieces = cols // LANES
    for out, old, src, first, at, src_at in (
        (up, old_end, src_end, rows - 8, 5, 6),
        (down, old_top, src_top, 0, 0, 0),
    ):
        y_left = left[first : first + 8, :]
        y_right = right[first : first + 8, :]
        for level in range(levels):
            for ref, shift, row, count, base in (
                (old, 0, at, 3, 0),
                (src, SOURCE_AT, src_at, 2, SOURCE_ROW),
            ):
                tiles = [tile(ref, level, piece) for piece in range(pieces)]
                tiles = with_columns(
                    tiles, y_left, y_right, me, parts, STRIDE * level + shift
                )
                for piece, value in enumerate(tiles):
                    out[
                        base + count * level : base + count * (level + 1),
                        piece * LANES : (piece + 1) * LANES,
                    ] = value[row : row + count]
    parent_cols = par_top.shape[2]
    for level in range(levels):
        up[TAIL_ROW + level : TAIL_ROW + level + 1, :parent_cols] = par_end[level, 7:8, :]
        down[TAIL_ROW + level : TAIL_ROW + level + 1, :parent_cols] = par_top[level, 0:1, :]
    up[TAIL_ROW : TAIL_ROW + 8, parent_cols : parent_cols + LANES] = strips[strip_rows - 8 :]
    down[TAIL_ROW : TAIL_ROW + 8, parent_cols : parent_cols + LANES] = strips[:8]
    down[TAIL_ROW + 8 : TAIL_ROW + 16, :LANES] = strips[8:16]
    down[TAIL_ROW + 8 : TAIL_ROW + 16, LANES : 2 * LANES] = strips[16:24]
    within[...] = both[0]
    across[...] = both[1]


def edges(
    parts,
    parent_cols,
    ox_ref,
    spread,
    sums,
    packs,
    window_old,
    window_src,
    strips,
    across,
    within,
    far,
    y_left,
    y_right,
    sides,
    windows,
    coarse_out,
    far_out,
    both,
    ping,
    pong,
    src,
):
    levels = ping.shape[0]
    width = ping.shape[3]
    rows = sides.shape[1]
    cols = sums.shape[0] * LANES
    pieces = cols // LANES
    me = lax.axis_index("gy")
    core = lax.axis_index("gz")
    both[0] = within[...]
    both[1] = across[...]
    before, after = both.at[1 - core], both.at[core]
    is_south = me == 0
    is_north = me == parts - 1

    far_out[...] = far[...]
    sub = iota((8, LANES), 0)
    old = jnp.concatenate(
        [
            strips[...],
            after[TAIL_ROW : TAIL_ROW + 8, parent_cols : parent_cols + LANES],
            after[TAIL_ROW + 8 : TAIL_ROW + 16, :LANES],
            after[TAIL_ROW + 8 : TAIL_ROW + 16, LANES : 2 * LANES],
            jnp.where(
                sub == 7,
                before[TAIL_ROW : TAIL_ROW + 8, parent_cols : parent_cols + LANES],
                0.0,
            ),
        ],
        axis=0,
    )
    count = old.shape[0]

    def packed_coef(which, height):
        return jnp.concatenate([spread[0, which]] * (height // 8), axis=0)

    def stacked(value):
        lane = iota(value.shape, 1)
        below = jnp.where(lane >= STRIDE, turned(value, STRIDE), 0.0)
        return below + jnp.where(lane < STRIDE * (levels - 1), turned(value, -STRIDE), 0.0)

    def around(value):
        return (
            pltpu.roll(value, 1, 0)
            + pltpu.roll(value, value.shape[0] - 1, 0)
            + turned(value, 1)
            + turned(value, -1)
        )

    diff = (
        packed_coef(0, count) * (around(old) - 4.0 * old)
        + packed_coef(1, count) * (stacked(old) - 2.0 * old)
        + turned(old, STRIP_AT - STRIP_SOURCE_AT)
    )
    index = iota((rows + 16, count), 0)
    nest_row = jnp.where(index < rows, index, jnp.where(index < rows + 8, index - rows - 3, index - 13))
    parent_row = ((nest_row + 3) * 171 >> 9) - 1 + ox_ref[0]
    pick = (iota((rows + 16, count), 1) == parent_row).astype(jnp.float32)
    picked = select_rows(pick, jnp.concatenate([old, diff], axis=1))
    picked_old, picked_diff = picked[:, :LANES], picked[:, LANES:]

    lane = iota((rows, LANES), 1)
    c = lane & (STRIDE - 1)
    rim_first = jnp.where(is_south, LEFT_AT, RIGHT_OWN - RIM)
    in_rim = (c >= rim_first) & (c < rim_first + RIM)
    at = lane - c + STRIP_AT + jnp.where(c >= rim_first + 3, 2, 1)
    rim_old = jnp.take_along_axis(picked_old[:rows], at, axis=1)
    rim_diff = jnp.take_along_axis(picked_diff[:rows], at, axis=1)
    ch = packed_coef(2, rows)
    cv = packed_coef(3, rows)
    centre = 1.0 - 4.0 * ch - 2.0 * cv
    left = jnp.where(c < 3, y_left[...], packs[0])
    left_src = jnp.where(c < 3, turned(y_left[...], -SOURCE_AT), packs[2])
    right = jnp.where(c >= RIGHT_OWN, turned(y_right[...], RIGHT_OWN), packs[1])
    right_src = jnp.where(c >= RIGHT_OWN, turned(y_right[...], RIGHT_OWN - SOURCE_AT), packs[3])
    for side, (value, forcing, rim) in enumerate(
        (
            (left, left_src, in_rim & is_south),
            (right, right_src, in_rim & is_north),
        )
    ):
        for substep in range(1, SUBSTEPS + 1):
            value = centre * value + ch * around(value) + (cv * stacked(value) + forcing)
            value = jnp.where(rim, rim_old + (substep / SUBSTEPS) * rim_diff, value)
        sides[side] = value

    sub = iota((8, width), 0)
    lane = iota((8, LANES), 1)
    ping[...] = window_old[...]
    src[...] = window_src[...]
    for level in range(levels):
        for buf, n, base in ((ping, 3, 0), (src, 2, SOURCE_ROW)):
            rows_of = slice(base + n * level, base + n * (level + 1))
            buf[level, 0, 3 - n : 3, :] = before[rows_of, :]
            buf[level, 1, 5 : 5 + n, :] = after[rows_of, :]
    rim_first = jnp.where(is_south, 0, LANES - RIM)
    column = STRIP_AT + jnp.where((lane >= rim_first + 3) & (lane < rim_first + RIM), 2, 1)
    rims = {}
    for level in range(levels):
        for window in range(2):
            span = slice(rows + 8 * window, rows + 8 * window + 8)
            at = column + STRIDE * level
            rims[level, window] = (
                jnp.take_along_axis(picked_old[span], at, axis=1),
                jnp.take_along_axis(picked_diff[span], at, axis=1),
            )
    for substep in range(1, SUBSTEPS + 1):
        here, there = (ping, pong) if substep % 2 else (pong, ping)
        there = windows if substep == SUBSTEPS else there
        low = 0 if substep == SUBSTEPS or parts > 2 else 3
        south = (lane >= low) & (lane < RIM) & is_south
        north = (lane >= LANES - RIM) & (lane < LANES - low) & is_north
        weight = substep / SUBSTEPS
        for level in range(levels):
            c_h, c_v = (
                jnp.concatenate([spread[1, which, level : level + 1, :]] * (width // LANES), axis=1)
                for which in (2, 3)
            )
            c_0 = 1.0 - 4.0 * c_h - 2.0 * c_v
            for window in range(2):
                now = here[level, window]
                up = pltpu.roll(now, 1, 0)
                down = pltpu.roll(now, 7, 0)
                if substep == 1:
                    beyond_row = window_old[level, window]
                    if window == 0:
                        down = jnp.where(sub == 7, pltpu.roll(beyond_row, 7, 0), down)
                    else:
                        up = jnp.where(sub == 0, pltpu.roll(beyond_row, 1, 0), up)
                beside = pltpu.roll(now, 1, 1) + pltpu.roll(now, width - 1, 1)
                value = c_0 * now + c_h * ((up + down) + beside) + src[level, window]
                if level > 0:
                    value = value + c_v * here[level - 1, window]
                if level < levels - 1:
                    value = value + c_v * here[level + 1, window]
                rim_o, rim_d = rims[level, window]
                rim = rim_o + weight * rim_d
                for piece in range(width // LANES):
                    span = slice(piece * LANES, (piece + 1) * LANES)
                    part = value[:, span]
                    if piece == 0:
                        part = jnp.where(south, rim, part)
                    if piece == pieces - 1:
                        part = jnp.where(north, rim, part)
                    there[level, window, :, span] = part

    parent_rows = rows // RATIO
    lane = iota((parent_rows, LANES), 1)
    row = iota((parent_rows, LANES), 0)
    side_sums = [sum_rows(sides.at[side]) for side in range(2)]
    replaced = [[] for _ in range(pieces)]
    for level in range(levels):
        span = slice(level * parent_rows, (level + 1) * parent_rows)
        top = windows[level, 0, 3:4, :] + windows[level, 0, 4:5, :] + windows[level, 0, 5:6, :]
        end = windows[level, 1, 2:3, :] + windows[level, 1, 3:4, :] + windows[level, 1, 4:5, :]
        for piece in range(pieces):
            value = sums[piece, span, :]
            if piece == 0:
                fixed = turned(side_sums[0], -STRIDE * level - LEFT_AT)
                value = jnp.where(lane < FIXED, fixed, value)
            if piece == pieces - 1:
                fixed = turned(side_sums[1], -STRIDE * level - RIGHT_OWN)
                value = jnp.where(lane >= LANES - FIXED, fixed, value)
            across_piece = slice(piece * LANES, (piece + 1) * LANES)
            value = jnp.where(row == 0, top[:, across_piece], value)
            value = jnp.where(row == parent_rows - 1, end[:, across_piece], value)
            replaced[piece].append(value)
    foot = cols // RATIO
    offset = iota((cols, foot), 0) - RATIO * iota((cols, foot), 1)
    gather = ((offset >= 0) & (offset < RATIO)).astype(jnp.float32)
    means = select_columns(
        jnp.concatenate([jnp.concatenate(values, axis=0) for values in replaced], axis=1), gather
    ) * (1.0 / 9.0)
    coarse_out[...] = means.reshape(coarse_out.shape)


def put_together(third, sides, windows, result):
    levels, rows, cols = third.shape
    pieces = cols // LANES
    lane = iota((rows, LANES), 1)
    sub = iota((8, cols), 0)
    for level in range(levels):
        fixed = turned(sides[0], -STRIDE * level - LEFT_AT)
        result[level, :, :LANES] = jnp.where(lane < FIXED, fixed, tile(third, level, 0))
        for piece in range(1, pieces - 1):
            result[level, :, piece * LANES : (piece + 1) * LANES] = tile(third, level, piece)
        fixed = turned(sides[1], -STRIDE * level - RIGHT_OWN)
        result[level, :, cols - LANES :] = jnp.where(
            lane >= LANES - FIXED, fixed, tile(third, level, pieces - 1)
        )
        top = pltpu.roll(windows[level, 0, :, :cols], 5, 0)
        result[level, :8, :] = jnp.where(sub < 3, top, result[level, :8, :])
        end = pltpu.roll(windows[level, 1, :, :cols], 3, 0)
        result[level, rows - 8 :, :] = jnp.where(sub >= 5, end, result[level, rows - 8 :, :])


def parent_step(
    parts,
    band,
    ox_ref,
    oy_ref,
    spread,
    third,
    sides,
    windows,
    parent,
    source,
    within,
    across,
    y_left,
    y_right,
    out,
    nest_out,
    late,
    tail,
    result,
    sem,
):
    put_together(third, sides, windows, result)
    store = pltpu.make_async_copy(result, nest_out, sem)
    store.start()
    core = lax.axis_index("gz")
    levels, rows, cols = parent.shape
    tail[0] = within[TAIL_ROW : TAIL_ROW + levels, : cols + LANES]
    tail[1] = across[TAIL_ROW : TAIL_ROW + levels, : cols + LANES]
    me = lax.axis_index("gy")
    is_last = ox_ref[0] == rows - 1
    wide = iota((1, cols), 1)
    south = (wide == oy_ref[0] + 2 - me * cols) & is_last
    north = (wide == oy_ref[0] + band - 3 - me * cols) & is_last
    row = iota((rows, cols), 0)
    lane = iota((rows, cols), 1)
    has_left = me > 0
    has_right = me < parts - 1
    left = y_left[:rows, :]
    right = y_right[:rows, :]
    zero = jnp.zeros((rows, cols), jnp.float32)
    for level in range(levels):
        now = parent[level]
        at = STRIDE * level + PARENT_AT
        from_left = left[:, at : at + 1]
        from_right = right[:, at : at + 1]
        top = tail[1 - core, level : level + 1, :cols]
        end = tail[core, level : level + 1, :cols]
        around = (
            jnp.where(row == 0, top, pltpu.roll(now, 1, 0))
            + jnp.where(row == rows - 1, end, pltpu.roll(now, rows - 1, 0))
            + jnp.where(
                lane == 0, jnp.where(has_left, from_left, 0.0), pltpu.roll(now, 1, 1)
            )
            + jnp.where(
                lane == cols - 1,
                jnp.where(has_right, from_right, 0.0),
                pltpu.roll(now, cols - 1, 1),
            )
        )
        stacked = (parent[level - 1] if level > 0 else zero) + (
            parent[level + 1] if level < levels - 1 else zero
        )
        ch, cv = (
            jnp.concatenate([spread[1, which, level : level + 1, :]] * (cols // LANES), axis=1)
            for which in (0, 1)
        )
        out[level] = (
            (1.0 - 4.0 * ch - 2.0 * cv) * now + ch * around + (cv * stacked + source[level])
        )
        at = cols + STRIDE * level + PARENT_AT
        before_end = jnp.where(
            wide == 0, tail[core, 0:1, at : at + 1], pltpu.roll(end, 1, 1)
        )
        after_end = jnp.where(
            wide == cols - 1, tail[core, 0:1, at + 1 : at + 2], pltpu.roll(end, cols - 1, 1)
        )
        nest_ch = spread[1, 2, level : level + 1, :]
        nest_ch = jnp.concatenate([nest_ch] * (cols // LANES), axis=1)
        share = nest_ch * nest_ch * ch * (1.0 / SUBSTEPS)
        late[level : level + 1, :] = (share * (1.0 / (RATIO * RATIO))) * (
            jnp.where(south, before_end, 0.0) + jnp.where(north, after_end, 0.0)
        )
    store.wait()


def merge(parts, band, ox_ref, oy_ref, late, step, nest, spread, beyond, *rest):
    previous = rest[1 : parts + 1]
    own = rest[:1] + rest[parts + 1 : 2 * parts]
    out, nest_out, joined, corner, sem, merged, out_sems = rest[2 * parts :]
    levels, rows, cols = step.shape
    foot = own[0].shape[2]
    me = lax.axis_index("gy")

    @pl.when((ox_ref[0] == rows - 1) & ((me == 0) | (me == parts - 1)))
    def _():
        nest_rows, nest_cols = nest.shape[1:]
        first = pl.multiple_of(jnp.where(me == 0, 0, nest_cols - LANES), LANES)
        place = (slice(None), pl.ds(nest_rows - 8, 8), pl.ds(first, LANES))
        load = pltpu.make_async_copy(nest_out.at[place], corner, sem)
        load.start()
        load.wait()
        sub = iota((8, LANES), 0)
        lane = iota((8, LANES), 1)
        cell = (sub == 7) & (lane == jnp.where(me == 0, RIM, LANES - RIM - 1))
        for level in range(levels):
            at = STRIDE * level + STRIP_AT
            value = jnp.where(me == 0, beyond[0:1, at + 2 : at + 3], beyond[0:1, at + 1 : at + 2])
            nest_ch = spread[1, 2, level : level + 1, :]
            share = nest_ch * nest_ch * spread[1, 0, level : level + 1, :] * (1.0 / SUBSTEPS)
            corner[level] += jnp.where(cell, share * value, 0.0)
        again = pltpu.make_async_copy(corner, nest_out.at[place], sem)
        again.start()
        again.wait()

    ox = ox_ref[0]
    oy = oy_ref[0]
    for k in range(parts):
        joined[k, :, :rows, :] = previous[k][...]
        joined[k, :, rows:, :] = own[k][...]
    lane = iota((rows, LANES), 1)
    row = iota((rows, LANES), 0)
    stores = []
    for level in range(levels):
        values = [tile(step, level, piece) for piece in range(cols // LANES)]
        for k in range(parts):
            source = lax.rem(me + parts - k, parts)
            block = joined[k, level, pl.ds(rows - ox, rows), :]
            begin = oy + source * foot - me * cols
            block = pltpu.roll(block, (16384 + begin) & (LANES - 1), 1)
            low = jnp.maximum(source * foot, 2)
            high = jnp.minimum((source + 1) * foot, band - 2)
            for piece in range(cols // LANES):
                at = lane + (piece * LANES + me * cols - oy)
                values[piece] = jnp.where((at >= low) & (at < high), block, values[piece])
        for piece, value in enumerate(values):
            term = late[level : level + 1, piece * LANES : (piece + 1) * LANES]
            value = value + jnp.where(row == rows - 2, term, 0.0)
            merged[level, :, piece * LANES : (piece + 1) * LANES] = value
        stores.append(pltpu.make_async_copy(merged.at[level], out.at[level], out_sems.at[level]))
        stores[-1].start()
    for copy in stores:
        copy.wait()


def shifted(value, axis, steps):
    count = lax.axis_size(axis)
    pairs = [(source, (source + steps) % count) for source in range(count)]
    return lax.ppermute(value, axis, pairs)


def shards(
    parent_old, parent_source, parent_coefs, nest_old, nest_source, nest_coefs, offset_x, offset_y
):
    parts = lax.axis_size("gy")
    along = ("gx", "gz")
    levels, parent_rows, parent_cols = parent_old.shape
    _, rows, cols = nest_old.shape
    foot = cols // RATIO
    band = foot * parts
    width = cols if parts == 2 else cols + LANES
    height = TAIL_ROW + 16
    f32 = jnp.float32
    shape = jax.ShapeDtypeStruct
    anywhere = pl.BlockSpec(memory_space=pl.ANY)
    in_hbm = pl.BlockSpec(memory_space=pltpu.HBM)
    sides = 1 if parts == 2 else 2
    if parts == 2:
        packed = [
            pl.pallas_call(
                pack_pair,
                out_shape=VMEM((rows, LANES), f32),
                in_specs=[in_hbm] * 4,
                out_specs=whole(),
                scratch_shapes=[
                    VMEM((2, levels, rows, LANES), f32),
                    VMEM((2, levels, parent_rows, LANES), f32),
                    pltpu.SemaphoreType.DMA((4,)),
                ],
                compiler_params=params(MOST),
                cost_estimate=cost(200000, 800000),
                name="pack_pair",
            )(nest_old, nest_source, parent_old, parent_source)
        ]
    else:
        packed = pl.pallas_call(
            functools.partial(pack_columns, parts, band),
            out_shape=[
                shape((rows if k in (1, parts - 1) else parent_rows, LANES), f32)
                for k in range(1, parts)
            ],
            in_specs=[in_hbm] * 5,
            out_specs=[whole()] * (parts - 1),
            scratch_shapes=[
                VMEM((sides, levels, rows, LANES), f32),
                VMEM((sides, levels, rows, LANES), f32),
                VMEM(parent_old.shape, f32),
                VMEM(parent_old.shape, f32),
                pltpu.SMEM(offset_y.shape, jnp.int32),
                pltpu.SemaphoreType.DMA((sides, 2)),
                pltpu.SemaphoreType.DMA((3,)),
            ],
            compiler_params=params(MOST),
            cost_estimate=cost(200000, 1000000),
            name="pack_columns",
        )(offset_y, nest_old, nest_source, parent_old, parent_source)
    columns = [shifted(packed[k - 1], "gy", k) for k in range(1, parts)]
    own_strip, first, spread, oy_rows = pl.pallas_call(
        functools.partial(inner_first, band),
        out_shape=[
            shape((parent_rows, LANES), f32),
            shape(nest_old.shape, f32),
            shape((2, 4, levels, LANES), f32),
            shape((8, LANES), jnp.int32),
        ],
        in_specs=[scalars()] * 3 + [whole()] * 4,
        out_specs=[whole()] * 4,
        compiler_params=params(),
        cost_estimate=cost(4000000, 3000000),
        name="inner_first",
    )(
        offset_y,
        parent_coefs,
        nest_coefs,
        nest_old,
        nest_source,
        parent_old,
        parent_source,
    )

    def block(ref, last):
        count = ref.shape[1] // 8 - 1 if last else 0
        return pl.BlockSpec((levels, 8, ref.shape[2]), lambda i, c=count: (0, c, 0))

    def full(extent):
        return pl.BlockSpec(extent, lambda i: (0,) * len(extent))

    outs = [
        shape((height, width), f32),
        shape((height, width), f32),
        shape((8, LANES), f32),
        shape((parent_rows, LANES), f32),
    ]
    across, within, far, strips = pl.pallas_call(
        functools.partial(pack_rows, parts),
        out_shape=outs,
        grid=(1,),
        in_specs=[
            block(nest_old, False),
            block(nest_old, True),
            block(nest_old, False),
            block(nest_old, True),
            block(parent_old, False),
            block(parent_old, True),
            full(own_strip.shape),
            full(oy_rows.shape),
        ]
        + [full(message.shape) for message in columns],
        out_specs=[full(out.shape) for out in outs],
        scratch_shapes=[VMEM((2, height, width), f32)],
        compiler_params=params(),
        cost_estimate=cost(100000, 700000),
        name="pack_rows",
    )(nest_old, nest_old, nest_source, nest_source, parent_old, parent_old, own_strip, oy_rows, *columns)
    across = swapped(across, 1)
    within = swapped(within, 0)
    third, packs, window_old, window_src, sums = pl.pallas_call(
        functools.partial(inner_rest, parts),
        out_shape=[
            shape(nest_old.shape, f32),
            shape((4, rows, LANES), f32),
            shape((levels, 2, 8, width), f32),
            shape((levels, 2, 8, width), f32),
            shape((cols // LANES, levels * parent_rows, LANES), f32),
        ],
        in_specs=[scalars()] + [whole()] * 5 + [anywhere],
        out_specs=[whole()] * 5,
        scratch_shapes=[
            VMEM(nest_old.shape, f32),
            VMEM((cols // LANES, levels * rows, LANES), f32),
        ],
        compiler_params=params(),
        cost_estimate=cost(8000000, 6000000),
        name="inner_rest",
    )(nest_coefs, nest_old, first, nest_source, columns[0], columns[-1], strips)
    sides, windows, coarse, far = pl.pallas_call(
        functools.partial(edges, parts, parent_cols),
        out_shape=[
            shape((2, rows, LANES), f32),
            shape((levels, 2, 8, width), f32),
            shape((levels, parent_rows, foot), f32),
            shape((8, LANES), f32),
        ],
        in_specs=[scalars()] + [whole()] * 11,
        out_specs=[whole()] * 4,
        scratch_shapes=[
            VMEM((2, height, width), f32),
            VMEM((levels, 2, 8, width), f32),
            VMEM((levels, 2, 8, width), f32),
            VMEM((levels, 2, 8, width), f32),
        ],
        compiler_params=params(),
        cost_estimate=cost(4000000, 3000000),
        name="edges",
    )(
        offset_x,
        spread,
        sums,
        packs,
        window_old,
        window_src,
        strips,
        across,
        within,
        far,
        columns[0],
        columns[-1],
    )
    previous = [shifted(coarse, along, 1)] + [shifted_both(coarse, k) for k in range(1, parts)]
    beside = [shifted(coarse, "gy", k) for k in range(1, parts)]
    beyond = shifted(far, along, -2)
    step, nest_stored, late = pl.pallas_call(
        functools.partial(parent_step, parts, band),
        out_shape=[
            shape(parent_old.shape, f32),
            shape(nest_old.shape, f32),
            shape((levels, parent_cols), f32),
        ],
        in_specs=[scalars()] * 2 + [whole()] * 10,
        out_specs=[whole(), in_hbm, whole()],
        scratch_shapes=[
            VMEM((2, levels, parent_cols + LANES), f32),
            VMEM(nest_old.shape, f32),
            pltpu.SemaphoreType.DMA,
        ],
        compiler_params=params(),
        cost_estimate=cost(800000, 2500000),
        name="parent_step",
    )(
        offset_x,
        offset_y,
        spread,
        third,
        sides,
        windows,
        parent_old,
        parent_source,
        within,
        across,
        columns[0],
        columns[-1],
    )
    parent_new, nest_new = pl.pallas_call(
        functools.partial(merge, parts, band),
        out_shape=[shape(parent_old.shape, f32), shape(nest_old.shape, f32)],
        in_specs=[scalars()] * 2 + [whole()] * 2 + [in_hbm] + [whole()] * (2 + 2 * parts),
        out_specs=[in_hbm, in_hbm],
        scratch_shapes=[
            VMEM((parts, levels, 2 * parent_rows, foot), f32),
            VMEM((levels, 8, LANES), f32),
            pltpu.SemaphoreType.DMA,
            VMEM(parent_old.shape, f32),
            pltpu.SemaphoreType.DMA((levels,)),
        ],
        input_output_aliases={4: 1},
        compiler_params=params(),
        cost_estimate=cost(200000, 800000),
        name="merge",
    )(offset_x, offset_y, late, step, nest_stored, spread, beyond, coarse, *previous, *beside)
    return (parent_new, nest_new)


def swapped(value, first):
    along = ("gx", "gz")
    count = lax.axis_size(along)
    pairs = []
    for at in range(first, count, 2):
        pairs += [(at, (at + 1) % count), ((at + 1) % count, at)]
    return lax.ppermute(value, along, pairs)


def shifted_both(value, steps):
    sizes = [lax.axis_size(axis) for axis in ("gx", "gy", "gz")]
    gx, gy, gz = sizes
    pairs = []
    for x in range(gx):
        for y in range(gy):
            for z in range(gz):
                place = (x * gz + z + 1) % (gx * gz)
                target = (place // gz * gy + (y + steps) % gy) * gz + place % gz
                pairs.append(((x * gy + y) * gz + z, target))
    return lax.ppermute(value, ("gx", "gy", "gz"), pairs)


def solution(mesh):
    return jax.shard_map(
        shards,
        mesh=mesh,
        in_specs=(
            P(None, ("grp", "gx", "gz"), "gy"),
            P(None, ("grp", "gx", "gz"), "gy"),
            P(),
            P(None, ("grp", "gx", "gz"), "gy"),
            P(None, ("grp", "gx", "gz"), "gy"),
            P(),
            P("grp"),
            P("grp"),
        ),
        out_specs=(P(None, ("grp", "gx", "gz"), "gy"), P(None, ("grp", "gx", "gz"), "gy")),
        check_vma=False,
    )
```

```python
import functools

import jax
import jax.numpy as jnp
from jax import lax
from jax.experimental import pallas as pl
from jax.experimental.pallas import tpu as pltpu
from jax.sharding import PartitionSpec as P

RATIO = 3
SUBSTEPS = 3
RIM = 6
LANES = 128
STRIDE = 16
SOURCE_AT = 3
PARENT_AT = 6
STRIP_AT = 8
STRIP_SOURCE_AT = 12
SOURCE_ROW = 24
TAIL_ROW = 40
FIXED = 8
LEFT_AT = 3
RIGHT_OWN = STRIDE - 3
VMEM = pltpu.VMEM
LIMIT = 24 * 1024 * 1024
MOST = 54 * 1024 * 1024


def iota(shape, dim):
    return lax.broadcasted_iota(jnp.int32, shape, dim)


def whole():
    return pl.BlockSpec(memory_space=VMEM)


def scalars():
    return pl.BlockSpec(memory_space=pltpu.SMEM)


def params(limit=LIMIT):
    return pltpu.CompilerParams(vmem_limit_bytes=limit)


def cost(flops, moved):
    return pl.CostEstimate(flops=flops, bytes_accessed=moved, transcendentals=0)


def tile(ref, level, index):
    return ref[level, :, index * LANES : (index + 1) * LANES]


def turned(value, lanes):
    lanes = lanes % LANES
    return pltpu.roll(value, lanes, 1) if lanes else value


def edge_strip(dest, band, oy, parent, parent_source):
    levels, rows, cols = parent.shape
    lane = iota((rows, LANES), 1)
    base = jnp.where(dest == 0, oy - 1, oy + band - 3) - lax.axis_index("gy") * cols
    total = jnp.zeros(lane.shape, jnp.float32)
    for ref, first in ((parent, STRIP_AT), (parent_source, STRIP_SOURCE_AT)):
        for level in range(levels):
            found = jnp.zeros(lane.shape, jnp.float32)
            for at in range(cols // LANES):
                place = lane + (at * LANES - base)
                found = jnp.where((place >= 0) & (place < 4), tile(ref, level, at), found)
            turn = (16384 + first + STRIDE * level - base) & (LANES - 1)
            total = total + pltpu.roll(found, turn, 1)
    return total


def pack_pair(nest, source, parent, parent_source, out, fine_buf, coarse_buf, sems):
    levels, rows, cols = nest.shape
    parent_rows, parent_cols = parent.shape[1:]
    right = lax.axis_index("gy") == 0
    loads = []
    for at, (ref, buf) in enumerate(
        (
            (parent, coarse_buf.at[0]),
            (parent_source, coarse_buf.at[1]),
            (nest, fine_buf.at[0]),
            (source, fine_buf.at[1]),
        )
    ):
        start = pl.multiple_of(jnp.where(right, ref.shape[2] - LANES, 0), LANES)
        loads.append(pltpu.make_async_copy(ref.at[:, :, pl.ds(start, LANES)], buf, sems.at[at]))
    for copy in loads:
        copy.start()

    def columns(value, count, to):
        first = jnp.where(right, LANES - count, 0)
        place = iota(value.shape, 1) - first
        value = jnp.where((place >= 0) & (place < count), value, 0.0)
        return pltpu.roll(value, (LANES + to - first) & (LANES - 1), 1)

    part = jnp.zeros((parent_rows, LANES), jnp.float32)
    loads[0].wait()
    loads[1].wait()
    for level in range(levels):
        base = STRIDE * level
        part = part + columns(coarse_buf[0, level], 1, base + PARENT_AT)
        part = part + columns(coarse_buf[0, level], 2, base + STRIP_AT)
        part = part + columns(coarse_buf[1, level], 2, base + STRIP_SOURCE_AT)
    total = jnp.zeros((rows, LANES), jnp.float32)
    loads[2].wait()
    loads[3].wait()
    for level in range(levels):
        base = STRIDE * level
        total = total + columns(fine_buf[0, level], 3, base)
        total = total + columns(fine_buf[1, level], 3, base + SOURCE_AT)
    out[...] = total
    out[:parent_rows, :] += part


def across_border(message, oy, parent_cols, me):
    c = iota(message.shape, 1) & (STRIDE - 1)
    place = jnp.where(me == 0, parent_cols + 1, 1) - oy
    total = jnp.zeros(message.shape, jnp.float32)
    for turn in (-1, 0, 2, 3):
        at = jnp.where(c >= STRIP_SOURCE_AT, c - STRIP_SOURCE_AT, c - STRIP_AT) - turn
        fits = (c >= STRIP_AT) & (at >= 0) & (at < 2) & (place == turn)
        total = total + jnp.where(fits, turned(message, turn), 0.0)
    return total


def pack_columns(parts, band, oy_hbm, nest, source, parent_hbm, parent_source_hbm, *rest):
    outs = rest[: parts - 1]
    old_buf, src_buf, parent, parent_source, oy_ref, sems, field_sems = rest[parts - 1 :]
    levels, rows, cols = nest.shape
    parent_cols = parent.shape[2]
    me = lax.axis_index("gy")
    sides = [1] if parts == 2 else [1, parts - 1]
    fields = [
        pltpu.make_async_copy(ref, buf, field_sems.at[at])
        for at, (ref, buf) in enumerate(
            ((oy_hbm, oy_ref), (parent_hbm, parent), (parent_source_hbm, parent_source))
        )
    ]
    for copy in fields:
        copy.start()
    copies = []
    for at, step in enumerate(sides):
        right = (me == 0) if parts == 2 else jnp.bool_(step == 1)
        start = pl.multiple_of(jnp.where(right, cols - LANES, 0), LANES)
        pair = [
            pltpu.make_async_copy(
                ref.at[:, :, pl.ds(start, LANES)], buf.at[at], sems.at[at, which]
            )
            for which, (ref, buf) in enumerate(((nest, old_buf), (source, src_buf)))
        ]
        for copy in pair:
            copy.start()
        copies.append((right, pair))
    for copy in fields:
        copy.wait()
    oy = oy_ref[0]
    lane = iota((parent.shape[1], LANES), 1)
    for step in range(1, parts):
        out = outs[step - 1]
        part = edge_strip(lax.rem(me + step, parts), band, oy, parent, parent_source)
        if step not in sides:
            out[...] = part
            continue
        at = sides.index(step)
        right, pair = copies[at]
        first = jnp.where(right, LANES - 3, 0)
        outer = jnp.where(right, LANES - 1, 0)
        for level in range(levels):
            edge = jnp.where(
                right, tile(parent, level, parent_cols // LANES - 1), tile(parent, level, 0)
            )
            edge = jnp.where(lane == outer, edge, 0.0)
            turn = (LANES + PARENT_AT + STRIDE * level - outer) & (LANES - 1)
            part = part + pltpu.roll(edge, turn, 1)
        for copy in pair:
            copy.wait()
        fine = iota((rows, LANES), 1) - first
        wanted = (fine >= 0) & (fine < 3)
        total = jnp.zeros((rows, LANES), jnp.float32)
        for level in range(levels):
            for buf, shift in ((old_buf, 0), (src_buf, SOURCE_AT)):
                value = jnp.where(wanted, buf[at, level], 0.0)
                turn = (LANES + STRIDE * level + shift - first) & (LANES - 1)
                total = total + pltpu.roll(value, turn, 1)
        out[...] = total
        out[: part.shape[0], :] += part


def three_terms(value):
    terms = []
    for _ in range(3):
        term = value.astype(jnp.bfloat16)
        terms.append(term)
        value = value - term.astype(jnp.float32)
    return terms


def select_rows(selector, value):
    selector = selector.astype(jnp.bfloat16)
    high, middle, low = (
        jnp.dot(selector, term, preferred_element_type=jnp.float32)
        for term in three_terms(value)
    )
    return high + (middle + low)


def select_columns(value, selector):
    selector = selector.astype(jnp.bfloat16)
    high, middle, low = (
        jnp.dot(term, selector, preferred_element_type=jnp.float32)
        for term in three_terms(value)
    )
    return high + (middle + low)


def sum_rows(ref):
    count = ref.shape[0] // RATIO
    first, second, third = (ref[pl.ds(at, count, RATIO), :] for at in range(RATIO))
    return first + second + third


def inner_substep(coefs, here, source, there):
    levels, rows, cols = here.shape
    sub = iota((8, cols), 0)
    tiles = rows // 8

    def one_level(level):
        ch = coefs[0, level]
        cv = coefs[1, level]
        centre = 1.0 - 4.0 * ch - 2.0 * cv
        below = jnp.maximum(level - 1, 0)
        above = jnp.minimum(level + 1, levels - 1)
        cv_below = jnp.where(level > 0, cv, 0.0)
        cv_above = jnp.where(level < levels - 1, cv, 0.0)

        def row_tile(t):
            t = t % tiles
            return here[level, 8 * t : 8 * t + 8, :]

        down_before = pltpu.roll(row_tile(-1), 1, 0)
        now = row_tile(0)
        up_now = pltpu.roll(now, 7, 0)
        for t in range(tiles):
            following = row_tile(t + 1)
            down_now = pltpu.roll(now, 1, 0)
            up_next = pltpu.roll(following, 7, 0)
            around = jnp.where(sub == 0, down_before, down_now) + jnp.where(
                sub == 7, up_next, up_now
            )
            around = around + (pltpu.roll(now, 1, 1) + pltpu.roll(now, cols - 1, 1))
            span = slice(8 * t, 8 * t + 8)
            stacked = cv_below * here[below, span, :] + cv_above * here[above, span, :]
            there[level, span, :] = centre * now + ch * around + (stacked + source[level, span, :])
            down_before, now, up_now = down_now, following, up_next

    def two_levels(pair, carry):
        one_level(2 * pair)
        one_level(2 * pair + 1)
        return carry

    lax.fori_loop(0, levels // 2, two_levels, 0)


def spread_coefs(parent_coefs, coefs, out):
    levels = out.shape[2]
    lane = iota((levels, LANES), 1)
    row = iota((levels, LANES), 0)
    for at, ref in enumerate((parent_coefs, coefs)):
        for which in range(2):
            packed = jnp.full(lane.shape, ref[which, 0], jnp.float32)
            rows = packed
            for level in range(1, levels):
                packed = jnp.where(lane >= STRIDE * level, ref[which, level], packed)
                rows = jnp.where(row == level, ref[which, level], rows)
            out[0, 2 * at + which] = packed
            out[1, 2 * at + which] = rows


def inner_first(
    band,
    oy_ref,
    parent_coefs,
    coefs,
    nest,
    source,
    parent,
    parent_source,
    strip,
    first,
    spread,
    oy_rows,
):
    oy = oy_ref[0]
    oy_rows[...] = jnp.full(oy_rows.shape, oy, jnp.int32)
    spread_coefs(parent_coefs, coefs, spread)
    strip[...] = edge_strip(lax.axis_index("gy"), band, oy, parent, parent_source)
    inner_substep(coefs, nest, source, first)


def own_windows(parts, nest, source, y_left, y_right, window_old, window_src):
    levels, rows, cols = nest.shape
    pieces = cols // LANES
    me = lax.axis_index("gy")
    for level in range(levels):
        for buf, field, shift in ((window_old, nest, 0), (window_src, source, SOURCE_AT)):
            for window, first, turn in ((0, 0, 3), (1, rows - 8, 5)):
                tiles = [
                    field[level, first : first + 8, piece * LANES : (piece + 1) * LANES]
                    for piece in range(pieces)
                ]
                tiles = with_columns(
                    tiles,
                    y_left[first : first + 8, :],
                    y_right[first : first + 8, :],
                    me,
                    parts,
                    STRIDE * level + shift,
                )
                for piece, value in enumerate(tiles):
                    buf[level, window, :, piece * LANES : (piece + 1) * LANES] = pltpu.roll(
                        value, turn, 0
                    )


def inner_rest(
    parts,
    coefs,
    nest,
    first,
    source,
    y_left,
    y_right,
    after_pack,
    third,
    packs,
    window_old,
    window_src,
    sums,
    second,
    split,
):
    levels, rows, cols = nest.shape
    own_windows(parts, nest, source, y_left, y_right, window_old, window_src)
    lane = iota((rows, LANES), 1)
    for at, ref in enumerate((nest, source)):
        left = jnp.zeros(lane.shape, jnp.float32)
        right = jnp.zeros(lane.shape, jnp.float32)
        for level in range(levels):
            value = jnp.where(lane < RIGHT_OWN, tile(ref, level, 0), 0.0)
            left = left + turned(value, STRIDE * level + LEFT_AT)
            value = jnp.where(lane >= LANES - RIGHT_OWN, tile(ref, level, cols // LANES - 1), 0.0)
            right = right + turned(value, STRIDE * level + RIGHT_OWN)
        packs[2 * at] = left
        packs[2 * at + 1] = right
    inner_substep(coefs, first, source, second)
    inner_substep(coefs, second, source, third)
    for level in range(levels):
        for piece in range(cols // LANES):
            split[piece, level * rows : (level + 1) * rows, :] = tile(third, level, piece)
    for piece in range(cols // LANES):
        sums[piece] = sum_rows(split.at[piece])


def with_columns(tiles, left, right, me, parts, place):
    lane = iota(left.shape, 1)
    from_right = turned(right, -place)
    from_left = turned(left, -3 - place)
    if parts == 2:
        tiles[0] = jnp.where((lane < 3) & (me == 0), from_right, tiles[0])
        tiles[-1] = jnp.where((lane >= LANES - 3) & (me == 1), from_left, tiles[-1])
        return tiles
    extra = jnp.where(lane < 3, from_right, jnp.where(lane >= LANES - 3, from_left, 0.0))
    return tiles + [extra]


def pack_rows(
    parts, old_top, old_end, src_top, src_end, par_top, par_end, own_strip, oy_rows, *rest
):
    columns = rest[: parts - 1]
    across, within, far, strip_out, both = rest[parts - 1 :]
    core = lax.axis_index("gz")
    up, down = both.at[core], both.at[1 - core]
    levels, _, cols = old_top.shape
    me = lax.axis_index("gy")
    left, right = columns[0], columns[-1]
    rows = left.shape[0]
    strip_rows = own_strip.shape[0]
    lane = iota((strip_rows, LANES), 1)
    strips = own_strip[...]
    if parts == 2:
        oy = jnp.concatenate([oy_rows[...]] * (strip_rows // 8), axis=0)
        strips = strips + across_border(left[:strip_rows, :], oy, par_top.shape[2], me)
    else:
        for message in columns:
            strips = strips + message[:strip_rows, :]
    c = lane & (STRIDE - 1)
    strips = jnp.where(c >= STRIP_AT, strips, 0.0)
    strips = jnp.where(c == PARENT_AT, left[:strip_rows, :], strips)
    strips = jnp.where(c == PARENT_AT + 1, turned(right[:strip_rows, :], 1), strips)
    strip_out[...] = strips
    far[...] = strips[:8]
    pieces = cols // LANES
    for out, old, src, first, at, src_at in (
        (up, old_end, src_end, rows - 8, 5, 6),
        (down, old_top, src_top, 0, 0, 0),
    ):
        y_left = left[first : first + 8, :]
        y_right = right[first : first + 8, :]
        for level in range(levels):
            for ref, shift, row, count, base in (
                (old, 0, at, 3, 0),
                (src, SOURCE_AT, src_at, 2, SOURCE_ROW),
            ):
                tiles = [tile(ref, level, piece) for piece in range(pieces)]
                tiles = with_columns(
                    tiles, y_left, y_right, me, parts, STRIDE * level + shift
                )
                for piece, value in enumerate(tiles):
                    out[
                        base + count * level : base + count * (level + 1),
                        piece * LANES : (piece + 1) * LANES,
                    ] = value[row : row + count]
    parent_cols = par_top.shape[2]
    for level in range(levels):
        up[TAIL_ROW + level : TAIL_ROW + level + 1, :parent_cols] = par_end[level, 7:8, :]
        down[TAIL_ROW + level : TAIL_ROW + level + 1, :parent_cols] = par_top[level, 0:1, :]
    up[TAIL_ROW : TAIL_ROW + 8, parent_cols : parent_cols + LANES] = strips[strip_rows - 8 :]
    down[TAIL_ROW : TAIL_ROW + 8, parent_cols : parent_cols + LANES] = strips[:8]
    down[TAIL_ROW + 8 : TAIL_ROW + 16, :LANES] = strips[8:16]
    down[TAIL_ROW + 8 : TAIL_ROW + 16, LANES : 2 * LANES] = strips[16:24]
    within[...] = both[0]
    across[...] = both[1]


def edges(
    parts,
    parent_cols,
    ox_ref,
    spread,
    sums,
    packs,
    window_old,
    window_src,
    strips,
    across,
    within,
    far,
    y_left,
    y_right,
    sides,
    windows,
    coarse_out,
    far_out,
    both,
    ping,
    pong,
    src,
):
    levels = ping.shape[0]
    width = ping.shape[3]
    rows = sides.shape[1]
    cols = sums.shape[0] * LANES
    pieces = cols // LANES
    me = lax.axis_index("gy")
    core = lax.axis_index("gz")
    both[0] = within[...]
    both[1] = across[...]
    before, after = both.at[1 - core], both.at[core]
    is_south = me == 0
    is_north = me == parts - 1

    far_out[...] = far[...]
    sub = iota((8, LANES), 0)
    old = jnp.concatenate(
        [
            strips[...],
            after[TAIL_ROW : TAIL_ROW + 8, parent_cols : parent_cols + LANES],
            after[TAIL_ROW + 8 : TAIL_ROW + 16, :LANES],
            after[TAIL_ROW + 8 : TAIL_ROW + 16, LANES : 2 * LANES],
            jnp.where(
                sub == 7,
                before[TAIL_ROW : TAIL_ROW + 8, parent_cols : parent_cols + LANES],
                0.0,
            ),
        ],
        axis=0,
    )
    count = old.shape[0]

    def packed_coef(which, height):
        return jnp.concatenate([spread[0, which]] * (height // 8), axis=0)

    def stacked(value):
        lane = iota(value.shape, 1)
        below = jnp.where(lane >= STRIDE, turned(value, STRIDE), 0.0)
        return below + jnp.where(lane < STRIDE * (levels - 1), turned(value, -STRIDE), 0.0)

    def around(value):
        return (
            pltpu.roll(value, 1, 0)
            + pltpu.roll(value, value.shape[0] - 1, 0)
            + turned(value, 1)
            + turned(value, -1)
        )

    diff = (
        packed_coef(0, count) * (around(old) - 4.0 * old)
        + packed_coef(1, count) * (stacked(old) - 2.0 * old)
        + turned(old, STRIP_AT - STRIP_SOURCE_AT)
    )
    index = iota((rows + 16, count), 0)
    nest_row = jnp.where(index < rows, index, jnp.where(index < rows + 8, index - rows - 3, index - 13))
    parent_row = ((nest_row + 3) * 171 >> 9) - 1 + ox_ref[0]
    pick = (iota((rows + 16, count), 1) == parent_row).astype(jnp.float32)
    picked = select_rows(pick, jnp.concatenate([old, diff], axis=1))
    picked_old, picked_diff = picked[:, :LANES], picked[:, LANES:]

    lane = iota((rows, LANES), 1)
    c = lane & (STRIDE - 1)
    rim_first = jnp.where(is_south, LEFT_AT, RIGHT_OWN - RIM)
    in_rim = (c >= rim_first) & (c < rim_first + RIM)
    at = lane - c + STRIP_AT + jnp.where(c >= rim_first + 3, 2, 1)
    rim_old = jnp.take_along_axis(picked_old[:rows], at, axis=1)
    rim_diff = jnp.take_along_axis(picked_diff[:rows], at, axis=1)
    ch = packed_coef(2, rows)
    cv = packed_coef(3, rows)
    centre = 1.0 - 4.0 * ch - 2.0 * cv
    left = jnp.where(c < 3, y_left[...], packs[0])
    left_src = jnp.where(c < 3, turned(y_left[...], -SOURCE_AT), packs[2])
    right = jnp.where(c >= RIGHT_OWN, turned(y_right[...], RIGHT_OWN), packs[1])
    right_src = jnp.where(c >= RIGHT_OWN, turned(y_right[...], RIGHT_OWN - SOURCE_AT), packs[3])
    for side, (value, forcing, rim) in enumerate(
        (
            (left, left_src, in_rim & is_south),
            (right, right_src, in_rim & is_north),
        )
    ):
        for substep in range(1, SUBSTEPS + 1):
            value = centre * value + ch * around(value) + (cv * stacked(value) + forcing)
            value = jnp.where(rim, rim_old + (substep / SUBSTEPS) * rim_diff, value)
        sides[side] = value

    sub = iota((8, width), 0)
    lane = iota((8, LANES), 1)
    ping[...] = window_old[...]
    src[...] = window_src[...]
    for level in range(levels):
        for buf, n, base in ((ping, 3, 0), (src, 2, SOURCE_ROW)):
            rows_of = slice(base + n * level, base + n * (level + 1))
            buf[level, 0, 3 - n : 3, :] = before[rows_of, :]
            buf[level, 1, 5 : 5 + n, :] = after[rows_of, :]
    rim_first = jnp.where(is_south, 0, LANES - RIM)
    column = STRIP_AT + jnp.where((lane >= rim_first + 3) & (lane < rim_first + RIM), 2, 1)
    rims = {}
    for level in range(levels):
        for window in range(2):
            span = slice(rows + 8 * window, rows + 8 * window + 8)
            at = column + STRIDE * level
            rims[level, window] = (
                jnp.take_along_axis(picked_old[span], at, axis=1),
                jnp.take_along_axis(picked_diff[span], at, axis=1),
            )
    for substep in range(1, SUBSTEPS + 1):
        here, there = (ping, pong) if substep % 2 else (pong, ping)
        there = windows if substep == SUBSTEPS else there
        low = 0 if substep == SUBSTEPS or parts > 2 else 3
        south = (lane >= low) & (lane < RIM) & is_south
        north = (lane >= LANES - RIM) & (lane < LANES - low) & is_north
        weight = substep / SUBSTEPS
        for level in range(levels):
            c_h, c_v = (
                jnp.concatenate([spread[1, which, level : level + 1, :]] * (width // LANES), axis=1)
                for which in (2, 3)
            )
            c_0 = 1.0 - 4.0 * c_h - 2.0 * c_v
            for window in range(2):
                now = here[level, window]
                up = pltpu.roll(now, 1, 0)
                down = pltpu.roll(now, 7, 0)
                if substep == 1:
                    beyond_row = window_old[level, window]
                    if window == 0:
                        down = jnp.where(sub == 7, pltpu.roll(beyond_row, 7, 0), down)
                    else:
                        up = jnp.where(sub == 0, pltpu.roll(beyond_row, 1, 0), up)
                beside = pltpu.roll(now, 1, 1) + pltpu.roll(now, width - 1, 1)
                value = c_0 * now + c_h * ((up + down) + beside) + src[level, window]
                if level > 0:
                    value = value + c_v * here[level - 1, window]
                if level < levels - 1:
                    value = value + c_v * here[level + 1, window]
                rim_o, rim_d = rims[level, window]
                rim = rim_o + weight * rim_d
                for piece in range(width // LANES):
                    span = slice(piece * LANES, (piece + 1) * LANES)
                    part = value[:, span]
                    if piece == 0:
                        part = jnp.where(south, rim, part)
                    if piece == pieces - 1:
                        part = jnp.where(north, rim, part)
                    there[level, window, :, span] = part

    parent_rows = rows // RATIO
    lane = iota((parent_rows, LANES), 1)
    row = iota((parent_rows, LANES), 0)
    side_sums = [sum_rows(sides.at[side]) for side in range(2)]
    replaced = [[] for _ in range(pieces)]
    for level in range(levels):
        span = slice(level * parent_rows, (level + 1) * parent_rows)
        top = windows[level, 0, 3:4, :] + windows[level, 0, 4:5, :] + windows[level, 0, 5:6, :]
        end = windows[level, 1, 2:3, :] + windows[level, 1, 3:4, :] + windows[level, 1, 4:5, :]
        for piece in range(pieces):
            value = sums[piece, span, :]
            if piece == 0:
                fixed = turned(side_sums[0], -STRIDE * level - LEFT_AT)
                value = jnp.where(lane < FIXED, fixed, value)
            if piece == pieces - 1:
                fixed = turned(side_sums[1], -STRIDE * level - RIGHT_OWN)
                value = jnp.where(lane >= LANES - FIXED, fixed, value)
            across_piece = slice(piece * LANES, (piece + 1) * LANES)
            value = jnp.where(row == 0, top[:, across_piece], value)
            value = jnp.where(row == parent_rows - 1, end[:, across_piece], value)
            replaced[piece].append(value)
    foot = cols // RATIO
    offset = iota((cols, foot), 0) - RATIO * iota((cols, foot), 1)
    gather = ((offset >= 0) & (offset < RATIO)).astype(jnp.float32)
    means = select_columns(
        jnp.concatenate([jnp.concatenate(values, axis=0) for values in replaced], axis=1), gather
    ) * (1.0 / 9.0)
    coarse_out[...] = means.reshape(coarse_out.shape)


def put_together(third, sides, windows, result):
    levels, rows, cols = third.shape
    pieces = cols // LANES
    lane = iota((rows, LANES), 1)
    sub = iota((8, cols), 0)
    for level in range(levels):
        fixed = turned(sides[0], -STRIDE * level - LEFT_AT)
        result[level, :, :LANES] = jnp.where(lane < FIXED, fixed, tile(third, level, 0))
        for piece in range(1, pieces - 1):
            result[level, :, piece * LANES : (piece + 1) * LANES] = tile(third, level, piece)
        fixed = turned(sides[1], -STRIDE * level - RIGHT_OWN)
        result[level, :, cols - LANES :] = jnp.where(
            lane >= LANES - FIXED, fixed, tile(third, level, pieces - 1)
        )
        top = pltpu.roll(windows[level, 0, :, :cols], 5, 0)
        result[level, :8, :] = jnp.where(sub < 3, top, result[level, :8, :])
        end = pltpu.roll(windows[level, 1, :, :cols], 3, 0)
        result[level, rows - 8 :, :] = jnp.where(sub >= 5, end, result[level, rows - 8 :, :])


def parent_step(
    parts,
    band,
    ox_ref,
    oy_ref,
    spread,
    third,
    sides,
    windows,
    parent,
    source,
    within,
    across,
    y_left,
    y_right,
    out,
    nest_out,
    late,
    tail,
    result,
    sem,
):
    put_together(third, sides, windows, result)
    store = pltpu.make_async_copy(result, nest_out, sem)
    store.start()
    core = lax.axis_index("gz")
    levels, rows, cols = parent.shape
    tail[0] = within[TAIL_ROW : TAIL_ROW + levels, : cols + LANES]
    tail[1] = across[TAIL_ROW : TAIL_ROW + levels, : cols + LANES]
    me = lax.axis_index("gy")
    is_last = ox_ref[0] == rows - 1
    wide = iota((1, cols), 1)
    south = (wide == oy_ref[0] + 2 - me * cols) & is_last
    north = (wide == oy_ref[0] + band - 3 - me * cols) & is_last
    row = iota((rows, cols), 0)
    lane = iota((rows, cols), 1)
    has_left = me > 0
    has_right = me < parts - 1
    left = y_left[:rows, :]
    right = y_right[:rows, :]
    zero = jnp.zeros((rows, cols), jnp.float32)
    for level in range(levels):
        now = parent[level]
        at = STRIDE * level + PARENT_AT
        from_left = left[:, at : at + 1]
        from_right = right[:, at : at + 1]
        top = tail[1 - core, level : level + 1, :cols]
        end = tail[core, level : level + 1, :cols]
        around = (
            jnp.where(row == 0, top, pltpu.roll(now, 1, 0))
            + jnp.where(row == rows - 1, end, pltpu.roll(now, rows - 1, 0))
            + jnp.where(
                lane == 0, jnp.where(has_left, from_left, 0.0), pltpu.roll(now, 1, 1)
            )
            + jnp.where(
                lane == cols - 1,
                jnp.where(has_right, from_right, 0.0),
                pltpu.roll(now, cols - 1, 1),
            )
        )
        stacked = (parent[level - 1] if level > 0 else zero) + (
            parent[level + 1] if level < levels - 1 else zero
        )
        ch, cv = (
            jnp.concatenate([spread[1, which, level : level + 1, :]] * (cols // LANES), axis=1)
            for which in (0, 1)
        )
        out[level] = (
            (1.0 - 4.0 * ch - 2.0 * cv) * now + ch * around + (cv * stacked + source[level])
        )
        at = cols + STRIDE * level + PARENT_AT
        before_end = jnp.where(
            wide == 0, tail[core, 0:1, at : at + 1], pltpu.roll(end, 1, 1)
        )
        after_end = jnp.where(
            wide == cols - 1, tail[core, 0:1, at + 1 : at + 2], pltpu.roll(end, cols - 1, 1)
        )
        nest_ch = spread[1, 2, level : level + 1, :]
        nest_ch = jnp.concatenate([nest_ch] * (cols // LANES), axis=1)
        share = nest_ch * nest_ch * ch * (1.0 / SUBSTEPS)
        late[level : level + 1, :] = (share * (1.0 / (RATIO * RATIO))) * (
            jnp.where(south, before_end, 0.0) + jnp.where(north, after_end, 0.0)
        )
    store.wait()


def merge(parts, band, ox_ref, oy_ref, late, step, nest, spread, beyond, *rest):
    arrived = rest[1 : 2 * parts]
    out, nest_out, joined, corner, sem, merged, out_sems = rest[2 * parts :]
    levels, rows, cols = step.shape
    foot = rest[0].shape[2]
    me = lax.axis_index("gy")

    @pl.when((ox_ref[0] == rows - 1) & ((me == 0) | (me == parts - 1)))
    def _():
        nest_rows, nest_cols = nest.shape[1:]
        first = pl.multiple_of(jnp.where(me == 0, 0, nest_cols - LANES), LANES)
        place = (slice(None), pl.ds(nest_rows - 8, 8), pl.ds(first, LANES))
        load = pltpu.make_async_copy(nest_out.at[place], corner, sem)
        load.start()
        load.wait()
        sub = iota((8, LANES), 0)
        lane = iota((8, LANES), 1)
        cell = (sub == 7) & (lane == jnp.where(me == 0, RIM, LANES - RIM - 1))
        for level in range(levels):
            at = STRIDE * level + STRIP_AT
            value = jnp.where(me == 0, beyond[0:1, at + 2 : at + 3], beyond[0:1, at + 1 : at + 2])
            nest_ch = spread[1, 2, level : level + 1, :]
            share = nest_ch * nest_ch * spread[1, 0, level : level + 1, :] * (1.0 / SUBSTEPS)
            corner[level] += jnp.where(cell, share * value, 0.0)
        again = pltpu.make_async_copy(corner, nest_out.at[place], sem)
        again.start()
        again.wait()

    ox = ox_ref[0]
    oy = oy_ref[0]
    joined[0, :, rows:, :] = rest[0][...]
    if parts == 2:
        mixed, straight, other = arrived
        joined[0, :, :rows, :] = straight[...]
        joined[1, :, :rows, :] = jnp.where(me == 0, mixed[...], other[...])
        joined[1, :, rows:, :] = jnp.where(me == 0, other[...], mixed[...])
    else:
        for k in range(parts):
            joined[k, :, :rows, :] = arrived[k][...]
        for k in range(1, parts):
            joined[k, :, rows:, :] = arrived[parts + k - 1][...]
    lane = iota((rows, LANES), 1)
    row = iota((rows, LANES), 0)
    stores = []
    for level in range(levels):
        values = [tile(step, level, piece) for piece in range(cols // LANES)]
        for k in range(parts):
            source = lax.rem(me + parts - k, parts)
            block = joined[k, level, pl.ds(rows - ox, rows), :]
            begin = oy + source * foot - me * cols
            block = pltpu.roll(block, (16384 + begin) & (LANES - 1), 1)
            low = jnp.maximum(source * foot, 2)
            high = jnp.minimum((source + 1) * foot, band - 2)
            for piece in range(cols // LANES):
                at = lane + (piece * LANES + me * cols - oy)
                values[piece] = jnp.where((at >= low) & (at < high), block, values[piece])
        for piece, value in enumerate(values):
            term = late[level : level + 1, piece * LANES : (piece + 1) * LANES]
            value = value + jnp.where(row == rows - 2, term, 0.0)
            merged[level, :, piece * LANES : (piece + 1) * LANES] = value
        stores.append(pltpu.make_async_copy(merged.at[level], out.at[level], out_sems.at[level]))
        stores[-1].start()
    for copy in stores:
        copy.wait()


def shifted(value, axis, steps):
    count = lax.axis_size(axis)
    pairs = [(source, (source + steps) % count) for source in range(count)]
    return lax.ppermute(value, axis, pairs)


def shards(
    parent_old, parent_source, parent_coefs, nest_old, nest_source, nest_coefs, offset_x, offset_y
):
    parts = lax.axis_size("gy")
    along = ("gx", "gz")
    levels, parent_rows, parent_cols = parent_old.shape
    _, rows, cols = nest_old.shape
    foot = cols // RATIO
    band = foot * parts
    width = cols if parts == 2 else cols + LANES
    height = TAIL_ROW + 16
    f32 = jnp.float32
    shape = jax.ShapeDtypeStruct
    anywhere = pl.BlockSpec(memory_space=pl.ANY)
    in_hbm = pl.BlockSpec(memory_space=pltpu.HBM)
    sides = 1 if parts == 2 else 2
    if parts == 2:
        packed = [
            pl.pallas_call(
                pack_pair,
                out_shape=VMEM((rows, LANES), f32),
                in_specs=[in_hbm] * 4,
                out_specs=whole(),
                scratch_shapes=[
                    VMEM((2, levels, rows, LANES), f32),
                    VMEM((2, levels, parent_rows, LANES), f32),
                    pltpu.SemaphoreType.DMA((4,)),
                ],
                compiler_params=params(MOST),
                cost_estimate=cost(200000, 800000),
                name="pack_pair",
            )(nest_old, nest_source, parent_old, parent_source)
        ]
    else:
        packed = pl.pallas_call(
            functools.partial(pack_columns, parts, band),
            out_shape=[
                shape((rows if k in (1, parts - 1) else parent_rows, LANES), f32)
                for k in range(1, parts)
            ],
            in_specs=[in_hbm] * 5,
            out_specs=[whole()] * (parts - 1),
            scratch_shapes=[
                VMEM((sides, levels, rows, LANES), f32),
                VMEM((sides, levels, rows, LANES), f32),
                VMEM(parent_old.shape, f32),
                VMEM(parent_old.shape, f32),
                pltpu.SMEM(offset_y.shape, jnp.int32),
                pltpu.SemaphoreType.DMA((sides, 2)),
                pltpu.SemaphoreType.DMA((3,)),
            ],
            compiler_params=params(MOST),
            cost_estimate=cost(200000, 1000000),
            name="pack_columns",
        )(offset_y, nest_old, nest_source, parent_old, parent_source)
    columns = [shifted(packed[k - 1], "gy", k) for k in range(1, parts)]
    own_strip, first, spread, oy_rows = pl.pallas_call(
        functools.partial(inner_first, band),
        out_shape=[
            shape((parent_rows, LANES), f32),
            shape(nest_old.shape, f32),
            shape((2, 4, levels, LANES), f32),
            shape((8, LANES), jnp.int32),
        ],
        in_specs=[scalars()] * 3 + [whole()] * 4,
        out_specs=[whole()] * 4,
        compiler_params=params(),
        cost_estimate=cost(4000000, 3000000),
        name="inner_first",
    )(
        offset_y,
        parent_coefs,
        nest_coefs,
        nest_old,
        nest_source,
        parent_old,
        parent_source,
    )

    def block(ref, last):
        count = ref.shape[1] // 8 - 1 if last else 0
        return pl.BlockSpec((levels, 8, ref.shape[2]), lambda i, c=count: (0, c, 0))

    def full(extent):
        return pl.BlockSpec(extent, lambda i: (0,) * len(extent))

    outs = [
        shape((height, width), f32),
        shape((height, width), f32),
        shape((8, LANES), f32),
        shape((parent_rows, LANES), f32),
    ]
    across, within, far, strips = pl.pallas_call(
        functools.partial(pack_rows, parts),
        out_shape=outs,
        grid=(1,),
        in_specs=[
            block(nest_old, False),
            block(nest_old, True),
            block(nest_old, False),
            block(nest_old, True),
            block(parent_old, False),
            block(parent_old, True),
            full(own_strip.shape),
            full(oy_rows.shape),
        ]
        + [full(message.shape) for message in columns],
        out_specs=[full(out.shape) for out in outs],
        scratch_shapes=[VMEM((2, height, width), f32)],
        compiler_params=params(),
        cost_estimate=cost(100000, 700000),
        name="pack_rows",
    )(nest_old, nest_old, nest_source, nest_source, parent_old, parent_old, own_strip, oy_rows, *columns)
    across = swapped(across, 1)
    within = swapped(within, 0)
    third, packs, window_old, window_src, sums = pl.pallas_call(
        functools.partial(inner_rest, parts),
        out_shape=[
            shape(nest_old.shape, f32),
            shape((4, rows, LANES), f32),
            shape((levels, 2, 8, width), f32),
            shape((levels, 2, 8, width), f32),
            shape((cols // LANES, levels * parent_rows, LANES), f32),
        ],
        in_specs=[scalars()] + [whole()] * 5 + [anywhere],
        out_specs=[whole()] * 5,
        scratch_shapes=[
            VMEM(nest_old.shape, f32),
            VMEM((cols // LANES, levels * rows, LANES), f32),
        ],
        compiler_params=params(),
        cost_estimate=cost(8000000, 6000000),
        name="inner_rest",
    )(nest_coefs, nest_old, first, nest_source, columns[0], columns[-1], strips)
    sides, windows, coarse, far = pl.pallas_call(
        functools.partial(edges, parts, parent_cols),
        out_shape=[
            shape((2, rows, LANES), f32),
            shape((levels, 2, 8, width), f32),
            shape((levels, parent_rows, foot), f32),
            shape((8, LANES), f32),
        ],
        in_specs=[scalars()] + [whole()] * 11,
        out_specs=[whole()] * 4,
        scratch_shapes=[
            VMEM((2, height, width), f32),
            VMEM((levels, 2, 8, width), f32),
            VMEM((levels, 2, 8, width), f32),
            VMEM((levels, 2, 8, width), f32),
        ],
        compiler_params=params(),
        cost_estimate=cost(4000000, 3000000),
        name="edges",
    )(
        offset_x,
        spread,
        sums,
        packs,
        window_old,
        window_src,
        strips,
        across,
        within,
        far,
        columns[0],
        columns[-1],
    )
    if parts == 2:
        arrived = [
            shifted_both(coarse, 1, (0, 1)),
            shifted(coarse, along, 1),
            shifted_both(coarse, 1, (1, 0)),
        ]
    else:
        arrived = [shifted(coarse, along, 1)]
        arrived += [shifted_both(coarse, k) for k in range(1, parts)]
        arrived += [shifted(coarse, "gy", k) for k in range(1, parts)]
    beyond = shifted(far, along, -2)
    step, nest_stored, late = pl.pallas_call(
        functools.partial(parent_step, parts, band),
        out_shape=[
            shape(parent_old.shape, f32),
            shape(nest_old.shape, f32),
            shape((levels, parent_cols), f32),
        ],
        in_specs=[scalars()] * 2 + [whole()] * 10,
        out_specs=[whole(), in_hbm, whole()],
        scratch_shapes=[
            VMEM((2, levels, parent_cols + LANES), f32),
            VMEM(nest_old.shape, f32),
            pltpu.SemaphoreType.DMA,
        ],
        compiler_params=params(),
        cost_estimate=cost(800000, 2500000),
        name="parent_step",
    )(
        offset_x,
        offset_y,
        spread,
        third,
        sides,
        windows,
        parent_old,
        parent_source,
        within,
        across,
        columns[0],
        columns[-1],
    )
    parent_new, nest_new = pl.pallas_call(
        functools.partial(merge, parts, band),
        out_shape=[shape(parent_old.shape, f32), shape(nest_old.shape, f32)],
        in_specs=[scalars()] * 2 + [whole()] * 2 + [in_hbm] + [whole()] * (2 + 2 * parts),
        out_specs=[in_hbm, in_hbm],
        scratch_shapes=[
            VMEM((parts, levels, 2 * parent_rows, foot), f32),
            VMEM((levels, 8, LANES), f32),
            pltpu.SemaphoreType.DMA,
            VMEM(parent_old.shape, f32),
            pltpu.SemaphoreType.DMA((levels,)),
        ],
        input_output_aliases={4: 1},
        compiler_params=params(),
        cost_estimate=cost(200000, 800000),
        name="merge",
    )(offset_x, offset_y, late, step, nest_stored, spread, beyond, coarse, *arrived)
    return (parent_new, nest_new)


def swapped(value, first):
    along = ("gx", "gz")
    count = lax.axis_size(along)
    pairs = []
    for at in range(first, count, 2):
        pairs += [(at, (at + 1) % count), ((at + 1) % count, at)]
    return lax.ppermute(value, along, pairs)


def shifted_both(value, steps, rows=None):
    sizes = [lax.axis_size(axis) for axis in ("gx", "gy", "gz")]
    gx, gy, gz = sizes
    pairs = []
    for x in range(gx):
        for y in range(gy):
            for z in range(gz):
                place = (x * gz + z + (1 if rows is None else rows[y])) % (gx * gz)
                target = (place // gz * gy + (y + steps) % gy) * gz + place % gz
                pairs.append(((x * gy + y) * gz + z, target))
    return lax.ppermute(value, ("gx", "gy", "gz"), pairs)


def solution(mesh):
    return jax.shard_map(
        shards,
        mesh=mesh,
        in_specs=(
            P(None, ("grp", "gx", "gz"), "gy"),
            P(None, ("grp", "gx", "gz"), "gy"),
            P(),
            P(None, ("grp", "gx", "gz"), "gy"),
            P(None, ("grp", "gx", "gz"), "gy"),
            P(),
            P("grp"),
            P("grp"),
        ),
        out_specs=(P(None, ("grp", "gx", "gz"), "gy"), P(None, ("grp", "gx", "gz"), "gy")),
        check_vma=False,
    )
```

```python
import functools

import jax
import jax.numpy as jnp
from jax import lax
from jax.experimental import pallas as pl
from jax.experimental.pallas import tpu as pltpu
from jax.sharding import PartitionSpec as P

RATIO = 3
SUBSTEPS = 3
RIM = 6
LANES = 128
STRIDE = 16
SOURCE_AT = 3
PARENT_AT = 6
STRIP_AT = 8
STRIP_SOURCE_AT = 12
SOURCE_ROW = 24
TAIL_ROW = 40
FIXED = 8
LEFT_AT = 3
RIGHT_OWN = STRIDE - 3
VMEM = pltpu.VMEM
LIMIT = 24 * 1024 * 1024
MOST = 54 * 1024 * 1024


def iota(shape, dim):
    return lax.broadcasted_iota(jnp.int32, shape, dim)


def whole():
    return pl.BlockSpec(memory_space=VMEM)


def scalars():
    return pl.BlockSpec(memory_space=pltpu.SMEM)


def params(limit=LIMIT):
    return pltpu.CompilerParams(vmem_limit_bytes=limit)


def cost(flops, moved):
    return pl.CostEstimate(flops=flops, bytes_accessed=moved, transcendentals=0)


def tile(ref, level, index):
    return ref[level, :, index * LANES : (index + 1) * LANES]


def turned(value, lanes):
    lanes = lanes % LANES
    return pltpu.roll(value, lanes, 1) if lanes else value


def edge_strip(dest, band, oy, parent, parent_source):
    levels, rows, cols = parent.shape
    lane = iota((rows, LANES), 1)
    base = jnp.where(dest == 0, oy - 1, oy + band - 3) - lax.axis_index("gy") * cols
    total = jnp.zeros(lane.shape, jnp.float32)
    for ref, first in ((parent, STRIP_AT), (parent_source, STRIP_SOURCE_AT)):
        for level in range(levels):
            found = jnp.zeros(lane.shape, jnp.float32)
            for at in range(cols // LANES):
                place = lane + (at * LANES - base)
                found = jnp.where((place >= 0) & (place < 4), tile(ref, level, at), found)
            turn = (16384 + first + STRIDE * level - base) & (LANES - 1)
            total = total + pltpu.roll(found, turn, 1)
    return total


def pack_pair(nest, source, parent, parent_source, out, fine_buf, coarse_buf, sems):
    levels, rows, cols = nest.shape
    parent_rows, parent_cols = parent.shape[1:]
    right = lax.axis_index("gy") == 0
    half = levels // 2
    halves = [range(half), range(half, levels)]

    def load(at, ref, buf):
        start = pl.multiple_of(jnp.where(right, ref.shape[2] - LANES, 0), LANES)
        copy = pltpu.make_async_copy(ref.at[:, :, pl.ds(start, LANES)], buf, sems.at[at])
        copy.start()
        return copy

    loads = []
    for part in range(2):
        span = pl.ds(part * half, half)
        for at, ref in enumerate((nest, source)):
            loads.append(load(2 * part + at, ref.at[span], fine_buf.at[at, span]))
    for at, ref in enumerate((parent, parent_source)):
        loads.append(load(4 + at, ref, coarse_buf.at[at]))

    def columns(value, count, to):
        first = jnp.where(right, LANES - count, 0)
        place = iota(value.shape, 1) - first
        value = jnp.where((place >= 0) & (place < count), value, 0.0)
        return pltpu.roll(value, (LANES + to - first) & (LANES - 1), 1)

    total = jnp.zeros((rows, LANES), jnp.float32)
    for part in range(2):
        loads[2 * part].wait()
        loads[2 * part + 1].wait()
        for level in halves[part]:
            base = STRIDE * level
            total = total + columns(fine_buf[0, level], 3, base)
            total = total + columns(fine_buf[1, level], 3, base + SOURCE_AT)
    part = total[:parent_rows]
    loads[4].wait()
    loads[5].wait()
    for level in range(levels):
        base = STRIDE * level
        part = part + columns(coarse_buf[0, level], 1, base + PARENT_AT)
        part = part + columns(coarse_buf[0, level], 2, base + STRIP_AT)
        part = part + columns(coarse_buf[1, level], 2, base + STRIP_SOURCE_AT)
    out[:parent_rows, :] = part
    out[parent_rows:, :] = total[parent_rows:]


def across_border(message, oy, parent_cols, me):
    c = iota(message.shape, 1) & (STRIDE - 1)
    place = jnp.where(me == 0, parent_cols + 1, 1) - oy
    total = jnp.zeros(message.shape, jnp.float32)
    for turn in (-1, 0, 2, 3):
        at = jnp.where(c >= STRIP_SOURCE_AT, c - STRIP_SOURCE_AT, c - STRIP_AT) - turn
        fits = (c >= STRIP_AT) & (at >= 0) & (at < 2) & (place == turn)
        total = total + jnp.where(fits, turned(message, turn), 0.0)
    return total


def pack_columns(parts, band, oy_hbm, nest, source, parent_hbm, parent_source_hbm, *rest):
    outs = rest[: parts - 1]
    old_buf, src_buf, parent, parent_source, oy_ref, sems, field_sems = rest[parts - 1 :]
    levels, rows, cols = nest.shape
    parent_cols = parent.shape[2]
    me = lax.axis_index("gy")
    sides = [1] if parts == 2 else [1, parts - 1]
    fields = [
        pltpu.make_async_copy(ref, buf, field_sems.at[at])
        for at, (ref, buf) in enumerate(
            ((oy_hbm, oy_ref), (parent_hbm, parent), (parent_source_hbm, parent_source))
        )
    ]
    for copy in fields:
        copy.start()
    copies = []
    for at, step in enumerate(sides):
        right = (me == 0) if parts == 2 else jnp.bool_(step == 1)
        start = pl.multiple_of(jnp.where(right, cols - LANES, 0), LANES)
        pair = [
            pltpu.make_async_copy(
                ref.at[:, :, pl.ds(start, LANES)], buf.at[at], sems.at[at, which]
            )
            for which, (ref, buf) in enumerate(((nest, old_buf), (source, src_buf)))
        ]
        for copy in pair:
            copy.start()
        copies.append((right, pair))
    for copy in fields:
        copy.wait()
    oy = oy_ref[0]
    lane = iota((parent.shape[1], LANES), 1)
    for step in range(1, parts):
        out = outs[step - 1]
        part = edge_strip(lax.rem(me + step, parts), band, oy, parent, parent_source)
        if step not in sides:
            out[...] = part
            continue
        at = sides.index(step)
        right, pair = copies[at]
        first = jnp.where(right, LANES - 3, 0)
        outer = jnp.where(right, LANES - 1, 0)
        for level in range(levels):
            edge = jnp.where(
                right, tile(parent, level, parent_cols // LANES - 1), tile(parent, level, 0)
            )
            edge = jnp.where(lane == outer, edge, 0.0)
            turn = (LANES + PARENT_AT + STRIDE * level - outer) & (LANES - 1)
            part = part + pltpu.roll(edge, turn, 1)
        for copy in pair:
            copy.wait()
        fine = iota((rows, LANES), 1) - first
        wanted = (fine >= 0) & (fine < 3)
        total = jnp.zeros((rows, LANES), jnp.float32)
        for level in range(levels):
            for buf, shift in ((old_buf, 0), (src_buf, SOURCE_AT)):
                value = jnp.where(wanted, buf[at, level], 0.0)
                turn = (LANES + STRIDE * level + shift - first) & (LANES - 1)
                total = total + pltpu.roll(value, turn, 1)
        out[...] = total
        out[: part.shape[0], :] += part


def three_terms(value):
    terms = []
    for _ in range(3):
        term = value.astype(jnp.bfloat16)
        terms.append(term)
        value = value - term.astype(jnp.float32)
    return terms


def select_rows(selector, value):
    selector = selector.astype(jnp.bfloat16)
    high, middle, low = (
        jnp.dot(selector, term, preferred_element_type=jnp.float32)
        for term in three_terms(value)
    )
    return high + (middle + low)


def select_columns(value, selector):
    selector = selector.astype(jnp.bfloat16)
    high, middle, low = (
        jnp.dot(term, selector, preferred_element_type=jnp.float32)
        for term in three_terms(value)
    )
    return high + (middle + low)


def sum_rows(ref):
    count = ref.shape[0] // RATIO
    first, second, third = (ref[pl.ds(at, count, RATIO), :] for at in range(RATIO))
    return first + second + third


def inner_substep(coefs, here, source, there):
    levels, rows, cols = here.shape
    sub = iota((8, cols), 0)
    tiles = rows // 8

    def one_level(level):
        ch = coefs[0, level]
        cv = coefs[1, level]
        centre = 1.0 - 4.0 * ch - 2.0 * cv
        below = jnp.maximum(level - 1, 0)
        above = jnp.minimum(level + 1, levels - 1)
        cv_below = jnp.where(level > 0, cv, 0.0)
        cv_above = jnp.where(level < levels - 1, cv, 0.0)

        def row_tile(t):
            t = t % tiles
            return here[level, 8 * t : 8 * t + 8, :]

        down_before = pltpu.roll(row_tile(-1), 1, 0)
        now = row_tile(0)
        up_now = pltpu.roll(now, 7, 0)
        for t in range(tiles):
            following = row_tile(t + 1)
            down_now = pltpu.roll(now, 1, 0)
            up_next = pltpu.roll(following, 7, 0)
            around = jnp.where(sub == 0, down_before, down_now) + jnp.where(
                sub == 7, up_next, up_now
            )
            around = around + (pltpu.roll(now, 1, 1) + pltpu.roll(now, cols - 1, 1))
            span = slice(8 * t, 8 * t + 8)
            stacked = cv_below * here[below, span, :] + cv_above * here[above, span, :]
            there[level, span, :] = centre * now + ch * around + (stacked + source[level, span, :])
            down_before, now, up_now = down_now, following, up_next

    def two_levels(pair, carry):
        one_level(2 * pair)
        one_level(2 * pair + 1)
        return carry

    lax.fori_loop(0, levels // 2, two_levels, 0)


def spread_coefs(parent_coefs, coefs, out):
    levels = out.shape[2]
    lane = iota((levels, LANES), 1)
    row = iota((levels, LANES), 0)
    for at, ref in enumerate((parent_coefs, coefs)):
        for which in range(2):
            packed = jnp.full(lane.shape, ref[which, 0], jnp.float32)
            rows = packed
            for level in range(1, levels):
                packed = jnp.where(lane >= STRIDE * level, ref[which, level], packed)
                rows = jnp.where(row == level, ref[which, level], rows)
            out[0, 2 * at + which] = packed
            out[1, 2 * at + which] = rows


def inner_first(
    band,
    oy_ref,
    parent_coefs,
    coefs,
    nest,
    source,
    parent,
    parent_source,
    strip,
    first,
    spread,
    oy_rows,
):
    oy = oy_ref[0]
    oy_rows[...] = jnp.full(oy_rows.shape, oy, jnp.int32)
    spread_coefs(parent_coefs, coefs, spread)
    strip[...] = edge_strip(lax.axis_index("gy"), band, oy, parent, parent_source)
    inner_substep(coefs, nest, source, first)


def own_windows(parts, nest, source, y_left, y_right, window_old, window_src):
    levels, rows, cols = nest.shape
    pieces = cols // LANES
    me = lax.axis_index("gy")
    for level in range(levels):
        for buf, field, shift in ((window_old, nest, 0), (window_src, source, SOURCE_AT)):
            for window, first, turn in ((0, 0, 3), (1, rows - 8, 5)):
                tiles = [
                    field[level, first : first + 8, piece * LANES : (piece + 1) * LANES]
                    for piece in range(pieces)
                ]
                tiles = with_columns(
                    tiles,
                    y_left[first : first + 8, :],
                    y_right[first : first + 8, :],
                    me,
                    parts,
                    STRIDE * level + shift,
                )
                for piece, value in enumerate(tiles):
                    buf[level, window, :, piece * LANES : (piece + 1) * LANES] = pltpu.roll(
                        value, turn, 0
                    )


def inner_rest(
    parts,
    coefs,
    nest,
    first,
    source,
    y_left,
    y_right,
    after_pack,
    third,
    packs,
    window_old,
    window_src,
    sums,
    second,
    split,
):
    levels, rows, cols = nest.shape
    own_windows(parts, nest, source, y_left, y_right, window_old, window_src)
    lane = iota((rows, LANES), 1)
    for at, ref in enumerate((nest, source)):
        left = jnp.zeros(lane.shape, jnp.float32)
        right = jnp.zeros(lane.shape, jnp.float32)
        for level in range(levels):
            value = jnp.where(lane < RIGHT_OWN, tile(ref, level, 0), 0.0)
            left = left + turned(value, STRIDE * level + LEFT_AT)
            value = jnp.where(lane >= LANES - RIGHT_OWN, tile(ref, level, cols // LANES - 1), 0.0)
            right = right + turned(value, STRIDE * level + RIGHT_OWN)
        packs[2 * at] = left
        packs[2 * at + 1] = right
    inner_substep(coefs, first, source, second)
    inner_substep(coefs, second, source, third)
    for level in range(levels):
        for piece in range(cols // LANES):
            split[piece, level * rows : (level + 1) * rows, :] = tile(third, level, piece)
    for piece in range(cols // LANES):
        sums[piece] = sum_rows(split.at[piece])


def with_columns(tiles, left, right, me, parts, place):
    lane = iota(left.shape, 1)
    from_right = turned(right, -place)
    from_left = turned(left, -3 - place)
    if parts == 2:
        tiles[0] = jnp.where((lane < 3) & (me == 0), from_right, tiles[0])
        tiles[-1] = jnp.where((lane >= LANES - 3) & (me == 1), from_left, tiles[-1])
        return tiles
    extra = jnp.where(lane < 3, from_right, jnp.where(lane >= LANES - 3, from_left, 0.0))
    return tiles + [extra]


def pack_rows(
    parts, old_top, old_end, src_top, src_end, par_top, par_end, own_strip, oy_rows, *rest
):
    columns = rest[: parts - 1]
    across, within, far, strip_out, both = rest[parts - 1 :]
    core = lax.axis_index("gz")
    up, down = both.at[core], both.at[1 - core]
    levels, _, cols = old_top.shape
    me = lax.axis_index("gy")
    left, right = columns[0], columns[-1]
    rows = left.shape[0]
    strip_rows = own_strip.shape[0]
    lane = iota((strip_rows, LANES), 1)
    strips = own_strip[...]
    if parts == 2:
        oy = jnp.concatenate([oy_rows[...]] * (strip_rows // 8), axis=0)
        strips = strips + across_border(left[:strip_rows, :], oy, par_top.shape[2], me)
    else:
        for message in columns:
            strips = strips + message[:strip_rows, :]
    c = lane & (STRIDE - 1)
    strips = jnp.where(c >= STRIP_AT, strips, 0.0)
    strips = jnp.where(c == PARENT_AT, left[:strip_rows, :], strips)
    strips = jnp.where(c == PARENT_AT + 1, turned(right[:strip_rows, :], 1), strips)
    strip_out[...] = strips
    far[...] = strips[:8]
    pieces = cols // LANES
    for out, old, src, first, at, src_at in (
        (up, old_end, src_end, rows - 8, 5, 6),
        (down, old_top, src_top, 0, 0, 0),
    ):
        y_left = left[first : first + 8, :]
        y_right = right[first : first + 8, :]
        for level in range(levels):
            for ref, shift, row, count, base in (
                (old, 0, at, 3, 0),
                (src, SOURCE_AT, src_at, 2, SOURCE_ROW),
            ):
                tiles = [tile(ref, level, piece) for piece in range(pieces)]
                tiles = with_columns(
                    tiles, y_left, y_right, me, parts, STRIDE * level + shift
                )
                for piece, value in enumerate(tiles):
                    out[
                        base + count * level : base + count * (level + 1),
                        piece * LANES : (piece + 1) * LANES,
                    ] = value[row : row + count]
    parent_cols = par_top.shape[2]
    for level in range(levels):
        up[TAIL_ROW + level : TAIL_ROW + level + 1, :parent_cols] = par_end[level, 7:8, :]
        down[TAIL_ROW + level : TAIL_ROW + level + 1, :parent_cols] = par_top[level, 0:1, :]
    up[TAIL_ROW : TAIL_ROW + 8, parent_cols : parent_cols + LANES] = strips[strip_rows - 8 :]
    down[TAIL_ROW : TAIL_ROW + 8, parent_cols : parent_cols + LANES] = strips[:8]
    down[TAIL_ROW + 8 : TAIL_ROW + 16, :LANES] = strips[8:16]
    down[TAIL_ROW + 8 : TAIL_ROW + 16, LANES : 2 * LANES] = strips[16:24]
    within[...] = both[0]
    across[...] = both[1]


def edges(
    parts,
    parent_cols,
    ox_ref,
    spread,
    sums,
    packs,
    window_old,
    window_src,
    strips,
    across,
    within,
    far,
    y_left,
    y_right,
    sides,
    windows,
    coarse_out,
    far_out,
    both,
    ping,
    pong,
    src,
):
    levels = ping.shape[0]
    width = ping.shape[3]
    rows = sides.shape[1]
    cols = sums.shape[0] * LANES
    pieces = cols // LANES
    me = lax.axis_index("gy")
    core = lax.axis_index("gz")
    both[0] = within[...]
    both[1] = across[...]
    before, after = both.at[1 - core], both.at[core]
    is_south = me == 0
    is_north = me == parts - 1

    far_out[...] = far[...]
    sub = iota((8, LANES), 0)
    old = jnp.concatenate(
        [
            strips[...],
            after[TAIL_ROW : TAIL_ROW + 8, parent_cols : parent_cols + LANES],
            after[TAIL_ROW + 8 : TAIL_ROW + 16, :LANES],
            after[TAIL_ROW + 8 : TAIL_ROW + 16, LANES : 2 * LANES],
            jnp.where(
                sub == 7,
                before[TAIL_ROW : TAIL_ROW + 8, parent_cols : parent_cols + LANES],
                0.0,
            ),
        ],
        axis=0,
    )
    count = old.shape[0]

    def packed_coef(which, height):
        return jnp.concatenate([spread[0, which]] * (height // 8), axis=0)

    def stacked(value):
        lane = iota(value.shape, 1)
        below = jnp.where(lane >= STRIDE, turned(value, STRIDE), 0.0)
        return below + jnp.where(lane < STRIDE * (levels - 1), turned(value, -STRIDE), 0.0)

    def around(value):
        return (
            pltpu.roll(value, 1, 0)
            + pltpu.roll(value, value.shape[0] - 1, 0)
            + turned(value, 1)
            + turned(value, -1)
        )

    diff = (
        packed_coef(0, count) * (around(old) - 4.0 * old)
        + packed_coef(1, count) * (stacked(old) - 2.0 * old)
        + turned(old, STRIP_AT - STRIP_SOURCE_AT)
    )
    index = iota((rows + 16, count), 0)
    nest_row = jnp.where(index < rows, index, jnp.where(index < rows + 8, index - rows - 3, index - 13))
    parent_row = ((nest_row + 3) * 171 >> 9) - 1 + ox_ref[0]
    pick = (iota((rows + 16, count), 1) == parent_row).astype(jnp.float32)
    picked = select_rows(pick, jnp.concatenate([old, diff], axis=1))
    picked_old, picked_diff = picked[:, :LANES], picked[:, LANES:]

    lane = iota((rows, LANES), 1)
    c = lane & (STRIDE - 1)
    rim_first = jnp.where(is_south, LEFT_AT, RIGHT_OWN - RIM)
    in_rim = (c >= rim_first) & (c < rim_first + RIM)
    at = lane - c + STRIP_AT + jnp.where(c >= rim_first + 3, 2, 1)
    rim_old = jnp.take_along_axis(picked_old[:rows], at, axis=1)
    rim_diff = jnp.take_along_axis(picked_diff[:rows], at, axis=1)
    ch = packed_coef(2, rows)
    cv = packed_coef(3, rows)
    centre = 1.0 - 4.0 * ch - 2.0 * cv
    left = jnp.where(c < 3, y_left[...], packs[0])
    left_src = jnp.where(c < 3, turned(y_left[...], -SOURCE_AT), packs[2])
    right = jnp.where(c >= RIGHT_OWN, turned(y_right[...], RIGHT_OWN), packs[1])
    right_src = jnp.where(c >= RIGHT_OWN, turned(y_right[...], RIGHT_OWN - SOURCE_AT), packs[3])
    for side, (value, forcing, rim) in enumerate(
        (
            (left, left_src, in_rim & is_south),
            (right, right_src, in_rim & is_north),
        )
    ):
        for substep in range(1, SUBSTEPS + 1):
            value = centre * value + ch * around(value) + (cv * stacked(value) + forcing)
            value = jnp.where(rim, rim_old + (substep / SUBSTEPS) * rim_diff, value)
        sides[side] = value

    sub = iota((8, width), 0)
    lane = iota((8, LANES), 1)
    ping[...] = window_old[...]
    src[...] = window_src[...]
    for level in range(levels):
        for buf, n, base in ((ping, 3, 0), (src, 2, SOURCE_ROW)):
            rows_of = slice(base + n * level, base + n * (level + 1))
            buf[level, 0, 3 - n : 3, :] = before[rows_of, :]
            buf[level, 1, 5 : 5 + n, :] = after[rows_of, :]
    rim_first = jnp.where(is_south, 0, LANES - RIM)
    column = STRIP_AT + jnp.where((lane >= rim_first + 3) & (lane < rim_first + RIM), 2, 1)
    rims = {}
    for level in range(levels):
        for window in range(2):
            span = slice(rows + 8 * window, rows + 8 * window + 8)
            at = column + STRIDE * level
            rims[level, window] = (
                jnp.take_along_axis(picked_old[span], at, axis=1),
                jnp.take_along_axis(picked_diff[span], at, axis=1),
            )
    for substep in range(1, SUBSTEPS + 1):
        here, there = (ping, pong) if substep % 2 else (pong, ping)
        there = windows if substep == SUBSTEPS else there
        low = 0 if substep == SUBSTEPS or parts > 2 else 3
        south = (lane >= low) & (lane < RIM) & is_south
        north = (lane >= LANES - RIM) & (lane < LANES - low) & is_north
        weight = substep / SUBSTEPS
        for level in range(levels):
            c_h, c_v = (
                jnp.concatenate([spread[1, which, level : level + 1, :]] * (width // LANES), axis=1)
                for which in (2, 3)
            )
            c_0 = 1.0 - 4.0 * c_h - 2.0 * c_v
            for window in range(2):
                now = here[level, window]
                up = pltpu.roll(now, 1, 0)
                down = pltpu.roll(now, 7, 0)
                if substep == 1:
                    beyond_row = window_old[level, window]
                    if window == 0:
                        down = jnp.where(sub == 7, pltpu.roll(beyond_row, 7, 0), down)
                    else:
                        up = jnp.where(sub == 0, pltpu.roll(beyond_row, 1, 0), up)
                beside = pltpu.roll(now, 1, 1) + pltpu.roll(now, width - 1, 1)
                value = c_0 * now + c_h * ((up + down) + beside) + src[level, window]
                if level > 0:
                    value = value + c_v * here[level - 1, window]
                if level < levels - 1:
                    value = value + c_v * here[level + 1, window]
                rim_o, rim_d = rims[level, window]
                rim = rim_o + weight * rim_d
                for piece in range(width // LANES):
                    span = slice(piece * LANES, (piece + 1) * LANES)
                    part = value[:, span]
                    if piece == 0:
                        part = jnp.where(south, rim, part)
                    if piece == pieces - 1:
                        part = jnp.where(north, rim, part)
                    there[level, window, :, span] = part

    parent_rows = rows // RATIO
    lane = iota((parent_rows, LANES), 1)
    row = iota((parent_rows, LANES), 0)
    side_sums = [sum_rows(sides.at[side]) for side in range(2)]
    replaced = [[] for _ in range(pieces)]
    for level in range(levels):
        span = slice(level * parent_rows, (level + 1) * parent_rows)
        top = windows[level, 0, 3:4, :] + windows[level, 0, 4:5, :] + windows[level, 0, 5:6, :]
        end = windows[level, 1, 2:3, :] + windows[level, 1, 3:4, :] + windows[level, 1, 4:5, :]
        for piece in range(pieces):
            value = sums[piece, span, :]
            if piece == 0:
                fixed = turned(side_sums[0], -STRIDE * level - LEFT_AT)
                value = jnp.where(lane < FIXED, fixed, value)
            if piece == pieces - 1:
                fixed = turned(side_sums[1], -STRIDE * level - RIGHT_OWN)
                value = jnp.where(lane >= LANES - FIXED, fixed, value)
            across_piece = slice(piece * LANES, (piece + 1) * LANES)
            value = jnp.where(row == 0, top[:, across_piece], value)
            value = jnp.where(row == parent_rows - 1, end[:, across_piece], value)
            replaced[piece].append(value)
    foot = cols // RATIO
    offset = iota((cols, foot), 0) - RATIO * iota((cols, foot), 1)
    gather = ((offset >= 0) & (offset < RATIO)).astype(jnp.float32)
    means = select_columns(
        jnp.concatenate([jnp.concatenate(values, axis=0) for values in replaced], axis=1), gather
    ) * (1.0 / 9.0)
    coarse_out[...] = means.reshape(coarse_out.shape)


def put_together(third, sides, windows, result):
    levels, rows, cols = third.shape
    pieces = cols // LANES
    lane = iota((rows, LANES), 1)
    sub = iota((8, cols), 0)
    for level in range(levels):
        fixed = turned(sides[0], -STRIDE * level - LEFT_AT)
        result[level, :, :LANES] = jnp.where(lane < FIXED, fixed, tile(third, level, 0))
        for piece in range(1, pieces - 1):
            result[level, :, piece * LANES : (piece + 1) * LANES] = tile(third, level, piece)
        fixed = turned(sides[1], -STRIDE * level - RIGHT_OWN)
        result[level, :, cols - LANES :] = jnp.where(
            lane >= LANES - FIXED, fixed, tile(third, level, pieces - 1)
        )
        top = pltpu.roll(windows[level, 0, :, :cols], 5, 0)
        result[level, :8, :] = jnp.where(sub < 3, top, result[level, :8, :])
        end = pltpu.roll(windows[level, 1, :, :cols], 3, 0)
        result[level, rows - 8 :, :] = jnp.where(sub >= 5, end, result[level, rows - 8 :, :])


def parent_step(
    parts,
    band,
    ox_ref,
    oy_ref,
    spread,
    third,
    sides,
    windows,
    parent,
    source,
    within,
    across,
    y_left,
    y_right,
    out,
    nest_out,
    late,
    tail,
    result,
    sem,
):
    put_together(third, sides, windows, result)
    store = pltpu.make_async_copy(result, nest_out, sem)
    store.start()
    core = lax.axis_index("gz")
    levels, rows, cols = parent.shape
    tail[0] = within[TAIL_ROW : TAIL_ROW + levels, : cols + LANES]
    tail[1] = across[TAIL_ROW : TAIL_ROW + levels, : cols + LANES]
    me = lax.axis_index("gy")
    is_last = ox_ref[0] == rows - 1
    wide = iota((1, cols), 1)
    south = (wide == oy_ref[0] + 2 - me * cols) & is_last
    north = (wide == oy_ref[0] + band - 3 - me * cols) & is_last
    row = iota((rows, cols), 0)
    lane = iota((rows, cols), 1)
    has_left = me > 0
    has_right = me < parts - 1
    left = y_left[:rows, :]
    right = y_right[:rows, :]
    zero = jnp.zeros((rows, cols), jnp.float32)
    for level in range(levels):
        now = parent[level]
        at = STRIDE * level + PARENT_AT
        from_left = left[:, at : at + 1]
        from_right = right[:, at : at + 1]
        top = tail[1 - core, level : level + 1, :cols]
        end = tail[core, level : level + 1, :cols]
        around = (
            jnp.where(row == 0, top, pltpu.roll(now, 1, 0))
            + jnp.where(row == rows - 1, end, pltpu.roll(now, rows - 1, 0))
            + jnp.where(
                lane == 0, jnp.where(has_left, from_left, 0.0), pltpu.roll(now, 1, 1)
            )
            + jnp.where(
                lane == cols - 1,
                jnp.where(has_right, from_right, 0.0),
                pltpu.roll(now, cols - 1, 1),
            )
        )
        stacked = (parent[level - 1] if level > 0 else zero) + (
            parent[level + 1] if level < levels - 1 else zero
        )
        ch, cv = (
            jnp.concatenate([spread[1, which, level : level + 1, :]] * (cols // LANES), axis=1)
            for which in (0, 1)
        )
        out[level] = (
            (1.0 - 4.0 * ch - 2.0 * cv) * now + ch * around + (cv * stacked + source[level])
        )
        at = cols + STRIDE * level + PARENT_AT
        before_end = jnp.where(
            wide == 0, tail[core, 0:1, at : at + 1], pltpu.roll(end, 1, 1)
        )
        after_end = jnp.where(
            wide == cols - 1, tail[core, 0:1, at + 1 : at + 2], pltpu.roll(end, cols - 1, 1)
        )
        nest_ch = spread[1, 2, level : level + 1, :]
        nest_ch = jnp.concatenate([nest_ch] * (cols // LANES), axis=1)
        share = nest_ch * nest_ch * ch * (1.0 / SUBSTEPS)
        late[level : level + 1, :] = (share * (1.0 / (RATIO * RATIO))) * (
            jnp.where(south, before_end, 0.0) + jnp.where(north, after_end, 0.0)
        )
    store.wait()


def merge(parts, band, ox_ref, oy_ref, late, step, nest, spread, beyond, *rest):
    arrived = rest[1 : 2 * parts]
    out, nest_out, joined, corner, sem, merged, out_sems = rest[2 * parts :]
    levels, rows, cols = step.shape
    foot = rest[0].shape[2]
    me = lax.axis_index("gy")

    @pl.when((ox_ref[0] == rows - 1) & ((me == 0) | (me == parts - 1)))
    def _():
        nest_rows, nest_cols = nest.shape[1:]
        first = pl.multiple_of(jnp.where(me == 0, 0, nest_cols - LANES), LANES)
        place = (slice(None), pl.ds(nest_rows - 8, 8), pl.ds(first, LANES))
        load = pltpu.make_async_copy(nest_out.at[place], corner, sem)
        load.start()
        load.wait()
        sub = iota((8, LANES), 0)
        lane = iota((8, LANES), 1)
        cell = (sub == 7) & (lane == jnp.where(me == 0, RIM, LANES - RIM - 1))
        for level in range(levels):
            at = STRIDE * level + STRIP_AT
            value = jnp.where(me == 0, beyond[0:1, at + 2 : at + 3], beyond[0:1, at + 1 : at + 2])
            nest_ch = spread[1, 2, level : level + 1, :]
            share = nest_ch * nest_ch * spread[1, 0, level : level + 1, :] * (1.0 / SUBSTEPS)
            corner[level] += jnp.where(cell, share * value, 0.0)
        again = pltpu.make_async_copy(corner, nest_out.at[place], sem)
        again.start()
        again.wait()

    ox = ox_ref[0]
    oy = oy_ref[0]
    joined[0, :, rows:, :] = rest[0][...]
    if parts == 2:
        mixed, straight, other = arrived
        joined[0, :, :rows, :] = straight[...]
        joined[1, :, :rows, :] = jnp.where(me == 0, mixed[...], other[...])
        joined[1, :, rows:, :] = jnp.where(me == 0, other[...], mixed[...])
    else:
        for k in range(parts):
            joined[k, :, :rows, :] = arrived[k][...]
        for k in range(1, parts):
            joined[k, :, rows:, :] = arrived[parts + k - 1][...]
    lane = iota((rows, LANES), 1)
    row = iota((rows, LANES), 0)
    stores = []
    for level in range(levels):
        values = [tile(step, level, piece) for piece in range(cols // LANES)]
        for k in range(parts):
            source = lax.rem(me + parts - k, parts)
            block = joined[k, level, pl.ds(rows - ox, rows), :]
            begin = oy + source * foot - me * cols
            block = pltpu.roll(block, (16384 + begin) & (LANES - 1), 1)
            low = jnp.maximum(source * foot, 2)
            high = jnp.minimum((source + 1) * foot, band - 2)
            for piece in range(cols // LANES):
                at = lane + (piece * LANES + me * cols - oy)
                values[piece] = jnp.where((at >= low) & (at < high), block, values[piece])
        for piece, value in enumerate(values):
            term = late[level : level + 1, piece * LANES : (piece + 1) * LANES]
            value = value + jnp.where(row == rows - 2, term, 0.0)
            merged[level, :, piece * LANES : (piece + 1) * LANES] = value
        stores.append(pltpu.make_async_copy(merged.at[level], out.at[level], out_sems.at[level]))
        stores[-1].start()
    for copy in stores:
        copy.wait()


def shifted(value, axis, steps):
    count = lax.axis_size(axis)
    pairs = [(source, (source + steps) % count) for source in range(count)]
    return lax.ppermute(value, axis, pairs)


def shards(
    parent_old, parent_source, parent_coefs, nest_old, nest_source, nest_coefs, offset_x, offset_y
):
    parts = lax.axis_size("gy")
    along = ("gx", "gz")
    levels, parent_rows, parent_cols = parent_old.shape
    _, rows, cols = nest_old.shape
    foot = cols // RATIO
    band = foot * parts
    width = cols if parts == 2 else cols + LANES
    height = TAIL_ROW + 16
    f32 = jnp.float32
    shape = jax.ShapeDtypeStruct
    anywhere = pl.BlockSpec(memory_space=pl.ANY)
    in_hbm = pl.BlockSpec(memory_space=pltpu.HBM)
    sides = 1 if parts == 2 else 2
    if parts == 2:
        packed = [
            pl.pallas_call(
                pack_pair,
                out_shape=VMEM((rows, LANES), f32),
                in_specs=[in_hbm] * 4,
                out_specs=whole(),
                scratch_shapes=[
                    VMEM((2, levels, rows, LANES), f32),
                    VMEM((2, levels, parent_rows, LANES), f32),
                    pltpu.SemaphoreType.DMA((6,)),
                ],
                compiler_params=params(MOST),
                cost_estimate=cost(200000, 800000),
                name="pack_pair",
            )(nest_old, nest_source, parent_old, parent_source)
        ]
    else:
        packed = pl.pallas_call(
            functools.partial(pack_columns, parts, band),
            out_shape=[
                shape((rows if k in (1, parts - 1) else parent_rows, LANES), f32)
                for k in range(1, parts)
            ],
            in_specs=[in_hbm] * 5,
            out_specs=[whole()] * (parts - 1),
            scratch_shapes=[
                VMEM((sides, levels, rows, LANES), f32),
                VMEM((sides, levels, rows, LANES), f32),
                VMEM(parent_old.shape, f32),
                VMEM(parent_old.shape, f32),
                pltpu.SMEM(offset_y.shape, jnp.int32),
                pltpu.SemaphoreType.DMA((sides, 2)),
                pltpu.SemaphoreType.DMA((3,)),
            ],
            compiler_params=params(MOST),
            cost_estimate=cost(200000, 1000000),
            name="pack_columns",
        )(offset_y, nest_old, nest_source, parent_old, parent_source)
    columns = [shifted(packed[k - 1], "gy", k) for k in range(1, parts)]
    own_strip, first, spread, oy_rows = pl.pallas_call(
        functools.partial(inner_first, band),
        out_shape=[
            shape((parent_rows, LANES), f32),
            shape(nest_old.shape, f32),
            shape((2, 4, levels, LANES), f32),
            shape((8, LANES), jnp.int32),
        ],
        in_specs=[scalars()] * 3 + [whole()] * 4,
        out_specs=[whole()] * 4,
        compiler_params=params(),
        cost_estimate=cost(4000000, 3000000),
        name="inner_first",
    )(
        offset_y,
        parent_coefs,
        nest_coefs,
        nest_old,
        nest_source,
        parent_old,
        parent_source,
    )

    def block(ref, last):
        count = ref.shape[1] // 8 - 1 if last else 0
        return pl.BlockSpec((levels, 8, ref.shape[2]), lambda i, c=count: (0, c, 0))

    def full(extent):
        return pl.BlockSpec(extent, lambda i: (0,) * len(extent))

    outs = [
        shape((height, width), f32),
        shape((height, width), f32),
        shape((8, LANES), f32),
        shape((parent_rows, LANES), f32),
    ]
    across, within, far, strips = pl.pallas_call(
        functools.partial(pack_rows, parts),
        out_shape=outs,
        grid=(1,),
        in_specs=[
            block(nest_old, False),
            block(nest_old, True),
            block(nest_old, False),
            block(nest_old, True),
            block(parent_old, False),
            block(parent_old, True),
            full(own_strip.shape),
            full(oy_rows.shape),
        ]
        + [full(message.shape) for message in columns],
        out_specs=[full(out.shape) for out in outs],
        scratch_shapes=[VMEM((2, height, width), f32)],
        compiler_params=params(),
        cost_estimate=cost(100000, 700000),
        name="pack_rows",
    )(nest_old, nest_old, nest_source, nest_source, parent_old, parent_old, own_strip, oy_rows, *columns)
    across = swapped(across, 1)
    within = swapped(within, 0)
    third, packs, window_old, window_src, sums = pl.pallas_call(
        functools.partial(inner_rest, parts),
        out_shape=[
            shape(nest_old.shape, f32),
            shape((4, rows, LANES), f32),
            shape((levels, 2, 8, width), f32),
            shape((levels, 2, 8, width), f32),
            shape((cols // LANES, levels * parent_rows, LANES), f32),
        ],
        in_specs=[scalars()] + [whole()] * 5 + [anywhere],
        out_specs=[whole()] * 5,
        scratch_shapes=[
            VMEM(nest_old.shape, f32),
            VMEM((cols // LANES, levels * rows, LANES), f32),
        ],
        compiler_params=params(),
        cost_estimate=cost(8000000, 6000000),
        name="inner_rest",
    )(nest_coefs, nest_old, first, nest_source, columns[0], columns[-1], strips)
    sides, windows, coarse, far = pl.pallas_call(
        functools.partial(edges, parts, parent_cols),
        out_shape=[
            shape((2, rows, LANES), f32),
            shape((levels, 2, 8, width), f32),
            shape((levels, parent_rows, foot), f32),
            shape((8, LANES), f32),
        ],
        in_specs=[scalars()] + [whole()] * 11,
        out_specs=[whole()] * 4,
        scratch_shapes=[
            VMEM((2, height, width), f32),
            VMEM((levels, 2, 8, width), f32),
            VMEM((levels, 2, 8, width), f32),
            VMEM((levels, 2, 8, width), f32),
        ],
        compiler_params=params(),
        cost_estimate=cost(4000000, 3000000),
        name="edges",
    )(
        offset_x,
        spread,
        sums,
        packs,
        window_old,
        window_src,
        strips,
        across,
        within,
        far,
        columns[0],
        columns[-1],
    )
    if parts == 2:
        arrived = [
            shifted_both(coarse, 1, (0, 1)),
            shifted(coarse, along, 1),
            shifted_both(coarse, 1, (1, 0)),
        ]
    else:
        arrived = [shifted(coarse, along, 1)]
        arrived += [shifted_both(coarse, k) for k in range(1, parts)]
        arrived += [shifted(coarse, "gy", k) for k in range(1, parts)]
    beyond = shifted(far, along, -2)
    step, nest_stored, late = pl.pallas_call(
        functools.partial(parent_step, parts, band),
        out_shape=[
            shape(parent_old.shape, f32),
            shape(nest_old.shape, f32),
            shape((levels, parent_cols), f32),
        ],
        in_specs=[scalars()] * 2 + [whole()] * 10,
        out_specs=[whole(), in_hbm, whole()],
        scratch_shapes=[
            VMEM((2, levels, parent_cols + LANES), f32),
            VMEM(nest_old.shape, f32),
            pltpu.SemaphoreType.DMA,
        ],
        compiler_params=params(),
        cost_estimate=cost(800000, 2500000),
        name="parent_step",
    )(
        offset_x,
        offset_y,
        spread,
        third,
        sides,
        windows,
        parent_old,
        parent_source,
        within,
        across,
        columns[0],
        columns[-1],
    )
    parent_new, nest_new = pl.pallas_call(
        functools.partial(merge, parts, band),
        out_shape=[shape(parent_old.shape, f32), shape(nest_old.shape, f32)],
        in_specs=[scalars()] * 2 + [whole()] * 2 + [in_hbm] + [whole()] * (2 + 2 * parts),
        out_specs=[in_hbm, in_hbm],
        scratch_shapes=[
            VMEM((parts, levels, 2 * parent_rows, foot), f32),
            VMEM((levels, 8, LANES), f32),
            pltpu.SemaphoreType.DMA,
            VMEM(parent_old.shape, f32),
            pltpu.SemaphoreType.DMA((levels,)),
        ],
        input_output_aliases={4: 1},
        compiler_params=params(),
        cost_estimate=cost(200000, 800000),
        name="merge",
    )(offset_x, offset_y, late, step, nest_stored, spread, beyond, coarse, *arrived)
    return (parent_new, nest_new)


def swapped(value, first):
    along = ("gx", "gz")
    count = lax.axis_size(along)
    pairs = []
    for at in range(first, count, 2):
        pairs += [(at, (at + 1) % count), ((at + 1) % count, at)]
    return lax.ppermute(value, along, pairs)


def shifted_both(value, steps, rows=None):
    sizes = [lax.axis_size(axis) for axis in ("gx", "gy", "gz")]
    gx, gy, gz = sizes
    pairs = []
    for x in range(gx):
        for y in range(gy):
            for z in range(gz):
                place = (x * gz + z + (1 if rows is None else rows[y])) % (gx * gz)
                target = (place // gz * gy + (y + steps) % gy) * gz + place % gz
                pairs.append(((x * gy + y) * gz + z, target))
    return lax.ppermute(value, ("gx", "gy", "gz"), pairs)


def solution(mesh):
    return jax.shard_map(
        shards,
        mesh=mesh,
        in_specs=(
            P(None, ("grp", "gx", "gz"), "gy"),
            P(None, ("grp", "gx", "gz"), "gy"),
            P(),
            P(None, ("grp", "gx", "gz"), "gy"),
            P(None, ("grp", "gx", "gz"), "gy"),
            P(),
            P("grp"),
            P("grp"),
        ),
        out_specs=(P(None, ("grp", "gx", "gz"), "gy"), P(None, ("grp", "gx", "gz"), "gy")),
        check_vma=False,
    )
```

```python
import functools

import jax
import jax.numpy as jnp
from jax import lax
from jax.experimental import pallas as pl
from jax.experimental.pallas import tpu as pltpu
from jax.sharding import PartitionSpec as P

RATIO = 3
SUBSTEPS = 3
RIM = 6
LANES = 128
STRIDE = 16
SOURCE_AT = 3
PARENT_AT = 6
STRIP_AT = 8
STRIP_SOURCE_AT = 12
SOURCE_ROW = 24
TAIL_ROW = 40
FIXED = 8
LEFT_AT = 3
RIGHT_OWN = STRIDE - 3
VMEM = pltpu.VMEM
LIMIT = 24 * 1024 * 1024
MOST = 54 * 1024 * 1024


def iota(shape, dim):
    return lax.broadcasted_iota(jnp.int32, shape, dim)


def whole():
    return pl.BlockSpec(memory_space=VMEM)


def scalars():
    return pl.BlockSpec(memory_space=pltpu.SMEM)


def params(limit=LIMIT):
    return pltpu.CompilerParams(vmem_limit_bytes=limit)


def cost(flops, moved):
    return pl.CostEstimate(flops=flops, bytes_accessed=moved, transcendentals=0)


def tile(ref, level, index):
    return ref[level, :, index * LANES : (index + 1) * LANES]


def turned(value, lanes):
    lanes = lanes % LANES
    return pltpu.roll(value, lanes, 1) if lanes else value


def edge_strip(dest, band, oy, parent, parent_source):
    levels, rows, cols = parent.shape
    lane = iota((rows, LANES), 1)
    base = jnp.where(dest == 0, oy - 1, oy + band - 3) - lax.axis_index("gy") * cols
    total = jnp.zeros(lane.shape, jnp.float32)
    for ref, first in ((parent, STRIP_AT), (parent_source, STRIP_SOURCE_AT)):
        for level in range(levels):
            found = jnp.zeros(lane.shape, jnp.float32)
            for at in range(cols // LANES):
                place = lane + (at * LANES - base)
                found = jnp.where((place >= 0) & (place < 4), tile(ref, level, at), found)
            turn = (16384 + first + STRIDE * level - base) & (LANES - 1)
            total = total + pltpu.roll(found, turn, 1)
    return total


def pack_pair(nest, source, parent, parent_source, out, fine_buf, coarse_buf, sems):
    levels, rows, cols = nest.shape
    parent_rows, parent_cols = parent.shape[1:]
    right = lax.axis_index("gy") == 0
    loads = []
    for at, (ref, buf) in enumerate(
        (
            (parent, coarse_buf.at[0]),
            (parent_source, coarse_buf.at[1]),
            (nest, fine_buf.at[0]),
            (source, fine_buf.at[1]),
        )
    ):
        start = pl.multiple_of(jnp.where(right, ref.shape[2] - LANES, 0), LANES)
        loads.append(pltpu.make_async_copy(ref.at[:, :, pl.ds(start, LANES)], buf, sems.at[at]))
    for copy in loads:
        copy.start()

    def columns(value, count, to):
        first = jnp.where(right, LANES - count, 0)
        place = iota(value.shape, 1) - first
        value = jnp.where((place >= 0) & (place < count), value, 0.0)
        return pltpu.roll(value, (LANES + to - first) & (LANES - 1), 1)

    part = jnp.zeros((parent_rows, LANES), jnp.float32)
    loads[0].wait()
    loads[1].wait()
    for level in range(levels):
        base = STRIDE * level
        part = part + columns(coarse_buf[0, level], 1, base + PARENT_AT)
        part = part + columns(coarse_buf[0, level], 2, base + STRIP_AT)
        part = part + columns(coarse_buf[1, level], 2, base + STRIP_SOURCE_AT)
    total = jnp.zeros((rows, LANES), jnp.float32)
    loads[2].wait()
    loads[3].wait()
    for level in range(levels):
        base = STRIDE * level
        total = total + columns(fine_buf[0, level], 3, base)
        total = total + columns(fine_buf[1, level], 3, base + SOURCE_AT)
    out[...] = total
    out[:parent_rows, :] += part


def across_border(message, oy, parent_cols, me):
    c = iota(message.shape, 1) & (STRIDE - 1)
    place = jnp.where(me == 0, parent_cols + 1, 1) - oy
    total = jnp.zeros(message.shape, jnp.float32)
    for turn in (-1, 0, 2, 3):
        at = jnp.where(c >= STRIP_SOURCE_AT, c - STRIP_SOURCE_AT, c - STRIP_AT) - turn
        fits = (c >= STRIP_AT) & (at >= 0) & (at < 2) & (place == turn)
        total = total + jnp.where(fits, turned(message, turn), 0.0)
    return total


def pack_columns(parts, band, oy_hbm, nest, source, parent_hbm, parent_source_hbm, *rest):
    outs = rest[: parts - 1]
    old_buf, src_buf, parent, parent_source, oy_ref, sems, field_sems = rest[parts - 1 :]
    levels, rows, cols = nest.shape
    parent_cols = parent.shape[2]
    me = lax.axis_index("gy")
    sides = [1] if parts == 2 else [1, parts - 1]
    fields = [
        pltpu.make_async_copy(ref, buf, field_sems.at[at])
        for at, (ref, buf) in enumerate(
            ((oy_hbm, oy_ref), (parent_hbm, parent), (parent_source_hbm, parent_source))
        )
    ]
    for copy in fields:
        copy.start()
    copies = []
    for at, step in enumerate(sides):
        right = (me == 0) if parts == 2 else jnp.bool_(step == 1)
        start = pl.multiple_of(jnp.where(right, cols - LANES, 0), LANES)
        pair = [
            pltpu.make_async_copy(
                ref.at[:, :, pl.ds(start, LANES)], buf.at[at], sems.at[at, which]
            )
            for which, (ref, buf) in enumerate(((nest, old_buf), (source, src_buf)))
        ]
        for copy in pair:
            copy.start()
        copies.append((right, pair))
    for copy in fields:
        copy.wait()
    oy = oy_ref[0]
    lane = iota((parent.shape[1], LANES), 1)
    for step in range(1, parts):
        out = outs[step - 1]
        part = edge_strip(lax.rem(me + step, parts), band, oy, parent, parent_source)
        if step not in sides:
            out[...] = part
            continue
        at = sides.index(step)
        right, pair = copies[at]
        first = jnp.where(right, LANES - 3, 0)
        outer = jnp.where(right, LANES - 1, 0)
        for level in range(levels):
            edge = jnp.where(
                right, tile(parent, level, parent_cols // LANES - 1), tile(parent, level, 0)
            )
            edge = jnp.where(lane == outer, edge, 0.0)
            turn = (LANES + PARENT_AT + STRIDE * level - outer) & (LANES - 1)
            part = part + pltpu.roll(edge, turn, 1)
        for copy in pair:
            copy.wait()
        fine = iota((rows, LANES), 1) - first
        wanted = (fine >= 0) & (fine < 3)
        total = jnp.zeros((rows, LANES), jnp.float32)
        for level in range(levels):
            for buf, shift in ((old_buf, 0), (src_buf, SOURCE_AT)):
                value = jnp.where(wanted, buf[at, level], 0.0)
                turn = (LANES + STRIDE * level + shift - first) & (LANES - 1)
                total = total + pltpu.roll(value, turn, 1)
        out[...] = total
        out[: part.shape[0], :] += part


def three_terms(value):
    terms = []
    for _ in range(3):
        term = value.astype(jnp.bfloat16)
        terms.append(term)
        value = value - term.astype(jnp.float32)
    return terms


def select_rows(selector, value):
    selector = selector.astype(jnp.bfloat16)
    high, middle, low = (
        jnp.dot(selector, term, preferred_element_type=jnp.float32)
        for term in three_terms(value)
    )
    return high + (middle + low)


def select_columns(value, selector):
    selector = selector.astype(jnp.bfloat16)
    high, middle, low = (
        jnp.dot(term, selector, preferred_element_type=jnp.float32)
        for term in three_terms(value)
    )
    return high + (middle + low)


def sum_rows(ref):
    count = ref.shape[0] // RATIO
    first, second, third = (ref[pl.ds(at, count, RATIO), :] for at in range(RATIO))
    return first + second + third


def inner_substep(coefs, here, source, there):
    levels, rows, cols = here.shape
    sub = iota((8, cols), 0)
    tiles = rows // 8

    def one_level(level):
        ch = coefs[0, level]
        cv = coefs[1, level]
        centre = 1.0 - 4.0 * ch - 2.0 * cv
        below = jnp.maximum(level - 1, 0)
        above = jnp.minimum(level + 1, levels - 1)
        cv_below = jnp.where(level > 0, cv, 0.0)
        cv_above = jnp.where(level < levels - 1, cv, 0.0)

        def row_tile(t):
            t = t % tiles
            return here[level, 8 * t : 8 * t + 8, :]

        down_before = pltpu.roll(row_tile(-1), 1, 0)
        now = row_tile(0)
        up_now = pltpu.roll(now, 7, 0)
        for t in range(tiles):
            following = row_tile(t + 1)
            down_now = pltpu.roll(now, 1, 0)
            up_next = pltpu.roll(following, 7, 0)
            around = jnp.where(sub == 0, down_before, down_now) + jnp.where(
                sub == 7, up_next, up_now
            )
            around = around + (pltpu.roll(now, 1, 1) + pltpu.roll(now, cols - 1, 1))
            span = slice(8 * t, 8 * t + 8)
            stacked = cv_below * here[below, span, :] + cv_above * here[above, span, :]
            there[level, span, :] = centre * now + ch * around + (stacked + source[level, span, :])
            down_before, now, up_now = down_now, following, up_next

    def two_levels(pair, carry):
        one_level(2 * pair)
        one_level(2 * pair + 1)
        return carry

    lax.fori_loop(0, levels // 2, two_levels, 0)


def spread_coefs(parent_coefs, coefs, out):
    levels = out.shape[2]
    lane = iota((levels, LANES), 1)
    row = iota((levels, LANES), 0)
    for at, ref in enumerate((parent_coefs, coefs)):
        for which in range(2):
            packed = jnp.full(lane.shape, ref[which, 0], jnp.float32)
            rows = packed
            for level in range(1, levels):
                packed = jnp.where(lane >= STRIDE * level, ref[which, level], packed)
                rows = jnp.where(row == level, ref[which, level], rows)
            out[0, 2 * at + which] = packed
            out[1, 2 * at + which] = rows


def inner_first(
    band,
    oy_ref,
    parent_coefs,
    coefs,
    nest,
    source,
    parent,
    parent_source,
    strip,
    first,
    spread,
    oy_rows,
):
    oy = oy_ref[0]
    oy_rows[...] = jnp.full(oy_rows.shape, oy, jnp.int32)
    spread_coefs(parent_coefs, coefs, spread)
    strip[...] = edge_strip(lax.axis_index("gy"), band, oy, parent, parent_source)
    inner_substep(coefs, nest, source, first)


def own_windows(parts, nest, source, y_left, y_right, window_old, window_src):
    levels, rows, cols = nest.shape
    pieces = cols // LANES
    me = lax.axis_index("gy")
    for level in range(levels):
        for buf, field, shift in ((window_old, nest, 0), (window_src, source, SOURCE_AT)):
            for window, first, turn in ((0, 0, 3), (1, rows - 8, 5)):
                tiles = [
                    field[level, first : first + 8, piece * LANES : (piece + 1) * LANES]
                    for piece in range(pieces)
                ]
                tiles = with_columns(
                    tiles,
                    y_left[first : first + 8, :],
                    y_right[first : first + 8, :],
                    me,
                    parts,
                    STRIDE * level + shift,
                )
                for piece, value in enumerate(tiles):
                    buf[level, window, :, piece * LANES : (piece + 1) * LANES] = pltpu.roll(
                        value, turn, 0
                    )


def inner_rest(
    parts,
    coefs,
    nest,
    first,
    source,
    y_left,
    y_right,
    after_pack,
    third,
    packs,
    window_old,
    window_src,
    sums,
    second,
    split,
):
    levels, rows, cols = nest.shape
    own_windows(parts, nest, source, y_left, y_right, window_old, window_src)
    lane = iota((rows, LANES), 1)
    for at, ref in enumerate((nest, source)):
        left = jnp.zeros(lane.shape, jnp.float32)
        right = jnp.zeros(lane.shape, jnp.float32)
        for level in range(levels):
            value = jnp.where(lane < RIGHT_OWN, tile(ref, level, 0), 0.0)
            left = left + turned(value, STRIDE * level + LEFT_AT)
            value = jnp.where(lane >= LANES - RIGHT_OWN, tile(ref, level, cols // LANES - 1), 0.0)
            right = right + turned(value, STRIDE * level + RIGHT_OWN)
        packs[2 * at] = left
        packs[2 * at + 1] = right
    inner_substep(coefs, first, source, second)
    inner_substep(coefs, second, source, third)
    for level in range(levels):
        for piece in range(cols // LANES):
            split[piece, level * rows : (level + 1) * rows, :] = tile(third, level, piece)
    for piece in range(cols // LANES):
        sums[piece] = sum_rows(split.at[piece])


def with_columns(tiles, left, right, me, parts, place):
    lane = iota(left.shape, 1)
    from_right = turned(right, -place)
    from_left = turned(left, -3 - place)
    if parts == 2:
        tiles[0] = jnp.where((lane < 3) & (me == 0), from_right, tiles[0])
        tiles[-1] = jnp.where((lane >= LANES - 3) & (me == 1), from_left, tiles[-1])
        return tiles
    extra = jnp.where(lane < 3, from_right, jnp.where(lane >= LANES - 3, from_left, 0.0))
    return tiles + [extra]


def pack_rows(
    parts, old_top, old_end, src_top, src_end, par_top, par_end, own_strip, oy_rows, *rest
):
    columns = rest[: parts - 1]
    across, within, far, strip_out, both = rest[parts - 1 :]
    core = lax.axis_index("gz")
    up, down = both.at[core], both.at[1 - core]
    levels, _, cols = old_top.shape
    me = lax.axis_index("gy")
    left, right = columns[0], columns[-1]
    rows = left.shape[0]
    strip_rows = own_strip.shape[0]
    lane = iota((strip_rows, LANES), 1)
    strips = own_strip[...]
    if parts == 2:
        oy = jnp.concatenate([oy_rows[...]] * (strip_rows // 8), axis=0)
        strips = strips + across_border(left[:strip_rows, :], oy, par_top.shape[2], me)
    else:
        for message in columns:
            strips = strips + message[:strip_rows, :]
    c = lane & (STRIDE - 1)
    strips = jnp.where(c >= STRIP_AT, strips, 0.0)
    strips = jnp.where(c == PARENT_AT, left[:strip_rows, :], strips)
    strips = jnp.where(c == PARENT_AT + 1, turned(right[:strip_rows, :], 1), strips)
    strip_out[...] = strips
    far[...] = strips[:8]
    pieces = cols // LANES
    for out, old, src, first, at, src_at in (
        (up, old_end, src_end, rows - 8, 5, 6),
        (down, old_top, src_top, 0, 0, 0),
    ):
        y_left = left[first : first + 8, :]
        y_right = right[first : first + 8, :]
        for level in range(levels):
            for ref, shift, row, count, base in (
                (old, 0, at, 3, 0),
                (src, SOURCE_AT, src_at, 2, SOURCE_ROW),
            ):
                tiles = [tile(ref, level, piece) for piece in range(pieces)]
                tiles = with_columns(
                    tiles, y_left, y_right, me, parts, STRIDE * level + shift
                )
                for piece, value in enumerate(tiles):
                    out[
                        base + count * level : base + count * (level + 1),
                        piece * LANES : (piece + 1) * LANES,
                    ] = value[row : row + count]
    parent_cols = par_top.shape[2]
    for level in range(levels):
        up[TAIL_ROW + level : TAIL_ROW + level + 1, :parent_cols] = par_end[level, 7:8, :]
        down[TAIL_ROW + level : TAIL_ROW + level + 1, :parent_cols] = par_top[level, 0:1, :]
    up[TAIL_ROW : TAIL_ROW + 8, parent_cols : parent_cols + LANES] = strips[strip_rows - 8 :]
    down[TAIL_ROW : TAIL_ROW + 8, parent_cols : parent_cols + LANES] = strips[:8]
    down[TAIL_ROW + 8 : TAIL_ROW + 16, :LANES] = strips[8:16]
    down[TAIL_ROW + 8 : TAIL_ROW + 16, LANES : 2 * LANES] = strips[16:24]
    within[...] = both[0]
    across[...] = both[1]


def edges(
    parts,
    parent_cols,
    ox_ref,
    spread,
    sums,
    packs,
    window_old,
    window_src,
    strips,
    across,
    within,
    far,
    y_left,
    y_right,
    sides,
    windows,
    coarse_out,
    far_out,
    both,
    ping,
    pong,
    src,
):
    levels = ping.shape[0]
    width = ping.shape[3]
    rows = sides.shape[1]
    cols = sums.shape[0] * LANES
    pieces = cols // LANES
    me = lax.axis_index("gy")
    core = lax.axis_index("gz")
    both[0] = within[...]
    both[1] = across[...]
    before, after = both.at[1 - core], both.at[core]
    is_south = me == 0
    is_north = me == parts - 1

    far_out[...] = far[...]
    sub = iota((8, LANES), 0)
    old = jnp.concatenate(
        [
            strips[...],
            after[TAIL_ROW : TAIL_ROW + 8, parent_cols : parent_cols + LANES],
            after[TAIL_ROW + 8 : TAIL_ROW + 16, :LANES],
            after[TAIL_ROW + 8 : TAIL_ROW + 16, LANES : 2 * LANES],
            jnp.where(
                sub == 7,
                before[TAIL_ROW : TAIL_ROW + 8, parent_cols : parent_cols + LANES],
                0.0,
            ),
        ],
        axis=0,
    )
    count = old.shape[0]

    def packed_coef(which, height):
        return jnp.concatenate([spread[0, which]] * (height // 8), axis=0)

    def stacked(value):
        lane = iota(value.shape, 1)
        below = jnp.where(lane >= STRIDE, turned(value, STRIDE), 0.0)
        return below + jnp.where(lane < STRIDE * (levels - 1), turned(value, -STRIDE), 0.0)

    def around(value):
        return (
            pltpu.roll(value, 1, 0)
            + pltpu.roll(value, value.shape[0] - 1, 0)
            + turned(value, 1)
            + turned(value, -1)
        )

    diff = (
        packed_coef(0, count) * (around(old) - 4.0 * old)
        + packed_coef(1, count) * (stacked(old) - 2.0 * old)
        + turned(old, STRIP_AT - STRIP_SOURCE_AT)
    )
    index = iota((rows + 16, count), 0)
    nest_row = jnp.where(index < rows, index, jnp.where(index < rows + 8, index - rows - 3, index - 13))
    parent_row = ((nest_row + 3) * 171 >> 9) - 1 + ox_ref[0]
    pick = (iota((rows + 16, count), 1) == parent_row).astype(jnp.float32)
    picked = select_rows(pick, jnp.concatenate([old, diff], axis=1))
    picked_old, picked_diff = picked[:, :LANES], picked[:, LANES:]

    lane = iota((rows, LANES), 1)
    c = lane & (STRIDE - 1)
    rim_first = jnp.where(is_south, LEFT_AT, RIGHT_OWN - RIM)
    in_rim = (c >= rim_first) & (c < rim_first + RIM)
    at = lane - c + STRIP_AT + jnp.where(c >= rim_first + 3, 2, 1)
    rim_old = jnp.take_along_axis(picked_old[:rows], at, axis=1)
    rim_diff = jnp.take_along_axis(picked_diff[:rows], at, axis=1)
    ch = packed_coef(2, rows)
    cv = packed_coef(3, rows)
    centre = 1.0 - 4.0 * ch - 2.0 * cv
    left = jnp.where(c < 3, y_left[...], packs[0])
    left_src = jnp.where(c < 3, turned(y_left[...], -SOURCE_AT), packs[2])
    right = jnp.where(c >= RIGHT_OWN, turned(y_right[...], RIGHT_OWN), packs[1])
    right_src = jnp.where(c >= RIGHT_OWN, turned(y_right[...], RIGHT_OWN - SOURCE_AT), packs[3])
    for side, (value, forcing, rim) in enumerate(
        (
            (left, left_src, in_rim & is_south),
            (right, right_src, in_rim & is_north),
        )
    ):
        for substep in range(1, SUBSTEPS + 1):
            value = centre * value + ch * around(value) + (cv * stacked(value) + forcing)
            value = jnp.where(rim, rim_old + (substep / SUBSTEPS) * rim_diff, value)
        sides[side] = value

    sub = iota((8, width), 0)
    lane = iota((8, LANES), 1)
    ping[...] = window_old[...]
    src[...] = window_src[...]
    for level in range(levels):
        for buf, n, base in ((ping, 3, 0), (src, 2, SOURCE_ROW)):
            rows_of = slice(base + n * level, base + n * (level + 1))
            buf[level, 0, 3 - n : 3, :] = before[rows_of, :]
            buf[level, 1, 5 : 5 + n, :] = after[rows_of, :]
    rim_first = jnp.where(is_south, 0, LANES - RIM)
    column = STRIP_AT + jnp.where((lane >= rim_first + 3) & (lane < rim_first + RIM), 2, 1)
    rims = {}
    for level in range(levels):
        for window in range(2):
            span = slice(rows + 8 * window, rows + 8 * window + 8)
            at = column + STRIDE * level
            rims[level, window] = (
                jnp.take_along_axis(picked_old[span], at, axis=1),
                jnp.take_along_axis(picked_diff[span], at, axis=1),
            )
    for substep in range(1, SUBSTEPS + 1):
        here, there = (ping, pong) if substep % 2 else (pong, ping)
        there = windows if substep == SUBSTEPS else there
        low = 0 if substep == SUBSTEPS or parts > 2 else 3
        south = (lane >= low) & (lane < RIM) & is_south
        north = (lane >= LANES - RIM) & (lane < LANES - low) & is_north
        weight = substep / SUBSTEPS
        for level in range(levels):
            c_h, c_v = (
                jnp.concatenate([spread[1, which, level : level + 1, :]] * (width // LANES), axis=1)
                for which in (2, 3)
            )
            c_0 = 1.0 - 4.0 * c_h - 2.0 * c_v
            for window in range(2):
                now = here[level, window]
                up = pltpu.roll(now, 1, 0)
                down = pltpu.roll(now, 7, 0)
                if substep == 1:
                    beyond_row = window_old[level, window]
                    if window == 0:
                        down = jnp.where(sub == 7, pltpu.roll(beyond_row, 7, 0), down)
                    else:
                        up = jnp.where(sub == 0, pltpu.roll(beyond_row, 1, 0), up)
                beside = pltpu.roll(now, 1, 1) + pltpu.roll(now, width - 1, 1)
                value = c_0 * now + c_h * ((up + down) + beside) + src[level, window]
                if level > 0:
                    value = value + c_v * here[level - 1, window]
                if level < levels - 1:
                    value = value + c_v * here[level + 1, window]
                rim_o, rim_d = rims[level, window]
                rim = rim_o + weight * rim_d
                for piece in range(width // LANES):
                    span = slice(piece * LANES, (piece + 1) * LANES)
                    part = value[:, span]
                    if piece == 0:
                        part = jnp.where(south, rim, part)
                    if piece == pieces - 1:
                        part = jnp.where(north, rim, part)
                    there[level, window, :, span] = part

    parent_rows = rows // RATIO
    lane = iota((parent_rows, LANES), 1)
    row = iota((parent_rows, LANES), 0)
    side_sums = [sum_rows(sides.at[side]) for side in range(2)]
    replaced = [[] for _ in range(pieces)]
    for level in range(levels):
        span = slice(level * parent_rows, (level + 1) * parent_rows)
        top = windows[level, 0, 3:4, :] + windows[level, 0, 4:5, :] + windows[level, 0, 5:6, :]
        end = windows[level, 1, 2:3, :] + windows[level, 1, 3:4, :] + windows[level, 1, 4:5, :]
        for piece in range(pieces):
            value = sums[piece, span, :]
            if piece == 0:
                fixed = turned(side_sums[0], -STRIDE * level - LEFT_AT)
                value = jnp.where(lane < FIXED, fixed, value)
            if piece == pieces - 1:
                fixed = turned(side_sums[1], -STRIDE * level - RIGHT_OWN)
                value = jnp.where(lane >= LANES - FIXED, fixed, value)
            across_piece = slice(piece * LANES, (piece + 1) * LANES)
            value = jnp.where(row == 0, top[:, across_piece], value)
            value = jnp.where(row == parent_rows - 1, end[:, across_piece], value)
            replaced[piece].append(value)
    foot = cols // RATIO
    offset = iota((cols, foot), 0) - RATIO * iota((cols, foot), 1)
    gather = ((offset >= 0) & (offset < RATIO)).astype(jnp.float32)
    means = select_columns(
        jnp.concatenate([jnp.concatenate(values, axis=0) for values in replaced], axis=1), gather
    ) * (1.0 / 9.0)
    coarse_out[...] = means.reshape(coarse_out.shape)


def put_together(third, sides, windows, result):
    levels, rows, cols = third.shape
    pieces = cols // LANES
    lane = iota((rows, LANES), 1)
    sub = iota((8, cols), 0)
    for level in range(levels):
        fixed = turned(sides[0], -STRIDE * level - LEFT_AT)
        result[level, :, :LANES] = jnp.where(lane < FIXED, fixed, tile(third, level, 0))
        for piece in range(1, pieces - 1):
            result[level, :, piece * LANES : (piece + 1) * LANES] = tile(third, level, piece)
        fixed = turned(sides[1], -STRIDE * level - RIGHT_OWN)
        result[level, :, cols - LANES :] = jnp.where(
            lane >= LANES - FIXED, fixed, tile(third, level, pieces - 1)
        )
        top = pltpu.roll(windows[level, 0, :, :cols], 5, 0)
        result[level, :8, :] = jnp.where(sub < 3, top, result[level, :8, :])
        end = pltpu.roll(windows[level, 1, :, :cols], 3, 0)
        result[level, rows - 8 :, :] = jnp.where(sub >= 5, end, result[level, rows - 8 :, :])


def parent_step(
    parts,
    band,
    ox_ref,
    oy_ref,
    spread,
    third,
    sides,
    windows,
    parent,
    source,
    within,
    across,
    y_left,
    y_right,
    out,
    nest_out,
    late,
    tail,
    result,
    sem,
):
    put_together(third, sides, windows, result)
    store = pltpu.make_async_copy(result, nest_out, sem)
    store.start()
    core = lax.axis_index("gz")
    levels, rows, cols = parent.shape
    tail[0] = within[TAIL_ROW : TAIL_ROW + levels, : cols + LANES]
    tail[1] = across[TAIL_ROW : TAIL_ROW + levels, : cols + LANES]
    me = lax.axis_index("gy")
    is_last = ox_ref[0] == rows - 1
    wide = iota((1, cols), 1)
    south = (wide == oy_ref[0] + 2 - me * cols) & is_last
    north = (wide == oy_ref[0] + band - 3 - me * cols) & is_last
    row = iota((rows, cols), 0)
    lane = iota((rows, cols), 1)
    has_left = me > 0
    has_right = me < parts - 1
    left = y_left[:rows, :]
    right = y_right[:rows, :]
    zero = jnp.zeros((rows, cols), jnp.float32)
    for level in range(levels):
        now = parent[level]
        at = STRIDE * level + PARENT_AT
        from_left = left[:, at : at + 1]
        from_right = right[:, at : at + 1]
        top = tail[1 - core, level : level + 1, :cols]
        end = tail[core, level : level + 1, :cols]
        around = (
            jnp.where(row == 0, top, pltpu.roll(now, 1, 0))
            + jnp.where(row == rows - 1, end, pltpu.roll(now, rows - 1, 0))
            + jnp.where(
                lane == 0, jnp.where(has_left, from_left, 0.0), pltpu.roll(now, 1, 1)
            )
            + jnp.where(
                lane == cols - 1,
                jnp.where(has_right, from_right, 0.0),
                pltpu.roll(now, cols - 1, 1),
            )
        )
        stacked = (parent[level - 1] if level > 0 else zero) + (
            parent[level + 1] if level < levels - 1 else zero
        )
        ch, cv = (
            jnp.concatenate([spread[1, which, level : level + 1, :]] * (cols // LANES), axis=1)
            for which in (0, 1)
        )
        out[level] = (
            (1.0 - 4.0 * ch - 2.0 * cv) * now + ch * around + (cv * stacked + source[level])
        )
        at = cols + STRIDE * level + PARENT_AT
        before_end = jnp.where(
            wide == 0, tail[core, 0:1, at : at + 1], pltpu.roll(end, 1, 1)
        )
        after_end = jnp.where(
            wide == cols - 1, tail[core, 0:1, at + 1 : at + 2], pltpu.roll(end, cols - 1, 1)
        )
        nest_ch = spread[1, 2, level : level + 1, :]
        nest_ch = jnp.concatenate([nest_ch] * (cols // LANES), axis=1)
        share = nest_ch * nest_ch * ch * (1.0 / SUBSTEPS)
        late[level : level + 1, :] = (share * (1.0 / (RATIO * RATIO))) * (
            jnp.where(south, before_end, 0.0) + jnp.where(north, after_end, 0.0)
        )
    store.wait()


def merge(parts, band, ox_ref, oy_ref, late, step, nest, spread, beyond, *rest):
    arrived = rest[1 : 2 * parts]
    out, nest_out, joined, corner, sem, merged, out_sems = rest[2 * parts :]
    levels, rows, cols = step.shape
    foot = rest[0].shape[2]
    me = lax.axis_index("gy")

    @pl.when((ox_ref[0] == rows - 1) & ((me == 0) | (me == parts - 1)))
    def _():
        nest_rows, nest_cols = nest.shape[1:]
        first = pl.multiple_of(jnp.where(me == 0, 0, nest_cols - LANES), LANES)
        place = (slice(None), pl.ds(nest_rows - 8, 8), pl.ds(first, LANES))
        load = pltpu.make_async_copy(nest_out.at[place], corner, sem)
        load.start()
        load.wait()
        sub = iota((8, LANES), 0)
        lane = iota((8, LANES), 1)
        cell = (sub == 7) & (lane == jnp.where(me == 0, RIM, LANES - RIM - 1))
        for level in range(levels):
            at = STRIDE * level + STRIP_AT
            value = jnp.where(me == 0, beyond[0:1, at + 2 : at + 3], beyond[0:1, at + 1 : at + 2])
            nest_ch = spread[1, 2, level : level + 1, :]
            share = nest_ch * nest_ch * spread[1, 0, level : level + 1, :] * (1.0 / SUBSTEPS)
            corner[level] += jnp.where(cell, share * value, 0.0)
        again = pltpu.make_async_copy(corner, nest_out.at[place], sem)
        again.start()
        again.wait()

    ox = ox_ref[0]
    oy = oy_ref[0]
    joined[0, :, rows:, :] = rest[0][...]
    if parts == 2:
        straight, mixed, other = arrived
        joined[0, :, :rows, :] = straight[...]
        joined[1, :, :rows, :] = jnp.where(me == 0, mixed[...], other[...])
        joined[1, :, rows:, :] = jnp.where(me == 0, other[...], mixed[...])
    else:
        for k in range(parts):
            joined[k, :, :rows, :] = arrived[k][...]
        for k in range(1, parts):
            joined[k, :, rows:, :] = arrived[parts + k - 1][...]
    lane = iota((rows, LANES), 1)
    row = iota((rows, LANES), 0)
    stores = []
    for level in range(levels):
        values = [tile(step, level, piece) for piece in range(cols // LANES)]
        for k in range(parts):
            source = lax.rem(me + parts - k, parts)
            block = joined[k, level, pl.ds(rows - ox, rows), :]
            begin = oy + source * foot - me * cols
            block = pltpu.roll(block, (16384 + begin) & (LANES - 1), 1)
            low = jnp.maximum(source * foot, 2)
            high = jnp.minimum((source + 1) * foot, band - 2)
            for piece in range(cols // LANES):
                at = lane + (piece * LANES + me * cols - oy)
                values[piece] = jnp.where((at >= low) & (at < high), block, values[piece])
        for piece, value in enumerate(values):
            term = late[level : level + 1, piece * LANES : (piece + 1) * LANES]
            value = value + jnp.where(row == rows - 2, term, 0.0)
            merged[level, :, piece * LANES : (piece + 1) * LANES] = value
        stores.append(pltpu.make_async_copy(merged.at[level], out.at[level], out_sems.at[level]))
        stores[-1].start()
    for copy in stores:
        copy.wait()


def shifted(value, axis, steps):
    count = lax.axis_size(axis)
    pairs = [(source, (source + steps) % count) for source in range(count)]
    return lax.ppermute(value, axis, pairs)


def shards(
    parent_old, parent_source, parent_coefs, nest_old, nest_source, nest_coefs, offset_x, offset_y
):
    parts = lax.axis_size("gy")
    along = ("gx", "gz")
    levels, parent_rows, parent_cols = parent_old.shape
    _, rows, cols = nest_old.shape
    foot = cols // RATIO
    band = foot * parts
    width = cols if parts == 2 else cols + LANES
    height = TAIL_ROW + 16
    f32 = jnp.float32
    shape = jax.ShapeDtypeStruct
    anywhere = pl.BlockSpec(memory_space=pl.ANY)
    in_hbm = pl.BlockSpec(memory_space=pltpu.HBM)
    sides = 1 if parts == 2 else 2
    if parts == 2:
        packed = [
            pl.pallas_call(
                pack_pair,
                out_shape=VMEM((rows, LANES), f32),
                in_specs=[in_hbm] * 4,
                out_specs=whole(),
                scratch_shapes=[
                    VMEM((2, levels, rows, LANES), f32),
                    VMEM((2, levels, parent_rows, LANES), f32),
                    pltpu.SemaphoreType.DMA((4,)),
                ],
                compiler_params=params(MOST),
                cost_estimate=cost(200000, 800000),
                name="pack_pair",
            )(nest_old, nest_source, parent_old, parent_source)
        ]
    else:
        packed = pl.pallas_call(
            functools.partial(pack_columns, parts, band),
            out_shape=[
                shape((rows if k in (1, parts - 1) else parent_rows, LANES), f32)
                for k in range(1, parts)
            ],
            in_specs=[in_hbm] * 5,
            out_specs=[whole()] * (parts - 1),
            scratch_shapes=[
                VMEM((sides, levels, rows, LANES), f32),
                VMEM((sides, levels, rows, LANES), f32),
                VMEM(parent_old.shape, f32),
                VMEM(parent_old.shape, f32),
                pltpu.SMEM(offset_y.shape, jnp.int32),
                pltpu.SemaphoreType.DMA((sides, 2)),
                pltpu.SemaphoreType.DMA((3,)),
            ],
            compiler_params=params(MOST),
            cost_estimate=cost(200000, 1000000),
            name="pack_columns",
        )(offset_y, nest_old, nest_source, parent_old, parent_source)
    columns = [shifted(packed[k - 1], "gy", k) for k in range(1, parts)]
    own_strip, first, spread, oy_rows = pl.pallas_call(
        functools.partial(inner_first, band),
        out_shape=[
            shape((parent_rows, LANES), f32),
            shape(nest_old.shape, f32),
            shape((2, 4, levels, LANES), f32),
            shape((8, LANES), jnp.int32),
        ],
        in_specs=[scalars()] * 3 + [whole()] * 4,
        out_specs=[whole()] * 4,
        compiler_params=params(),
        cost_estimate=cost(4000000, 3000000),
        name="inner_first",
    )(
        offset_y,
        parent_coefs,
        nest_coefs,
        nest_old,
        nest_source,
        parent_old,
        parent_source,
    )

    def block(ref, last):
        count = ref.shape[1] // 8 - 1 if last else 0
        return pl.BlockSpec((levels, 8, ref.shape[2]), lambda i, c=count: (0, c, 0))

    def full(extent):
        return pl.BlockSpec(extent, lambda i: (0,) * len(extent))

    outs = [
        shape((height, width), f32),
        shape((height, width), f32),
        shape((8, LANES), f32),
        shape((parent_rows, LANES), f32),
    ]
    across, within, far, strips = pl.pallas_call(
        functools.partial(pack_rows, parts),
        out_shape=outs,
        grid=(1,),
        in_specs=[
            block(nest_old, False),
            block(nest_old, True),
            block(nest_old, False),
            block(nest_old, True),
            block(parent_old, False),
            block(parent_old, True),
            full(own_strip.shape),
            full(oy_rows.shape),
        ]
        + [full(message.shape) for message in columns],
        out_specs=[full(out.shape) for out in outs],
        scratch_shapes=[VMEM((2, height, width), f32)],
        compiler_params=params(),
        cost_estimate=cost(100000, 700000),
        name="pack_rows",
    )(nest_old, nest_old, nest_source, nest_source, parent_old, parent_old, own_strip, oy_rows, *columns)
    across = swapped(across, 1)
    within = swapped(within, 0)
    third, packs, window_old, window_src, sums = pl.pallas_call(
        functools.partial(inner_rest, parts),
        out_shape=[
            shape(nest_old.shape, f32),
            shape((4, rows, LANES), f32),
            shape((levels, 2, 8, width), f32),
            shape((levels, 2, 8, width), f32),
            shape((cols // LANES, levels * parent_rows, LANES), f32),
        ],
        in_specs=[scalars()] + [whole()] * 5 + [anywhere],
        out_specs=[whole()] * 5,
        scratch_shapes=[
            VMEM(nest_old.shape, f32),
            VMEM((cols // LANES, levels * rows, LANES), f32),
        ],
        compiler_params=params(),
        cost_estimate=cost(8000000, 6000000),
        name="inner_rest",
    )(nest_coefs, nest_old, first, nest_source, columns[0], columns[-1], strips)
    sides, windows, coarse, far = pl.pallas_call(
        functools.partial(edges, parts, parent_cols),
        out_shape=[
            shape((2, rows, LANES), f32),
            shape((levels, 2, 8, width), f32),
            shape((levels, parent_rows, foot), f32),
            shape((8, LANES), f32),
        ],
        in_specs=[scalars()] + [whole()] * 11,
        out_specs=[whole()] * 4,
        scratch_shapes=[
            VMEM((2, height, width), f32),
            VMEM((levels, 2, 8, width), f32),
            VMEM((levels, 2, 8, width), f32),
            VMEM((levels, 2, 8, width), f32),
        ],
        compiler_params=params(),
        cost_estimate=cost(4000000, 3000000),
        name="edges",
    )(
        offset_x,
        spread,
        sums,
        packs,
        window_old,
        window_src,
        strips,
        across,
        within,
        far,
        columns[0],
        columns[-1],
    )
    if parts == 2:
        arrived = [
            shifted(coarse, along, 1),
            shifted_both(coarse, 1, (0, 1)),
            shifted_both(coarse, 1, (1, 0)),
        ]
    else:
        arrived = [shifted(coarse, along, 1)]
        arrived += [shifted_both(coarse, k) for k in range(1, parts)]
        arrived += [shifted(coarse, "gy", k) for k in range(1, parts)]
    beyond = shifted(far, along, -2)
    step, nest_stored, late = pl.pallas_call(
        functools.partial(parent_step, parts, band),
        out_shape=[
            shape(parent_old.shape, f32),
            shape(nest_old.shape, f32),
            shape((levels, parent_cols), f32),
        ],
        in_specs=[scalars()] * 2 + [whole()] * 10,
        out_specs=[whole(), in_hbm, whole()],
        scratch_shapes=[
            VMEM((2, levels, parent_cols + LANES), f32),
            VMEM(nest_old.shape, f32),
            pltpu.SemaphoreType.DMA,
        ],
        compiler_params=params(),
        cost_estimate=cost(800000, 2500000),
        name="parent_step",
    )(
        offset_x,
        offset_y,
        spread,
        third,
        sides,
        windows,
        parent_old,
        parent_source,
        within,
        across,
        columns[0],
        columns[-1],
    )
    parent_new, nest_new = pl.pallas_call(
        functools.partial(merge, parts, band),
        out_shape=[shape(parent_old.shape, f32), shape(nest_old.shape, f32)],
        in_specs=[scalars()] * 2 + [whole()] * 2 + [in_hbm] + [whole()] * (2 + 2 * parts),
        out_specs=[in_hbm, in_hbm],
        scratch_shapes=[
            VMEM((parts, levels, 2 * parent_rows, foot), f32),
            VMEM((levels, 8, LANES), f32),
            pltpu.SemaphoreType.DMA,
            VMEM(parent_old.shape, f32),
            pltpu.SemaphoreType.DMA((levels,)),
        ],
        input_output_aliases={4: 1},
        compiler_params=params(),
        cost_estimate=cost(200000, 800000),
        name="merge",
    )(offset_x, offset_y, late, step, nest_stored, spread, beyond, coarse, *arrived)
    return (parent_new, nest_new)


def swapped(value, first):
    along = ("gx", "gz")
    count = lax.axis_size(along)
    pairs = []
    for at in range(first, count, 2):
        pairs += [(at, (at + 1) % count), ((at + 1) % count, at)]
    return lax.ppermute(value, along, pairs)


def shifted_both(value, steps, rows=None):
    sizes = [lax.axis_size(axis) for axis in ("gx", "gy", "gz")]
    gx, gy, gz = sizes
    pairs = []
    for x in range(gx):
        for y in range(gy):
            for z in range(gz):
                place = (x * gz + z + (1 if rows is None else rows[y])) % (gx * gz)
                target = (place // gz * gy + (y + steps) % gy) * gz + place % gz
                pairs.append(((x * gy + y) * gz + z, target))
    return lax.ppermute(value, ("gx", "gy", "gz"), pairs)


def solution(mesh):
    return jax.shard_map(
        shards,
        mesh=mesh,
        in_specs=(
            P(None, ("grp", "gx", "gz"), "gy"),
            P(None, ("grp", "gx", "gz"), "gy"),
            P(),
            P(None, ("grp", "gx", "gz"), "gy"),
            P(None, ("grp", "gx", "gz"), "gy"),
            P(),
            P("grp"),
            P("grp"),
        ),
        out_specs=(P(None, ("grp", "gx", "gz"), "gy"), P(None, ("grp", "gx", "gz"), "gy")),
        check_vma=False,
    )
```

```python
import functools

import jax
import jax.numpy as jnp
from jax import lax
from jax.experimental import pallas as pl
from jax.experimental.pallas import tpu as pltpu
from jax.sharding import PartitionSpec as P

RATIO = 3
SUBSTEPS = 3
RIM = 6
LANES = 128
STRIDE = 16
SOURCE_AT = 3
PARENT_AT = 6
STRIP_AT = 8
STRIP_SOURCE_AT = 12
SOURCE_ROW = 24
TAIL_ROW = 40
FIXED = 8
LEFT_AT = 3
RIGHT_OWN = STRIDE - 3
VMEM = pltpu.VMEM
LIMIT = 24 * 1024 * 1024
MOST = 54 * 1024 * 1024


def iota(shape, dim):
    return lax.broadcasted_iota(jnp.int32, shape, dim)


def whole():
    return pl.BlockSpec(memory_space=VMEM)


def scalars():
    return pl.BlockSpec(memory_space=pltpu.SMEM)


def params(limit=LIMIT):
    return pltpu.CompilerParams(vmem_limit_bytes=limit)


def cost(flops, moved):
    return pl.CostEstimate(flops=flops, bytes_accessed=moved, transcendentals=0)


def tile(ref, level, index):
    return ref[level, :, index * LANES : (index + 1) * LANES]


def turned(value, lanes):
    lanes = lanes % LANES
    return pltpu.roll(value, lanes, 1) if lanes else value


def edge_strip(dest, band, oy, parent, parent_source):
    levels, rows, cols = parent.shape
    lane = iota((rows, LANES), 1)
    base = jnp.where(dest == 0, oy - 1, oy + band - 3) - lax.axis_index("gy") * cols
    total = jnp.zeros(lane.shape, jnp.float32)
    for ref, first in ((parent, STRIP_AT), (parent_source, STRIP_SOURCE_AT)):
        for level in range(levels):
            found = jnp.zeros(lane.shape, jnp.float32)
            for at in range(cols // LANES):
                place = lane + (at * LANES - base)
                found = jnp.where((place >= 0) & (place < 4), tile(ref, level, at), found)
            turn = (16384 + first + STRIDE * level - base) & (LANES - 1)
            total = total + pltpu.roll(found, turn, 1)
    return total


def pack_pair(nest, source, parent, parent_source, out, fine_buf, coarse_buf, sems):
    levels, rows, cols = nest.shape
    parent_rows, parent_cols = parent.shape[1:]
    right = lax.axis_index("gy") == 0
    loads = []
    for at, (ref, buf) in enumerate(
        (
            (parent, coarse_buf.at[0]),
            (parent_source, coarse_buf.at[1]),
            (nest, fine_buf.at[0]),
            (source, fine_buf.at[1]),
        )
    ):
        start = pl.multiple_of(jnp.where(right, ref.shape[2] - LANES, 0), LANES)
        loads.append(pltpu.make_async_copy(ref.at[:, :, pl.ds(start, LANES)], buf, sems.at[at]))
    for copy in loads:
        copy.start()

    def columns(value, count, to):
        first = jnp.where(right, LANES - count, 0)
        place = iota(value.shape, 1) - first
        value = jnp.where((place >= 0) & (place < count), value, 0.0)
        return pltpu.roll(value, (LANES + to - first) & (LANES - 1), 1)

    part = jnp.zeros((parent_rows, LANES), jnp.float32)
    loads[0].wait()
    loads[1].wait()
    for level in range(levels):
        base = STRIDE * level
        part = part + columns(coarse_buf[0, level], 1, base + PARENT_AT)
        part = part + columns(coarse_buf[0, level], 2, base + STRIP_AT)
        part = part + columns(coarse_buf[1, level], 2, base + STRIP_SOURCE_AT)
    total = jnp.zeros((rows, LANES), jnp.float32)
    loads[2].wait()
    loads[3].wait()
    for level in range(levels):
        base = STRIDE * level
        total = total + columns(fine_buf[0, level], 3, base)
        total = total + columns(fine_buf[1, level], 3, base + SOURCE_AT)
    out[...] = total
    out[:parent_rows, :] += part


def across_border(message, oy, parent_cols, me):
    c = iota(message.shape, 1) & (STRIDE - 1)
    place = jnp.where(me == 0, parent_cols + 1, 1) - oy
    total = jnp.zeros(message.shape, jnp.float32)
    for turn in (-1, 0, 2, 3):
        at = jnp.where(c >= STRIP_SOURCE_AT, c - STRIP_SOURCE_AT, c - STRIP_AT) - turn
        fits = (c >= STRIP_AT) & (at >= 0) & (at < 2) & (place == turn)
        total = total + jnp.where(fits, turned(message, turn), 0.0)
    return total


def pack_columns(parts, band, oy_hbm, nest, source, parent_hbm, parent_source_hbm, *rest):
    outs = rest[: parts - 1]
    old_buf, src_buf, parent, parent_source, oy_ref, sems, field_sems = rest[parts - 1 :]
    levels, rows, cols = nest.shape
    parent_cols = parent.shape[2]
    me = lax.axis_index("gy")
    sides = [1] if parts == 2 else [1, parts - 1]
    fields = [
        pltpu.make_async_copy(ref, buf, field_sems.at[at])
        for at, (ref, buf) in enumerate(
            ((oy_hbm, oy_ref), (parent_hbm, parent), (parent_source_hbm, parent_source))
        )
    ]
    for copy in fields:
        copy.start()
    copies = []
    for at, step in enumerate(sides):
        right = (me == 0) if parts == 2 else jnp.bool_(step == 1)
        start = pl.multiple_of(jnp.where(right, cols - LANES, 0), LANES)
        pair = [
            pltpu.make_async_copy(
                ref.at[:, :, pl.ds(start, LANES)], buf.at[at], sems.at[at, which]
            )
            for which, (ref, buf) in enumerate(((nest, old_buf), (source, src_buf)))
        ]
        for copy in pair:
            copy.start()
        copies.append((right, pair))
    for copy in fields:
        copy.wait()
    oy = oy_ref[0]
    lane = iota((parent.shape[1], LANES), 1)
    for step in range(1, parts):
        out = outs[step - 1]
        part = edge_strip(lax.rem(me + step, parts), band, oy, parent, parent_source)
        if step not in sides:
            out[...] = part
            continue
        at = sides.index(step)
        right, pair = copies[at]
        first = jnp.where(right, LANES - 3, 0)
        outer = jnp.where(right, LANES - 1, 0)
        for level in range(levels):
            edge = jnp.where(
                right, tile(parent, level, parent_cols // LANES - 1), tile(parent, level, 0)
            )
            edge = jnp.where(lane == outer, edge, 0.0)
            turn = (LANES + PARENT_AT + STRIDE * level - outer) & (LANES - 1)
            part = part + pltpu.roll(edge, turn, 1)
        for copy in pair:
            copy.wait()
        fine = iota((rows, LANES), 1) - first
        wanted = (fine >= 0) & (fine < 3)
        total = jnp.zeros((rows, LANES), jnp.float32)
        for level in range(levels):
            for buf, shift in ((old_buf, 0), (src_buf, SOURCE_AT)):
                value = jnp.where(wanted, buf[at, level], 0.0)
                turn = (LANES + STRIDE * level + shift - first) & (LANES - 1)
                total = total + pltpu.roll(value, turn, 1)
        out[...] = total
        out[: part.shape[0], :] += part


def three_terms(value):
    terms = []
    for _ in range(3):
        term = value.astype(jnp.bfloat16)
        terms.append(term)
        value = value - term.astype(jnp.float32)
    return terms


def select_rows(selector, value):
    selector = selector.astype(jnp.bfloat16)
    high, middle, low = (
        jnp.dot(selector, term, preferred_element_type=jnp.float32)
        for term in three_terms(value)
    )
    return high + (middle + low)


def select_columns(value, selector):
    selector = selector.astype(jnp.bfloat16)
    high, middle, low = (
        jnp.dot(term, selector, preferred_element_type=jnp.float32)
        for term in three_terms(value)
    )
    return high + (middle + low)


def sum_rows(ref, count):
    first, second, third = (ref[pl.ds(at, count, RATIO), :] for at in range(RATIO))
    return first + second + third


def inner_substep(coefs, here, source, there):
    levels, rows, cols = here.shape
    sub = iota((8, cols), 0)
    tiles = rows // 8

    def one_level(level):
        ch = coefs[0, level]
        cv = coefs[1, level]
        centre = 1.0 - 4.0 * ch - 2.0 * cv
        below = jnp.maximum(level - 1, 0)
        above = jnp.minimum(level + 1, levels - 1)
        cv_below = jnp.where(level > 0, cv, 0.0)
        cv_above = jnp.where(level < levels - 1, cv, 0.0)

        def row_tile(t):
            t = t % tiles
            return here[level, 8 * t : 8 * t + 8, :]

        down_before = pltpu.roll(row_tile(-1), 1, 0)
        now = row_tile(0)
        up_now = pltpu.roll(now, 7, 0)
        for t in range(tiles):
            following = row_tile(t + 1)
            down_now = pltpu.roll(now, 1, 0)
            up_next = pltpu.roll(following, 7, 0)
            around = jnp.where(sub == 0, down_before, down_now) + jnp.where(
                sub == 7, up_next, up_now
            )
            around = around + (pltpu.roll(now, 1, 1) + pltpu.roll(now, cols - 1, 1))
            span = slice(8 * t, 8 * t + 8)
            stacked = cv_below * here[below, span, :] + cv_above * here[above, span, :]
            there[level, span, :] = centre * now + ch * around + (stacked + source[level, span, :])
            down_before, now, up_now = down_now, following, up_next

    def two_levels(pair, carry):
        one_level(2 * pair)
        one_level(2 * pair + 1)
        return carry

    lax.fori_loop(0, levels // 2, two_levels, 0)


def spread_coefs(parent_coefs, coefs, out):
    levels = out.shape[2]
    lane = iota((levels, LANES), 1)
    row = iota((levels, LANES), 0)
    for at, ref in enumerate((parent_coefs, coefs)):
        for which in range(2):
            packed = jnp.full(lane.shape, ref[which, 0], jnp.float32)
            rows = packed
            for level in range(1, levels):
                packed = jnp.where(lane >= STRIDE * level, ref[which, level], packed)
                rows = jnp.where(row == level, ref[which, level], rows)
            out[0, 2 * at + which] = packed
            out[1, 2 * at + which] = rows


def inner_first(
    band,
    oy_ref,
    parent_coefs,
    coefs,
    nest,
    source,
    parent,
    parent_source,
    strip,
    first,
    spread,
    oy_rows,
):
    oy = oy_ref[0]
    oy_rows[...] = jnp.full(oy_rows.shape, oy, jnp.int32)
    spread_coefs(parent_coefs, coefs, spread)
    strip[...] = edge_strip(lax.axis_index("gy"), band, oy, parent, parent_source)
    inner_substep(coefs, nest, source, first)


def own_windows(parts, nest, source, y_left, y_right, window_old, window_src):
    levels, rows, cols = nest.shape
    pieces = cols // LANES
    me = lax.axis_index("gy")
    for level in range(levels):
        for buf, field, shift in ((window_old, nest, 0), (window_src, source, SOURCE_AT)):
            for window, first, turn in ((0, 0, 3), (1, rows - 8, 5)):
                tiles = [
                    field[level, first : first + 8, piece * LANES : (piece + 1) * LANES]
                    for piece in range(pieces)
                ]
                tiles = with_columns(
                    tiles,
                    y_left[first : first + 8, :],
                    y_right[first : first + 8, :],
                    me,
                    parts,
                    STRIDE * level + shift,
                )
                for piece, value in enumerate(tiles):
                    buf[level, window, :, piece * LANES : (piece + 1) * LANES] = pltpu.roll(
                        value, turn, 0
                    )


def inner_rest(
    parts,
    coefs,
    nest,
    first,
    source,
    y_left,
    y_right,
    after_pack,
    third,
    packs,
    window_old,
    window_src,
    sums,
    second,
    split,
):
    levels, rows, cols = nest.shape
    own_windows(parts, nest, source, y_left, y_right, window_old, window_src)
    lane = iota((rows, LANES), 1)
    for at, ref in enumerate((nest, source)):
        left = jnp.zeros(lane.shape, jnp.float32)
        right = jnp.zeros(lane.shape, jnp.float32)
        for level in range(levels):
            value = jnp.where(lane < RIGHT_OWN, tile(ref, level, 0), 0.0)
            left = left + turned(value, STRIDE * level + LEFT_AT)
            value = jnp.where(lane >= LANES - RIGHT_OWN, tile(ref, level, cols // LANES - 1), 0.0)
            right = right + turned(value, STRIDE * level + RIGHT_OWN)
        packs[2 * at] = left
        packs[2 * at + 1] = right
    inner_substep(coefs, first, source, second)
    inner_substep(coefs, second, source, third)
    for level in range(levels):
        for piece in range(cols // LANES):
            split[piece, level * rows : (level + 1) * rows, :] = tile(third, level, piece)
    for piece in range(cols // LANES):
        sums[piece] = sum_rows(split.at[piece], levels * rows // RATIO)


def with_columns(tiles, left, right, me, parts, place):
    lane = iota(left.shape, 1)
    from_right = turned(right, -place)
    from_left = turned(left, -3 - place)
    if parts == 2:
        tiles[0] = jnp.where((lane < 3) & (me == 0), from_right, tiles[0])
        tiles[-1] = jnp.where((lane >= LANES - 3) & (me == 1), from_left, tiles[-1])
        return tiles
    extra = jnp.where(lane < 3, from_right, jnp.where(lane >= LANES - 3, from_left, 0.0))
    return tiles + [extra]


def pack_rows(
    parts, old_top, old_end, src_top, src_end, par_top, par_end, own_strip, oy_rows, *rest
):
    columns = rest[: parts - 1]
    across, within, far, strip_out, both = rest[parts - 1 :]
    core = lax.axis_index("gz")
    up, down = both.at[core], both.at[1 - core]
    levels, _, cols = old_top.shape
    me = lax.axis_index("gy")
    left, right = columns[0], columns[-1]
    rows = left.shape[0]
    strip_rows = own_strip.shape[0]
    lane = iota((strip_rows, LANES), 1)
    strips = own_strip[...]
    if parts == 2:
        oy = jnp.concatenate([oy_rows[...]] * (strip_rows // 8), axis=0)
        strips = strips + across_border(left[:strip_rows, :], oy, par_top.shape[2], me)
    else:
        for message in columns:
            strips = strips + message[:strip_rows, :]
    c = lane & (STRIDE - 1)
    strips = jnp.where(c >= STRIP_AT, strips, 0.0)
    strips = jnp.where(c == PARENT_AT, left[:strip_rows, :], strips)
    strips = jnp.where(c == PARENT_AT + 1, turned(right[:strip_rows, :], 1), strips)
    strip_out[...] = strips
    far[...] = strips[:8]
    pieces = cols // LANES
    for out, old, src, first, at, src_at in (
        (up, old_end, src_end, rows - 8, 5, 6),
        (down, old_top, src_top, 0, 0, 0),
    ):
        y_left = left[first : first + 8, :]
        y_right = right[first : first + 8, :]
        for level in range(levels):
            for ref, shift, row, count, base in (
                (old, 0, at, 3, 0),
                (src, SOURCE_AT, src_at, 2, SOURCE_ROW),
            ):
                tiles = [tile(ref, level, piece) for piece in range(pieces)]
                tiles = with_columns(
                    tiles, y_left, y_right, me, parts, STRIDE * level + shift
                )
                for piece, value in enumerate(tiles):
                    out[
                        base + count * level : base + count * (level + 1),
                        piece * LANES : (piece + 1) * LANES,
                    ] = value[row : row + count]
    parent_cols = par_top.shape[2]
    for level in range(levels):
        up[TAIL_ROW + level : TAIL_ROW + level + 1, :parent_cols] = par_end[level, 7:8, :]
        down[TAIL_ROW + level : TAIL_ROW + level + 1, :parent_cols] = par_top[level, 0:1, :]
    up[TAIL_ROW : TAIL_ROW + 8, parent_cols : parent_cols + LANES] = strips[strip_rows - 8 :]
    down[TAIL_ROW : TAIL_ROW + 8, parent_cols : parent_cols + LANES] = strips[:8]
    down[TAIL_ROW + 8 : TAIL_ROW + 16, :LANES] = strips[8:16]
    down[TAIL_ROW + 8 : TAIL_ROW + 16, LANES : 2 * LANES] = strips[16:24]
    within[...] = both[0]
    across[...] = both[1]


def edges(
    parts,
    parent_cols,
    ox_ref,
    spread,
    sums,
    packs,
    window_old,
    window_src,
    strips,
    across,
    within,
    far,
    y_left,
    y_right,
    sides,
    windows,
    coarse_out,
    far_out,
    both,
    ping,
    pong,
    src,
):
    levels = ping.shape[0]
    width = ping.shape[3]
    rows = packs.shape[1]
    cols = sums.shape[0] * LANES
    pieces = cols // LANES
    me = lax.axis_index("gy")
    core = lax.axis_index("gz")
    both[0] = within[...]
    both[1] = across[...]
    before, after = both.at[1 - core], both.at[core]
    is_south = me == 0
    is_north = me == parts - 1

    far_out[...] = far[...]
    sub = iota((8, LANES), 0)
    old = jnp.concatenate(
        [
            strips[...],
            after[TAIL_ROW : TAIL_ROW + 8, parent_cols : parent_cols + LANES],
            after[TAIL_ROW + 8 : TAIL_ROW + 16, :LANES],
            after[TAIL_ROW + 8 : TAIL_ROW + 16, LANES : 2 * LANES],
            jnp.where(
                sub == 7,
                before[TAIL_ROW : TAIL_ROW + 8, parent_cols : parent_cols + LANES],
                0.0,
            ),
        ],
        axis=0,
    )
    count = old.shape[0]

    def packed_coef(which, height):
        return jnp.concatenate([spread[0, which]] * (height // 8), axis=0)

    def stacked(value):
        lane = iota(value.shape, 1)
        below = jnp.where(lane >= STRIDE, turned(value, STRIDE), 0.0)
        return below + jnp.where(lane < STRIDE * (levels - 1), turned(value, -STRIDE), 0.0)

    def around(value):
        return (
            pltpu.roll(value, 1, 0)
            + pltpu.roll(value, value.shape[0] - 1, 0)
            + turned(value, 1)
            + turned(value, -1)
        )

    diff = (
        packed_coef(0, count) * (around(old) - 4.0 * old)
        + packed_coef(1, count) * (stacked(old) - 2.0 * old)
        + turned(old, STRIP_AT - STRIP_SOURCE_AT)
    )
    index = iota((rows + 16, count), 0)
    nest_row = jnp.where(index < rows, index, jnp.where(index < rows + 8, index - rows - 3, index - 13))
    parent_row = ((nest_row + 3) * 171 >> 9) - 1 + ox_ref[0]
    pick = (iota((rows + 16, count), 1) == parent_row).astype(jnp.float32)
    picked = select_rows(pick, jnp.concatenate([old, diff], axis=1))
    picked_old, picked_diff = picked[:, :LANES], picked[:, LANES:]

    lane = iota((rows, LANES), 1)
    c = lane & (STRIDE - 1)
    rim_first = jnp.where(is_south, LEFT_AT, RIGHT_OWN - RIM)
    in_rim = (c >= rim_first) & (c < rim_first + RIM)
    at = lane - c + STRIP_AT + jnp.where(c >= rim_first + 3, 2, 1)
    rim_old = jnp.take_along_axis(picked_old[:rows], at, axis=1)
    rim_diff = jnp.take_along_axis(picked_diff[:rows], at, axis=1)
    ch = packed_coef(2, rows)
    cv = packed_coef(3, rows)
    centre = 1.0 - 4.0 * ch - 2.0 * cv
    left = jnp.where(c < 3, y_left[...], packs[0])
    left_src = jnp.where(c < 3, turned(y_left[...], -SOURCE_AT), packs[2])
    right = jnp.where(c >= RIGHT_OWN, turned(y_right[...], RIGHT_OWN), packs[1])
    right_src = jnp.where(c >= RIGHT_OWN, turned(y_right[...], RIGHT_OWN - SOURCE_AT), packs[3])
    for side, (value, forcing, rim) in enumerate(
        (
            (left, left_src, in_rim & is_south),
            (right, right_src, in_rim & is_north),
        )
    ):
        for substep in range(1, SUBSTEPS + 1):
            value = centre * value + ch * around(value) + (cv * stacked(value) + forcing)
            value = jnp.where(rim, rim_old + (substep / SUBSTEPS) * rim_diff, value)
        sides[side, :rows, :] = value

    sub = iota((8, width), 0)
    lane = iota((8, LANES), 1)
    ping[...] = window_old[...]
    src[...] = window_src[...]
    for level in range(levels):
        for buf, n, base in ((ping, 3, 0), (src, 2, SOURCE_ROW)):
            rows_of = slice(base + n * level, base + n * (level + 1))
            buf[level, 0, 3 - n : 3, :] = before[rows_of, :]
            buf[level, 1, 5 : 5 + n, :] = after[rows_of, :]
    rim_first = jnp.where(is_south, 0, LANES - RIM)
    column = STRIP_AT + jnp.where((lane >= rim_first + 3) & (lane < rim_first + RIM), 2, 1)
    rims = {}
    for level in range(levels):
        for window in range(2):
            span = slice(rows + 8 * window, rows + 8 * window + 8)
            at = column + STRIDE * level
            rims[level, window] = (
                jnp.take_along_axis(picked_old[span], at, axis=1),
                jnp.take_along_axis(picked_diff[span], at, axis=1),
            )
    for substep in range(1, SUBSTEPS + 1):
        here, there = (ping, pong) if substep % 2 else (pong, ping)
        there = windows if substep == SUBSTEPS else there
        low = 0 if substep == SUBSTEPS or parts > 2 else 3
        south = (lane >= low) & (lane < RIM) & is_south
        north = (lane >= LANES - RIM) & (lane < LANES - low) & is_north
        weight = substep / SUBSTEPS
        for level in range(levels):
            c_h, c_v = (
                jnp.concatenate([spread[1, which, level : level + 1, :]] * (width // LANES), axis=1)
                for which in (2, 3)
            )
            c_0 = 1.0 - 4.0 * c_h - 2.0 * c_v
            for window in range(2):
                now = here[level, window]
                up = pltpu.roll(now, 1, 0)
                down = pltpu.roll(now, 7, 0)
                if substep == 1:
                    beyond_row = window_old[level, window]
                    if window == 0:
                        down = jnp.where(sub == 7, pltpu.roll(beyond_row, 7, 0), down)
                    else:
                        up = jnp.where(sub == 0, pltpu.roll(beyond_row, 1, 0), up)
                beside = pltpu.roll(now, 1, 1) + pltpu.roll(now, width - 1, 1)
                value = c_0 * now + c_h * ((up + down) + beside) + src[level, window]
                if level > 0:
                    value = value + c_v * here[level - 1, window]
                if level < levels - 1:
                    value = value + c_v * here[level + 1, window]
                rim_o, rim_d = rims[level, window]
                rim = rim_o + weight * rim_d
                for piece in range(width // LANES):
                    span = slice(piece * LANES, (piece + 1) * LANES)
                    part = value[:, span]
                    if piece == 0:
                        part = jnp.where(south, rim, part)
                    if piece == pieces - 1:
                        part = jnp.where(north, rim, part)
                    there[level, window, :, span] = part

    parent_rows = rows // RATIO
    lane = iota((parent_rows, LANES), 1)
    row = iota((parent_rows, LANES), 0)
    side_sums = [sum_rows(sides.at[side], parent_rows) for side in range(2)]
    replaced = [[] for _ in range(pieces)]
    for level in range(levels):
        span = slice(level * parent_rows, (level + 1) * parent_rows)
        top = windows[level, 0, 3:4, :] + windows[level, 0, 4:5, :] + windows[level, 0, 5:6, :]
        end = windows[level, 1, 2:3, :] + windows[level, 1, 3:4, :] + windows[level, 1, 4:5, :]
        for piece in range(pieces):
            value = sums[piece, span, :]
            if piece == 0:
                fixed = turned(side_sums[0], -STRIDE * level - LEFT_AT)
                value = jnp.where(lane < FIXED, fixed, value)
            if piece == pieces - 1:
                fixed = turned(side_sums[1], -STRIDE * level - RIGHT_OWN)
                value = jnp.where(lane >= LANES - FIXED, fixed, value)
            across_piece = slice(piece * LANES, (piece + 1) * LANES)
            value = jnp.where(row == 0, top[:, across_piece], value)
            value = jnp.where(row == parent_rows - 1, end[:, across_piece], value)
            replaced[piece].append(value)
    foot = cols // RATIO
    offset = iota((cols, foot), 0) - RATIO * iota((cols, foot), 1)
    gather = ((offset >= 0) & (offset < RATIO)).astype(jnp.float32)
    means = select_columns(
        jnp.concatenate([jnp.concatenate(values, axis=0) for values in replaced], axis=1), gather
    ) * (1.0 / 9.0)
    coarse_out[...] = means.reshape(coarse_out.shape)


def put_together(third, sides, windows, result):
    levels, rows, cols = third.shape
    pieces = cols // LANES
    lane = iota((rows, LANES), 1)
    sub = iota((8, cols), 0)
    for level in range(levels):
        fixed = turned(sides[0, :rows, :], -STRIDE * level - LEFT_AT)
        result[level, :, :LANES] = jnp.where(lane < FIXED, fixed, tile(third, level, 0))
        for piece in range(1, pieces - 1):
            result[level, :, piece * LANES : (piece + 1) * LANES] = tile(third, level, piece)
        fixed = turned(sides[1, :rows, :], -STRIDE * level - RIGHT_OWN)
        result[level, :, cols - LANES :] = jnp.where(
            lane >= LANES - FIXED, fixed, tile(third, level, pieces - 1)
        )
        top = pltpu.roll(windows[level, 0, :, :cols], 5, 0)
        result[level, :8, :] = jnp.where(sub < 3, top, result[level, :8, :])
        end = pltpu.roll(windows[level, 1, :, :cols], 3, 0)
        result[level, rows - 8 :, :] = jnp.where(sub >= 5, end, result[level, rows - 8 :, :])


def parent_step(
    parts,
    band,
    ox_ref,
    oy_ref,
    spread,
    third,
    sides,
    windows,
    parent,
    source,
    within,
    across,
    y_left,
    y_right,
    out,
    nest_out,
    late,
    tail,
    result,
    sem,
):
    put_together(third, sides, windows, result)
    store = pltpu.make_async_copy(result, nest_out, sem)
    store.start()
    core = lax.axis_index("gz")
    levels, rows, cols = parent.shape
    tail[0] = within[TAIL_ROW : TAIL_ROW + levels, : cols + LANES]
    tail[1] = across[TAIL_ROW : TAIL_ROW + levels, : cols + LANES]
    me = lax.axis_index("gy")
    is_last = ox_ref[0] == rows - 1
    wide = iota((1, cols), 1)
    south = (wide == oy_ref[0] + 2 - me * cols) & is_last
    north = (wide == oy_ref[0] + band - 3 - me * cols) & is_last
    row = iota((rows, cols), 0)
    lane = iota((rows, cols), 1)
    has_left = me > 0
    has_right = me < parts - 1
    left = y_left[:rows, :]
    right = y_right[:rows, :]
    zero = jnp.zeros((rows, cols), jnp.float32)
    for level in range(levels):
        now = parent[level]
        at = STRIDE * level + PARENT_AT
        from_left = left[:, at : at + 1]
        from_right = right[:, at : at + 1]
        top = tail[1 - core, level : level + 1, :cols]
        end = tail[core, level : level + 1, :cols]
        around = (
            jnp.where(row == 0, top, pltpu.roll(now, 1, 0))
            + jnp.where(row == rows - 1, end, pltpu.roll(now, rows - 1, 0))
            + jnp.where(
                lane == 0, jnp.where(has_left, from_left, 0.0), pltpu.roll(now, 1, 1)
            )
            + jnp.where(
                lane == cols - 1,
                jnp.where(has_right, from_right, 0.0),
                pltpu.roll(now, cols - 1, 1),
            )
        )
        stacked = (parent[level - 1] if level > 0 else zero) + (
            parent[level + 1] if level < levels - 1 else zero
        )
        ch, cv = (
            jnp.concatenate([spread[1, which, level : level + 1, :]] * (cols // LANES), axis=1)
            for which in (0, 1)
        )
        out[level] = (
            (1.0 - 4.0 * ch - 2.0 * cv) * now + ch * around + (cv * stacked + source[level])
        )
        at = cols + STRIDE * level + PARENT_AT
        before_end = jnp.where(
            wide == 0, tail[core, 0:1, at : at + 1], pltpu.roll(end, 1, 1)
        )
        after_end = jnp.where(
            wide == cols - 1, tail[core, 0:1, at + 1 : at + 2], pltpu.roll(end, cols - 1, 1)
        )
        nest_ch = spread[1, 2, level : level + 1, :]
        nest_ch = jnp.concatenate([nest_ch] * (cols // LANES), axis=1)
        share = nest_ch * nest_ch * ch * (1.0 / SUBSTEPS)
        late[level : level + 1, :] = (share * (1.0 / (RATIO * RATIO))) * (
            jnp.where(south, before_end, 0.0) + jnp.where(north, after_end, 0.0)
        )
    store.wait()


def merge(parts, band, ox_ref, oy_ref, late, step, nest, spread, beyond, *rest):
    arrived = rest[1 : 2 * parts]
    out, nest_out, joined, corner, sem, merged, out_sems = rest[2 * parts :]
    levels, rows, cols = step.shape
    foot = rest[0].shape[2]
    me = lax.axis_index("gy")

    @pl.when((ox_ref[0] == rows - 1) & ((me == 0) | (me == parts - 1)))
    def _():
        nest_rows, nest_cols = nest.shape[1:]
        first = pl.multiple_of(jnp.where(me == 0, 0, nest_cols - LANES), LANES)
        place = (slice(None), pl.ds(nest_rows - 8, 8), pl.ds(first, LANES))
        load = pltpu.make_async_copy(nest_out.at[place], corner, sem)
        load.start()
        load.wait()
        sub = iota((8, LANES), 0)
        lane = iota((8, LANES), 1)
        cell = (sub == 7) & (lane == jnp.where(me == 0, RIM, LANES - RIM - 1))
        for level in range(levels):
            at = STRIDE * level + STRIP_AT
            value = jnp.where(me == 0, beyond[0:1, at + 2 : at + 3], beyond[0:1, at + 1 : at + 2])
            nest_ch = spread[1, 2, level : level + 1, :]
            share = nest_ch * nest_ch * spread[1, 0, level : level + 1, :] * (1.0 / SUBSTEPS)
            corner[level] += jnp.where(cell, share * value, 0.0)
        again = pltpu.make_async_copy(corner, nest_out.at[place], sem)
        again.start()
        again.wait()

    ox = ox_ref[0]
    oy = oy_ref[0]
    joined[0, :, rows:, :] = rest[0][...]
    if parts == 2:
        mixed, straight, other = arrived
        joined[0, :, :rows, :] = straight[...]
        joined[1, :, :rows, :] = jnp.where(me == 0, mixed[...], other[...])
        joined[1, :, rows:, :] = jnp.where(me == 0, other[...], mixed[...])
    else:
        for k in range(parts):
            joined[k, :, :rows, :] = arrived[k][...]
        for k in range(1, parts):
            joined[k, :, rows:, :] = arrived[parts + k - 1][...]
    lane = iota((rows, LANES), 1)
    row = iota((rows, LANES), 0)
    stores = []
    for level in range(levels):
        values = [tile(step, level, piece) for piece in range(cols // LANES)]
        for k in range(parts):
            source = lax.rem(me + parts - k, parts)
            block = joined[k, level, pl.ds(rows - ox, rows), :]
            begin = oy + source * foot - me * cols
            block = pltpu.roll(block, (16384 + begin) & (LANES - 1), 1)
            low = jnp.maximum(source * foot, 2)
            high = jnp.minimum((source + 1) * foot, band - 2)
            for piece in range(cols // LANES):
                at = lane + (piece * LANES + me * cols - oy)
                values[piece] = jnp.where((at >= low) & (at < high), block, values[piece])
        for piece, value in enumerate(values):
            term = late[level : level + 1, piece * LANES : (piece + 1) * LANES]
            value = value + jnp.where(row == rows - 2, term, 0.0)
            merged[level, :, piece * LANES : (piece + 1) * LANES] = value
        stores.append(pltpu.make_async_copy(merged.at[level], out.at[level], out_sems.at[level]))
        stores[-1].start()
    for copy in stores:
        copy.wait()


def shifted(value, axis, steps):
    count = lax.axis_size(axis)
    pairs = [(source, (source + steps) % count) for source in range(count)]
    return lax.ppermute(value, axis, pairs)


def shards(
    parent_old, parent_source, parent_coefs, nest_old, nest_source, nest_coefs, offset_x, offset_y
):
    parts = lax.axis_size("gy")
    along = ("gx", "gz")
    levels, parent_rows, parent_cols = parent_old.shape
    _, rows, cols = nest_old.shape
    foot = cols // RATIO
    band = foot * parts
    width = cols if parts == 2 else cols + LANES
    height = TAIL_ROW + 16
    f32 = jnp.float32
    shape = jax.ShapeDtypeStruct
    anywhere = pl.BlockSpec(memory_space=pl.ANY)
    in_hbm = pl.BlockSpec(memory_space=pltpu.HBM)
    sides = 1 if parts == 2 else 2
    if parts == 2:
        packed = [
            pl.pallas_call(
                pack_pair,
                out_shape=VMEM((rows, LANES), f32),
                in_specs=[in_hbm] * 4,
                out_specs=whole(),
                scratch_shapes=[
                    VMEM((2, levels, rows, LANES), f32),
                    VMEM((2, levels, parent_rows, LANES), f32),
                    pltpu.SemaphoreType.DMA((4,)),
                ],
                compiler_params=params(MOST),
                cost_estimate=cost(200000, 800000),
                name="pack_pair",
            )(nest_old, nest_source, parent_old, parent_source)
        ]
    else:
        packed = pl.pallas_call(
            functools.partial(pack_columns, parts, band),
            out_shape=[
                shape((rows if k in (1, parts - 1) else parent_rows, LANES), f32)
                for k in range(1, parts)
            ],
            in_specs=[in_hbm] * 5,
            out_specs=[whole()] * (parts - 1),
            scratch_shapes=[
                VMEM((sides, levels, rows, LANES), f32),
                VMEM((sides, levels, rows, LANES), f32),
                VMEM(parent_old.shape, f32),
                VMEM(parent_old.shape, f32),
                pltpu.SMEM(offset_y.shape, jnp.int32),
                pltpu.SemaphoreType.DMA((sides, 2)),
                pltpu.SemaphoreType.DMA((3,)),
            ],
            compiler_params=params(MOST),
            cost_estimate=cost(200000, 1000000),
            name="pack_columns",
        )(offset_y, nest_old, nest_source, parent_old, parent_source)
    columns = [shifted(packed[k - 1], "gy", k) for k in range(1, parts)]
    own_strip, first, spread, oy_rows = pl.pallas_call(
        functools.partial(inner_first, band),
        out_shape=[
            shape((parent_rows, LANES), f32),
            shape(nest_old.shape, f32),
            shape((2, 4, levels, LANES), f32),
            shape((8, LANES), jnp.int32),
        ],
        in_specs=[scalars()] * 3 + [whole()] * 4,
        out_specs=[whole()] * 4,
        compiler_params=params(),
        cost_estimate=cost(4000000, 3000000),
        name="inner_first",
    )(
        offset_y,
        parent_coefs,
        nest_coefs,
        nest_old,
        nest_source,
        parent_old,
        parent_source,
    )

    def block(ref, last):
        count = ref.shape[1] // 8 - 1 if last else 0
        return pl.BlockSpec((levels, 8, ref.shape[2]), lambda i, c=count: (0, c, 0))

    def full(extent):
        return pl.BlockSpec(extent, lambda i: (0,) * len(extent))

    outs = [
        shape((height, width), f32),
        shape((height, width), f32),
        shape((8, LANES), f32),
        shape((parent_rows, LANES), f32),
    ]
    across, within, far, strips = pl.pallas_call(
        functools.partial(pack_rows, parts),
        out_shape=outs,
        grid=(1,),
        in_specs=[
            block(nest_old, False),
            block(nest_old, True),
            block(nest_old, False),
            block(nest_old, True),
            block(parent_old, False),
            block(parent_old, True),
            full(own_strip.shape),
            full(oy_rows.shape),
        ]
        + [full(message.shape) for message in columns],
        out_specs=[full(out.shape) for out in outs],
        scratch_shapes=[VMEM((2, height, width), f32)],
        compiler_params=params(),
        cost_estimate=cost(100000, 700000),
        name="pack_rows",
    )(nest_old, nest_old, nest_source, nest_source, parent_old, parent_old, own_strip, oy_rows, *columns)
    across = swapped(across, 1)
    within = swapped(within, 0)
    third, packs, window_old, window_src, sums = pl.pallas_call(
        functools.partial(inner_rest, parts),
        out_shape=[
            shape(nest_old.shape, f32),
            shape((4, rows, LANES), f32),
            shape((levels, 2, 8, width), f32),
            shape((levels, 2, 8, width), f32),
            shape((cols // LANES, levels * parent_rows, LANES), f32),
        ],
        in_specs=[scalars()] + [whole()] * 5 + [anywhere],
        out_specs=[whole()] * 5,
        scratch_shapes=[
            VMEM(nest_old.shape, f32),
            VMEM((cols // LANES, levels * rows + 8, LANES), f32),
        ],
        compiler_params=params(),
        cost_estimate=cost(8000000, 6000000),
        name="inner_rest",
    )(nest_coefs, nest_old, first, nest_source, columns[0], columns[-1], strips)
    sides, windows, coarse, far = pl.pallas_call(
        functools.partial(edges, parts, parent_cols),
        out_shape=[
            shape((2, rows + 8, LANES), f32),
            shape((levels, 2, 8, width), f32),
            shape((levels, parent_rows, foot), f32),
            shape((8, LANES), f32),
        ],
        in_specs=[scalars()] + [whole()] * 11,
        out_specs=[whole()] * 4,
        scratch_shapes=[
            VMEM((2, height, width), f32),
            VMEM((levels, 2, 8, width), f32),
            VMEM((levels, 2, 8, width), f32),
            VMEM((levels, 2, 8, width), f32),
        ],
        compiler_params=params(),
        cost_estimate=cost(4000000, 3000000),
        name="edges",
    )(
        offset_x,
        spread,
        sums,
        packs,
        window_old,
        window_src,
        strips,
        across,
        within,
        far,
        columns[0],
        columns[-1],
    )
    if parts == 2:
        arrived = [
            shifted_both(coarse, 1, (0, 1)),
            shifted(coarse, along, 1),
            shifted_both(coarse, 1, (1, 0)),
        ]
    else:
        arrived = [shifted(coarse, along, 1)]
        arrived += [shifted_both(coarse, k) for k in range(1, parts)]
        arrived += [shifted(coarse, "gy", k) for k in range(1, parts)]
    beyond = shifted(far, along, -2)
    step, nest_stored, late = pl.pallas_call(
        functools.partial(parent_step, parts, band),
        out_shape=[
            shape(parent_old.shape, f32),
            shape(nest_old.shape, f32),
            shape((levels, parent_cols), f32),
        ],
        in_specs=[scalars()] * 2 + [whole()] * 10,
        out_specs=[whole(), in_hbm, whole()],
        scratch_shapes=[
            VMEM((2, levels, parent_cols + LANES), f32),
            VMEM(nest_old.shape, f32),
            pltpu.SemaphoreType.DMA,
        ],
        compiler_params=params(),
        cost_estimate=cost(800000, 2500000),
        name="parent_step",
    )(
        offset_x,
        offset_y,
        spread,
        third,
        sides,
        windows,
        parent_old,
        parent_source,
        within,
        across,
        columns[0],
        columns[-1],
    )
    parent_new, nest_new = pl.pallas_call(
        functools.partial(merge, parts, band),
        out_shape=[shape(parent_old.shape, f32), shape(nest_old.shape, f32)],
        in_specs=[scalars()] * 2 + [whole()] * 2 + [in_hbm] + [whole()] * (2 + 2 * parts),
        out_specs=[in_hbm, in_hbm],
        scratch_shapes=[
            VMEM((parts, levels, 2 * parent_rows, foot), f32),
            VMEM((levels, 8, LANES), f32),
            pltpu.SemaphoreType.DMA,
            VMEM(parent_old.shape, f32),
            pltpu.SemaphoreType.DMA((levels,)),
        ],
        input_output_aliases={4: 1},
        compiler_params=params(),
        cost_estimate=cost(200000, 800000),
        name="merge",
    )(offset_x, offset_y, late, step, nest_stored, spread, beyond, coarse, *arrived)
    return (parent_new, nest_new)


def swapped(value, first):
    along = ("gx", "gz")
    count = lax.axis_size(along)
    pairs = []
    for at in range(first, count, 2):
        pairs += [(at, (at + 1) % count), ((at + 1) % count, at)]
    return lax.ppermute(value, along, pairs)


def shifted_both(value, steps, rows=None):
    sizes = [lax.axis_size(axis) for axis in ("gx", "gy", "gz")]
    gx, gy, gz = sizes
    pairs = []
    for x in range(gx):
        for y in range(gy):
            for z in range(gz):
                place = (x * gz + z + (1 if rows is None else rows[y])) % (gx * gz)
                target = (place // gz * gy + (y + steps) % gy) * gz + place % gz
                pairs.append(((x * gy + y) * gz + z, target))
    return lax.ppermute(value, ("gx", "gy", "gz"), pairs)


def solution(mesh):
    return jax.shard_map(
        shards,
        mesh=mesh,
        in_specs=(
            P(None, ("grp", "gx", "gz"), "gy"),
            P(None, ("grp", "gx", "gz"), "gy"),
            P(),
            P(None, ("grp", "gx", "gz"), "gy"),
            P(None, ("grp", "gx", "gz"), "gy"),
            P(),
            P("grp"),
            P("grp"),
        ),
        out_specs=(P(None, ("grp", "gx", "gz"), "gy"), P(None, ("grp", "gx", "gz"), "gy")),
        check_vma=False,
    )
```

```python
import functools

import jax
import jax.numpy as jnp
from jax import lax
from jax.experimental import pallas as pl
from jax.experimental.pallas import tpu as pltpu
from jax.sharding import PartitionSpec as P

RATIO = 3
SUBSTEPS = 3
RIM = 6
LANES = 128
STRIDE = 16
SOURCE_AT = 3
PARENT_AT = 6
STRIP_AT = 8
STRIP_SOURCE_AT = 12
SOURCE_ROW = 24
TAIL_ROW = 40
FIXED = 8
LEFT_AT = 3
RIGHT_OWN = STRIDE - 3
VMEM = pltpu.VMEM
LIMIT = 24 * 1024 * 1024
MOST = 54 * 1024 * 1024


def iota(shape, dim):
    return lax.broadcasted_iota(jnp.int32, shape, dim)


def whole():
    return pl.BlockSpec(memory_space=VMEM)


def scalars():
    return pl.BlockSpec(memory_space=pltpu.SMEM)


def params(limit=LIMIT):
    return pltpu.CompilerParams(vmem_limit_bytes=limit)


def cost(flops, moved):
    return pl.CostEstimate(flops=flops, bytes_accessed=moved, transcendentals=0)


def tile(ref, level, index):
    return ref[level, :, index * LANES : (index + 1) * LANES]


def turned(value, lanes):
    lanes = lanes % LANES
    return pltpu.roll(value, lanes, 1) if lanes else value


def edge_strip(dest, band, oy, parent, parent_source):
    levels, rows, cols = parent.shape
    lane = iota((rows, LANES), 1)
    base = jnp.where(dest == 0, oy - 1, oy + band - 3) - lax.axis_index("gy") * cols
    total = jnp.zeros(lane.shape, jnp.float32)
    for ref, first in ((parent, STRIP_AT), (parent_source, STRIP_SOURCE_AT)):
        for level in range(levels):
            found = jnp.zeros(lane.shape, jnp.float32)
            for at in range(cols // LANES):
                place = lane + (at * LANES - base)
                found = jnp.where((place >= 0) & (place < 4), tile(ref, level, at), found)
            turn = (16384 + first + STRIDE * level - base) & (LANES - 1)
            total = total + pltpu.roll(found, turn, 1)
    return total


def pack_pair(nest, source, parent, parent_source, out, fine_buf, coarse_buf, sems):
    levels, rows, cols = nest.shape
    parent_rows, parent_cols = parent.shape[1:]
    right = lax.axis_index("gy") == 0
    loads = []
    for at, (ref, buf) in enumerate(
        (
            (parent, coarse_buf.at[0]),
            (parent_source, coarse_buf.at[1]),
            (nest, fine_buf.at[0]),
            (source, fine_buf.at[1]),
        )
    ):
        start = pl.multiple_of(jnp.where(right, ref.shape[2] - LANES, 0), LANES)
        loads.append(pltpu.make_async_copy(ref.at[:, :, pl.ds(start, LANES)], buf, sems.at[at]))
    for copy in loads:
        copy.start()

    def columns(value, count, to):
        first = jnp.where(right, LANES - count, 0)
        place = iota(value.shape, 1) - first
        value = jnp.where((place >= 0) & (place < count), value, 0.0)
        return pltpu.roll(value, (LANES + to - first) & (LANES - 1), 1)

    part = jnp.zeros((parent_rows, LANES), jnp.float32)
    loads[0].wait()
    loads[1].wait()
    for level in range(levels):
        base = STRIDE * level
        part = part + columns(coarse_buf[0, level], 1, base + PARENT_AT)
        part = part + columns(coarse_buf[0, level], 2, base + STRIP_AT)
        part = part + columns(coarse_buf[1, level], 2, base + STRIP_SOURCE_AT)
    total = jnp.zeros((rows, LANES), jnp.float32)
    loads[2].wait()
    loads[3].wait()
    for level in range(levels):
        base = STRIDE * level
        total = total + columns(fine_buf[0, level], 3, base)
        total = total + columns(fine_buf[1, level], 3, base + SOURCE_AT)
    out[...] = total
    out[:parent_rows, :] += part


def across_border(message, oy, parent_cols, me):
    c = iota(message.shape, 1) & (STRIDE - 1)
    place = jnp.where(me == 0, parent_cols + 1, 1) - oy
    total = jnp.zeros(message.shape, jnp.float32)
    for turn in (-1, 0, 2, 3):
        at = jnp.where(c >= STRIP_SOURCE_AT, c - STRIP_SOURCE_AT, c - STRIP_AT) - turn
        fits = (c >= STRIP_AT) & (at >= 0) & (at < 2) & (place == turn)
        total = total + jnp.where(fits, turned(message, turn), 0.0)
    return total


def pack_columns(parts, band, oy_hbm, nest, source, parent_hbm, parent_source_hbm, *rest):
    outs = rest[: parts - 1]
    old_buf, src_buf, parent, parent_source, oy_ref, sems, field_sems = rest[parts - 1 :]
    levels, rows, cols = nest.shape
    parent_cols = parent.shape[2]
    me = lax.axis_index("gy")
    sides = [1] if parts == 2 else [1, parts - 1]
    fields = [
        pltpu.make_async_copy(ref, buf, field_sems.at[at])
        for at, (ref, buf) in enumerate(
            ((oy_hbm, oy_ref), (parent_hbm, parent), (parent_source_hbm, parent_source))
        )
    ]
    for copy in fields:
        copy.start()
    copies = []
    for at, step in enumerate(sides):
        right = (me == 0) if parts == 2 else jnp.bool_(step == 1)
        start = pl.multiple_of(jnp.where(right, cols - LANES, 0), LANES)
        pair = [
            pltpu.make_async_copy(
                ref.at[:, :, pl.ds(start, LANES)], buf.at[at], sems.at[at, which]
            )
            for which, (ref, buf) in enumerate(((nest, old_buf), (source, src_buf)))
        ]
        for copy in pair:
            copy.start()
        copies.append((right, pair))
    for copy in fields:
        copy.wait()
    oy = oy_ref[0]
    lane = iota((parent.shape[1], LANES), 1)
    for step in range(1, parts):
        out = outs[step - 1]
        part = edge_strip(lax.rem(me + step, parts), band, oy, parent, parent_source)
        if step not in sides:
            out[...] = part
            continue
        at = sides.index(step)
        right, pair = copies[at]
        first = jnp.where(right, LANES - 3, 0)
        outer = jnp.where(right, LANES - 1, 0)
        for level in range(levels):
            edge = jnp.where(
                right, tile(parent, level, parent_cols // LANES - 1), tile(parent, level, 0)
            )
            edge = jnp.where(lane == outer, edge, 0.0)
            turn = (LANES + PARENT_AT + STRIDE * level - outer) & (LANES - 1)
            part = part + pltpu.roll(edge, turn, 1)
        for copy in pair:
            copy.wait()
        fine = iota((rows, LANES), 1) - first
        wanted = (fine >= 0) & (fine < 3)
        total = jnp.zeros((rows, LANES), jnp.float32)
        for level in range(levels):
            for buf, shift in ((old_buf, 0), (src_buf, SOURCE_AT)):
                value = jnp.where(wanted, buf[at, level], 0.0)
                turn = (LANES + STRIDE * level + shift - first) & (LANES - 1)
                total = total + pltpu.roll(value, turn, 1)
        out[...] = total
        out[: part.shape[0], :] += part


def three_terms(value):
    terms = []
    for _ in range(3):
        term = value.astype(jnp.bfloat16)
        terms.append(term)
        value = value - term.astype(jnp.float32)
    return terms


def select_rows(selector, value):
    selector = selector.astype(jnp.bfloat16)
    high, middle, low = (
        jnp.dot(selector, term, preferred_element_type=jnp.float32)
        for term in three_terms(value)
    )
    return high + (middle + low)


def select_columns(value, selector):
    selector = selector.astype(jnp.bfloat16)
    high, middle, low = (
        jnp.dot(term, selector, preferred_element_type=jnp.float32)
        for term in three_terms(value)
    )
    return high + (middle + low)


def sum_rows(ref, count):
    first, second, third = (ref[pl.ds(at, count, RATIO), :] for at in range(RATIO))
    return first + second + third


def inner_substep(coefs, here, source, there):
    levels, rows, cols = here.shape
    sub = iota((8, cols), 0)
    tiles = rows // 8

    def one_level(level):
        ch = coefs[0, level]
        cv = coefs[1, level]
        centre = 1.0 - 4.0 * ch - 2.0 * cv
        below = jnp.maximum(level - 1, 0)
        above = jnp.minimum(level + 1, levels - 1)
        cv_below = jnp.where(level > 0, cv, 0.0)
        cv_above = jnp.where(level < levels - 1, cv, 0.0)

        def row_tile(t):
            t = t % tiles
            return here[level, 8 * t : 8 * t + 8, :]

        down_before = pltpu.roll(row_tile(-1), 1, 0)
        now = row_tile(0)
        up_now = pltpu.roll(now, 7, 0)
        for t in range(tiles):
            following = row_tile(t + 1)
            down_now = pltpu.roll(now, 1, 0)
            up_next = pltpu.roll(following, 7, 0)
            around = jnp.where(sub == 0, down_before, down_now) + jnp.where(
                sub == 7, up_next, up_now
            )
            around = around + (pltpu.roll(now, 1, 1) + pltpu.roll(now, cols - 1, 1))
            span = slice(8 * t, 8 * t + 8)
            stacked = cv_below * here[below, span, :] + cv_above * here[above, span, :]
            there[level, span, :] = centre * now + ch * around + (stacked + source[level, span, :])
            down_before, now, up_now = down_now, following, up_next

    def two_levels(pair, carry):
        one_level(2 * pair)
        one_level(2 * pair + 1)
        return carry

    lax.fori_loop(0, levels // 2, two_levels, 0)


def spread_coefs(parent_coefs, coefs, out):
    levels = out.shape[2]
    lane = iota((levels, LANES), 1)
    row = iota((levels, LANES), 0)
    for at, ref in enumerate((parent_coefs, coefs)):
        for which in range(2):
            packed = jnp.full(lane.shape, ref[which, 0], jnp.float32)
            rows = packed
            for level in range(1, levels):
                packed = jnp.where(lane >= STRIDE * level, ref[which, level], packed)
                rows = jnp.where(row == level, ref[which, level], rows)
            out[0, 2 * at + which] = packed
            out[1, 2 * at + which] = rows


def inner_first(
    band,
    oy_ref,
    parent_coefs,
    coefs,
    nest,
    source,
    parent,
    parent_source,
    strip,
    first,
    spread,
    oy_rows,
):
    oy = oy_ref[0]
    oy_rows[...] = jnp.full(oy_rows.shape, oy, jnp.int32)
    spread_coefs(parent_coefs, coefs, spread)
    strip[...] = edge_strip(lax.axis_index("gy"), band, oy, parent, parent_source)
    inner_substep(coefs, nest, source, first)


def own_windows(parts, nest, source, y_left, y_right, window_old, window_src):
    levels, rows, cols = nest.shape
    pieces = cols // LANES
    me = lax.axis_index("gy")
    for level in range(levels):
        for buf, field, shift in ((window_old, nest, 0), (window_src, source, SOURCE_AT)):
            for window, first, turn in ((0, 0, 3), (1, rows - 8, 5)):
                tiles = [
                    field[level, first : first + 8, piece * LANES : (piece + 1) * LANES]
                    for piece in range(pieces)
                ]
                tiles = with_columns(
                    tiles,
                    y_left[first : first + 8, :],
                    y_right[first : first + 8, :],
                    me,
                    parts,
                    STRIDE * level + shift,
                )
                for piece, value in enumerate(tiles):
                    buf[level, window, :, piece * LANES : (piece + 1) * LANES] = pltpu.roll(
                        value, turn, 0
                    )


def inner_rest(
    parts,
    coefs,
    nest,
    first,
    source,
    y_left,
    y_right,
    after_pack,
    third,
    packs,
    window_old,
    window_src,
    sums,
    second,
    split,
):
    levels, rows, cols = nest.shape
    own_windows(parts, nest, source, y_left, y_right, window_old, window_src)
    lane = iota((rows, LANES), 1)
    for at, ref in enumerate((nest, source)):
        left = jnp.zeros(lane.shape, jnp.float32)
        right = jnp.zeros(lane.shape, jnp.float32)
        for level in range(levels):
            value = jnp.where(lane < RIGHT_OWN, tile(ref, level, 0), 0.0)
            left = left + turned(value, STRIDE * level + LEFT_AT)
            value = jnp.where(lane >= LANES - RIGHT_OWN, tile(ref, level, cols // LANES - 1), 0.0)
            right = right + turned(value, STRIDE * level + RIGHT_OWN)
        packs[2 * at] = left
        packs[2 * at + 1] = right
    inner_substep(coefs, first, source, second)
    inner_substep(coefs, second, source, third)
    for level in range(levels):
        for piece in range(cols // LANES):
            split[piece, level * rows : (level + 1) * rows, :] = tile(third, level, piece)
    for piece in range(cols // LANES):
        sums[piece] = sum_rows(split.at[piece], levels * rows // RATIO)


def with_columns(tiles, left, right, me, parts, place):
    lane = iota(left.shape, 1)
    from_right = turned(right, -place)
    from_left = turned(left, -3 - place)
    if parts == 2:
        tiles[0] = jnp.where((lane < 3) & (me == 0), from_right, tiles[0])
        tiles[-1] = jnp.where((lane >= LANES - 3) & (me == 1), from_left, tiles[-1])
        return tiles
    extra = jnp.where(lane < 3, from_right, jnp.where(lane >= LANES - 3, from_left, 0.0))
    return tiles + [extra]


def pack_rows(
    parts, old_top, old_end, src_top, src_end, par_top, par_end, own_strip, oy_rows, *rest
):
    columns = rest[: parts - 1]
    across, within, far, strip_out, both = rest[parts - 1 :]
    core = lax.axis_index("gz")
    up, down = both.at[core], both.at[1 - core]
    levels, _, cols = old_top.shape
    me = lax.axis_index("gy")
    left, right = columns[0], columns[-1]
    rows = left.shape[0]
    strip_rows = own_strip.shape[0]
    lane = iota((strip_rows, LANES), 1)
    strips = own_strip[...]
    if parts == 2:
        oy = jnp.concatenate([oy_rows[...]] * (strip_rows // 8), axis=0)
        strips = strips + across_border(left[:strip_rows, :], oy, par_top.shape[2], me)
    else:
        for message in columns:
            strips = strips + message[:strip_rows, :]
    c = lane & (STRIDE - 1)
    strips = jnp.where(c >= STRIP_AT, strips, 0.0)
    strips = jnp.where(c == PARENT_AT, left[:strip_rows, :], strips)
    strips = jnp.where(c == PARENT_AT + 1, turned(right[:strip_rows, :], 1), strips)
    strip_out[...] = strips
    far[...] = strips[:8]
    pieces = cols // LANES
    for out, old, src, first, at, src_at in (
        (up, old_end, src_end, rows - 8, 5, 6),
        (down, old_top, src_top, 0, 0, 0),
    ):
        y_left = left[first : first + 8, :]
        y_right = right[first : first + 8, :]
        for level in range(levels):
            for ref, shift, row, count, base in (
                (old, 0, at, 3, 0),
                (src, SOURCE_AT, src_at, 2, SOURCE_ROW),
            ):
                tiles = [tile(ref, level, piece) for piece in range(pieces)]
                tiles = with_columns(
                    tiles, y_left, y_right, me, parts, STRIDE * level + shift
                )
                for piece, value in enumerate(tiles):
                    out[
                        base + count * level : base + count * (level + 1),
                        piece * LANES : (piece + 1) * LANES,
                    ] = value[row : row + count]
    parent_cols = par_top.shape[2]
    for level in range(levels):
        up[TAIL_ROW + level : TAIL_ROW + level + 1, :parent_cols] = par_end[level, 7:8, :]
        down[TAIL_ROW + level : TAIL_ROW + level + 1, :parent_cols] = par_top[level, 0:1, :]
    up[TAIL_ROW : TAIL_ROW + 8, parent_cols : parent_cols + LANES] = strips[strip_rows - 8 :]
    down[TAIL_ROW : TAIL_ROW + 8, parent_cols : parent_cols + LANES] = strips[:8]
    down[TAIL_ROW + 8 : TAIL_ROW + 16, :LANES] = strips[8:16]
    down[TAIL_ROW + 8 : TAIL_ROW + 16, LANES : 2 * LANES] = strips[16:24]
    within[...] = both[0]
    across[...] = both[1]


def edges(
    parts,
    parent_cols,
    ox_ref,
    spread,
    sums,
    packs,
    window_old,
    window_src,
    strips,
    across,
    within,
    far,
    y_left,
    y_right,
    sides,
    windows,
    coarse_out,
    far_out,
    both,
    ping,
    pong,
    src,
):
    levels = ping.shape[0]
    width = ping.shape[3]
    rows = packs.shape[1]
    cols = sums.shape[0] * LANES
    pieces = cols // LANES
    me = lax.axis_index("gy")
    core = lax.axis_index("gz")
    both[0] = within[...]
    both[1] = across[...]
    before, after = both.at[1 - core], both.at[core]
    is_south = me == 0
    is_north = me == parts - 1

    far_out[...] = far[...]
    sub = iota((8, LANES), 0)
    old = jnp.concatenate(
        [
            strips[...],
            after[TAIL_ROW : TAIL_ROW + 8, parent_cols : parent_cols + LANES],
            after[TAIL_ROW + 8 : TAIL_ROW + 16, :LANES],
            after[TAIL_ROW + 8 : TAIL_ROW + 16, LANES : 2 * LANES],
            jnp.where(
                sub == 7,
                before[TAIL_ROW : TAIL_ROW + 8, parent_cols : parent_cols + LANES],
                0.0,
            ),
        ],
        axis=0,
    )
    count = old.shape[0]

    def packed_coef(which, height):
        return jnp.concatenate([spread[0, which]] * (height // 8), axis=0)

    def stacked(value):
        lane = iota(value.shape, 1)
        below = jnp.where(lane >= STRIDE, turned(value, STRIDE), 0.0)
        return below + jnp.where(lane < STRIDE * (levels - 1), turned(value, -STRIDE), 0.0)

    def around(value):
        return (
            pltpu.roll(value, 1, 0)
            + pltpu.roll(value, value.shape[0] - 1, 0)
            + turned(value, 1)
            + turned(value, -1)
        )

    diff = (
        packed_coef(0, count) * (around(old) - 4.0 * old)
        + packed_coef(1, count) * (stacked(old) - 2.0 * old)
        + turned(old, STRIP_AT - STRIP_SOURCE_AT)
    )
    index = iota((rows + 16, count), 0)
    nest_row = jnp.where(index < rows, index, jnp.where(index < rows + 8, index - rows - 3, index - 13))
    parent_row = ((nest_row + 3) * 171 >> 9) - 1 + ox_ref[0]
    pick = (iota((rows + 16, count), 1) == parent_row).astype(jnp.float32)
    picked = select_rows(pick, jnp.concatenate([old, diff], axis=1))
    picked_old, picked_diff = picked[:, :LANES], picked[:, LANES:]

    lane = iota((rows, LANES), 1)
    c = lane & (STRIDE - 1)
    rim_first = jnp.where(is_south, LEFT_AT, RIGHT_OWN - RIM)
    in_rim = (c >= rim_first) & (c < rim_first + RIM)
    at = lane - c + STRIP_AT + jnp.where(c >= rim_first + 3, 2, 1)
    rim_old = jnp.take_along_axis(picked_old[:rows], at, axis=1)
    rim_diff = jnp.take_along_axis(picked_diff[:rows], at, axis=1)
    ch = packed_coef(2, rows)
    cv = packed_coef(3, rows)
    centre = 1.0 - 4.0 * ch - 2.0 * cv
    left = jnp.where(c < 3, y_left[...], packs[0])
    left_src = jnp.where(c < 3, turned(y_left[...], -SOURCE_AT), packs[2])
    right = jnp.where(c >= RIGHT_OWN, turned(y_right[...], RIGHT_OWN), packs[1])
    right_src = jnp.where(c >= RIGHT_OWN, turned(y_right[...], RIGHT_OWN - SOURCE_AT), packs[3])
    for side, (value, forcing, rim) in enumerate(
        (
            (left, left_src, in_rim & is_south),
            (right, right_src, in_rim & is_north),
        )
    ):
        for substep in range(1, SUBSTEPS + 1):
            value = centre * value + ch * around(value) + (cv * stacked(value) + forcing)
            value = jnp.where(rim, rim_old + (substep / SUBSTEPS) * rim_diff, value)
        sides[side, :rows, :] = value

    sub = iota((8, width), 0)
    lane = iota((8, LANES), 1)
    ping[...] = window_old[...]
    src[...] = window_src[...]
    for level in range(levels):
        for buf, n, base in ((ping, 3, 0), (src, 2, SOURCE_ROW)):
            rows_of = slice(base + n * level, base + n * (level + 1))
            buf[level, 0, 3 - n : 3, :] = before[rows_of, :]
            buf[level, 1, 5 : 5 + n, :] = after[rows_of, :]
    rim_first = jnp.where(is_south, 0, LANES - RIM)
    column = STRIP_AT + jnp.where((lane >= rim_first + 3) & (lane < rim_first + RIM), 2, 1)
    rims = {}
    for level in range(levels):
        for window in range(2):
            span = slice(rows + 8 * window, rows + 8 * window + 8)
            at = column + STRIDE * level
            rims[level, window] = (
                jnp.take_along_axis(picked_old[span], at, axis=1),
                jnp.take_along_axis(picked_diff[span], at, axis=1),
            )
    for substep in range(1, SUBSTEPS + 1):
        here, there = (ping, pong) if substep % 2 else (pong, ping)
        there = windows if substep == SUBSTEPS else there
        low = 0 if substep == SUBSTEPS or parts > 2 else 3
        south = (lane >= low) & (lane < RIM) & is_south
        north = (lane >= LANES - RIM) & (lane < LANES - low) & is_north
        weight = substep / SUBSTEPS
        for level in range(levels):
            c_h, c_v = (
                jnp.concatenate([spread[1, which, level : level + 1, :]] * (width // LANES), axis=1)
                for which in (2, 3)
            )
            c_0 = 1.0 - 4.0 * c_h - 2.0 * c_v
            for window in range(2):
                now = here[level, window]
                up = pltpu.roll(now, 1, 0)
                down = pltpu.roll(now, 7, 0)
                if substep == 1:
                    beyond_row = window_old[level, window]
                    if window == 0:
                        down = jnp.where(sub == 7, pltpu.roll(beyond_row, 7, 0), down)
                    else:
                        up = jnp.where(sub == 0, pltpu.roll(beyond_row, 1, 0), up)
                beside = pltpu.roll(now, 1, 1) + pltpu.roll(now, width - 1, 1)
                value = c_0 * now + c_h * ((up + down) + beside) + src[level, window]
                if level > 0:
                    value = value + c_v * here[level - 1, window]
                if level < levels - 1:
                    value = value + c_v * here[level + 1, window]
                rim_o, rim_d = rims[level, window]
                rim = rim_o + weight * rim_d
                for piece in range(width // LANES):
                    span = slice(piece * LANES, (piece + 1) * LANES)
                    part = value[:, span]
                    if piece == 0:
                        part = jnp.where(south, rim, part)
                    if piece == pieces - 1:
                        part = jnp.where(north, rim, part)
                    there[level, window, :, span] = part

    parent_rows = rows // RATIO
    lane = iota((parent_rows, LANES), 1)
    row = iota((parent_rows, LANES), 0)
    side_sums = [sum_rows(sides.at[side], parent_rows) for side in range(2)]
    replaced = [[] for _ in range(pieces)]
    for level in range(levels):
        span = slice(level * parent_rows, (level + 1) * parent_rows)
        top = windows[level, 0, 3:4, :] + windows[level, 0, 4:5, :] + windows[level, 0, 5:6, :]
        end = windows[level, 1, 2:3, :] + windows[level, 1, 3:4, :] + windows[level, 1, 4:5, :]
        for piece in range(pieces):
            value = sums[piece, span, :]
            if piece == 0:
                fixed = turned(side_sums[0], -STRIDE * level - LEFT_AT)
                value = jnp.where(lane < FIXED, fixed, value)
            if piece == pieces - 1:
                fixed = turned(side_sums[1], -STRIDE * level - RIGHT_OWN)
                value = jnp.where(lane >= LANES - FIXED, fixed, value)
            across_piece = slice(piece * LANES, (piece + 1) * LANES)
            value = jnp.where(row == 0, top[:, across_piece], value)
            value = jnp.where(row == parent_rows - 1, end[:, across_piece], value)
            replaced[piece].append(value)
    foot = cols // RATIO
    offset = iota((cols, foot), 0) - RATIO * iota((cols, foot), 1)
    gather = ((offset >= 0) & (offset < RATIO)).astype(jnp.float32)
    means = select_columns(
        jnp.concatenate([jnp.concatenate(values, axis=0) for values in replaced], axis=1), gather
    ) * (1.0 / 9.0)
    coarse_out[...] = means.reshape(coarse_out.shape)


def put_together(third, sides, windows, result):
    levels, rows, cols = third.shape
    pieces = cols // LANES
    lane = iota((rows, LANES), 1)
    sub = iota((8, cols), 0)
    for level in range(levels):
        fixed = turned(sides[0, :rows, :], -STRIDE * level - LEFT_AT)
        result[level, :, :LANES] = jnp.where(lane < FIXED, fixed, tile(third, level, 0))
        for piece in range(1, pieces - 1):
            result[level, :, piece * LANES : (piece + 1) * LANES] = tile(third, level, piece)
        fixed = turned(sides[1, :rows, :], -STRIDE * level - RIGHT_OWN)
        result[level, :, cols - LANES :] = jnp.where(
            lane >= LANES - FIXED, fixed, tile(third, level, pieces - 1)
        )
        top = pltpu.roll(windows[level, 0, :, :cols], 5, 0)
        result[level, :8, :] = jnp.where(sub < 3, top, result[level, :8, :])
        end = pltpu.roll(windows[level, 1, :, :cols], 3, 0)
        result[level, rows - 8 :, :] = jnp.where(sub >= 5, end, result[level, rows - 8 :, :])


def parent_step(
    parts,
    band,
    ox_ref,
    oy_ref,
    spread,
    third,
    sides,
    windows,
    parent,
    source,
    within,
    across,
    y_left,
    y_right,
    out,
    nest_out,
    late,
    tail,
    result,
    sem,
):
    put_together(third, sides, windows, result)
    store = pltpu.make_async_copy(result, nest_out, sem)
    store.start()
    core = lax.axis_index("gz")
    levels, rows, cols = parent.shape
    tail[0] = within[TAIL_ROW : TAIL_ROW + levels, : cols + LANES]
    tail[1] = across[TAIL_ROW : TAIL_ROW + levels, : cols + LANES]
    me = lax.axis_index("gy")
    is_last = ox_ref[0] == rows - 1
    wide = iota((1, cols), 1)
    south = (wide == oy_ref[0] + 2 - me * cols) & is_last
    north = (wide == oy_ref[0] + band - 3 - me * cols) & is_last
    row = iota((rows, cols), 0)
    lane = iota((rows, cols), 1)
    has_left = me > 0
    has_right = me < parts - 1
    left = y_left[:rows, :]
    right = y_right[:rows, :]
    zero = jnp.zeros((rows, cols), jnp.float32)
    for level in range(levels):
        now = parent[level]
        at = STRIDE * level + PARENT_AT
        from_left = left[:, at : at + 1]
        from_right = right[:, at : at + 1]
        top = tail[1 - core, level : level + 1, :cols]
        end = tail[core, level : level + 1, :cols]
        around = (
            jnp.where(row == 0, top, pltpu.roll(now, 1, 0))
            + jnp.where(row == rows - 1, end, pltpu.roll(now, rows - 1, 0))
            + jnp.where(
                lane == 0, jnp.where(has_left, from_left, 0.0), pltpu.roll(now, 1, 1)
            )
            + jnp.where(
                lane == cols - 1,
                jnp.where(has_right, from_right, 0.0),
                pltpu.roll(now, cols - 1, 1),
            )
        )
        stacked = (parent[level - 1] if level > 0 else zero) + (
            parent[level + 1] if level < levels - 1 else zero
        )
        ch, cv = (
            jnp.concatenate([spread[1, which, level : level + 1, :]] * (cols // LANES), axis=1)
            for which in (0, 1)
        )
        out[level] = (
            (1.0 - 4.0 * ch - 2.0 * cv) * now + ch * around + (cv * stacked + source[level])
        )
        at = cols + STRIDE * level + PARENT_AT
        before_end = jnp.where(
            wide == 0, tail[core, 0:1, at : at + 1], pltpu.roll(end, 1, 1)
        )
        after_end = jnp.where(
            wide == cols - 1, tail[core, 0:1, at + 1 : at + 2], pltpu.roll(end, cols - 1, 1)
        )
        nest_ch = spread[1, 2, level : level + 1, :]
        nest_ch = jnp.concatenate([nest_ch] * (cols // LANES), axis=1)
        share = nest_ch * nest_ch * ch * (1.0 / SUBSTEPS)
        late[level : level + 1, :] = (share * (1.0 / (RATIO * RATIO))) * (
            jnp.where(south, before_end, 0.0) + jnp.where(north, after_end, 0.0)
        )
    store.wait()


def merge(parts, band, ox_ref, oy_ref, late, step, nest, spread, beyond, *rest):
    arrived = rest[1 : 2 * parts]
    out, nest_out, joined, corner, sem, merged, out_sems = rest[2 * parts :]
    levels, rows, cols = step.shape
    foot = rest[0].shape[2]
    me = lax.axis_index("gy")

    @pl.when((ox_ref[0] == rows - 1) & ((me == 0) | (me == parts - 1)))
    def _():
        nest_rows, nest_cols = nest.shape[1:]
        first = pl.multiple_of(jnp.where(me == 0, 0, nest_cols - LANES), LANES)
        place = (slice(None), pl.ds(nest_rows - 8, 8), pl.ds(first, LANES))
        load = pltpu.make_async_copy(nest_out.at[place], corner, sem)
        load.start()
        load.wait()
        sub = iota((8, LANES), 0)
        lane = iota((8, LANES), 1)
        cell = (sub == 7) & (lane == jnp.where(me == 0, RIM, LANES - RIM - 1))
        for level in range(levels):
            at = STRIDE * level + STRIP_AT
            value = jnp.where(me == 0, beyond[0:1, at + 2 : at + 3], beyond[0:1, at + 1 : at + 2])
            nest_ch = spread[1, 2, level : level + 1, :]
            share = nest_ch * nest_ch * spread[1, 0, level : level + 1, :] * (1.0 / SUBSTEPS)
            corner[level] += jnp.where(cell, share * value, 0.0)
        again = pltpu.make_async_copy(corner, nest_out.at[place], sem)
        again.start()
        again.wait()

    ox = ox_ref[0]
    oy = oy_ref[0]
    joined[0, :, rows:, :] = rest[0][...]
    if parts == 2:
        diagonal, straight, beside = arrived
        joined[0, :, :rows, :] = straight[...]
        joined[1, :, :rows, :] = diagonal[...]
        joined[1, :, rows:, :] = beside[...]
    else:
        for k in range(parts):
            joined[k, :, :rows, :] = arrived[k][...]
        for k in range(1, parts):
            joined[k, :, rows:, :] = arrived[parts + k - 1][...]
    lane = iota((rows, LANES), 1)
    row = iota((rows, LANES), 0)
    stores = []
    for level in range(levels):
        values = [tile(step, level, piece) for piece in range(cols // LANES)]
        for k in range(parts):
            source = lax.rem(me + parts - k, parts)
            block = joined[k, level, pl.ds(rows - ox, rows), :]
            begin = oy + source * foot - me * cols
            block = pltpu.roll(block, (16384 + begin) & (LANES - 1), 1)
            low = jnp.maximum(source * foot, 2)
            high = jnp.minimum((source + 1) * foot, band - 2)
            for piece in range(cols // LANES):
                at = lane + (piece * LANES + me * cols - oy)
                values[piece] = jnp.where((at >= low) & (at < high), block, values[piece])
        for piece, value in enumerate(values):
            term = late[level : level + 1, piece * LANES : (piece + 1) * LANES]
            value = value + jnp.where(row == rows - 2, term, 0.0)
            merged[level, :, piece * LANES : (piece + 1) * LANES] = value
        stores.append(pltpu.make_async_copy(merged.at[level], out.at[level], out_sems.at[level]))
        stores[-1].start()
    for copy in stores:
        copy.wait()


def shifted(value, axis, steps):
    count = lax.axis_size(axis)
    pairs = [(source, (source + steps) % count) for source in range(count)]
    return lax.ppermute(value, axis, pairs)


def shards(
    parent_old, parent_source, parent_coefs, nest_old, nest_source, nest_coefs, offset_x, offset_y
):
    parts = lax.axis_size("gy")
    along = ("gx", "gz")
    levels, parent_rows, parent_cols = parent_old.shape
    _, rows, cols = nest_old.shape
    foot = cols // RATIO
    band = foot * parts
    width = cols if parts == 2 else cols + LANES
    height = TAIL_ROW + 16
    f32 = jnp.float32
    shape = jax.ShapeDtypeStruct
    anywhere = pl.BlockSpec(memory_space=pl.ANY)
    in_hbm = pl.BlockSpec(memory_space=pltpu.HBM)
    sides = 1 if parts == 2 else 2
    if parts == 2:
        packed = [
            pl.pallas_call(
                pack_pair,
                out_shape=VMEM((rows, LANES), f32),
                in_specs=[in_hbm] * 4,
                out_specs=whole(),
                scratch_shapes=[
                    VMEM((2, levels, rows, LANES), f32),
                    VMEM((2, levels, parent_rows, LANES), f32),
                    pltpu.SemaphoreType.DMA((4,)),
                ],
                compiler_params=params(MOST),
                cost_estimate=cost(200000, 800000),
                name="pack_pair",
            )(nest_old, nest_source, parent_old, parent_source)
        ]
    else:
        packed = pl.pallas_call(
            functools.partial(pack_columns, parts, band),
            out_shape=[
                shape((rows if k in (1, parts - 1) else parent_rows, LANES), f32)
                for k in range(1, parts)
            ],
            in_specs=[in_hbm] * 5,
            out_specs=[whole()] * (parts - 1),
            scratch_shapes=[
                VMEM((sides, levels, rows, LANES), f32),
                VMEM((sides, levels, rows, LANES), f32),
                VMEM(parent_old.shape, f32),
                VMEM(parent_old.shape, f32),
                pltpu.SMEM(offset_y.shape, jnp.int32),
                pltpu.SemaphoreType.DMA((sides, 2)),
                pltpu.SemaphoreType.DMA((3,)),
            ],
            compiler_params=params(MOST),
            cost_estimate=cost(200000, 1000000),
            name="pack_columns",
        )(offset_y, nest_old, nest_source, parent_old, parent_source)
    columns = [shifted(packed[k - 1], "gy", k) for k in range(1, parts)]
    own_strip, first, spread, oy_rows = pl.pallas_call(
        functools.partial(inner_first, band),
        out_shape=[
            shape((parent_rows, LANES), f32),
            shape(nest_old.shape, f32),
            shape((2, 4, levels, LANES), f32),
            shape((8, LANES), jnp.int32),
        ],
        in_specs=[scalars()] * 3 + [whole()] * 4,
        out_specs=[whole()] * 4,
        compiler_params=params(),
        cost_estimate=cost(4000000, 3000000),
        name="inner_first",
    )(
        offset_y,
        parent_coefs,
        nest_coefs,
        nest_old,
        nest_source,
        parent_old,
        parent_source,
    )

    def block(ref, last):
        count = ref.shape[1] // 8 - 1 if last else 0
        return pl.BlockSpec((levels, 8, ref.shape[2]), lambda i, c=count: (0, c, 0))

    def full(extent):
        return pl.BlockSpec(extent, lambda i: (0,) * len(extent))

    outs = [
        shape((height, width), f32),
        shape((height, width), f32),
        shape((8, LANES), f32),
        shape((parent_rows, LANES), f32),
    ]
    across, within, far, strips = pl.pallas_call(
        functools.partial(pack_rows, parts),
        out_shape=outs,
        grid=(1,),
        in_specs=[
            block(nest_old, False),
            block(nest_old, True),
            block(nest_old, False),
            block(nest_old, True),
            block(parent_old, False),
            block(parent_old, True),
            full(own_strip.shape),
            full(oy_rows.shape),
        ]
        + [full(message.shape) for message in columns],
        out_specs=[full(out.shape) for out in outs],
        scratch_shapes=[VMEM((2, height, width), f32)],
        compiler_params=params(),
        cost_estimate=cost(100000, 700000),
        name="pack_rows",
    )(nest_old, nest_old, nest_source, nest_source, parent_old, parent_old, own_strip, oy_rows, *columns)
    across = swapped(across, 1)
    within = swapped(within, 0)
    third, packs, window_old, window_src, sums = pl.pallas_call(
        functools.partial(inner_rest, parts),
        out_shape=[
            shape(nest_old.shape, f32),
            shape((4, rows, LANES), f32),
            shape((levels, 2, 8, width), f32),
            shape((levels, 2, 8, width), f32),
            shape((cols // LANES, levels * parent_rows, LANES), f32),
        ],
        in_specs=[scalars()] + [whole()] * 5 + [anywhere],
        out_specs=[whole()] * 5,
        scratch_shapes=[
            VMEM(nest_old.shape, f32),
            VMEM((cols // LANES, levels * rows + 8, LANES), f32),
        ],
        compiler_params=params(),
        cost_estimate=cost(8000000, 6000000),
        name="inner_rest",
    )(nest_coefs, nest_old, first, nest_source, columns[0], columns[-1], strips)
    sides, windows, coarse, far = pl.pallas_call(
        functools.partial(edges, parts, parent_cols),
        out_shape=[
            shape((2, rows + 8, LANES), f32),
            shape((levels, 2, 8, width), f32),
            shape((levels, parent_rows, foot), f32),
            shape((8, LANES), f32),
        ],
        in_specs=[scalars()] + [whole()] * 11,
        out_specs=[whole()] * 4,
        scratch_shapes=[
            VMEM((2, height, width), f32),
            VMEM((levels, 2, 8, width), f32),
            VMEM((levels, 2, 8, width), f32),
            VMEM((levels, 2, 8, width), f32),
        ],
        compiler_params=params(),
        cost_estimate=cost(4000000, 3000000),
        name="edges",
    )(
        offset_x,
        spread,
        sums,
        packs,
        window_old,
        window_src,
        strips,
        across,
        within,
        far,
        columns[0],
        columns[-1],
    )
    if parts == 2:
        arrived = [
            shifted_both(coarse, 1),
            shifted(coarse, along, 1),
            shifted(coarse, "gy", 1),
        ]
    else:
        arrived = [shifted(coarse, along, 1)]
        arrived += [shifted_both(coarse, k) for k in range(1, parts)]
        arrived += [shifted(coarse, "gy", k) for k in range(1, parts)]
    beyond = shifted(far, along, -2)
    step, nest_stored, late = pl.pallas_call(
        functools.partial(parent_step, parts, band),
        out_shape=[
            shape(parent_old.shape, f32),
            shape(nest_old.shape, f32),
            shape((levels, parent_cols), f32),
        ],
        in_specs=[scalars()] * 2 + [whole()] * 10,
        out_specs=[whole(), in_hbm, whole()],
        scratch_shapes=[
            VMEM((2, levels, parent_cols + LANES), f32),
            VMEM(nest_old.shape, f32),
            pltpu.SemaphoreType.DMA,
        ],
        compiler_params=params(),
        cost_estimate=cost(800000, 2500000),
        name="parent_step",
    )(
        offset_x,
        offset_y,
        spread,
        third,
        sides,
        windows,
        parent_old,
        parent_source,
        within,
        across,
        columns[0],
        columns[-1],
    )
    parent_new, nest_new = pl.pallas_call(
        functools.partial(merge, parts, band),
        out_shape=[shape(parent_old.shape, f32), shape(nest_old.shape, f32)],
        in_specs=[scalars()] * 2 + [whole()] * 2 + [in_hbm] + [whole()] * (2 + 2 * parts),
        out_specs=[in_hbm, in_hbm],
        scratch_shapes=[
            VMEM((parts, levels, 2 * parent_rows, foot), f32),
            VMEM((levels, 8, LANES), f32),
            pltpu.SemaphoreType.DMA,
            VMEM(parent_old.shape, f32),
            pltpu.SemaphoreType.DMA((levels,)),
        ],
        input_output_aliases={4: 1},
        compiler_params=params(),
        cost_estimate=cost(200000, 800000),
        name="merge",
    )(offset_x, offset_y, late, step, nest_stored, spread, beyond, coarse, *arrived)
    return (parent_new, nest_new)


def swapped(value, first):
    along = ("gx", "gz")
    count = lax.axis_size(along)
    pairs = []
    for at in range(first, count, 2):
        pairs += [(at, (at + 1) % count), ((at + 1) % count, at)]
    return lax.ppermute(value, along, pairs)


def shifted_both(value, steps, rows=None):
    sizes = [lax.axis_size(axis) for axis in ("gx", "gy", "gz")]
    gx, gy, gz = sizes
    pairs = []
    for x in range(gx):
        for y in range(gy):
            for z in range(gz):
                place = (x * gz + z + (1 if rows is None else rows[y])) % (gx * gz)
                target = (place // gz * gy + (y + steps) % gy) * gz + place % gz
                pairs.append(((x * gy + y) * gz + z, target))
    return lax.ppermute(value, ("gx", "gy", "gz"), pairs)


def solution(mesh):
    return jax.shard_map(
        shards,
        mesh=mesh,
        in_specs=(
            P(None, ("grp", "gx", "gz"), "gy"),
            P(None, ("grp", "gx", "gz"), "gy"),
            P(),
            P(None, ("grp", "gx", "gz"), "gy"),
            P(None, ("grp", "gx", "gz"), "gy"),
            P(),
            P("grp"),
            P("grp"),
        ),
        out_specs=(P(None, ("grp", "gx", "gz"), "gy"), P(None, ("grp", "gx", "gz"), "gy")),
        check_vma=False,
    )
```

```python
import functools

import jax
import jax.numpy as jnp
from jax import lax
from jax.experimental import pallas as pl
from jax.experimental.pallas import tpu as pltpu
from jax.sharding import PartitionSpec as P

RATIO = 3
SUBSTEPS = 3
RIM = 6
LANES = 128
STRIDE = 16
SOURCE_AT = 3
PARENT_AT = 6
STRIP_AT = 8
STRIP_SOURCE_AT = 12
SOURCE_ROW = 24
TAIL_ROW = 40
FIXED = 8
LEFT_AT = 3
RIGHT_OWN = STRIDE - 3
VMEM = pltpu.VMEM
LIMIT = 24 * 1024 * 1024
MOST = 54 * 1024 * 1024


def iota(shape, dim):
    return lax.broadcasted_iota(jnp.int32, shape, dim)


def whole():
    return pl.BlockSpec(memory_space=VMEM)


def scalars():
    return pl.BlockSpec(memory_space=pltpu.SMEM)


def params(limit=LIMIT):
    return pltpu.CompilerParams(vmem_limit_bytes=limit)


def cost(flops, moved):
    return pl.CostEstimate(flops=flops, bytes_accessed=moved, transcendentals=0)


def tile(ref, level, index):
    return ref[level, :, index * LANES : (index + 1) * LANES]


def turned(value, lanes):
    lanes = lanes % LANES
    return pltpu.roll(value, lanes, 1) if lanes else value


def edge_strip(dest, band, oy, parent, parent_source):
    levels, rows, cols = parent.shape
    lane = iota((rows, LANES), 1)
    base = jnp.where(dest == 0, oy - 1, oy + band - 3) - lax.axis_index("gy") * cols
    total = jnp.zeros(lane.shape, jnp.float32)
    for ref, first in ((parent, STRIP_AT), (parent_source, STRIP_SOURCE_AT)):
        for level in range(levels):
            found = jnp.zeros(lane.shape, jnp.float32)
            for at in range(cols // LANES):
                place = lane + (at * LANES - base)
                found = jnp.where((place >= 0) & (place < 4), tile(ref, level, at), found)
            turn = (16384 + first + STRIDE * level - base) & (LANES - 1)
            total = total + pltpu.roll(found, turn, 1)
    return total


def pack_pair(nest, source, parent, parent_source, out, fine_buf, coarse_buf, sems):
    levels, rows, cols = nest.shape
    parent_rows, parent_cols = parent.shape[1:]
    right = lax.axis_index("gy") == 0
    loads = []
    for at, (ref, buf) in enumerate(
        (
            (parent, coarse_buf.at[0]),
            (parent_source, coarse_buf.at[1]),
            (nest, fine_buf.at[0]),
            (source, fine_buf.at[1]),
        )
    ):
        start = pl.multiple_of(jnp.where(right, ref.shape[2] - LANES, 0), LANES)
        loads.append(pltpu.make_async_copy(ref.at[:, :, pl.ds(start, LANES)], buf, sems.at[at]))
    for copy in loads:
        copy.start()

    def columns(value, count, to):
        first = jnp.where(right, LANES - count, 0)
        place = iota(value.shape, 1) - first
        value = jnp.where((place >= 0) & (place < count), value, 0.0)
        return pltpu.roll(value, (LANES + to - first) & (LANES - 1), 1)

    part = jnp.zeros((parent_rows, LANES), jnp.float32)
    loads[0].wait()
    loads[1].wait()
    for level in range(levels):
        base = STRIDE * level
        part = part + columns(coarse_buf[0, level], 1, base + PARENT_AT)
        part = part + columns(coarse_buf[0, level], 2, base + STRIP_AT)
        part = part + columns(coarse_buf[1, level], 2, base + STRIP_SOURCE_AT)
    total = jnp.zeros((rows, LANES), jnp.float32)
    loads[2].wait()
    loads[3].wait()
    for level in range(levels):
        base = STRIDE * level
        total = total + columns(fine_buf[0, level], 3, base)
        total = total + columns(fine_buf[1, level], 3, base + SOURCE_AT)
    out[...] = total
    out[:parent_rows, :] += part


def across_border(message, oy, parent_cols, me):
    c = iota(message.shape, 1) & (STRIDE - 1)
    place = jnp.where(me == 0, parent_cols + 1, 1) - oy
    total = jnp.zeros(message.shape, jnp.float32)
    for turn in (-1, 0, 2, 3):
        at = jnp.where(c >= STRIP_SOURCE_AT, c - STRIP_SOURCE_AT, c - STRIP_AT) - turn
        fits = (c >= STRIP_AT) & (at >= 0) & (at < 2) & (place == turn)
        total = total + jnp.where(fits, turned(message, turn), 0.0)
    return total


def pack_columns(parts, band, oy_hbm, nest, source, parent_hbm, parent_source_hbm, *rest):
    outs = rest[: parts - 1]
    old_buf, src_buf, parent, parent_source, oy_ref, sems, field_sems = rest[parts - 1 :]
    levels, rows, cols = nest.shape
    parent_cols = parent.shape[2]
    me = lax.axis_index("gy")
    sides = [1] if parts == 2 else [1, parts - 1]
    fields = [
        pltpu.make_async_copy(ref, buf, field_sems.at[at])
        for at, (ref, buf) in enumerate(
            ((oy_hbm, oy_ref), (parent_hbm, parent), (parent_source_hbm, parent_source))
        )
    ]
    for copy in fields:
        copy.start()
    copies = []
    for at, step in enumerate(sides):
        right = (me == 0) if parts == 2 else jnp.bool_(step == 1)
        start = pl.multiple_of(jnp.where(right, cols - LANES, 0), LANES)
        pair = [
            pltpu.make_async_copy(
                ref.at[:, :, pl.ds(start, LANES)], buf.at[at], sems.at[at, which]
            )
            for which, (ref, buf) in enumerate(((nest, old_buf), (source, src_buf)))
        ]
        for copy in pair:
            copy.start()
        copies.append((right, pair))
    for copy in fields:
        copy.wait()
    oy = oy_ref[0]
    lane = iota((parent.shape[1], LANES), 1)
    for step in range(1, parts):
        out = outs[step - 1]
        part = edge_strip(lax.rem(me + step, parts), band, oy, parent, parent_source)
        if step not in sides:
            out[...] = part
            continue
        at = sides.index(step)
        right, pair = copies[at]
        first = jnp.where(right, LANES - 3, 0)
        outer = jnp.where(right, LANES - 1, 0)
        for level in range(levels):
            edge = jnp.where(
                right, tile(parent, level, parent_cols // LANES - 1), tile(parent, level, 0)
            )
            edge = jnp.where(lane == outer, edge, 0.0)
            turn = (LANES + PARENT_AT + STRIDE * level - outer) & (LANES - 1)
            part = part + pltpu.roll(edge, turn, 1)
        for copy in pair:
            copy.wait()
        fine = iota((rows, LANES), 1) - first
        wanted = (fine >= 0) & (fine < 3)
        total = jnp.zeros((rows, LANES), jnp.float32)
        for level in range(levels):
            for buf, shift in ((old_buf, 0), (src_buf, SOURCE_AT)):
                value = jnp.where(wanted, buf[at, level], 0.0)
                turn = (LANES + STRIDE * level + shift - first) & (LANES - 1)
                total = total + pltpu.roll(value, turn, 1)
        out[...] = total
        out[: part.shape[0], :] += part


def three_terms(value):
    terms = []
    for _ in range(3):
        term = value.astype(jnp.bfloat16)
        terms.append(term)
        value = value - term.astype(jnp.float32)
    return terms


def select_rows(selector, value):
    selector = selector.astype(jnp.bfloat16)
    high, middle, low = (
        jnp.dot(selector, term, preferred_element_type=jnp.float32)
        for term in three_terms(value)
    )
    return high + (middle + low)


def select_columns(value, selector):
    selector = selector.astype(jnp.bfloat16)
    high, middle, low = (
        jnp.dot(term, selector, preferred_element_type=jnp.float32)
        for term in three_terms(value)
    )
    return high + (middle + low)


def sum_rows(ref, count):
    first, second, third = (ref[pl.ds(at, count, RATIO), :] for at in range(RATIO))
    return first + second + third


def inner_substep(coefs, here, source, there):
    levels, rows, cols = here.shape
    sub = iota((8, cols), 0)
    tiles = rows // 8

    def one_level(level):
        ch = coefs[0, level]
        cv = coefs[1, level]
        centre = 1.0 - 4.0 * ch - 2.0 * cv
        below = jnp.maximum(level - 1, 0)
        above = jnp.minimum(level + 1, levels - 1)
        cv_below = jnp.where(level > 0, cv, 0.0)
        cv_above = jnp.where(level < levels - 1, cv, 0.0)

        def row_tile(t):
            t = t % tiles
            return here[level, 8 * t : 8 * t + 8, :]

        down_before = pltpu.roll(row_tile(-1), 1, 0)
        now = row_tile(0)
        up_now = pltpu.roll(now, 7, 0)
        for t in range(tiles):
            following = row_tile(t + 1)
            down_now = pltpu.roll(now, 1, 0)
            up_next = pltpu.roll(following, 7, 0)
            around = jnp.where(sub == 0, down_before, down_now) + jnp.where(
                sub == 7, up_next, up_now
            )
            around = around + (pltpu.roll(now, 1, 1) + pltpu.roll(now, cols - 1, 1))
            span = slice(8 * t, 8 * t + 8)
            stacked = cv_below * here[below, span, :] + cv_above * here[above, span, :]
            there[level, span, :] = centre * now + ch * around + (stacked + source[level, span, :])
            down_before, now, up_now = down_now, following, up_next

    def two_levels(pair, carry):
        one_level(2 * pair)
        one_level(2 * pair + 1)
        return carry

    lax.fori_loop(0, levels // 2, two_levels, 0)


def spread_coefs(parent_coefs, coefs, out):
    levels = out.shape[2]
    lane = iota((levels, LANES), 1)
    row = iota((levels, LANES), 0)
    for at, ref in enumerate((parent_coefs, coefs)):
        for which in range(2):
            packed = jnp.full(lane.shape, ref[which, 0], jnp.float32)
            rows = packed
            for level in range(1, levels):
                packed = jnp.where(lane >= STRIDE * level, ref[which, level], packed)
                rows = jnp.where(row == level, ref[which, level], rows)
            out[0, 2 * at + which] = packed
            out[1, 2 * at + which] = rows


def inner_first(
    band,
    oy_ref,
    coefs,
    nest,
    source,
    parent,
    parent_source,
    strip,
    first,
    oy_rows,
):
    oy = oy_ref[0]
    oy_rows[...] = jnp.full(oy_rows.shape, oy, jnp.int32)
    strip[...] = edge_strip(lax.axis_index("gy"), band, oy, parent, parent_source)
    inner_substep(coefs, nest, source, first)


def own_windows(parts, nest, source, y_left, y_right, window_old, window_src):
    levels, rows, cols = nest.shape
    pieces = cols // LANES
    me = lax.axis_index("gy")
    for level in range(levels):
        for buf, field, shift in ((window_old, nest, 0), (window_src, source, SOURCE_AT)):
            for window, first, turn in ((0, 0, 3), (1, rows - 8, 5)):
                tiles = [
                    field[level, first : first + 8, piece * LANES : (piece + 1) * LANES]
                    for piece in range(pieces)
                ]
                tiles = with_columns(
                    tiles,
                    y_left[first : first + 8, :],
                    y_right[first : first + 8, :],
                    me,
                    parts,
                    STRIDE * level + shift,
                )
                for piece, value in enumerate(tiles):
                    buf[level, window, :, piece * LANES : (piece + 1) * LANES] = pltpu.roll(
                        value, turn, 0
                    )


def inner_rest(
    parts,
    parent_coefs,
    coefs,
    nest,
    first,
    source,
    y_left,
    y_right,
    after_pack,
    third,
    packs,
    window_old,
    window_src,
    sums,
    spread,
    second,
    split,
):
    levels, rows, cols = nest.shape
    spread_coefs(parent_coefs, coefs, spread)
    own_windows(parts, nest, source, y_left, y_right, window_old, window_src)
    lane = iota((rows, LANES), 1)
    for at, ref in enumerate((nest, source)):
        left = jnp.zeros(lane.shape, jnp.float32)
        right = jnp.zeros(lane.shape, jnp.float32)
        for level in range(levels):
            value = jnp.where(lane < RIGHT_OWN, tile(ref, level, 0), 0.0)
            left = left + turned(value, STRIDE * level + LEFT_AT)
            value = jnp.where(lane >= LANES - RIGHT_OWN, tile(ref, level, cols // LANES - 1), 0.0)
            right = right + turned(value, STRIDE * level + RIGHT_OWN)
        packs[2 * at] = left
        packs[2 * at + 1] = right
    inner_substep(coefs, first, source, second)
    inner_substep(coefs, second, source, third)
    for level in range(levels):
        for piece in range(cols // LANES):
            split[piece, level * rows : (level + 1) * rows, :] = tile(third, level, piece)
    for piece in range(cols // LANES):
        sums[piece] = sum_rows(split.at[piece], levels * rows // RATIO)


def with_columns(tiles, left, right, me, parts, place):
    lane = iota(left.shape, 1)
    from_right = turned(right, -place)
    from_left = turned(left, -3 - place)
    if parts == 2:
        tiles[0] = jnp.where((lane < 3) & (me == 0), from_right, tiles[0])
        tiles[-1] = jnp.where((lane >= LANES - 3) & (me == 1), from_left, tiles[-1])
        return tiles
    extra = jnp.where(lane < 3, from_right, jnp.where(lane >= LANES - 3, from_left, 0.0))
    return tiles + [extra]


def pack_rows(
    parts, old_top, old_end, src_top, src_end, par_top, par_end, own_strip, oy_rows, *rest
):
    columns = rest[: parts - 1]
    across, within, far, strip_out, both = rest[parts - 1 :]
    core = lax.axis_index("gz")
    up, down = both.at[core], both.at[1 - core]
    levels, _, cols = old_top.shape
    me = lax.axis_index("gy")
    left, right = columns[0], columns[-1]
    rows = left.shape[0]
    strip_rows = own_strip.shape[0]
    lane = iota((strip_rows, LANES), 1)
    strips = own_strip[...]
    if parts == 2:
        oy = jnp.concatenate([oy_rows[...]] * (strip_rows // 8), axis=0)
        strips = strips + across_border(left[:strip_rows, :], oy, par_top.shape[2], me)
    else:
        for message in columns:
            strips = strips + message[:strip_rows, :]
    c = lane & (STRIDE - 1)
    strips = jnp.where(c >= STRIP_AT, strips, 0.0)
    strips = jnp.where(c == PARENT_AT, left[:strip_rows, :], strips)
    strips = jnp.where(c == PARENT_AT + 1, turned(right[:strip_rows, :], 1), strips)
    strip_out[...] = strips
    far[...] = strips[:8]
    pieces = cols // LANES
    for out, old, src, first, at, src_at in (
        (up, old_end, src_end, rows - 8, 5, 6),
        (down, old_top, src_top, 0, 0, 0),
    ):
        y_left = left[first : first + 8, :]
        y_right = right[first : first + 8, :]
        for level in range(levels):
            for ref, shift, row, count, base in (
                (old, 0, at, 3, 0),
                (src, SOURCE_AT, src_at, 2, SOURCE_ROW),
            ):
                tiles = [tile(ref, level, piece) for piece in range(pieces)]
                tiles = with_columns(
                    tiles, y_left, y_right, me, parts, STRIDE * level + shift
                )
                for piece, value in enumerate(tiles):
                    out[
                        base + count * level : base + count * (level + 1),
                        piece * LANES : (piece + 1) * LANES,
                    ] = value[row : row + count]
    parent_cols = par_top.shape[2]
    for level in range(levels):
        up[TAIL_ROW + level : TAIL_ROW + level + 1, :parent_cols] = par_end[level, 7:8, :]
        down[TAIL_ROW + level : TAIL_ROW + level + 1, :parent_cols] = par_top[level, 0:1, :]
    up[TAIL_ROW : TAIL_ROW + 8, parent_cols : parent_cols + LANES] = strips[strip_rows - 8 :]
    down[TAIL_ROW : TAIL_ROW + 8, parent_cols : parent_cols + LANES] = strips[:8]
    down[TAIL_ROW + 8 : TAIL_ROW + 16, :LANES] = strips[8:16]
    down[TAIL_ROW + 8 : TAIL_ROW + 16, LANES : 2 * LANES] = strips[16:24]
    within[...] = both[0]
    across[...] = both[1]


def edges(
    parts,
    parent_cols,
    ox_ref,
    spread,
    sums,
    packs,
    window_old,
    window_src,
    strips,
    across,
    within,
    far,
    y_left,
    y_right,
    sides,
    windows,
    coarse_out,
    far_out,
    both,
    ping,
    pong,
    src,
):
    levels = ping.shape[0]
    width = ping.shape[3]
    rows = packs.shape[1]
    cols = sums.shape[0] * LANES
    pieces = cols // LANES
    me = lax.axis_index("gy")
    core = lax.axis_index("gz")
    both[0] = within[...]
    both[1] = across[...]
    before, after = both.at[1 - core], both.at[core]
    is_south = me == 0
    is_north = me == parts - 1

    far_out[...] = far[...]
    sub = iota((8, LANES), 0)
    old = jnp.concatenate(
        [
            strips[...],
            after[TAIL_ROW : TAIL_ROW + 8, parent_cols : parent_cols + LANES],
            after[TAIL_ROW + 8 : TAIL_ROW + 16, :LANES],
            after[TAIL_ROW + 8 : TAIL_ROW + 16, LANES : 2 * LANES],
            jnp.where(
                sub == 7,
                before[TAIL_ROW : TAIL_ROW + 8, parent_cols : parent_cols + LANES],
                0.0,
            ),
        ],
        axis=0,
    )
    count = old.shape[0]

    def packed_coef(which, height):
        return jnp.concatenate([spread[0, which]] * (height // 8), axis=0)

    def stacked(value):
        lane = iota(value.shape, 1)
        below = jnp.where(lane >= STRIDE, turned(value, STRIDE), 0.0)
        return below + jnp.where(lane < STRIDE * (levels - 1), turned(value, -STRIDE), 0.0)

    def around(value):
        return (
            pltpu.roll(value, 1, 0)
            + pltpu.roll(value, value.shape[0] - 1, 0)
            + turned(value, 1)
            + turned(value, -1)
        )

    diff = (
        packed_coef(0, count) * (around(old) - 4.0 * old)
        + packed_coef(1, count) * (stacked(old) - 2.0 * old)
        + turned(old, STRIP_AT - STRIP_SOURCE_AT)
    )
    index = iota((rows + 16, count), 0)
    nest_row = jnp.where(index < rows, index, jnp.where(index < rows + 8, index - rows - 3, index - 13))
    parent_row = ((nest_row + 3) * 171 >> 9) - 1 + ox_ref[0]
    pick = (iota((rows + 16, count), 1) == parent_row).astype(jnp.float32)
    picked = select_rows(pick, jnp.concatenate([old, diff], axis=1))
    picked_old, picked_diff = picked[:, :LANES], picked[:, LANES:]

    lane = iota((rows, LANES), 1)
    c = lane & (STRIDE - 1)
    rim_first = jnp.where(is_south, LEFT_AT, RIGHT_OWN - RIM)
    in_rim = (c >= rim_first) & (c < rim_first + RIM)
    at = lane - c + STRIP_AT + jnp.where(c >= rim_first + 3, 2, 1)
    rim_old = jnp.take_along_axis(picked_old[:rows], at, axis=1)
    rim_diff = jnp.take_along_axis(picked_diff[:rows], at, axis=1)
    ch = packed_coef(2, rows)
    cv = packed_coef(3, rows)
    centre = 1.0 - 4.0 * ch - 2.0 * cv
    left = jnp.where(c < 3, y_left[...], packs[0])
    left_src = jnp.where(c < 3, turned(y_left[...], -SOURCE_AT), packs[2])
    right = jnp.where(c >= RIGHT_OWN, turned(y_right[...], RIGHT_OWN), packs[1])
    right_src = jnp.where(c >= RIGHT_OWN, turned(y_right[...], RIGHT_OWN - SOURCE_AT), packs[3])
    for side, (value, forcing, rim) in enumerate(
        (
            (left, left_src, in_rim & is_south),
            (right, right_src, in_rim & is_north),
        )
    ):
        for substep in range(1, SUBSTEPS + 1):
            value = centre * value + ch * around(value) + (cv * stacked(value) + forcing)
            value = jnp.where(rim, rim_old + (substep / SUBSTEPS) * rim_diff, value)
        sides[side, :rows, :] = value

    sub = iota((8, width), 0)
    lane = iota((8, LANES), 1)
    ping[...] = window_old[...]
    src[...] = window_src[...]
    for level in range(levels):
        for buf, n, base in ((ping, 3, 0), (src, 2, SOURCE_ROW)):
            rows_of = slice(base + n * level, base + n * (level + 1))
            buf[level, 0, 3 - n : 3, :] = before[rows_of, :]
            buf[level, 1, 5 : 5 + n, :] = after[rows_of, :]
    rim_first = jnp.where(is_south, 0, LANES - RIM)
    column = STRIP_AT + jnp.where((lane >= rim_first + 3) & (lane < rim_first + RIM), 2, 1)
    rims = {}
    for level in range(levels):
        for window in range(2):
            span = slice(rows + 8 * window, rows + 8 * window + 8)
            at = column + STRIDE * level
            rims[level, window] = (
                jnp.take_along_axis(picked_old[span], at, axis=1),
                jnp.take_along_axis(picked_diff[span], at, axis=1),
            )
    for substep in range(1, SUBSTEPS + 1):
        here, there = (ping, pong) if substep % 2 else (pong, ping)
        there = windows if substep == SUBSTEPS else there
        low = 0 if substep == SUBSTEPS or parts > 2 else 3
        south = (lane >= low) & (lane < RIM) & is_south
        north = (lane >= LANES - RIM) & (lane < LANES - low) & is_north
        weight = substep / SUBSTEPS
        for level in range(levels):
            c_h, c_v = (
                jnp.concatenate([spread[1, which, level : level + 1, :]] * (width // LANES), axis=1)
                for which in (2, 3)
            )
            c_0 = 1.0 - 4.0 * c_h - 2.0 * c_v
            for window in range(2):
                now = here[level, window]
                up = pltpu.roll(now, 1, 0)
                down = pltpu.roll(now, 7, 0)
                if substep == 1:
                    beyond_row = window_old[level, window]
                    if window == 0:
                        down = jnp.where(sub == 7, pltpu.roll(beyond_row, 7, 0), down)
                    else:
                        up = jnp.where(sub == 0, pltpu.roll(beyond_row, 1, 0), up)
                beside = pltpu.roll(now, 1, 1) + pltpu.roll(now, width - 1, 1)
                value = c_0 * now + c_h * ((up + down) + beside) + src[level, window]
                near = [here[at, window] for at in (level - 1, level + 1) if 0 <= at < levels]
                value = value + c_v * sum(near[1:], near[0])
                rim_o, rim_d = rims[level, window]
                rim = rim_o + weight * rim_d
                for piece in range(width // LANES):
                    span = slice(piece * LANES, (piece + 1) * LANES)
                    part = value[:, span]
                    if piece == 0:
                        part = jnp.where(south, rim, part)
                    if piece == pieces - 1:
                        part = jnp.where(north, rim, part)
                    there[level, window, :, span] = part

    parent_rows = rows // RATIO
    lane = iota((parent_rows, LANES), 1)
    row = iota((parent_rows, LANES), 0)
    side_sums = [sum_rows(sides.at[side], parent_rows) for side in range(2)]
    replaced = [[] for _ in range(pieces)]
    for level in range(levels):
        span = slice(level * parent_rows, (level + 1) * parent_rows)
        top = windows[level, 0, 3:4, :] + windows[level, 0, 4:5, :] + windows[level, 0, 5:6, :]
        end = windows[level, 1, 2:3, :] + windows[level, 1, 3:4, :] + windows[level, 1, 4:5, :]
        for piece in range(pieces):
            value = sums[piece, span, :]
            if piece == 0:
                fixed = turned(side_sums[0], -STRIDE * level - LEFT_AT)
                value = jnp.where(lane < FIXED, fixed, value)
            if piece == pieces - 1:
                fixed = turned(side_sums[1], -STRIDE * level - RIGHT_OWN)
                value = jnp.where(lane >= LANES - FIXED, fixed, value)
            across_piece = slice(piece * LANES, (piece + 1) * LANES)
            value = jnp.where(row == 0, top[:, across_piece], value)
            value = jnp.where(row == parent_rows - 1, end[:, across_piece], value)
            replaced[piece].append(value)
    foot = cols // RATIO
    offset = iota((cols, foot), 0) - RATIO * iota((cols, foot), 1)
    gather = ((offset >= 0) & (offset < RATIO)).astype(jnp.float32)
    means = select_columns(
        jnp.concatenate([jnp.concatenate(values, axis=0) for values in replaced], axis=1), gather
    ) * (1.0 / 9.0)
    coarse_out[...] = means.reshape(coarse_out.shape)


def put_together(third, sides, windows, result):
    levels, rows, cols = third.shape
    pieces = cols // LANES
    lane = iota((rows, LANES), 1)
    sub = iota((8, cols), 0)
    for level in range(levels):
        fixed = turned(sides[0, :rows, :], -STRIDE * level - LEFT_AT)
        result[level, :, :LANES] = jnp.where(lane < FIXED, fixed, tile(third, level, 0))
        for piece in range(1, pieces - 1):
            result[level, :, piece * LANES : (piece + 1) * LANES] = tile(third, level, piece)
        fixed = turned(sides[1, :rows, :], -STRIDE * level - RIGHT_OWN)
        result[level, :, cols - LANES :] = jnp.where(
            lane >= LANES - FIXED, fixed, tile(third, level, pieces - 1)
        )
        top = pltpu.roll(windows[level, 0, :, :cols], 5, 0)
        result[level, :8, :] = jnp.where(sub < 3, top, result[level, :8, :])
        end = pltpu.roll(windows[level, 1, :, :cols], 3, 0)
        result[level, rows - 8 :, :] = jnp.where(sub >= 5, end, result[level, rows - 8 :, :])


def parent_step(
    parts,
    band,
    ox_ref,
    oy_ref,
    spread,
    third,
    sides,
    windows,
    parent,
    source,
    within,
    across,
    y_left,
    y_right,
    out,
    nest_out,
    late,
    tail,
    result,
    sem,
):
    put_together(third, sides, windows, result)
    store = pltpu.make_async_copy(result, nest_out, sem)
    store.start()
    core = lax.axis_index("gz")
    levels, rows, cols = parent.shape
    tail[0] = within[TAIL_ROW : TAIL_ROW + levels, : cols + LANES]
    tail[1] = across[TAIL_ROW : TAIL_ROW + levels, : cols + LANES]
    me = lax.axis_index("gy")
    is_last = ox_ref[0] == rows - 1
    wide = iota((1, cols), 1)
    south = (wide == oy_ref[0] + 2 - me * cols) & is_last
    north = (wide == oy_ref[0] + band - 3 - me * cols) & is_last
    row = iota((rows, cols), 0)
    lane = iota((rows, cols), 1)
    has_left = me > 0
    has_right = me < parts - 1
    left = y_left[:rows, :]
    right = y_right[:rows, :]
    zero = jnp.zeros((rows, cols), jnp.float32)
    for level in range(levels):
        now = parent[level]
        at = STRIDE * level + PARENT_AT
        from_left = left[:, at : at + 1]
        from_right = right[:, at : at + 1]
        top = tail[1 - core, level : level + 1, :cols]
        end = tail[core, level : level + 1, :cols]
        around = (
            jnp.where(row == 0, top, pltpu.roll(now, 1, 0))
            + jnp.where(row == rows - 1, end, pltpu.roll(now, rows - 1, 0))
            + jnp.where(
                lane == 0, jnp.where(has_left, from_left, 0.0), pltpu.roll(now, 1, 1)
            )
            + jnp.where(
                lane == cols - 1,
                jnp.where(has_right, from_right, 0.0),
                pltpu.roll(now, cols - 1, 1),
            )
        )
        stacked = (parent[level - 1] if level > 0 else zero) + (
            parent[level + 1] if level < levels - 1 else zero
        )
        ch, cv = (
            jnp.concatenate([spread[1, which, level : level + 1, :]] * (cols // LANES), axis=1)
            for which in (0, 1)
        )
        out[level] = (
            (1.0 - 4.0 * ch - 2.0 * cv) * now + ch * around + (cv * stacked + source[level])
        )
        at = cols + STRIDE * level + PARENT_AT
        before_end = jnp.where(
            wide == 0, tail[core, 0:1, at : at + 1], pltpu.roll(end, 1, 1)
        )
        after_end = jnp.where(
            wide == cols - 1, tail[core, 0:1, at + 1 : at + 2], pltpu.roll(end, cols - 1, 1)
        )
        nest_ch = spread[1, 2, level : level + 1, :]
        nest_ch = jnp.concatenate([nest_ch] * (cols // LANES), axis=1)
        share = nest_ch * nest_ch * ch * (1.0 / SUBSTEPS)
        late[level : level + 1, :] = (share * (1.0 / (RATIO * RATIO))) * (
            jnp.where(south, before_end, 0.0) + jnp.where(north, after_end, 0.0)
        )
    store.wait()


def merge(parts, band, ox_ref, oy_ref, late, step, nest, spread, beyond, *rest):
    arrived = rest[1 : 2 * parts]
    out, nest_out, joined, corner, sem, merged, out_sems = rest[2 * parts :]
    levels, rows, cols = step.shape
    foot = rest[0].shape[2]
    me = lax.axis_index("gy")

    @pl.when((ox_ref[0] == rows - 1) & ((me == 0) | (me == parts - 1)))
    def _():
        nest_rows, nest_cols = nest.shape[1:]
        first = pl.multiple_of(jnp.where(me == 0, 0, nest_cols - LANES), LANES)
        place = (slice(None), pl.ds(nest_rows - 8, 8), pl.ds(first, LANES))
        load = pltpu.make_async_copy(nest_out.at[place], corner, sem)
        load.start()
        load.wait()
        sub = iota((8, LANES), 0)
        lane = iota((8, LANES), 1)
        cell = (sub == 7) & (lane == jnp.where(me == 0, RIM, LANES - RIM - 1))
        for level in range(levels):
            at = STRIDE * level + STRIP_AT
            value = jnp.where(me == 0, beyond[0:1, at + 2 : at + 3], beyond[0:1, at + 1 : at + 2])
            nest_ch = spread[1, 2, level : level + 1, :]
            share = nest_ch * nest_ch * spread[1, 0, level : level + 1, :] * (1.0 / SUBSTEPS)
            corner[level] += jnp.where(cell, share * value, 0.0)
        again = pltpu.make_async_copy(corner, nest_out.at[place], sem)
        again.start()
        again.wait()

    ox = ox_ref[0]
    oy = oy_ref[0]
    joined[0, :, rows:, :] = rest[0][...]
    if parts == 2:
        mixed, straight, other = arrived
        joined[0, :, :rows, :] = straight[...]
        joined[1, :, :rows, :] = jnp.where(me == 0, mixed[...], other[...])
        joined[1, :, rows:, :] = jnp.where(me == 0, other[...], mixed[...])
    else:
        for k in range(parts):
            joined[k, :, :rows, :] = arrived[k][...]
        for k in range(1, parts):
            joined[k, :, rows:, :] = arrived[parts + k - 1][...]
    lane = iota((rows, LANES), 1)
    row = iota((rows, LANES), 0)
    stores = []
    for level in range(levels):
        values = [tile(step, level, piece) for piece in range(cols // LANES)]
        for k in range(parts):
            source = lax.rem(me + parts - k, parts)
            block = joined[k, level, pl.ds(rows - ox, rows), :]
            begin = oy + source * foot - me * cols
            block = pltpu.roll(block, (16384 + begin) & (LANES - 1), 1)
            low = jnp.maximum(source * foot, 2)
            high = jnp.minimum((source + 1) * foot, band - 2)
            for piece in range(cols // LANES):
                at = lane + (piece * LANES + me * cols - oy)
                values[piece] = jnp.where((at >= low) & (at < high), block, values[piece])
        for piece, value in enumerate(values):
            term = late[level : level + 1, piece * LANES : (piece + 1) * LANES]
            value = value + jnp.where(row == rows - 2, term, 0.0)
            merged[level, :, piece * LANES : (piece + 1) * LANES] = value
        stores.append(pltpu.make_async_copy(merged.at[level], out.at[level], out_sems.at[level]))
        stores[-1].start()
    for copy in stores:
        copy.wait()


def shifted(value, axis, steps):
    count = lax.axis_size(axis)
    pairs = [(source, (source + steps) % count) for source in range(count)]
    return lax.ppermute(value, axis, pairs)


def shards(
    parent_old, parent_source, parent_coefs, nest_old, nest_source, nest_coefs, offset_x, offset_y
):
    parts = lax.axis_size("gy")
    along = ("gx", "gz")
    levels, parent_rows, parent_cols = parent_old.shape
    _, rows, cols = nest_old.shape
    foot = cols // RATIO
    band = foot * parts
    width = cols if parts == 2 else cols + LANES
    height = TAIL_ROW + 16
    f32 = jnp.float32
    shape = jax.ShapeDtypeStruct
    anywhere = pl.BlockSpec(memory_space=pl.ANY)
    in_hbm = pl.BlockSpec(memory_space=pltpu.HBM)
    sides = 1 if parts == 2 else 2
    if parts == 2:
        packed = [
            pl.pallas_call(
                pack_pair,
                out_shape=VMEM((rows, LANES), f32),
                in_specs=[in_hbm] * 4,
                out_specs=whole(),
                scratch_shapes=[
                    VMEM((2, levels, rows, LANES), f32),
                    VMEM((2, levels, parent_rows, LANES), f32),
                    pltpu.SemaphoreType.DMA((4,)),
                ],
                compiler_params=params(MOST),
                cost_estimate=cost(200000, 800000),
                name="pack_pair",
            )(nest_old, nest_source, parent_old, parent_source)
        ]
    else:
        packed = pl.pallas_call(
            functools.partial(pack_columns, parts, band),
            out_shape=[
                shape((rows if k in (1, parts - 1) else parent_rows, LANES), f32)
                for k in range(1, parts)
            ],
            in_specs=[in_hbm] * 5,
            out_specs=[whole()] * (parts - 1),
            scratch_shapes=[
                VMEM((sides, levels, rows, LANES), f32),
                VMEM((sides, levels, rows, LANES), f32),
                VMEM(parent_old.shape, f32),
                VMEM(parent_old.shape, f32),
                pltpu.SMEM(offset_y.shape, jnp.int32),
                pltpu.SemaphoreType.DMA((sides, 2)),
                pltpu.SemaphoreType.DMA((3,)),
            ],
            compiler_params=params(MOST),
            cost_estimate=cost(200000, 1000000),
            name="pack_columns",
        )(offset_y, nest_old, nest_source, parent_old, parent_source)
    columns = [shifted(packed[k - 1], "gy", k) for k in range(1, parts)]
    own_strip, first, oy_rows = pl.pallas_call(
        functools.partial(inner_first, band),
        out_shape=[
            shape((parent_rows, LANES), f32),
            shape(nest_old.shape, f32),
            shape((8, LANES), jnp.int32),
        ],
        in_specs=[scalars()] * 2 + [whole()] * 4,
        out_specs=[whole()] * 3,
        compiler_params=params(),
        cost_estimate=cost(4000000, 3000000),
        name="inner_first",
    )(
        offset_y,
        nest_coefs,
        nest_old,
        nest_source,
        parent_old,
        parent_source,
    )

    def block(ref, last):
        count = ref.shape[1] // 8 - 1 if last else 0
        return pl.BlockSpec((levels, 8, ref.shape[2]), lambda i, c=count: (0, c, 0))

    def full(extent):
        return pl.BlockSpec(extent, lambda i: (0,) * len(extent))

    outs = [
        shape((height, width), f32),
        shape((height, width), f32),
        shape((8, LANES), f32),
        shape((parent_rows, LANES), f32),
    ]
    across, within, far, strips = pl.pallas_call(
        functools.partial(pack_rows, parts),
        out_shape=outs,
        grid=(1,),
        in_specs=[
            block(nest_old, False),
            block(nest_old, True),
            block(nest_old, False),
            block(nest_old, True),
            block(parent_old, False),
            block(parent_old, True),
            full(own_strip.shape),
            full(oy_rows.shape),
        ]
        + [full(message.shape) for message in columns],
        out_specs=[full(out.shape) for out in outs],
        scratch_shapes=[VMEM((2, height, width), f32)],
        compiler_params=params(),
        cost_estimate=cost(100000, 700000),
        name="pack_rows",
    )(nest_old, nest_old, nest_source, nest_source, parent_old, parent_old, own_strip, oy_rows, *columns)
    across = swapped(across, 1)
    within = swapped(within, 0)
    third, packs, window_old, window_src, sums, spread = pl.pallas_call(
        functools.partial(inner_rest, parts),
        out_shape=[
            shape(nest_old.shape, f32),
            shape((4, rows, LANES), f32),
            shape((levels, 2, 8, width), f32),
            shape((levels, 2, 8, width), f32),
            shape((cols // LANES, levels * parent_rows, LANES), f32),
            shape((2, 4, levels, LANES), f32),
        ],
        in_specs=[scalars()] * 2 + [whole()] * 5 + [anywhere],
        out_specs=[whole()] * 6,
        scratch_shapes=[
            VMEM(nest_old.shape, f32),
            VMEM((cols // LANES, levels * rows + 8, LANES), f32),
        ],
        compiler_params=params(),
        cost_estimate=cost(8000000, 6000000),
        name="inner_rest",
    )(parent_coefs, nest_coefs, nest_old, first, nest_source, columns[0], columns[-1], strips)
    sides, windows, coarse, far = pl.pallas_call(
        functools.partial(edges, parts, parent_cols),
        out_shape=[
            shape((2, rows + 8, LANES), f32),
            shape((levels, 2, 8, width), f32),
            shape((levels, parent_rows, foot), f32),
            shape((8, LANES), f32),
        ],
        in_specs=[scalars()] + [whole()] * 11,
        out_specs=[whole()] * 4,
        scratch_shapes=[
            VMEM((2, height, width), f32),
            VMEM((levels, 2, 8, width), f32),
            VMEM((levels, 2, 8, width), f32),
            VMEM((levels, 2, 8, width), f32),
        ],
        compiler_params=params(),
        cost_estimate=cost(4000000, 3000000),
        name="edges",
    )(
        offset_x,
        spread,
        sums,
        packs,
        window_old,
        window_src,
        strips,
        across,
        within,
        far,
        columns[0],
        columns[-1],
    )
    if parts == 2:
        arrived = [
            shifted_both(coarse, 1, (0, 1)),
            shifted(coarse, along, 1),
            shifted_both(coarse, 1, (1, 0)),
        ]
    else:
        arrived = [shifted(coarse, along, 1)]
        arrived += [shifted_both(coarse, k) for k in range(1, parts)]
        arrived += [shifted(coarse, "gy", k) for k in range(1, parts)]
    beyond = shifted(far, along, -2)
    step, nest_stored, late = pl.pallas_call(
        functools.partial(parent_step, parts, band),
        out_shape=[
            shape(parent_old.shape, f32),
            shape(nest_old.shape, f32),
            shape((levels, parent_cols), f32),
        ],
        in_specs=[scalars()] * 2 + [whole()] * 10,
        out_specs=[whole(), in_hbm, whole()],
        scratch_shapes=[
            VMEM((2, levels, parent_cols + LANES), f32),
            VMEM(nest_old.shape, f32),
            pltpu.SemaphoreType.DMA,
        ],
        compiler_params=params(),
        cost_estimate=cost(800000, 2500000),
        name="parent_step",
    )(
        offset_x,
        offset_y,
        spread,
        third,
        sides,
        windows,
        parent_old,
        parent_source,
        within,
        across,
        columns[0],
        columns[-1],
    )
    parent_new, nest_new = pl.pallas_call(
        functools.partial(merge, parts, band),
        out_shape=[shape(parent_old.shape, f32), shape(nest_old.shape, f32)],
        in_specs=[scalars()] * 2 + [whole()] * 2 + [in_hbm] + [whole()] * (2 + 2 * parts),
        out_specs=[in_hbm, in_hbm],
        scratch_shapes=[
            VMEM((parts, levels, 2 * parent_rows, foot), f32),
            VMEM((levels, 8, LANES), f32),
            pltpu.SemaphoreType.DMA,
            VMEM(parent_old.shape, f32),
            pltpu.SemaphoreType.DMA((levels,)),
        ],
        input_output_aliases={4: 1},
        compiler_params=params(),
        cost_estimate=cost(200000, 800000),
        name="merge",
    )(offset_x, offset_y, late, step, nest_stored, spread, beyond, coarse, *arrived)
    return (parent_new, nest_new)


def swapped(value, first):
    along = ("gx", "gz")
    count = lax.axis_size(along)
    pairs = []
    for at in range(first, count, 2):
        pairs += [(at, (at + 1) % count), ((at + 1) % count, at)]
    return lax.ppermute(value, along, pairs)


def shifted_both(value, steps, rows=None):
    sizes = [lax.axis_size(axis) for axis in ("gx", "gy", "gz")]
    gx, gy, gz = sizes
    pairs = []
    for x in range(gx):
        for y in range(gy):
            for z in range(gz):
                place = (x * gz + z + (1 if rows is None else rows[y])) % (gx * gz)
                target = (place // gz * gy + (y + steps) % gy) * gz + place % gz
                pairs.append(((x * gy + y) * gz + z, target))
    return lax.ppermute(value, ("gx", "gy", "gz"), pairs)


def solution(mesh):
    return jax.shard_map(
        shards,
        mesh=mesh,
        in_specs=(
            P(None, ("grp", "gx", "gz"), "gy"),
            P(None, ("grp", "gx", "gz"), "gy"),
            P(),
            P(None, ("grp", "gx", "gz"), "gy"),
            P(None, ("grp", "gx", "gz"), "gy"),
            P(),
            P("grp"),
            P("grp"),
        ),
        out_specs=(P(None, ("grp", "gx", "gz"), "gy"), P(None, ("grp", "gx", "gz"), "gy")),
        check_vma=False,
    )
```

```python
import functools

import jax
import jax.numpy as jnp
from jax import lax
from jax.experimental import pallas as pl
from jax.experimental.pallas import tpu as pltpu
from jax.sharding import PartitionSpec as P

RATIO = 3
SUBSTEPS = 3
RIM = 6
LANES = 128
STRIDE = 16
SOURCE_AT = 3
PARENT_AT = 6
STRIP_AT = 8
STRIP_SOURCE_AT = 12
SOURCE_ROW = 24
TAIL_ROW = 40
FIXED = 8
LEFT_AT = 3
RIGHT_OWN = STRIDE - 3
VMEM = pltpu.VMEM
LIMIT = 24 * 1024 * 1024
MOST = 54 * 1024 * 1024


def iota(shape, dim):
    return lax.broadcasted_iota(jnp.int32, shape, dim)


def whole():
    return pl.BlockSpec(memory_space=VMEM)


def scalars():
    return pl.BlockSpec(memory_space=pltpu.SMEM)


def params(limit=LIMIT):
    return pltpu.CompilerParams(vmem_limit_bytes=limit)


def cost(flops, moved):
    return pl.CostEstimate(flops=flops, bytes_accessed=moved, transcendentals=0)


def tile(ref, level, index):
    return ref[level, :, index * LANES : (index + 1) * LANES]


def turned(value, lanes):
    lanes = lanes % LANES
    return pltpu.roll(value, lanes, 1) if lanes else value


def edge_strip(dest, band, oy, parent, parent_source):
    levels, rows, cols = parent.shape
    lane = iota((rows, LANES), 1)
    base = jnp.where(dest == 0, oy - 1, oy + band - 3) - lax.axis_index("gy") * cols
    total = jnp.zeros(lane.shape, jnp.float32)
    for ref, first in ((parent, STRIP_AT), (parent_source, STRIP_SOURCE_AT)):
        for level in range(levels):
            found = jnp.zeros(lane.shape, jnp.float32)
            for at in range(cols // LANES):
                place = lane + (at * LANES - base)
                found = jnp.where((place >= 0) & (place < 4), tile(ref, level, at), found)
            turn = (16384 + first + STRIDE * level - base) & (LANES - 1)
            total = total + pltpu.roll(found, turn, 1)
    return total


def pack_pair(nest, source, parent, parent_source, out, fine_buf, coarse_buf, sems):
    levels, rows, cols = nest.shape
    parent_rows, parent_cols = parent.shape[1:]
    right = lax.axis_index("gy") == 0
    loads = []
    for at, (ref, buf) in enumerate(
        (
            (parent, coarse_buf.at[0]),
            (parent_source, coarse_buf.at[1]),
            (nest, fine_buf.at[0]),
            (source, fine_buf.at[1]),
        )
    ):
        start = pl.multiple_of(jnp.where(right, ref.shape[2] - LANES, 0), LANES)
        loads.append(pltpu.make_async_copy(ref.at[:, :, pl.ds(start, LANES)], buf, sems.at[at]))
    for copy in loads:
        copy.start()

    def columns(value, count, to):
        first = jnp.where(right, LANES - count, 0)
        place = iota(value.shape, 1) - first
        value = jnp.where((place >= 0) & (place < count), value, 0.0)
        return pltpu.roll(value, (LANES + to - first) & (LANES - 1), 1)

    part = jnp.zeros((parent_rows, LANES), jnp.float32)
    loads[0].wait()
    loads[1].wait()
    for level in range(levels):
        base = STRIDE * level
        part = part + columns(coarse_buf[0, level], 1, base + PARENT_AT)
        part = part + columns(coarse_buf[0, level], 2, base + STRIP_AT)
        part = part + columns(coarse_buf[1, level], 2, base + STRIP_SOURCE_AT)
    total = jnp.zeros((rows, LANES), jnp.float32)
    loads[2].wait()
    loads[3].wait()
    for level in range(levels):
        base = STRIDE * level
        total = total + columns(fine_buf[0, level], 3, base)
        total = total + columns(fine_buf[1, level], 3, base + SOURCE_AT)
    out[...] = total
    out[:parent_rows, :] += part


def across_border(message, oy, parent_cols, me):
    c = iota(message.shape, 1) & (STRIDE - 1)
    place = jnp.where(me == 0, parent_cols + 1, 1) - oy
    total = jnp.zeros(message.shape, jnp.float32)
    for turn in (-1, 0, 2, 3):
        at = jnp.where(c >= STRIP_SOURCE_AT, c - STRIP_SOURCE_AT, c - STRIP_AT) - turn
        fits = (c >= STRIP_AT) & (at >= 0) & (at < 2) & (place == turn)
        total = total + jnp.where(fits, turned(message, turn), 0.0)
    return total


def pack_columns(parts, band, oy_hbm, nest, source, parent_hbm, parent_source_hbm, *rest):
    outs = rest[: parts - 1]
    old_buf, src_buf, parent, parent_source, oy_ref, sems, field_sems = rest[parts - 1 :]
    levels, rows, cols = nest.shape
    parent_cols = parent.shape[2]
    me = lax.axis_index("gy")
    sides = [1] if parts == 2 else [1, parts - 1]
    fields = [
        pltpu.make_async_copy(ref, buf, field_sems.at[at])
        for at, (ref, buf) in enumerate(
            ((oy_hbm, oy_ref), (parent_hbm, parent), (parent_source_hbm, parent_source))
        )
    ]
    for copy in fields:
        copy.start()
    copies = []
    for at, step in enumerate(sides):
        right = (me == 0) if parts == 2 else jnp.bool_(step == 1)
        start = pl.multiple_of(jnp.where(right, cols - LANES, 0), LANES)
        pair = [
            pltpu.make_async_copy(
                ref.at[:, :, pl.ds(start, LANES)], buf.at[at], sems.at[at, which]
            )
            for which, (ref, buf) in enumerate(((nest, old_buf), (source, src_buf)))
        ]
        for copy in pair:
            copy.start()
        copies.append((right, pair))
    for copy in fields:
        copy.wait()
    oy = oy_ref[0]
    lane = iota((parent.shape[1], LANES), 1)
    for step in range(1, parts):
        out = outs[step - 1]
        part = edge_strip(lax.rem(me + step, parts), band, oy, parent, parent_source)
        if step not in sides:
            out[...] = part
            continue
        at = sides.index(step)
        right, pair = copies[at]
        first = jnp.where(right, LANES - 3, 0)
        outer = jnp.where(right, LANES - 1, 0)
        for level in range(levels):
            edge = jnp.where(
                right, tile(parent, level, parent_cols // LANES - 1), tile(parent, level, 0)
            )
            edge = jnp.where(lane == outer, edge, 0.0)
            turn = (LANES + PARENT_AT + STRIDE * level - outer) & (LANES - 1)
            part = part + pltpu.roll(edge, turn, 1)
        for copy in pair:
            copy.wait()
        fine = iota((rows, LANES), 1) - first
        wanted = (fine >= 0) & (fine < 3)
        total = jnp.zeros((rows, LANES), jnp.float32)
        for level in range(levels):
            for buf, shift in ((old_buf, 0), (src_buf, SOURCE_AT)):
                value = jnp.where(wanted, buf[at, level], 0.0)
                turn = (LANES + STRIDE * level + shift - first) & (LANES - 1)
                total = total + pltpu.roll(value, turn, 1)
        out[...] = total
        out[: part.shape[0], :] += part


def three_terms(value):
    terms = []
    for _ in range(3):
        term = value.astype(jnp.bfloat16)
        terms.append(term)
        value = value - term.astype(jnp.float32)
    return terms


def select_rows(selector, value):
    selector = selector.astype(jnp.bfloat16)
    high, middle, low = (
        jnp.dot(selector, term, preferred_element_type=jnp.float32)
        for term in three_terms(value)
    )
    return high + (middle + low)


def select_columns(value, selector):
    selector = selector.astype(jnp.bfloat16)
    high, middle, low = (
        jnp.dot(term, selector, preferred_element_type=jnp.float32)
        for term in three_terms(value)
    )
    return high + (middle + low)


def sum_rows(ref, count):
    first, second, third = (ref[pl.ds(at, count, RATIO), :] for at in range(RATIO))
    return first + second + third


def inner_substep(coefs, here, source, there):
    levels, rows, cols = here.shape
    sub = iota((8, cols), 0)
    tiles = rows // 8

    def one_level(level):
        ch = coefs[0, level]
        cv = coefs[1, level]
        centre = 1.0 - 4.0 * ch - 2.0 * cv
        below = jnp.maximum(level - 1, 0)
        above = jnp.minimum(level + 1, levels - 1)
        cv_below = jnp.where(level > 0, cv, 0.0)
        cv_above = jnp.where(level < levels - 1, cv, 0.0)

        def row_tile(t):
            t = t % tiles
            return here[level, 8 * t : 8 * t + 8, :]

        down_before = pltpu.roll(row_tile(-1), 1, 0)
        now = row_tile(0)
        up_now = pltpu.roll(now, 7, 0)
        for t in range(tiles):
            following = row_tile(t + 1)
            down_now = pltpu.roll(now, 1, 0)
            up_next = pltpu.roll(following, 7, 0)
            around = jnp.where(sub == 0, down_before, down_now) + jnp.where(
                sub == 7, up_next, up_now
            )
            around = around + (pltpu.roll(now, 1, 1) + pltpu.roll(now, cols - 1, 1))
            span = slice(8 * t, 8 * t + 8)
            stacked = cv_below * here[below, span, :] + cv_above * here[above, span, :]
            there[level, span, :] = centre * now + ch * around + (stacked + source[level, span, :])
            down_before, now, up_now = down_now, following, up_next

    def two_levels(pair, carry):
        one_level(2 * pair)
        one_level(2 * pair + 1)
        return carry

    lax.fori_loop(0, levels // 2, two_levels, 0)


def spread_coefs(parent_coefs, coefs, out):
    levels = out.shape[2]
    lane = iota((levels, LANES), 1)
    row = iota((levels, LANES), 0)
    for at, ref in enumerate((parent_coefs, coefs)):
        for which in range(2):
            packed = jnp.full(lane.shape, ref[which, 0], jnp.float32)
            rows = packed
            for level in range(1, levels):
                packed = jnp.where(lane >= STRIDE * level, ref[which, level], packed)
                rows = jnp.where(row == level, ref[which, level], rows)
            out[0, 2 * at + which] = packed
            out[1, 2 * at + which] = rows


def inner_first(
    band,
    oy_ref,
    parent_coefs,
    coefs,
    nest,
    source,
    parent,
    parent_source,
    strip,
    first,
    spread,
    oy_rows,
):
    oy = oy_ref[0]
    oy_rows[...] = jnp.full(oy_rows.shape, oy, jnp.int32)
    spread_coefs(parent_coefs, coefs, spread)
    strip[...] = edge_strip(lax.axis_index("gy"), band, oy, parent, parent_source)
    inner_substep(coefs, nest, source, first)


def own_windows(parts, nest, source, y_left, y_right, window_old, window_src):
    levels, rows, cols = nest.shape
    pieces = cols // LANES
    me = lax.axis_index("gy")
    for level in range(levels):
        for buf, field, shift in ((window_old, nest, 0), (window_src, source, SOURCE_AT)):
            for window, first, turn in ((0, 0, 3), (1, rows - 8, 5)):
                tiles = [
                    field[level, first : first + 8, piece * LANES : (piece + 1) * LANES]
                    for piece in range(pieces)
                ]
                tiles = with_columns(
                    tiles,
                    y_left[first : first + 8, :],
                    y_right[first : first + 8, :],
                    me,
                    parts,
                    STRIDE * level + shift,
                )
                for piece, value in enumerate(tiles):
                    buf[level, window, :, piece * LANES : (piece + 1) * LANES] = pltpu.roll(
                        value, turn, 0
                    )


def inner_rest(
    parts,
    coefs,
    nest,
    first,
    source,
    y_left,
    y_right,
    after_pack,
    third,
    packs,
    window_old,
    window_src,
    sums,
    second,
    split,
):
    levels, rows, cols = nest.shape
    own_windows(parts, nest, source, y_left, y_right, window_old, window_src)
    lane = iota((rows, LANES), 1)
    for at, ref in enumerate((nest, source)):
        left = jnp.zeros(lane.shape, jnp.float32)
        right = jnp.zeros(lane.shape, jnp.float32)
        for level in range(levels):
            value = jnp.where(lane < RIGHT_OWN, tile(ref, level, 0), 0.0)
            left = left + turned(value, STRIDE * level + LEFT_AT)
            value = jnp.where(lane >= LANES - RIGHT_OWN, tile(ref, level, cols // LANES - 1), 0.0)
            right = right + turned(value, STRIDE * level + RIGHT_OWN)
        packs[2 * at] = left
        packs[2 * at + 1] = right
    inner_substep(coefs, first, source, second)
    inner_substep(coefs, second, source, third)
    for level in range(levels):
        for piece in range(cols // LANES):
            split[piece, level * rows : (level + 1) * rows, :] = tile(third, level, piece)
    for piece in range(cols // LANES):
        sums[piece] = sum_rows(split.at[piece], levels * rows // RATIO)


def with_columns(tiles, left, right, me, parts, place):
    lane = iota(left.shape, 1)
    from_right = turned(right, -place)
    from_left = turned(left, -3 - place)
    if parts == 2:
        tiles[0] = jnp.where((lane < 3) & (me == 0), from_right, tiles[0])
        tiles[-1] = jnp.where((lane >= LANES - 3) & (me == 1), from_left, tiles[-1])
        return tiles
    extra = jnp.where(lane < 3, from_right, jnp.where(lane >= LANES - 3, from_left, 0.0))
    return tiles + [extra]


def pack_rows(
    parts, old_top, old_end, src_top, src_end, par_top, par_end, own_strip, oy_rows, *rest
):
    columns = rest[: parts - 1]
    across, within, far, strip_out, both = rest[parts - 1 :]
    core = lax.axis_index("gz")
    up, down = both.at[core], both.at[1 - core]
    levels, _, cols = old_top.shape
    me = lax.axis_index("gy")
    left, right = columns[0], columns[-1]
    rows = left.shape[0]
    strip_rows = own_strip.shape[0]
    lane = iota((strip_rows, LANES), 1)
    strips = own_strip[...]
    if parts == 2:
        oy = jnp.concatenate([oy_rows[...]] * (strip_rows // 8), axis=0)
        strips = strips + across_border(left[:strip_rows, :], oy, par_top.shape[2], me)
    else:
        for message in columns:
            strips = strips + message[:strip_rows, :]
    c = lane & (STRIDE - 1)
    strips = jnp.where(c >= STRIP_AT, strips, 0.0)
    strips = jnp.where(c == PARENT_AT, left[:strip_rows, :], strips)
    strips = jnp.where(c == PARENT_AT + 1, turned(right[:strip_rows, :], 1), strips)
    strip_out[...] = strips
    far[...] = strips[:8]
    pieces = cols // LANES
    for out, old, src, first, at, src_at in (
        (up, old_end, src_end, rows - 8, 5, 6),
        (down, old_top, src_top, 0, 0, 0),
    ):
        y_left = left[first : first + 8, :]
        y_right = right[first : first + 8, :]
        for level in range(levels):
            for ref, shift, row, count, base in (
                (old, 0, at, 3, 0),
                (src, SOURCE_AT, src_at, 2, SOURCE_ROW),
            ):
                tiles = [tile(ref, level, piece) for piece in range(pieces)]
                tiles = with_columns(
                    tiles, y_left, y_right, me, parts, STRIDE * level + shift
                )
                for piece, value in enumerate(tiles):
                    out[
                        base + count * level : base + count * (level + 1),
                        piece * LANES : (piece + 1) * LANES,
                    ] = value[row : row + count]
    parent_cols = par_top.shape[2]
    for level in range(levels):
        up[TAIL_ROW + level : TAIL_ROW + level + 1, :parent_cols] = par_end[level, 7:8, :]
        down[TAIL_ROW + level : TAIL_ROW + level + 1, :parent_cols] = par_top[level, 0:1, :]
    up[TAIL_ROW : TAIL_ROW + 8, parent_cols : parent_cols + LANES] = strips[strip_rows - 8 :]
    down[TAIL_ROW : TAIL_ROW + 8, parent_cols : parent_cols + LANES] = strips[:8]
    down[TAIL_ROW + 8 : TAIL_ROW + 16, :LANES] = strips[8:16]
    down[TAIL_ROW + 8 : TAIL_ROW + 16, LANES : 2 * LANES] = strips[16:24]
    within[...] = both[0]
    across[...] = both[1]


def edges(
    parts,
    parent_cols,
    ox_ref,
    spread,
    sums,
    packs,
    window_old,
    window_src,
    strips,
    across,
    within,
    far,
    y_left,
    y_right,
    sides,
    windows,
    coarse_out,
    far_out,
    both,
    ping,
    pong,
    src,
):
    levels = ping.shape[0]
    width = ping.shape[3]
    rows = packs.shape[1]
    cols = sums.shape[0] * LANES
    pieces = cols // LANES
    me = lax.axis_index("gy")
    core = lax.axis_index("gz")
    both[0] = within[...]
    both[1] = across[...]
    before, after = both.at[1 - core], both.at[core]
    is_south = me == 0
    is_north = me == parts - 1

    far_out[...] = far[...]
    sub = iota((8, LANES), 0)
    old = jnp.concatenate(
        [
            strips[...],
            after[TAIL_ROW : TAIL_ROW + 8, parent_cols : parent_cols + LANES],
            after[TAIL_ROW + 8 : TAIL_ROW + 16, :LANES],
            after[TAIL_ROW + 8 : TAIL_ROW + 16, LANES : 2 * LANES],
            jnp.where(
                sub == 7,
                before[TAIL_ROW : TAIL_ROW + 8, parent_cols : parent_cols + LANES],
                0.0,
            ),
        ],
        axis=0,
    )
    count = old.shape[0]

    def packed_coef(which, height):
        return jnp.concatenate([spread[0, which]] * (height // 8), axis=0)

    def stacked(value):
        lane = iota(value.shape, 1)
        below = jnp.where(lane >= STRIDE, turned(value, STRIDE), 0.0)
        return below + jnp.where(lane < STRIDE * (levels - 1), turned(value, -STRIDE), 0.0)

    def around(value):
        return (
            pltpu.roll(value, 1, 0)
            + pltpu.roll(value, value.shape[0] - 1, 0)
            + turned(value, 1)
            + turned(value, -1)
        )

    diff = (
        packed_coef(0, count) * (around(old) - 4.0 * old)
        + packed_coef(1, count) * (stacked(old) - 2.0 * old)
        + turned(old, STRIP_AT - STRIP_SOURCE_AT)
    )
    index = iota((rows + 16, count), 0)
    nest_row = jnp.where(index < rows, index, jnp.where(index < rows + 8, index - rows - 3, index - 13))
    parent_row = ((nest_row + 3) * 171 >> 9) - 1 + ox_ref[0]
    pick = (iota((rows + 16, count), 1) == parent_row).astype(jnp.float32)
    picked = select_rows(pick, jnp.concatenate([old, diff], axis=1))
    picked_old, picked_diff = picked[:, :LANES], picked[:, LANES:]

    lane = iota((rows, LANES), 1)
    c = lane & (STRIDE - 1)
    rim_first = jnp.where(is_south, LEFT_AT, RIGHT_OWN - RIM)
    in_rim = (c >= rim_first) & (c < rim_first + RIM)
    at = lane - c + STRIP_AT + jnp.where(c >= rim_first + 3, 2, 1)
    rim_old = jnp.take_along_axis(picked_old[:rows], at, axis=1)
    rim_diff = jnp.take_along_axis(picked_diff[:rows], at, axis=1)
    ch = packed_coef(2, rows)
    cv = packed_coef(3, rows)
    centre = 1.0 - 4.0 * ch - 2.0 * cv
    left = jnp.where(c < 3, y_left[...], packs[0])
    left_src = jnp.where(c < 3, turned(y_left[...], -SOURCE_AT), packs[2])
    right = jnp.where(c >= RIGHT_OWN, turned(y_right[...], RIGHT_OWN), packs[1])
    right_src = jnp.where(c >= RIGHT_OWN, turned(y_right[...], RIGHT_OWN - SOURCE_AT), packs[3])
    for side, (value, forcing, rim) in enumerate(
        (
            (left, left_src, in_rim & is_south),
            (right, right_src, in_rim & is_north),
        )
    ):
        for substep in range(1, SUBSTEPS + 1):
            value = centre * value + ch * around(value) + (cv * stacked(value) + forcing)
            value = jnp.where(rim, rim_old + (substep / SUBSTEPS) * rim_diff, value)
        sides[side, :rows, :] = value

    sub = iota((8, width), 0)
    lane = iota((8, LANES), 1)
    ping[...] = window_old[...]
    src[...] = window_src[...]
    for level in range(levels):
        for buf, n, base in ((ping, 3, 0), (src, 2, SOURCE_ROW)):
            rows_of = slice(base + n * level, base + n * (level + 1))
            buf[level, 0, 3 - n : 3, :] = before[rows_of, :]
            buf[level, 1, 5 : 5 + n, :] = after[rows_of, :]
    rim_first = jnp.where(is_south, 0, LANES - RIM)
    column = STRIP_AT + jnp.where((lane >= rim_first + 3) & (lane < rim_first + RIM), 2, 1)
    rims = {}
    for level in range(levels):
        for window in range(2):
            span = slice(rows + 8 * window, rows + 8 * window + 8)
            at = column + STRIDE * level
            rims[level, window] = (
                jnp.take_along_axis(picked_old[span], at, axis=1),
                jnp.take_along_axis(picked_diff[span], at, axis=1),
            )
    for substep in range(1, SUBSTEPS + 1):
        here, there = (ping, pong) if substep % 2 else (pong, ping)
        there = windows if substep == SUBSTEPS else there
        low = 0 if substep == SUBSTEPS or parts > 2 else 3
        south = (lane >= low) & (lane < RIM) & is_south
        north = (lane >= LANES - RIM) & (lane < LANES - low) & is_north
        weight = substep / SUBSTEPS
        for level in range(levels):
            c_h, c_v = (
                jnp.concatenate([spread[1, which, level : level + 1, :]] * (width // LANES), axis=1)
                for which in (2, 3)
            )
            c_0 = 1.0 - 4.0 * c_h - 2.0 * c_v
            for window in range(2):
                now = here[level, window]
                up = pltpu.roll(now, 1, 0)
                down = pltpu.roll(now, 7, 0)
                if substep == 1:
                    beyond_row = window_old[level, window]
                    if window == 0:
                        down = jnp.where(sub == 7, pltpu.roll(beyond_row, 7, 0), down)
                    else:
                        up = jnp.where(sub == 0, pltpu.roll(beyond_row, 1, 0), up)
                beside = pltpu.roll(now, 1, 1) + pltpu.roll(now, width - 1, 1)
                value = c_0 * now + c_h * ((up + down) + beside) + src[level, window]
                near = [here[at, window] for at in (level - 1, level + 1) if 0 <= at < levels]
                value = value + c_v * sum(near[1:], near[0])
                rim_o, rim_d = rims[level, window]
                rim = rim_o + weight * rim_d
                for piece in range(width // LANES):
                    span = slice(piece * LANES, (piece + 1) * LANES)
                    part = value[:, span]
                    if piece == 0:
                        part = jnp.where(south, rim, part)
                    if piece == pieces - 1:
                        part = jnp.where(north, rim, part)
                    there[level, window, :, span] = part

    parent_rows = rows // RATIO
    lane = iota((parent_rows, LANES), 1)
    row = iota((parent_rows, LANES), 0)
    side_sums = [sum_rows(sides.at[side], parent_rows) for side in range(2)]
    replaced = [[] for _ in range(pieces)]
    for level in range(levels):
        span = slice(level * parent_rows, (level + 1) * parent_rows)
        top = windows[level, 0, 3:4, :] + windows[level, 0, 4:5, :] + windows[level, 0, 5:6, :]
        end = windows[level, 1, 2:3, :] + windows[level, 1, 3:4, :] + windows[level, 1, 4:5, :]
        for piece in range(pieces):
            value = sums[piece, span, :]
            if piece == 0:
                fixed = turned(side_sums[0], -STRIDE * level - LEFT_AT)
                value = jnp.where(lane < FIXED, fixed, value)
            if piece == pieces - 1:
                fixed = turned(side_sums[1], -STRIDE * level - RIGHT_OWN)
                value = jnp.where(lane >= LANES - FIXED, fixed, value)
            across_piece = slice(piece * LANES, (piece + 1) * LANES)
            value = jnp.where(row == 0, top[:, across_piece], value)
            value = jnp.where(row == parent_rows - 1, end[:, across_piece], value)
            replaced[piece].append(value)
    foot = cols // RATIO
    offset = iota((cols, foot), 0) - RATIO * iota((cols, foot), 1)
    gather = ((offset >= 0) & (offset < RATIO)).astype(jnp.float32)
    means = select_columns(
        jnp.concatenate([jnp.concatenate(values, axis=0) for values in replaced], axis=1), gather
    ) * (1.0 / 9.0)
    coarse_out[...] = means.reshape(coarse_out.shape)


def put_together(third, sides, windows, result):
    levels, rows, cols = third.shape
    pieces = cols // LANES
    lane = iota((rows, LANES), 1)
    sub = iota((8, cols), 0)
    for level in range(levels):
        fixed = turned(sides[0, :rows, :], -STRIDE * level - LEFT_AT)
        result[level, :, :LANES] = jnp.where(lane < FIXED, fixed, tile(third, level, 0))
        for piece in range(1, pieces - 1):
            result[level, :, piece * LANES : (piece + 1) * LANES] = tile(third, level, piece)
        fixed = turned(sides[1, :rows, :], -STRIDE * level - RIGHT_OWN)
        result[level, :, cols - LANES :] = jnp.where(
            lane >= LANES - FIXED, fixed, tile(third, level, pieces - 1)
        )
        top = pltpu.roll(windows[level, 0, :, :cols], 5, 0)
        result[level, :8, :] = jnp.where(sub < 3, top, result[level, :8, :])
        end = pltpu.roll(windows[level, 1, :, :cols], 3, 0)
        result[level, rows - 8 :, :] = jnp.where(sub >= 5, end, result[level, rows - 8 :, :])


def parent_step(
    parts,
    band,
    ox_ref,
    oy_ref,
    spread,
    third,
    sides,
    windows,
    parent,
    source,
    within,
    across,
    y_left,
    y_right,
    out,
    nest_out,
    late,
    tail,
    result,
    sem,
):
    put_together(third, sides, windows, result)
    store = pltpu.make_async_copy(result, nest_out, sem)
    store.start()
    core = lax.axis_index("gz")
    levels, rows, cols = parent.shape
    tail[0] = within[TAIL_ROW : TAIL_ROW + levels, : cols + LANES]
    tail[1] = across[TAIL_ROW : TAIL_ROW + levels, : cols + LANES]
    me = lax.axis_index("gy")
    is_last = ox_ref[0] == rows - 1
    wide = iota((1, cols), 1)
    south = (wide == oy_ref[0] + 2 - me * cols) & is_last
    north = (wide == oy_ref[0] + band - 3 - me * cols) & is_last
    row = iota((rows, cols), 0)
    lane = iota((rows, cols), 1)
    has_left = me > 0
    has_right = me < parts - 1
    left = y_left[:rows, :]
    right = y_right[:rows, :]
    zero = jnp.zeros((rows, cols), jnp.float32)
    for level in range(levels):
        now = parent[level]
        at = STRIDE * level + PARENT_AT
        from_left = left[:, at : at + 1]
        from_right = right[:, at : at + 1]
        top = tail[1 - core, level : level + 1, :cols]
        end = tail[core, level : level + 1, :cols]
        around = (
            jnp.where(row == 0, top, pltpu.roll(now, 1, 0))
            + jnp.where(row == rows - 1, end, pltpu.roll(now, rows - 1, 0))
            + jnp.where(
                lane == 0, jnp.where(has_left, from_left, 0.0), pltpu.roll(now, 1, 1)
            )
            + jnp.where(
                lane == cols - 1,
                jnp.where(has_right, from_right, 0.0),
                pltpu.roll(now, cols - 1, 1),
            )
        )
        stacked = (parent[level - 1] if level > 0 else zero) + (
            parent[level + 1] if level < levels - 1 else zero
        )
        ch, cv = (
            jnp.concatenate([spread[1, which, level : level + 1, :]] * (cols // LANES), axis=1)
            for which in (0, 1)
        )
        out[level] = (
            (1.0 - 4.0 * ch - 2.0 * cv) * now + ch * around + (cv * stacked + source[level])
        )
        at = cols + STRIDE * level + PARENT_AT
        before_end = jnp.where(
            wide == 0, tail[core, 0:1, at : at + 1], pltpu.roll(end, 1, 1)
        )
        after_end = jnp.where(
            wide == cols - 1, tail[core, 0:1, at + 1 : at + 2], pltpu.roll(end, cols - 1, 1)
        )
        nest_ch = spread[1, 2, level : level + 1, :]
        nest_ch = jnp.concatenate([nest_ch] * (cols // LANES), axis=1)
        share = nest_ch * nest_ch * ch * (1.0 / SUBSTEPS)
        late[level : level + 1, :] = (share * (1.0 / (RATIO * RATIO))) * (
            jnp.where(south, before_end, 0.0) + jnp.where(north, after_end, 0.0)
        )
    store.wait()


def merge(parts, band, ox_ref, oy_ref, late, step, nest, spread, beyond, *rest):
    arrived = rest[1 : 2 * parts]
    out, nest_out, joined, corner, sem, merged, out_sems = rest[2 * parts :]
    levels, rows, cols = step.shape
    foot = rest[0].shape[2]
    me = lax.axis_index("gy")

    @pl.when((ox_ref[0] == rows - 1) & ((me == 0) | (me == parts - 1)))
    def _():
        nest_rows, nest_cols = nest.shape[1:]
        first = pl.multiple_of(jnp.where(me == 0, 0, nest_cols - LANES), LANES)
        place = (slice(None), pl.ds(nest_rows - 8, 8), pl.ds(first, LANES))
        load = pltpu.make_async_copy(nest_out.at[place], corner, sem)
        load.start()
        load.wait()
        sub = iota((8, LANES), 0)
        lane = iota((8, LANES), 1)
        cell = (sub == 7) & (lane == jnp.where(me == 0, RIM, LANES - RIM - 1))
        for level in range(levels):
            at = STRIDE * level + STRIP_AT
            value = jnp.where(me == 0, beyond[0:1, at + 2 : at + 3], beyond[0:1, at + 1 : at + 2])
            nest_ch = spread[1, 2, level : level + 1, :]
            share = nest_ch * nest_ch * spread[1, 0, level : level + 1, :] * (1.0 / SUBSTEPS)
            corner[level] += jnp.where(cell, share * value, 0.0)
        again = pltpu.make_async_copy(corner, nest_out.at[place], sem)
        again.start()
        again.wait()

    ox = ox_ref[0]
    oy = oy_ref[0]
    joined[0, :, rows:, :] = rest[0][...]
    if parts == 2:
        mixed, straight, other = arrived
        joined[0, :, :rows, :] = straight[...]
        joined[1, :, :rows, :] = jnp.where(me == 0, mixed[...], other[...])
        joined[1, :, rows:, :] = jnp.where(me == 0, other[...], mixed[...])
    else:
        for k in range(parts):
            joined[k, :, :rows, :] = arrived[k][...]
        for k in range(1, parts):
            joined[k, :, rows:, :] = arrived[parts + k - 1][...]
    lane = iota((rows, LANES), 1)
    row = iota((rows, LANES), 0)
    stores = []
    for level in range(levels):
        values = [tile(step, level, piece) for piece in range(cols // LANES)]
        for k in range(parts):
            source = lax.rem(me + parts - k, parts)
            block = joined[k, level, pl.ds(rows - ox, rows), :]
            begin = oy + source * foot - me * cols
            block = pltpu.roll(block, (16384 + begin) & (LANES - 1), 1)
            low = jnp.maximum(source * foot, 2)
            high = jnp.minimum((source + 1) * foot, band - 2)
            for piece in range(cols // LANES):
                at = lane + (piece * LANES + me * cols - oy)
                values[piece] = jnp.where((at >= low) & (at < high), block, values[piece])
        for piece, value in enumerate(values):
            term = late[level : level + 1, piece * LANES : (piece + 1) * LANES]
            value = value + jnp.where(row == rows - 2, term, 0.0)
            merged[level, :, piece * LANES : (piece + 1) * LANES] = value
        stores.append(pltpu.make_async_copy(merged.at[level], out.at[level], out_sems.at[level]))
        stores[-1].start()
    for copy in stores:
        copy.wait()


def shifted(value, axis, steps):
    count = lax.axis_size(axis)
    pairs = [(source, (source + steps) % count) for source in range(count)]
    return lax.ppermute(value, axis, pairs)


def shards(
    parent_old, parent_source, parent_coefs, nest_old, nest_source, nest_coefs, offset_x, offset_y
):
    parts = lax.axis_size("gy")
    along = ("gx", "gz")
    levels, parent_rows, parent_cols = parent_old.shape
    _, rows, cols = nest_old.shape
    foot = cols // RATIO
    band = foot * parts
    width = cols if parts == 2 else cols + LANES
    height = TAIL_ROW + 16
    f32 = jnp.float32
    shape = jax.ShapeDtypeStruct
    anywhere = pl.BlockSpec(memory_space=pl.ANY)
    in_hbm = pl.BlockSpec(memory_space=pltpu.HBM)
    sides = 1 if parts == 2 else 2
    if parts == 2:
        packed = [
            pl.pallas_call(
                pack_pair,
                out_shape=VMEM((rows, LANES), f32),
                in_specs=[in_hbm] * 4,
                out_specs=whole(),
                scratch_shapes=[
                    VMEM((2, levels, rows, LANES), f32),
                    VMEM((2, levels, parent_rows, LANES), f32),
                    pltpu.SemaphoreType.DMA((4,)),
                ],
                compiler_params=params(MOST),
                cost_estimate=cost(200000, 800000),
                name="pack_pair",
            )(nest_old, nest_source, parent_old, parent_source)
        ]
    else:
        packed = pl.pallas_call(
            functools.partial(pack_columns, parts, band),
            out_shape=[
                shape((rows if k in (1, parts - 1) else parent_rows, LANES), f32)
                for k in range(1, parts)
            ],
            in_specs=[in_hbm] * 5,
            out_specs=[whole()] * (parts - 1),
            scratch_shapes=[
                VMEM((sides, levels, rows, LANES), f32),
                VMEM((sides, levels, rows, LANES), f32),
                VMEM(parent_old.shape, f32),
                VMEM(parent_old.shape, f32),
                pltpu.SMEM(offset_y.shape, jnp.int32),
                pltpu.SemaphoreType.DMA((sides, 2)),
                pltpu.SemaphoreType.DMA((3,)),
            ],
            compiler_params=params(MOST),
            cost_estimate=cost(200000, 1000000),
            name="pack_columns",
        )(offset_y, nest_old, nest_source, parent_old, parent_source)
    columns = [shifted(packed[k - 1], "gy", k) for k in range(1, parts)]
    own_strip, first, spread, oy_rows = pl.pallas_call(
        functools.partial(inner_first, band),
        out_shape=[
            shape((parent_rows, LANES), f32),
            shape(nest_old.shape, f32),
            shape((2, 4, levels, LANES), f32),
            shape((8, LANES), jnp.int32),
        ],
        in_specs=[scalars()] * 3 + [whole()] * 4,
        out_specs=[whole()] * 4,
        compiler_params=params(),
        cost_estimate=cost(4000000, 3000000),
        name="inner_first",
    )(
        offset_y,
        parent_coefs,
        nest_coefs,
        nest_old,
        nest_source,
        parent_old,
        parent_source,
    )

    def block(ref, last):
        count = ref.shape[1] // 8 - 1 if last else 0
        return pl.BlockSpec((levels, 8, ref.shape[2]), lambda i, c=count: (0, c, 0))

    def full(extent):
        return pl.BlockSpec(extent, lambda i: (0,) * len(extent))

    outs = [
        shape((height, width), f32),
        shape((height, width), f32),
        shape((8, LANES), f32),
        shape((parent_rows, LANES), f32),
    ]
    across, within, far, strips = pl.pallas_call(
        functools.partial(pack_rows, parts),
        out_shape=outs,
        grid=(1,),
        in_specs=[
            block(nest_old, False),
            block(nest_old, True),
            block(nest_old, False),
            block(nest_old, True),
            block(parent_old, False),
            block(parent_old, True),
            full(own_strip.shape),
            full(oy_rows.shape),
        ]
        + [full(message.shape) for message in columns],
        out_specs=[full(out.shape) for out in outs],
        scratch_shapes=[VMEM((2, height, width), f32)],
        compiler_params=params(),
        cost_estimate=cost(100000, 700000),
        name="pack_rows",
    )(nest_old, nest_old, nest_source, nest_source, parent_old, parent_old, own_strip, oy_rows, *columns)
    across = swapped(across, 1)
    within = swapped(within, 0)
    third, packs, window_old, window_src, sums = pl.pallas_call(
        functools.partial(inner_rest, parts),
        out_shape=[
            shape(nest_old.shape, f32),
            shape((4, rows, LANES), f32),
            shape((levels, 2, 8, width), f32),
            shape((levels, 2, 8, width), f32),
            shape((cols // LANES, levels * parent_rows, LANES), f32),
        ],
        in_specs=[scalars()] + [whole()] * 5 + [anywhere],
        out_specs=[whole()] * 5,
        scratch_shapes=[
            VMEM(nest_old.shape, f32),
            VMEM((cols // LANES, levels * rows + 8, LANES), f32),
        ],
        compiler_params=params(),
        cost_estimate=cost(8000000, 6000000),
        name="inner_rest",
    )(nest_coefs, nest_old, first, nest_source, columns[0], columns[-1], strips)
    sides, windows, coarse, far = pl.pallas_call(
        functools.partial(edges, parts, parent_cols),
        out_shape=[
            shape((2, rows + 8, LANES), f32),
            shape((levels, 2, 8, width), f32),
            shape((levels, parent_rows, foot), f32),
            shape((8, LANES), f32),
        ],
        in_specs=[scalars()] + [whole()] * 11,
        out_specs=[whole()] * 4,
        scratch_shapes=[
            VMEM((2, height, width), f32),
            VMEM((levels, 2, 8, width), f32),
            VMEM((levels, 2, 8, width), f32),
            VMEM((levels, 2, 8, width), f32),
        ],
        compiler_params=params(),
        cost_estimate=cost(4000000, 3000000),
        name="edges",
    )(
        offset_x,
        spread,
        sums,
        packs,
        window_old,
        window_src,
        strips,
        across,
        within,
        far,
        columns[0],
        columns[-1],
    )
    if parts == 2:
        arrived = [
            shifted_both(coarse, 1, (0, 1)),
            shifted(coarse, along, 1),
            shifted_both(coarse, 1, (1, 0)),
        ]
    else:
        arrived = [shifted(coarse, along, 1)]
        arrived += [shifted_both(coarse, k) for k in range(1, parts)]
        arrived += [shifted(coarse, "gy", k) for k in range(1, parts)]
    beyond = shifted(far, along, -2)
    step, nest_stored, late = pl.pallas_call(
        functools.partial(parent_step, parts, band),
        out_shape=[
            shape(parent_old.shape, f32),
            shape(nest_old.shape, f32),
            shape((levels, parent_cols), f32),
        ],
        in_specs=[scalars()] * 2 + [whole()] * 10,
        out_specs=[whole(), in_hbm, whole()],
        scratch_shapes=[
            VMEM((2, levels, parent_cols + LANES), f32),
            VMEM(nest_old.shape, f32),
            pltpu.SemaphoreType.DMA,
        ],
        compiler_params=params(),
        cost_estimate=cost(800000, 2500000),
        name="parent_step",
    )(
        offset_x,
        offset_y,
        spread,
        third,
        sides,
        windows,
        parent_old,
        parent_source,
        within,
        across,
        columns[0],
        columns[-1],
    )
    parent_new, nest_new = pl.pallas_call(
        functools.partial(merge, parts, band),
        out_shape=[shape(parent_old.shape, f32), shape(nest_old.shape, f32)],
        in_specs=[scalars()] * 2 + [whole()] * 2 + [in_hbm] + [whole()] * (2 + 2 * parts),
        out_specs=[in_hbm, in_hbm],
        scratch_shapes=[
            VMEM((parts, levels, 2 * parent_rows, foot), f32),
            VMEM((levels, 8, LANES), f32),
            pltpu.SemaphoreType.DMA,
            VMEM(parent_old.shape, f32),
            pltpu.SemaphoreType.DMA((levels,)),
        ],
        input_output_aliases={4: 1},
        compiler_params=params(),
        cost_estimate=cost(200000, 800000),
        name="merge",
    )(offset_x, offset_y, late, step, nest_stored, spread, beyond, coarse, *arrived)
    return (parent_new, nest_new)


def swapped(value, first):
    along = ("gx", "gz")
    count = lax.axis_size(along)
    pairs = []
    for at in range(first, count, 2):
        pairs += [(at, (at + 1) % count), ((at + 1) % count, at)]
    return lax.ppermute(value, along, pairs)


def shifted_both(value, steps, rows=None):
    sizes = [lax.axis_size(axis) for axis in ("gx", "gy", "gz")]
    gx, gy, gz = sizes
    pairs = []
    for x in range(gx):
        for y in range(gy):
            for z in range(gz):
                place = (x * gz + z + (1 if rows is None else rows[y])) % (gx * gz)
                target = (place // gz * gy + (y + steps) % gy) * gz + place % gz
                pairs.append(((x * gy + y) * gz + z, target))
    return lax.ppermute(value, ("gx", "gy", "gz"), pairs)


def solution(mesh):
    return jax.shard_map(
        shards,
        mesh=mesh,
        in_specs=(
            P(None, ("grp", "gx", "gz"), "gy"),
            P(None, ("grp", "gx", "gz"), "gy"),
            P(),
            P(None, ("grp", "gx", "gz"), "gy"),
            P(None, ("grp", "gx", "gz"), "gy"),
            P(),
            P("grp"),
            P("grp"),
        ),
        out_specs=(P(None, ("grp", "gx", "gz"), "gy"), P(None, ("grp", "gx", "gz"), "gy")),
        check_vma=False,
    )
```
